32 devices in a mesh: wide: 8 (over z, x), narrow: 4 (over y, core).
Axes of the slice: x: 2, y: 2, z: 4, core: 2. Of those that a mesh axis runs over, the one named last changes fastest.
Arguments:
- particles_first: bfloat16 [32, 384, 1536], P(('wide', 'narrow')), may hold values from -24 to 24
- particles_second: bfloat16 [32, 1536, 384], P(('wide', 'narrow')), may hold values from -24 to 24
- pool_images: bfloat16 [8, 197, 384], replicated, may hold values from -6 to 6
- pool_targets: bfloat16 [8, 197, 384], replicated, may hold values from -6 to 6
- batch_index: int32 [32, 8], P(('wide', 'narrow')), may hold values from 0 to 7
- kernel_scale: float32 [1], replicated, may hold values from 589824 to 1179648
Outputs:
- attract_first: bfloat16 [32, 384, 1536], P(('wide', 'narrow'))
- attract_second: bfloat16 [32, 1536, 384], P(('wide', 'narrow'))
- spread_first: bfloat16 [32, 384, 1536], P(('wide', 'narrow'))
- spread_second: bfloat16 [32, 1536, 384], P(('wide', 'narrow'))
The draws below stay inside these ranges and needn't reach their ends.
All inputs are finite; a program needn't handle non-finite values.
Results may differ from the reference program's by a relative error of at most 0.005.
Values may be sent and summed in bfloat16 or wider, within the bound.
No kernel may reach another device: no remote copies, remote signals or barrier semaphores. Data moves between devices by JAX's collectives and lax.ppermute only.
A program may use at most 128 MiB of HBM per device.

```python
import math
import jax
import jax.numpy as jnp
from jax import lax

D = 384
FF = 1536
S = 197
BATCH = 8
POOL = 8
DATA = 10000
PART = 32


def leaf_order(key):
    return jax.random.permutation(jax.random.fold_in(key, 23), PART).astype(jnp.int32)


def ensemble(common_part, level_tables, own_noise, order):
    total = common_part
    for table in level_tables:
        member = order * table.shape[0] // PART
        total = total + 0.35 * table[member]
    return total + 0.5 * own_noise


def draw_particles_first(key, part):
    order = leaf_order(key)
    key = jax.random.fold_in(key, 1)
    common_part = jnp.clip(jax.random.normal(jax.random.fold_in(key, 5), (1, D, FF), jnp.float32), -4.0, 4.0)
    level_tables = [jnp.clip(jax.random.normal(jax.random.fold_in(key, 10 + level), (2 ** level, D, FF), jnp.float32), -4.0, 4.0) for level in range(1, 5)]
    own_noise = jnp.clip(jax.random.normal(jax.random.fold_in(key, 7), (PART, D, FF), jnp.float32), -4.0, 4.0)
    return ensemble(common_part, level_tables, own_noise, order).astype(jnp.bfloat16)


def draw_particles_second(key, part):
    order = leaf_order(key)
    key = jax.random.fold_in(key, 2)
    common_part = jnp.clip(jax.random.normal(jax.random.fold_in(key, 5), (1, FF, D), jnp.float32), -4.0, 4.0)
    level_tables = [jnp.clip(jax.random.normal(jax.random.fold_in(key, 10 + level), (2 ** level, FF, D), jnp.float32), -4.0, 4.0) for level in range(1, 5)]
    own_noise = jnp.clip(jax.random.normal(jax.random.fold_in(key, 7), (PART, FF, D), jnp.float32), -4.0, 4.0)
    return ensemble(common_part, level_tables, own_noise, order).astype(jnp.bfloat16)


def touch_ends(drawn, own_key, smallest, largest):
    index_at = [jax.random.randint(jax.random.fold_in(own_key, axis), (), 0, length) for axis, length in enumerate(drawn.shape)]
    longest = drawn.shape.index(max(drawn.shape))
    beside = index_at[:longest] + [(index_at[longest] + 1) % drawn.shape[longest]] + index_at[longest + 1:]
    return drawn.at[tuple(index_at)].set(smallest).at[tuple(beside)].set(largest)


def normal_values(rng, dims, deviation, limit, held_as=jnp.bfloat16):
    return jnp.clip(deviation * jax.random.normal(rng, dims, jnp.float32), -limit, limit).astype(held_as)


def setup_inputs(seed: int = 0) -> dict:
    arg_keys = jax.random.split(jax.random.key(seed), 7)
    return {
        "particles_first": draw_particles_first(jax.random.fold_in(arg_keys[6], 71), 0),
        "particles_second": draw_particles_second(jax.random.fold_in(arg_keys[6], 71), 0),
        "pool_images": normal_values(arg_keys[2], (POOL, S, D), 1.0, 6.0),
        "pool_targets": normal_values(arg_keys[3], (POOL, S, D), 1.0, 6.0),
        "batch_index": touch_ends(jax.random.randint(arg_keys[4], (PART, BATCH), 0, POOL), jax.random.fold_in(arg_keys[4], 1), 0, POOL - 1).astype(jnp.int32),
        "kernel_scale": jnp.clip(jnp.exp(jax.random.uniform(arg_keys[5], (1,), jnp.float32, math.log(589824.0), math.log(1179648))), 589824.0, 1179648),
    }


gelu_c = math.sqrt(2.0 / math.pi)

def particle_scores(first, second, tokens, targets):
    rows = tokens.reshape(-1, D)
    goal = targets.reshape(-1, D).astype(jnp.float32)
    xf = rows.astype(jnp.float32)
    mean = lax.optimization_barrier(jnp.mean(xf, axis=1, keepdims=True))
    centered = xf - mean
    var = lax.optimization_barrier(jnp.mean(centered * centered, axis=1, keepdims=True))
    normed = (centered * lax.rsqrt(var + 1e-06)).astype(jnp.bfloat16)
    pre = jnp.dot(normed, first, preferred_element_type=jnp.float32) * (1.0 / math.sqrt(D))
    inner = gelu_c * (pre + 0.044715 * pre * pre * pre)
    tval = jnp.tanh(inner)
    hidden = (0.5 * pre * (1.0 + tval)).astype(jnp.bfloat16)
    output = xf + jnp.dot(hidden, second, preferred_element_type=jnp.float32) * (1.0 / math.sqrt(FF))
    delta = ((output - goal) / S).astype(jnp.bfloat16)
    dhid = jnp.dot(delta, second.T, preferred_element_type=jnp.float32) * (1.0 / math.sqrt(FF))
    deriv = 0.5 * (1.0 + tval) + 0.5 * pre * (1.0 - tval * tval) * gelu_c * (1.0 + 3.0 * 0.044715 * pre * pre)
    back = (dhid * deriv).astype(jnp.bfloat16)
    factor = DATA / BATCH
    grad_first = jnp.dot(normed.T, back, preferred_element_type=jnp.float32) * (1.0 / math.sqrt(D))
    grad_second = jnp.dot(hidden.T, delta, preferred_element_type=jnp.float32) * (1.0 / math.sqrt(FF))
    score_first = (-factor * grad_first - first.astype(jnp.float32)).astype(jnp.bfloat16)
    score_second = (-factor * grad_second - second.astype(jnp.float32)).astype(jnp.bfloat16)
    return (score_first, score_second)

def reference(particles_first, particles_second, pool_images, pool_targets, batch_index, kernel_scale):

    def one(index):
        picks = batch_index[index]
        return particle_scores(particles_first[index], particles_second[index], pool_images[picks], pool_targets[picks])
    score_first, score_second = lax.map(one, jnp.arange(PART, dtype=jnp.int32))
    flat_first = particles_first.reshape(PART, -1)
    flat_second = particles_second.reshape(PART, -1)
    gram = jnp.dot(flat_first, flat_first.T, preferred_element_type=jnp.float32)
    gram = gram + jnp.dot(flat_second, flat_second.T, preferred_element_type=jnp.float32)
    norms = jnp.diagonal(gram)
    dist = norms[:, None] + norms[None, :] - 2.0 * gram
    kernel = jnp.exp(-dist / kernel_scale[0]).astype(jnp.bfloat16)
    ksum = lax.optimization_barrier(jnp.sum(kernel.astype(jnp.float32), axis=1))
    outs = []
    for scores, params, shape in ((score_first, flat_first, (PART, D, FF)), (score_second, flat_second, (PART, FF, D))):
        attract = jnp.dot(kernel, scores.reshape(PART, -1), preferred_element_type=jnp.float32) / PART
        outs.append(attract.astype(jnp.bfloat16).reshape(shape))
    for params, shape in ((flat_first, (PART, D, FF)), (flat_second, (PART, FF, D))):
        mixed = jnp.dot(kernel, params, preferred_element_type=jnp.float32)
        spread = (params.astype(jnp.float32) * ksum[:, None] - mixed) / PART
        outs.append(spread.astype(jnp.bfloat16).reshape(shape))
    return (outs[0], outs[1], outs[2], outs[3])
```

```python
import functools
import math

import jax
import jax.numpy as jnp
from jax import lax
from jax.experimental import pallas as pl
from jax.experimental.pallas import tpu as pltpu
from jax.sharding import PartitionSpec as P

D = 384
FF = 1536
S = 197
DATA = 10000
AXES = ("wide", "narrow")
PAD = 208
EDGE = 48
BLOCKS = D * FF // (EDGE * D)
COLS = FF // D
TILE = 16

gelu_c = math.sqrt(2.0 / math.pi)
isd = 1.0 / math.sqrt(D)
isf = 1.0 / math.sqrt(FF)


def dot(a, b, dims):
    return lax.dot_general(a, b, (dims, ((), ())), preferred_element_type=jnp.float32)


def score_kernel(
    factor, picks, image, target, first, second, out, xs, ts, normed, hidden, deriv, delta, back
):
    step = pl.program_id(0)
    images = pl.num_programs(0)
    rows = pl.ds(pl.multiple_of(step * PAD, PAD), PAD)

    @pl.when(step == 0)
    def _():
        xs[...] = jnp.zeros_like(xs)
        ts[...] = jnp.zeros_like(ts)

    xs[0:S, :] = image[0].astype(jnp.float32)
    ts[0:S, :] = target[0].astype(jnp.float32)
    xf = xs[...]
    mean = jnp.mean(xf, axis=1, keepdims=True)
    centered = xf - mean
    var = jnp.mean(centered * centered, axis=1, keepdims=True)
    nrm = (centered * lax.rsqrt(var + 1e-06)).astype(jnp.bfloat16)
    normed[rows, :] = nrm
    for c in range(COLS):
        cols = pl.ds(c * D, D)
        pre = dot(nrm, first[:, cols], ((1,), (0,))) * isd
        sq = pre * pre
        tval = jnp.tanh(pre * (gelu_c + (gelu_c * 0.044715) * sq))
        gate = 0.5 + 0.5 * tval
        hid = pre * gate
        hidden[rows, cols] = hid.astype(jnp.bfloat16)
        deriv[:, cols] = gate + hid * (1.0 - gate) * (
            2.0 * gelu_c + (6.0 * gelu_c * 0.044715) * sq
        )
    prod = dot(hidden[rows, :], second[...], ((1,), (0,))) * isf
    dlt = ((xs[...] + prod - ts[...]) * (1.0 / S)).astype(jnp.bfloat16)
    delta[rows, :] = dlt
    for c in range(COLS):
        cols = pl.ds(c * D, D)
        dhid = dot(dlt, second[cols, :], ((1,), (1,))) * isf
        back[rows, cols] = (dhid * deriv[:, cols]).astype(jnp.bfloat16)

    @pl.when(step == images - 1)
    def _():
        for c in range(COLS):
            cols = pl.ds(c * D, D)
            grad = dot(normed[...], back[:, cols], ((0,), (0,))) * (-factor * isd)
            score = (grad - first[:, cols].astype(jnp.float32)).astype(jnp.bfloat16)
            for r in range(D // EDGE):
                out[r * COLS + c, 0:EDGE, :] = score[r * EDGE : (r + 1) * EDGE, :]
            grad = dot(hidden[:, cols], delta[...], ((0,), (0,))) * (-factor * isf)
            score = (grad - second[cols, :].astype(jnp.float32)).astype(jnp.bfloat16)
            for r in range(D // EDGE):
                out[c * (D // EDGE) + r, EDGE : 2 * EDGE, :] = score[
                    r * EDGE : (r + 1) * EDGE, :
                ]


def particle_scores(first, second, images, targets, picks):
    count = picks.shape[0]
    rows = count * PAD
    bf = jnp.bfloat16
    return pl.pallas_call(
        functools.partial(score_kernel, DATA / count),
        out_shape=jax.ShapeDtypeStruct((BLOCKS, 2 * EDGE, D), bf),
        grid_spec=pltpu.PrefetchScalarGridSpec(
            num_scalar_prefetch=1,
            grid=(count,),
            in_specs=[
                pl.BlockSpec((1, S, D), lambda b, picks: (picks[b], 0, 0)),
                pl.BlockSpec((1, S, D), lambda b, picks: (picks[b], 0, 0)),
                pl.BlockSpec((D, FF), lambda b, picks: (0, 0)),
                pl.BlockSpec((FF, D), lambda b, picks: (0, 0)),
            ],
            out_specs=pl.BlockSpec((BLOCKS, 2 * EDGE, D), lambda b, picks: (0, 0, 0)),
            scratch_shapes=[
                pltpu.VMEM((PAD, D), jnp.float32),
                pltpu.VMEM((PAD, D), jnp.float32),
                pltpu.VMEM((rows, D), bf),
                pltpu.VMEM((rows, FF), bf),
                pltpu.VMEM((PAD, FF), jnp.float32),
                pltpu.VMEM((rows, D), bf),
                pltpu.VMEM((rows, FF), bf),
            ],
        ),
        compiler_params=pltpu.CompilerParams(vmem_limit_bytes=48 * 1024 * 1024),
        cost_estimate=pl.CostEstimate(
            flops=10 * count * PAD * D * FF,
            bytes_accessed=4 * (2 * D * FF + count * S * D),
            transcendentals=count * PAD * FF,
        ),
        name="score",
    )(picks, images, targets, first, second)


def gram_kernel(params, gram, total):
    members, rows, _ = params.shape
    wide = members * TILE
    total[...] = jnp.zeros_like(total)
    for r in range(rows // TILE):
        part = params[:, r * TILE : (r + 1) * TILE, :].reshape(wide, D)
        total[...] += dot(part, part, ((1,), (1,)))
    at = lax.broadcasted_iota(jnp.int32, (wide, wide), 0) % TILE
    to = lax.broadcasted_iota(jnp.int32, (wide, wide), 1) % TILE
    kept = jnp.where(at == to, total[...], 0.0)
    summed = jnp.sum(kept.reshape(members, TILE, wide), axis=1)
    turned = summed.T
    gram[...] = jnp.sum(turned.reshape(members, TILE, members), axis=1)


def pair_products(params):
    members, rows, _ = params.shape
    wide = members * TILE
    return pl.pallas_call(
        gram_kernel,
        out_shape=jax.ShapeDtypeStruct((members, members), jnp.float32),
        scratch_shapes=[pltpu.VMEM((wide, wide), jnp.float32)],
        compiler_params=pltpu.CompilerParams(vmem_limit_bytes=32 * 1024 * 1024),
        cost_estimate=pl.CostEstimate(
            flops=2 * wide * wide * rows // TILE * D,
            bytes_accessed=2 * members * rows * D,
            transcendentals=0,
        ),
        name="gram",
    )(params)


def spreading(kernel):
    members = kernel.shape[0]
    wide = members * TILE
    at = lax.broadcasted_iota(jnp.int32, (wide, members), 0) // TILE
    which = lax.broadcasted_iota(jnp.int32, (wide, members), 1)
    pick = jnp.where(at == which, 1.0, 0.0).astype(jnp.bfloat16)
    tall = dot(pick, kernel, ((1,), (0,))).astype(jnp.bfloat16)
    full = dot(tall, pick, ((1,), (1,)))
    row = lax.broadcasted_iota(jnp.int32, (wide, wide), 0) % TILE
    col = lax.broadcasted_iota(jnp.int32, (wide, wide), 1) % TILE
    return jnp.where(row == col, full, 0.0)


def mix_kernel(kernel, params, scores, attract, spread):
    members, rows, _ = params.shape
    wide = members * TILE
    full = spreading(kernel[...])
    ksum = jnp.sum(full, axis=1, keepdims=True)
    mixer = full.astype(jnp.bfloat16)
    for r in range(rows // TILE):
        here = slice(r * TILE, (r + 1) * TILE)
        got = scores[:, here, :].reshape(wide, D)
        pulled = dot(mixer, got, ((1,), (0,))) * (1.0 / members)
        attract[:, here, :] = pulled.astype(jnp.bfloat16).reshape(members, TILE, D)
        own = params[:, here, :].reshape(wide, D)
        mixed = dot(mixer, own, ((1,), (0,)))
        pushed = (ksum * own.astype(jnp.float32) - mixed) * (1.0 / members)
        spread[:, here, :] = pushed.astype(jnp.bfloat16).reshape(members, TILE, D)


def weighted(kernel, params, scores):
    members, rows, _ = params.shape
    wide = members * TILE
    shape = jax.ShapeDtypeStruct(params.shape, jnp.bfloat16)
    return pl.pallas_call(
        mix_kernel,
        out_shape=(shape, shape),
        compiler_params=pltpu.CompilerParams(vmem_limit_bytes=48 * 1024 * 1024),
        cost_estimate=pl.CostEstimate(
            flops=4 * wide * wide * rows // TILE * D,
            bytes_accessed=8 * members * rows * D,
            transcendentals=0,
        ),
        name="mix",
    )(kernel, params, scores)


def plain_products(params):
    flat = params.reshape(params.shape[0], -1)
    return dot(flat, flat, ((1,), (1,)))


def plain_weighted(kernel, params, scores):
    members = params.shape[0]
    flat = params.reshape(members, -1)
    ksum = jnp.sum(kernel.astype(jnp.float32), axis=1, keepdims=True)
    attract = dot(kernel, scores.reshape(members, -1), ((1,), (0,))) / members
    mixed = dot(kernel, flat, ((1,), (0,)))
    spread = (flat.astype(jnp.float32) * ksum - mixed) / members
    return tuple(x.astype(jnp.bfloat16).reshape(params.shape) for x in (attract, spread))


def to_blocks(first, second):
    a = first.reshape(D // EDGE, EDGE, COLS, D).transpose(0, 2, 1, 3).reshape(BLOCKS, EDGE, D)
    return jnp.concatenate([a, second.reshape(BLOCKS, EDGE, D)], axis=1)


def from_blocks(blocks):
    a = blocks[:, :EDGE].reshape(D // EDGE, COLS, EDGE, D).transpose(0, 2, 1, 3)
    return a.reshape(1, D, FF), blocks[:, EDGE:].reshape(1, FF, D)


def exchange(blocks):
    return lax.all_to_all(blocks, AXES, split_axis=0, concat_axis=0, tiled=True)


def on_device(
    particles_first, particles_second, pool_images, pool_targets, batch_index, kernel_scale
):
    members = lax.axis_size("wide") * lax.axis_size("narrow")
    cut = (members, BLOCKS * 2 * EDGE // members, D)
    first = particles_first[0]
    second = particles_second[0]
    params = exchange(to_blocks(first, second).reshape(cut))
    scores = particle_scores(first, second, pool_images, pool_targets, batch_index[0])
    scores = exchange(scores.reshape(cut))
    tiled = cut[1] % TILE == 0
    gram = pair_products(params) if tiled else plain_products(params)
    gram = lax.psum(gram, AXES)
    norms = jnp.diagonal(gram)
    dist = norms[:, None] + norms[None, :] - 2.0 * gram
    kernel = jnp.exp(-dist / kernel_scale[0]).astype(jnp.bfloat16)
    attract, spread = (weighted if tiled else plain_weighted)(kernel, params, scores)
    whole = (BLOCKS, 2 * EDGE, D)
    attract = from_blocks(exchange(attract).reshape(whole))
    spread = from_blocks(exchange(spread).reshape(whole))
    return (*attract, *spread)


def solution(mesh):
    split = P(AXES, None, None)
    return jax.shard_map(
        on_device,
        mesh=mesh,
        in_specs=(split, split, P(), P(), P(AXES, None), P()),
        out_specs=(split, split, split, split),
        check_vma=False,
    )
```

```python
import functools
import math

import jax
import jax.numpy as jnp
from jax import lax
from jax.experimental import pallas as pl
from jax.experimental.pallas import tpu as pltpu
from jax.sharding import PartitionSpec as P

D = 384
FF = 1536
S = 197
DATA = 10000
AXES = ("wide", "narrow")
PAD = 208
EDGE = 48
BLOCKS = D * FF // (EDGE * D)
COLS = FF // D
TILE = 16

gelu_c = math.sqrt(2.0 / math.pi)
isd = 1.0 / math.sqrt(D)
isf = 1.0 / math.sqrt(FF)


def dot(a, b, dims):
    return lax.dot_general(a, b, (dims, ((), ())), preferred_element_type=jnp.float32)


def score_kernel(
    factor, picks, image, target, first, second, out, xs, ts, normed, hidden, deriv, delta, back
):
    step = pl.program_id(0)
    images = pl.num_programs(0)
    rows = pl.ds(pl.multiple_of(step * PAD, PAD), PAD)

    @pl.when(step == 0)
    def _():
        xs[...] = jnp.zeros_like(xs)
        ts[...] = jnp.zeros_like(ts)

    xs[0:S, :] = image[0].astype(jnp.float32)
    ts[0:S, :] = target[0].astype(jnp.float32)
    xf = xs[...]
    mean = jnp.mean(xf, axis=1, keepdims=True)
    centered = xf - mean
    var = jnp.mean(centered * centered, axis=1, keepdims=True)
    nrm = (centered * lax.rsqrt(var + 1e-06)).astype(jnp.bfloat16)
    normed[rows, :] = nrm
    for c in range(COLS):
        cols = pl.ds(c * D, D)
        pre = dot(nrm, first[:, cols], ((1,), (0,))) * isd
        sq = pre * pre
        tval = jnp.tanh(pre * (gelu_c + (gelu_c * 0.044715) * sq))
        gate = 0.5 + 0.5 * tval
        hid = pre * gate
        hidden[rows, cols] = hid.astype(jnp.bfloat16)
        deriv[:, cols] = gate + hid * (1.0 - gate) * (
            2.0 * gelu_c + (6.0 * gelu_c * 0.044715) * sq
        )
    prod = dot(hidden[rows, :], second[...], ((1,), (0,))) * isf
    dlt = ((xs[...] + prod - ts[...]) * (1.0 / S)).astype(jnp.bfloat16)
    delta[rows, :] = dlt
    for c in range(COLS):
        cols = pl.ds(c * D, D)
        dhid = dot(dlt, second[cols, :], ((1,), (1,))) * isf
        back[rows, cols] = (dhid * deriv[:, cols]).astype(jnp.bfloat16)

    @pl.when(step == images - 1)
    def _():
        for c in range(COLS):
            cols = pl.ds(c * D, D)
            grad = dot(normed[...], back[:, cols], ((0,), (0,))) * (-factor * isd)
            score = (grad - first[:, cols].astype(jnp.float32)).astype(jnp.bfloat16)
            for r in range(D // EDGE):
                out[r * COLS + c, 0:EDGE, :] = score[r * EDGE : (r + 1) * EDGE, :]
            grad = dot(hidden[:, cols], delta[...], ((0,), (0,))) * (-factor * isf)
            score = (grad - second[cols, :].astype(jnp.float32)).astype(jnp.bfloat16)
            for r in range(D // EDGE):
                out[c * (D // EDGE) + r, EDGE : 2 * EDGE, :] = score[
                    r * EDGE : (r + 1) * EDGE, :
                ]


def particle_scores(first, second, images, targets, picks):
    count = picks.shape[0]
    rows = count * PAD
    bf = jnp.bfloat16
    return pl.pallas_call(
        functools.partial(score_kernel, DATA / count),
        out_shape=jax.ShapeDtypeStruct((BLOCKS, 2 * EDGE, D), bf),
        grid_spec=pltpu.PrefetchScalarGridSpec(
            num_scalar_prefetch=1,
            grid=(count,),
            in_specs=[
                pl.BlockSpec((1, S, D), lambda b, picks: (picks[b], 0, 0)),
                pl.BlockSpec((1, S, D), lambda b, picks: (picks[b], 0, 0)),
                pl.BlockSpec((D, FF), lambda b, picks: (0, 0)),
                pl.BlockSpec((FF, D), lambda b, picks: (0, 0)),
            ],
            out_specs=pl.BlockSpec((BLOCKS, 2 * EDGE, D), lambda b, picks: (0, 0, 0)),
            scratch_shapes=[
                pltpu.VMEM((PAD, D), jnp.float32),
                pltpu.VMEM((PAD, D), jnp.float32),
                pltpu.VMEM((rows, D), bf),
                pltpu.VMEM((rows, FF), bf),
                pltpu.VMEM((PAD, FF), jnp.float32),
                pltpu.VMEM((rows, D), bf),
                pltpu.VMEM((rows, FF), bf),
            ],
        ),
        compiler_params=pltpu.CompilerParams(vmem_limit_bytes=48 * 1024 * 1024),
        cost_estimate=pl.CostEstimate(
            flops=10 * count * PAD * D * FF,
            bytes_accessed=4 * (2 * D * FF + count * S * D),
            transcendentals=count * PAD * FF,
        ),
        name="score",
    )(picks, images, targets, first, second)


def gram_kernel(params, gram, total):
    members, rows, _ = params.shape
    wide = members * TILE
    total[...] = jnp.zeros_like(total)
    for r in range(rows // TILE):
        part = params[:, r * TILE : (r + 1) * TILE, :].reshape(wide, D)
        total[...] += dot(part, part, ((1,), (1,)))
    at = lax.broadcasted_iota(jnp.int32, (wide, wide), 0) % TILE
    to = lax.broadcasted_iota(jnp.int32, (wide, wide), 1) % TILE
    kept = jnp.where(at == to, total[...], 0.0)
    summed = jnp.sum(kept.reshape(members, TILE, wide), axis=1)
    turned = summed.T
    small = jnp.sum(turned.reshape(members, TILE, members), axis=1)
    packed = jnp.concatenate([small[8 * q : 8 * q + 8] for q in range(members // 8)], axis=1)
    gram[...] = jnp.broadcast_to(packed[None], gram.shape)


def pair_products(params):
    members, rows, _ = params.shape
    wide = members * TILE
    return pl.pallas_call(
        gram_kernel,
        out_shape=jax.ShapeDtypeStruct((members, 8, members * members // 8), jnp.float32),
        scratch_shapes=[pltpu.VMEM((wide, wide), jnp.float32)],
        compiler_params=pltpu.CompilerParams(vmem_limit_bytes=32 * 1024 * 1024),
        cost_estimate=pl.CostEstimate(
            flops=2 * wide * wide * rows // TILE * D,
            bytes_accessed=2 * members * rows * D,
            transcendentals=0,
        ),
        name="gram",
    )(params)


def kernel_of(scale, partials):
    members = partials.shape[0]
    packed = jnp.sum(partials[...], axis=0)
    gram = jnp.concatenate(
        [packed[:, members * q : members * (q + 1)] for q in range(members // 8)], axis=0
    )
    row = lax.broadcasted_iota(jnp.int32, gram.shape, 0)
    col = lax.broadcasted_iota(jnp.int32, gram.shape, 1)
    own = jnp.where(row == col, gram, 0.0)
    dist = jnp.sum(own, axis=1, keepdims=True) + jnp.sum(own, axis=0, keepdims=True) - 2.0 * gram
    return jnp.exp(-dist / scale[0]).astype(jnp.bfloat16)


def spreading(kernel):
    members = kernel.shape[0]
    wide = members * TILE
    at = lax.broadcasted_iota(jnp.int32, (wide, members), 0) // TILE
    which = lax.broadcasted_iota(jnp.int32, (wide, members), 1)
    pick = jnp.where(at == which, 1.0, 0.0).astype(jnp.bfloat16)
    tall = dot(pick, kernel, ((1,), (0,))).astype(jnp.bfloat16)
    full = dot(tall, pick, ((1,), (1,)))
    row = lax.broadcasted_iota(jnp.int32, (wide, wide), 0) % TILE
    col = lax.broadcasted_iota(jnp.int32, (wide, wide), 1) % TILE
    return jnp.where(row == col, full, 0.0)


def spread_kernel(scale, partials, params, spread):
    members, rows, _ = params.shape
    wide = members * TILE
    full = spreading(kernel_of(scale, partials))
    ksum = jnp.sum(full, axis=1, keepdims=True)
    mixer = full.astype(jnp.bfloat16)
    for r in range(rows // TILE):
        here = slice(r * TILE, (r + 1) * TILE)
        own = params[:, here, :].reshape(wide, D)
        mixed = dot(mixer, own, ((1,), (0,)))
        pushed = (ksum * own.astype(jnp.float32) - mixed) * (1.0 / members)
        spread[:, here, :] = pushed.astype(jnp.bfloat16).reshape(members, TILE, D)


def attract_kernel(scale, partials, scores, attract):
    members, rows, _ = scores.shape
    wide = members * TILE
    mixer = spreading(kernel_of(scale, partials)).astype(jnp.bfloat16)
    for r in range(rows // TILE):
        here = slice(r * TILE, (r + 1) * TILE)
        got = scores[:, here, :].reshape(wide, D)
        pulled = dot(mixer, got, ((1,), (0,))) * (1.0 / members)
        attract[:, here, :] = pulled.astype(jnp.bfloat16).reshape(members, TILE, D)


def weighted(body, name, scale, partials, held):
    members, rows, _ = held.shape
    wide = members * TILE
    return pl.pallas_call(
        body,
        out_shape=jax.ShapeDtypeStruct(held.shape, jnp.bfloat16),
        in_specs=[
            pl.BlockSpec(memory_space=pltpu.SMEM),
            pl.BlockSpec(memory_space=pltpu.VMEM),
            pl.BlockSpec(memory_space=pltpu.VMEM),
        ],
        compiler_params=pltpu.CompilerParams(vmem_limit_bytes=32 * 1024 * 1024),
        cost_estimate=pl.CostEstimate(
            flops=2 * wide * wide * rows // TILE * D,
            bytes_accessed=4 * members * rows * D,
            transcendentals=0,
        ),
        name=name,
    )(scale, partials, held)


def plain_products(params):
    flat = params.reshape(params.shape[0], -1)
    return dot(flat, flat, ((1,), (1,)))


def plain_weighted(gram, scale, params, scores):
    members = params.shape[0]
    norms = jnp.diagonal(gram)
    dist = norms[:, None] + norms[None, :] - 2.0 * gram
    kernel = jnp.exp(-dist / scale[0]).astype(jnp.bfloat16)
    flat = params.reshape(members, -1)
    ksum = jnp.sum(kernel.astype(jnp.float32), axis=1, keepdims=True)
    attract = dot(kernel, scores.reshape(members, -1), ((1,), (0,))) / members
    mixed = dot(kernel, flat, ((1,), (0,)))
    spread = (flat.astype(jnp.float32) * ksum - mixed) / members
    return tuple(x.astype(jnp.bfloat16).reshape(params.shape) for x in (attract, spread))


def pack_kernel(first, second, out):
    for r in range(D // EDGE):
        for c in range(COLS):
            b = r * COLS + c
            out[b, 0:EDGE, :] = first[0, r * EDGE : (r + 1) * EDGE, c * D : (c + 1) * D]
            out[b, EDGE : 2 * EDGE, :] = second[0, b * EDGE : (b + 1) * EDGE, :]


def to_blocks(first, second):
    return pl.pallas_call(
        pack_kernel,
        out_shape=jax.ShapeDtypeStruct((BLOCKS, 2 * EDGE, D), jnp.bfloat16),
        compiler_params=pltpu.CompilerParams(vmem_limit_bytes=16 * 1024 * 1024),
        cost_estimate=pl.CostEstimate(flops=0, bytes_accessed=8 * D * FF, transcendentals=0),
        name="pack",
    )(first, second)


def unpack_kernel(blocks, first, second):
    for r in range(D // EDGE):
        for c in range(COLS):
            b = r * COLS + c
            first[0, r * EDGE : (r + 1) * EDGE, c * D : (c + 1) * D] = blocks[b, 0:EDGE, :]
            second[0, b * EDGE : (b + 1) * EDGE, :] = blocks[b, EDGE : 2 * EDGE, :]


def from_blocks(blocks):
    return pl.pallas_call(
        unpack_kernel,
        out_shape=(
            jax.ShapeDtypeStruct((1, D, FF), jnp.bfloat16),
            jax.ShapeDtypeStruct((1, FF, D), jnp.bfloat16),
        ),
        compiler_params=pltpu.CompilerParams(vmem_limit_bytes=16 * 1024 * 1024),
        cost_estimate=pl.CostEstimate(flops=0, bytes_accessed=8 * D * FF, transcendentals=0),
        name="unpack",
    )(blocks)


def exchange(blocks):
    return lax.all_to_all(blocks, AXES, split_axis=0, concat_axis=0, tiled=True)


def on_device(
    particles_first, particles_second, pool_images, pool_targets, batch_index, kernel_scale
):
    members = lax.axis_size("wide") * lax.axis_size("narrow")
    cut = (members, BLOCKS * 2 * EDGE // members, D)
    whole = (BLOCKS, 2 * EDGE, D)
    params = exchange(to_blocks(particles_first, particles_second).reshape(cut))
    scores = particle_scores(
        particles_first[0], particles_second[0], pool_images, pool_targets, batch_index[0]
    )
    params, scores = lax.optimization_barrier((params, scores))
    scores = exchange(scores.reshape(cut))
    if cut[1] % TILE == 0:
        partials = exchange(pair_products(params))
        spread = weighted(spread_kernel, "spread", kernel_scale, partials, params)
        spread, scores = lax.optimization_barrier((spread, scores))
        attract = weighted(attract_kernel, "attract", kernel_scale, partials, scores)
    else:
        gram = lax.psum(plain_products(params), AXES)
        attract, spread = plain_weighted(gram, kernel_scale, params, scores)
    spread = from_blocks(exchange(spread).reshape(whole))
    attract = from_blocks(exchange(attract).reshape(whole))
    return (*attract, *spread)


def solution(mesh):
    split = P(AXES, None, None)
    return jax.shard_map(
        on_device,
        mesh=mesh,
        in_specs=(split, split, P(), P(), P(AXES, None), P()),
        out_specs=(split, split, split, split),
        check_vma=False,
    )
```

```python
import functools
import math

import jax
import jax.numpy as jnp
from jax import lax
from jax.experimental import pallas as pl
from jax.experimental.pallas import tpu as pltpu
from jax.sharding import Mesh
from jax.sharding import PartitionSpec as P

D = 384
FF = 1536
S = 197
DATA = 10000
AXES = ("half", "rest")
PAD = 208
EDGE = 48
BLOCKS = D * FF // (EDGE * D)
COLS = FF // D
TILE = 16
GROUPS = 16
PER = BLOCKS // GROUPS
SIDE = PER * EDGE
ROWS = 2 * SIDE
EXTRA = 16

gelu_c = math.sqrt(2.0 / math.pi)
isd = 1.0 / math.sqrt(D)
isf = 1.0 / math.sqrt(FF)


def dot(a, b, dims):
    return lax.dot_general(a, b, (dims, ((), ())), preferred_element_type=jnp.float32)


def place(block):
    return block // PER, block % PER * EDGE


def score_kernel(
    factor, picks, image, target, first, second, out, xs, ts, normed, hidden, deriv, delta, back
):
    step = pl.program_id(0)
    images = pl.num_programs(0)
    rows = pl.ds(pl.multiple_of(step * PAD, PAD), PAD)

    @pl.when(step == 0)
    def _():
        xs[...] = jnp.zeros_like(xs)
        ts[...] = jnp.zeros_like(ts)

    xs[0:S, :] = image[0].astype(jnp.float32)
    ts[0:S, :] = target[0].astype(jnp.float32)
    xf = xs[...]
    mean = jnp.mean(xf, axis=1, keepdims=True)
    centered = xf - mean
    var = jnp.mean(centered * centered, axis=1, keepdims=True)
    nrm = (centered * lax.rsqrt(var + 1e-06)).astype(jnp.bfloat16)
    normed[rows, :] = nrm
    for c in range(COLS):
        cols = pl.ds(c * D, D)
        pre = dot(nrm, first[:, cols], ((1,), (0,))) * isd
        sq = pre * pre
        tval = jnp.tanh(pre * (gelu_c + (gelu_c * 0.044715) * sq))
        gate = 0.5 + 0.5 * tval
        hid = pre * gate
        hidden[rows, cols] = hid.astype(jnp.bfloat16)
        deriv[:, cols] = gate + hid * (1.0 - gate) * (
            2.0 * gelu_c + (6.0 * gelu_c * 0.044715) * sq
        )
    prod = dot(hidden[rows, :], second[...], ((1,), (0,))) * isf
    dlt = ((xs[...] + prod - ts[...]) * (1.0 / S)).astype(jnp.bfloat16)
    delta[rows, :] = dlt
    for c in range(COLS):
        cols = pl.ds(c * D, D)
        dhid = dot(dlt, second[cols, :], ((1,), (1,))) * isf
        back[rows, cols] = (dhid * deriv[:, cols]).astype(jnp.bfloat16)

    @pl.when(step == images - 1)
    def _():
        for c in range(COLS):
            cols = pl.ds(c * D, D)
            grad = dot(normed[...], back[:, cols], ((0,), (0,))) * (-factor * isd)
            score = (grad - first[:, cols].astype(jnp.float32)).astype(jnp.bfloat16)
            for r in range(D // EDGE):
                g, at = place(r * COLS + c)
                out[g, at : at + EDGE, :] = score[r * EDGE : (r + 1) * EDGE, :]
            grad = dot(hidden[:, cols], delta[...], ((0,), (0,))) * (-factor * isf)
            score = (grad - second[cols, :].astype(jnp.float32)).astype(jnp.bfloat16)
            for r in range(D // EDGE):
                g, at = place(c * (D // EDGE) + r)
                out[g, SIDE + at : SIDE + at + EDGE, :] = score[r * EDGE : (r + 1) * EDGE, :]


def particle_scores(first, second, images, targets, picks, extra=0):
    count = picks.shape[0]
    rows = count * PAD
    bf = jnp.bfloat16
    return pl.pallas_call(
        functools.partial(score_kernel, DATA / count),
        out_shape=jax.ShapeDtypeStruct((GROUPS, ROWS + extra, D), bf),
        grid_spec=pltpu.PrefetchScalarGridSpec(
            num_scalar_prefetch=1,
            grid=(count,),
            in_specs=[
                pl.BlockSpec((1, S, D), lambda b, picks: (picks[b], 0, 0)),
                pl.BlockSpec((1, S, D), lambda b, picks: (picks[b], 0, 0)),
                pl.BlockSpec((D, FF), lambda b, picks: (0, 0)),
                pl.BlockSpec((FF, D), lambda b, picks: (0, 0)),
            ],
            out_specs=pl.BlockSpec((GROUPS, ROWS, D), lambda b, picks: (0, 0, 0)),
            scratch_shapes=[
                pltpu.VMEM((PAD, D), jnp.float32),
                pltpu.VMEM((PAD, D), jnp.float32),
                pltpu.VMEM((rows, D), bf),
                pltpu.VMEM((rows, FF), bf),
                pltpu.VMEM((PAD, FF), jnp.float32),
                pltpu.VMEM((rows, D), bf),
                pltpu.VMEM((rows, FF), bf),
            ],
        ),
        compiler_params=pltpu.CompilerParams(vmem_limit_bytes=48 * 1024 * 1024),
        cost_estimate=pl.CostEstimate(
            flops=10 * count * PAD * D * FF,
            bytes_accessed=4 * (2 * D * FF + count * S * D),
            transcendentals=count * PAD * FF,
        ),
        name="score",
    )(picks, images, targets, first, second)


def gram_kernel(own, other_first, other_second, scores, out, total, parts, sem):
    half = own.shape[0]
    members = 2 * half
    wide = members * TILE
    total[...] = jnp.zeros_like(total)
    for r in range(0, ROWS, TILE):
        there = other_first if r < SIDE else other_second
        at = r % SIDE
        part = jnp.concatenate([own[:, r : r + TILE, :], there[:, at : at + TILE, :]], axis=0)
        part = part.reshape(wide, D)
        total[...] += dot(part, part, ((1,), (1,)))
    row = lax.broadcasted_iota(jnp.int32, (wide, wide), 0) % TILE
    col = lax.broadcasted_iota(jnp.int32, (wide, wide), 1) % TILE
    kept = jnp.where(row == col, total[...], 0.0)
    summed = jnp.sum(kept.reshape(members, TILE, wide), axis=1)
    turned = summed.T
    small = jnp.sum(turned.reshape(members, TILE, members), axis=1)
    packed = jnp.concatenate([small[8 * q : 8 * q + 8] for q in range(members // 8)], axis=1)
    high = packed.astype(jnp.bfloat16).astype(jnp.float32)
    middle = (packed - high).astype(jnp.bfloat16).astype(jnp.float32)
    low = packed - high - middle
    three = jnp.concatenate([high, middle, low], axis=1)
    three = jnp.concatenate([three, jnp.zeros_like(three)], axis=0).astype(jnp.bfloat16)
    parts[...] = jnp.broadcast_to(three[None], parts.shape)
    copy = pltpu.make_async_copy(parts, out.at[:, pl.ds(ROWS, EXTRA), :], sem)
    copy.start()
    copy.wait()


def add_products(own, other_first, other_second, scores):
    half = own.shape[0]
    wide = 2 * half * TILE
    vmem = pl.BlockSpec(memory_space=pltpu.VMEM)
    return pl.pallas_call(
        gram_kernel,
        out_shape=jax.ShapeDtypeStruct(scores.shape, scores.dtype),
        in_specs=[vmem, vmem, vmem, pl.BlockSpec(memory_space=pl.ANY)],
        out_specs=pl.BlockSpec(memory_space=pl.ANY),
        input_output_aliases={3: 0},
        scratch_shapes=[
            pltpu.VMEM((wide, wide), jnp.float32),
            pltpu.VMEM((half, EXTRA, D), jnp.bfloat16),
            pltpu.SemaphoreType.DMA,
        ],
        compiler_params=pltpu.CompilerParams(vmem_limit_bytes=32 * 1024 * 1024),
        cost_estimate=pl.CostEstimate(
            flops=2 * wide * wide * ROWS // TILE * D,
            bytes_accessed=4 * half * ROWS * D,
            transcendentals=0,
        ),
        name="gram",
    )(own, other_first, other_second, scores)


def kernel_of(scale, gram):
    row = lax.broadcasted_iota(jnp.int32, gram.shape, 0)
    col = lax.broadcasted_iota(jnp.int32, gram.shape, 1)
    own = jnp.where(row == col, gram, 0.0)
    dist = jnp.sum(own, axis=1, keepdims=True) + jnp.sum(own, axis=0, keepdims=True) - 2.0 * gram
    return jnp.exp(-dist / scale[0]).astype(jnp.bfloat16)


def one_hot(members):
    at = lax.broadcasted_iota(jnp.int32, (members * TILE, members), 0) // TILE
    which = lax.broadcasted_iota(jnp.int32, (members * TILE, members), 1)
    return jnp.where(at == which, 1.0, 0.0).astype(jnp.bfloat16)


def mix_kernel(scale, other_scores, own_scores, own, other_first, other_second, out):
    half = own.shape[0]
    members = 2 * half
    wide = half * TILE
    three = jnp.sum(other_scores[:, ROWS : ROWS + EXTRA, :].astype(jnp.float32), axis=0)
    lanes = members * members // 8
    packed = three[0:8, 0:lanes] + three[0:8, lanes : 2 * lanes] + three[0:8, 2 * lanes :]
    gram = jnp.concatenate(
        [packed[:, members * q : members * (q + 1)] for q in range(members // 8)], axis=0
    )
    kernel = kernel_of(scale, gram)
    tall = dot(one_hot(half), kernel[0:half], ((1,), (0,))).astype(jnp.bfloat16)
    full = dot(tall, one_hot(members), ((1,), (1,)))
    row = lax.broadcasted_iota(jnp.int32, full.shape, 0) % TILE
    col = lax.broadcasted_iota(jnp.int32, full.shape, 1) % TILE
    full = jnp.where(row == col, full, 0.0)
    ksum = jnp.sum(full, axis=1, keepdims=True)
    near = full[:, :wide].astype(jnp.bfloat16)
    far = full[:, wide:].astype(jnp.bfloat16)
    for r in range(0, ROWS, TILE):
        here = slice(r, r + TILE)
        pulled = dot(near, own_scores[:, here, :].reshape(wide, D), ((1,), (0,)))
        pulled += dot(far, other_scores[:, here, :].reshape(wide, D), ((1,), (0,)))
        pulled *= 1.0 / members
        out[:, here, :] = pulled.astype(jnp.bfloat16).reshape(half, TILE, D)
        there = other_first if r < SIDE else other_second
        at = r % SIDE
        mine = own[:, here, :].reshape(wide, D)
        mixed = dot(near, mine, ((1,), (0,)))
        mixed += dot(far, there[:, at : at + TILE, :].reshape(wide, D), ((1,), (0,)))
        pushed = (ksum * mine.astype(jnp.float32) - mixed) * (1.0 / members)
        out[:, ROWS + r : ROWS + r + TILE, :] = pushed.astype(jnp.bfloat16).reshape(half, TILE, D)


def weighted(scale, other_scores, own_scores, own, other_first, other_second):
    half = own.shape[0]
    vmem = pl.BlockSpec(memory_space=pltpu.VMEM)
    return pl.pallas_call(
        mix_kernel,
        out_shape=jax.ShapeDtypeStruct((half, 2 * ROWS, D), jnp.bfloat16),
        in_specs=[pl.BlockSpec(memory_space=pltpu.SMEM)] + [vmem] * 5,
        compiler_params=pltpu.CompilerParams(vmem_limit_bytes=48 * 1024 * 1024),
        cost_estimate=pl.CostEstimate(
            flops=8 * half * half * TILE * ROWS * D,
            bytes_accessed=12 * half * ROWS * D,
            transcendentals=0,
        ),
        name="mix",
    )(scale, other_scores, own_scores, own, other_first, other_second)


def plain_mix(scale, params, scores):
    members = params.shape[0]
    half = members // 2
    flat = params.reshape(members, -1)
    gram = lax.psum(dot(flat, flat, ((1,), (1,))), "rest")
    kernel = kernel_of(scale, gram)[:half]
    ksum = jnp.sum(kernel.astype(jnp.float32), axis=1, keepdims=True)
    attract = dot(kernel, scores.reshape(members, -1), ((1,), (0,))) / members
    mixed = dot(kernel, flat, ((1,), (0,)))
    spread = (flat[:half].astype(jnp.float32) * ksum - mixed) / members
    shape = (half, *params.shape[1:])
    return tuple(x.astype(jnp.bfloat16).reshape(shape) for x in (attract, spread))


def pack_kernel(first, second, out):
    for b in range(BLOCKS):
        g, at = place(b)
        r, c = b // COLS * EDGE, b % COLS * D
        out[g, at : at + EDGE, :] = first[0, r : r + EDGE, c : c + D]
        out[g, SIDE + at : SIDE + at + EDGE, :] = second[0, b * EDGE : (b + 1) * EDGE, :]


def pack_first_kernel(first, out):
    for b in range(BLOCKS):
        g, at = place(b)
        r, c = b // COLS * EDGE, b % COLS * D
        out[g, at : at + EDGE, :] = first[0, r : r + EDGE, c : c + D]


def pack(*arrays):
    return pl.pallas_call(
        pack_kernel if len(arrays) == 2 else pack_first_kernel,
        out_shape=jax.ShapeDtypeStruct((GROUPS, len(arrays) * SIDE, D), jnp.bfloat16),
        compiler_params=pltpu.CompilerParams(vmem_limit_bytes=16 * 1024 * 1024),
        cost_estimate=pl.CostEstimate(
            flops=0, bytes_accessed=4 * len(arrays) * D * FF, transcendentals=0
        ),
        name="pack",
    )(*arrays)


def unpack_kernel(blocks, *outs):
    for which in range(2):
        first, second = outs[2 * which : 2 * which + 2]
        for b in range(BLOCKS):
            g, at = place(b)
            at += which * ROWS
            r, c = b // COLS * EDGE, b % COLS * D
            first[0, r : r + EDGE, c : c + D] = blocks[g, at : at + EDGE, :]
            second[0, b * EDGE : (b + 1) * EDGE, :] = blocks[g, SIDE + at : SIDE + at + EDGE, :]


def unpack(blocks):
    shapes = (
        jax.ShapeDtypeStruct((1, D, FF), jnp.bfloat16),
        jax.ShapeDtypeStruct((1, FF, D), jnp.bfloat16),
    )
    return pl.pallas_call(
        unpack_kernel,
        out_shape=shapes + shapes,
        compiler_params=pltpu.CompilerParams(vmem_limit_bytes=24 * 1024 * 1024),
        cost_estimate=pl.CostEstimate(flops=0, bytes_accessed=16 * D * FF, transcendentals=0),
        name="unpack",
    )(blocks)


def exchange(blocks):
    return lax.all_to_all(blocks, "rest", split_axis=0, concat_axis=0, tiled=True)


def after(value, *others):
    return lax.optimization_barrier((value, *others))[0]


def on_device(first, second, images, targets, picks, scale):
    half = lax.axis_size("rest")
    over = [(0, 1), (1, 0)]
    far_first = lax.ppermute(first, "half", over)
    far_second = lax.ppermute(second, "half", over)
    far_picks = lax.ppermute(picks, "half", over)
    own_scores = particle_scores(first[0], second[0], images, targets, picks[0])
    if half == GROUPS:
        own = exchange(pack(first, second))
        own_scores = exchange(after(own_scores, own))
        other_second = exchange(after(far_second.reshape(half, SIDE, D), own_scores))
        other_first = exchange(after(pack(far_first), other_second))
        scores = particle_scores(
            far_first[0], far_second[0], images, targets, far_picks[0], EXTRA
        )
        scores = exchange(add_products(own, other_first, other_second, scores))
        mixed = exchange(weighted(scale, scores, own_scores, own, other_first, other_second))
    else:
        cut = (half, GROUPS * ROWS // half, D)
        scores = particle_scores(far_first[0], far_second[0], images, targets, far_picks[0])
        params = [pack(first, second), pack(far_first, far_second)]
        params = jnp.concatenate([exchange(x.reshape(cut)) for x in params])
        scores = jnp.concatenate([exchange(x.reshape(cut)) for x in (own_scores, scores)])
        mixed = [exchange(x) for x in plain_mix(scale, params, scores)]
        mixed = jnp.concatenate([x.reshape(GROUPS, ROWS, D) for x in mixed], axis=1)
    return unpack(mixed)


def solution(mesh):
    halves = Mesh(mesh.devices.reshape(2, -1), AXES)
    split = P(AXES, None, None)
    return jax.shard_map(
        on_device,
        mesh=halves,
        in_specs=(split, split, P(), P(), P(AXES, None), P()),
        out_specs=(split, split, split, split),
        check_vma=False,
    )
```

```python
import functools
import math

import jax
import jax.numpy as jnp
from jax import lax
from jax.experimental import pallas as pl
from jax.experimental.pallas import tpu as pltpu
from jax.sharding import PartitionSpec as P

D = 384
FF = 1536
S = 197
DATA = 10000
AXES = ("wide", "narrow")
PAD = 208
EDGE = 48
BLOCKS = D * FF // (EDGE * D)
COLS = FF // D
TILE = 16

gelu_c = math.sqrt(2.0 / math.pi)
isd = 1.0 / math.sqrt(D)
isf = 1.0 / math.sqrt(FF)


def dot(a, b, dims):
    return lax.dot_general(a, b, (dims, ((), ())), preferred_element_type=jnp.float32)


def score_kernel(
    factor, picks, image, target, first, second, out, xs, ts, normed, hidden, deriv, delta, back
):
    step = pl.program_id(0)
    images = pl.num_programs(0)
    rows = pl.ds(pl.multiple_of(step * PAD, PAD), PAD)

    @pl.when(step == 0)
    def _():
        xs[...] = jnp.zeros_like(xs)
        ts[...] = jnp.zeros_like(ts)

    xs[0:S, :] = image[0].astype(jnp.float32)
    ts[0:S, :] = target[0].astype(jnp.float32)
    xf = xs[...]
    mean = jnp.mean(xf, axis=1, keepdims=True)
    centered = xf - mean
    var = jnp.mean(centered * centered, axis=1, keepdims=True)
    nrm = (centered * lax.rsqrt(var + 1e-06)).astype(jnp.bfloat16)
    normed[rows, :] = nrm
    for c in range(COLS):
        cols = pl.ds(c * D, D)
        pre = dot(nrm, first[:, cols], ((1,), (0,))) * isd
        sq = pre * pre
        tval = jnp.tanh(pre * (gelu_c + (gelu_c * 0.044715) * sq))
        gate = 0.5 + 0.5 * tval
        hid = pre * gate
        hidden[rows, cols] = hid.astype(jnp.bfloat16)
        deriv[:, cols] = gate + hid * (1.0 - gate) * (
            2.0 * gelu_c + (6.0 * gelu_c * 0.044715) * sq
        )
    prod = dot(hidden[rows, :], second[...], ((1,), (0,))) * isf
    dlt = ((xs[...] + prod - ts[...]) * (1.0 / S)).astype(jnp.bfloat16)
    delta[rows, :] = dlt
    for c in range(COLS):
        cols = pl.ds(c * D, D)
        dhid = dot(dlt, second[cols, :], ((1,), (1,))) * isf
        back[rows, cols] = (dhid * deriv[:, cols]).astype(jnp.bfloat16)

    @pl.when(step == images - 1)
    def _():
        for c in range(COLS):
            cols = pl.ds(c * D, D)
            grad = dot(normed[...], back[:, cols], ((0,), (0,))) * (-factor * isd)
            score = (grad - first[:, cols].astype(jnp.float32)).astype(jnp.bfloat16)
            for r in range(D // EDGE):
                out[r * COLS + c, 0:EDGE, :] = score[r * EDGE : (r + 1) * EDGE, :]
            grad = dot(hidden[:, cols], delta[...], ((0,), (0,))) * (-factor * isf)
            score = (grad - second[cols, :].astype(jnp.float32)).astype(jnp.bfloat16)
            for r in range(D // EDGE):
                out[c * (D // EDGE) + r, EDGE : 2 * EDGE, :] = score[
                    r * EDGE : (r + 1) * EDGE, :
                ]


def particle_scores(first, second, images, targets, picks):
    count = picks.shape[0]
    rows = count * PAD
    bf = jnp.bfloat16
    return pl.pallas_call(
        functools.partial(score_kernel, DATA / count),
        out_shape=jax.ShapeDtypeStruct((BLOCKS, 2 * EDGE, D), bf),
        grid_spec=pltpu.PrefetchScalarGridSpec(
            num_scalar_prefetch=1,
            grid=(count,),
            in_specs=[
                pl.BlockSpec((1, S, D), lambda b, picks: (picks[b], 0, 0)),
                pl.BlockSpec((1, S, D), lambda b, picks: (picks[b], 0, 0)),
                pl.BlockSpec((D, FF), lambda b, picks: (0, 0)),
                pl.BlockSpec((FF, D), lambda b, picks: (0, 0)),
            ],
            out_specs=pl.BlockSpec((BLOCKS, 2 * EDGE, D), lambda b, picks: (0, 0, 0)),
            scratch_shapes=[
                pltpu.VMEM((PAD, D), jnp.float32),
                pltpu.VMEM((PAD, D), jnp.float32),
                pltpu.VMEM((rows, D), bf),
                pltpu.VMEM((rows, FF), bf),
                pltpu.VMEM((PAD, FF), jnp.float32),
                pltpu.VMEM((rows, D), bf),
                pltpu.VMEM((rows, FF), bf),
            ],
        ),
        compiler_params=pltpu.CompilerParams(vmem_limit_bytes=48 * 1024 * 1024),
        cost_estimate=pl.CostEstimate(
            flops=10 * count * PAD * D * FF,
            bytes_accessed=4 * (2 * D * FF + count * S * D),
            transcendentals=count * PAD * FF,
        ),
        name="score",
    )(picks, images, targets, first, second)


def gram_kernel(params, gram, total):
    members, rows, _ = params.shape
    wide = members * TILE
    total[...] = jnp.zeros_like(total)
    for r in range(rows // TILE):
        part = params[:, r * TILE : (r + 1) * TILE, :].reshape(wide, D)
        total[...] += dot(part, part, ((1,), (1,)))
    at = lax.broadcasted_iota(jnp.int32, (wide, wide), 0) % TILE
    to = lax.broadcasted_iota(jnp.int32, (wide, wide), 1) % TILE
    kept = jnp.where(at == to, total[...], 0.0)
    summed = jnp.sum(kept.reshape(members, TILE, wide), axis=1)
    turned = summed.T
    small = jnp.sum(turned.reshape(members, TILE, members), axis=1)
    packed = jnp.concatenate([small[8 * q : 8 * q + 8] for q in range(members // 8)], axis=1)
    gram[...] = packed


def pair_products(params):
    members, rows, _ = params.shape
    wide = members * TILE
    return pl.pallas_call(
        gram_kernel,
        out_shape=jax.ShapeDtypeStruct((8, members * members // 8), jnp.float32),
        scratch_shapes=[pltpu.VMEM((wide, wide), jnp.float32)],
        compiler_params=pltpu.CompilerParams(vmem_limit_bytes=32 * 1024 * 1024),
        cost_estimate=pl.CostEstimate(
            flops=2 * wide * wide * rows // TILE * D,
            bytes_accessed=2 * members * rows * D,
            transcendentals=0,
        ),
        name="gram",
    )(params)


def kernel_of(scale, partials):
    members = partials.shape[0]
    packed = jnp.sum(partials[...], axis=0)
    gram = jnp.concatenate(
        [packed[:, members * q : members * (q + 1)] for q in range(members // 8)], axis=0
    )
    row = lax.broadcasted_iota(jnp.int32, gram.shape, 0)
    col = lax.broadcasted_iota(jnp.int32, gram.shape, 1)
    own = jnp.where(row == col, gram, 0.0)
    dist = jnp.sum(own, axis=1, keepdims=True) + jnp.sum(own, axis=0, keepdims=True) - 2.0 * gram
    return jnp.exp(-dist / scale[0]).astype(jnp.bfloat16)


def spreading(kernel):
    members = kernel.shape[0]
    wide = members * TILE
    at = lax.broadcasted_iota(jnp.int32, (wide, members), 0) // TILE
    which = lax.broadcasted_iota(jnp.int32, (wide, members), 1)
    pick = jnp.where(at == which, 1.0, 0.0).astype(jnp.bfloat16)
    tall = dot(pick, kernel, ((1,), (0,))).astype(jnp.bfloat16)
    full = dot(tall, pick, ((1,), (1,)))
    row = lax.broadcasted_iota(jnp.int32, (wide, wide), 0) % TILE
    col = lax.broadcasted_iota(jnp.int32, (wide, wide), 1) % TILE
    return jnp.where(row == col, full, 0.0)


def spread_kernel(scale, partials, params, out, mixing):
    members, rows, _ = params.shape
    wide = members * TILE
    full = spreading(kernel_of(scale, partials))
    ksum = jnp.sum(full, axis=1, keepdims=True)
    mixer = full.astype(jnp.bfloat16)
    mixing[...] = mixer
    for r in range(rows // TILE):
        here = slice(r * TILE, (r + 1) * TILE)
        own = params[:, here, :].reshape(wide, D)
        mixed = dot(mixer, own, ((1,), (0,)))
        pushed = (ksum * own.astype(jnp.float32) - mixed) * (1.0 / members)
        out[:, here, :] = pushed.astype(jnp.bfloat16).reshape(members, TILE, D)


def spread_part(scale, partials, params):
    members, rows, _ = params.shape
    wide = members * TILE
    vmem = pl.BlockSpec(memory_space=pltpu.VMEM)
    return pl.pallas_call(
        spread_kernel,
        out_shape=(
            jax.ShapeDtypeStruct((members, 2 * rows, D), jnp.bfloat16),
            jax.ShapeDtypeStruct((wide, wide), jnp.bfloat16),
        ),
        grid=(1,),
        in_specs=[pl.BlockSpec(memory_space=pltpu.SMEM), vmem, vmem],
        out_specs=(
            pl.BlockSpec((members, rows, D), lambda i: (0, 1, 0)),
            pl.BlockSpec((wide, wide), lambda i: (0, 0)),
        ),
        compiler_params=pltpu.CompilerParams(vmem_limit_bytes=32 * 1024 * 1024),
        cost_estimate=pl.CostEstimate(
            flops=2 * wide * wide * rows // TILE * D,
            bytes_accessed=4 * members * rows * D,
            transcendentals=0,
        ),
        name="spread",
    )(scale, partials, params)


def attract_kernel(mixing, scores, half_done, out):
    members, rows, _ = scores.shape
    wide = members * TILE
    for r in range(rows // TILE):
        here = slice(r * TILE, (r + 1) * TILE)
        got = scores[:, here, :].reshape(wide, D)
        pulled = dot(mixing[...], got, ((1,), (0,))) * (1.0 / members)
        out[:, here, :] = pulled.astype(jnp.bfloat16).reshape(members, TILE, D)


def attract_part(mixing, scores, half_done):
    members, rows, _ = scores.shape
    wide = members * TILE
    vmem = pl.BlockSpec(memory_space=pltpu.VMEM)
    return pl.pallas_call(
        attract_kernel,
        out_shape=jax.ShapeDtypeStruct(half_done.shape, half_done.dtype),
        grid=(1,),
        in_specs=[vmem, vmem, pl.BlockSpec(memory_space=pl.ANY)],
        out_specs=pl.BlockSpec((members, rows, D), lambda i: (0, 0, 0)),
        input_output_aliases={2: 0},
        compiler_params=pltpu.CompilerParams(vmem_limit_bytes=32 * 1024 * 1024),
        cost_estimate=pl.CostEstimate(
            flops=2 * wide * wide * rows // TILE * D,
            bytes_accessed=4 * members * rows * D,
            transcendentals=0,
        ),
        name="attract",
    )(mixing, scores, half_done)


def plain_products(params):
    flat = params.reshape(params.shape[0], -1)
    return dot(flat, flat, ((1,), (1,)))


def plain_weighted(gram, scale, params, scores):
    members = params.shape[0]
    norms = jnp.diagonal(gram)
    dist = norms[:, None] + norms[None, :] - 2.0 * gram
    kernel = jnp.exp(-dist / scale[0]).astype(jnp.bfloat16)
    flat = params.reshape(members, -1)
    ksum = jnp.sum(kernel.astype(jnp.float32), axis=1, keepdims=True)
    attract = dot(kernel, scores.reshape(members, -1), ((1,), (0,))) / members
    mixed = dot(kernel, flat, ((1,), (0,)))
    spread = (flat.astype(jnp.float32) * ksum - mixed) / members
    return tuple(x.astype(jnp.bfloat16).reshape(params.shape) for x in (attract, spread))


def pack_kernel(first, second, out):
    for b in range(out.shape[0]):
        r, c = b // COLS * EDGE, b % COLS * D
        out[b, 0:EDGE, :] = first[0, r : r + EDGE, c : c + D]
        out[b, EDGE : 2 * EDGE, :] = second[0, b * EDGE : (b + 1) * EDGE, :]


def to_blocks(first, second):
    steps = 4
    return pl.pallas_call(
        pack_kernel,
        out_shape=jax.ShapeDtypeStruct((BLOCKS, 2 * EDGE, D), jnp.bfloat16),
        grid=(steps,),
        in_specs=[
            pl.BlockSpec((1, D // steps, FF), lambda i: (0, i, 0)),
            pl.BlockSpec((1, FF // steps, D), lambda i: (0, i, 0)),
        ],
        out_specs=pl.BlockSpec((BLOCKS // steps, 2 * EDGE, D), lambda i: (i, 0, 0)),
        compiler_params=pltpu.CompilerParams(vmem_limit_bytes=56 * 1024 * 1024),
        cost_estimate=pl.CostEstimate(flops=0, bytes_accessed=8 * D * FF, transcendentals=0),
        name="pack",
    )(first, second)


def unpack_kernel(blocks, first_a, second_a, first_s, second_s):
    for b in range(BLOCKS):
        r, c = b // COLS * EDGE, b % COLS * D
        first_a[0, r : r + EDGE, c : c + D] = blocks[b, 0:EDGE, :]
        second_a[0, b * EDGE : (b + 1) * EDGE, :] = blocks[b, EDGE : 2 * EDGE, :]
        first_s[0, r : r + EDGE, c : c + D] = blocks[b, 2 * EDGE : 3 * EDGE, :]
        second_s[0, b * EDGE : (b + 1) * EDGE, :] = blocks[b, 3 * EDGE : 4 * EDGE, :]


def from_blocks(blocks):
    shapes = (
        jax.ShapeDtypeStruct((1, D, FF), jnp.bfloat16),
        jax.ShapeDtypeStruct((1, FF, D), jnp.bfloat16),
    )
    return pl.pallas_call(
        unpack_kernel,
        out_shape=shapes + shapes,
        compiler_params=pltpu.CompilerParams(vmem_limit_bytes=24 * 1024 * 1024),
        cost_estimate=pl.CostEstimate(flops=0, bytes_accessed=16 * D * FF, transcendentals=0),
        name="unpack",
    )(blocks)


def exchange(blocks):
    return lax.all_to_all(blocks, AXES, split_axis=0, concat_axis=0, tiled=True)


def on_device(
    particles_first, particles_second, pool_images, pool_targets, batch_index, kernel_scale
):
    members = lax.axis_size("wide") * lax.axis_size("narrow")
    cut = (members, BLOCKS * 2 * EDGE // members, D)
    whole = (BLOCKS, 2 * EDGE, D)
    params = exchange(to_blocks(particles_first, particles_second).reshape(cut))
    scores = particle_scores(
        particles_first[0], particles_second[0], pool_images, pool_targets, batch_index[0]
    )
    if members == BLOCKS:
        partials = lax.all_gather(pair_products(params), AXES)
        params, scores = lax.optimization_barrier((params, scores))
        scores = exchange(scores)
        spread, mixing = spread_part(kernel_scale, partials, params)
        mixed = exchange(attract_part(mixing, scores, spread))
    else:
        scores = exchange(scores.reshape(cut))
        gram = lax.psum(plain_products(params), AXES)
        parts = plain_weighted(gram, kernel_scale, params, scores)
        mixed = jnp.concatenate([exchange(x).reshape(whole) for x in parts], axis=1)
    return from_blocks(mixed)


def solution(mesh):
    split = P(AXES, None, None)
    return jax.shard_map(
        on_device,
        mesh=mesh,
        in_specs=(split, split, P(), P(), P(AXES, None), P()),
        out_specs=(split, split, split, split),
        check_vma=False,
    )
```

```python
import functools
import math

import jax
import jax.numpy as jnp
from jax import lax
from jax.experimental import pallas as pl
from jax.experimental.pallas import tpu as pltpu
from jax.sharding import PartitionSpec as P

D = 384
FF = 1536
S = 197
DATA = 10000
AXES = ("wide", "narrow")
PAD = 208
EDGE = 48
BLOCKS = D * FF // (EDGE * D)
COLS = FF // D
TILE = 16
ROWS = 2 * EDGE
EXTRA = 8

gelu_c = math.sqrt(2.0 / math.pi)
isd = 1.0 / math.sqrt(D)
isf = 1.0 / math.sqrt(FF)


def dot(a, b, dims):
    return lax.dot_general(a, b, (dims, ((), ())), preferred_element_type=jnp.float32)


def score_kernel(
    factor, picks, image, target, first, second, out, xs, ts, normed, hidden, deriv, delta, back
):
    step = pl.program_id(0)
    images = pl.num_programs(0)
    rows = pl.ds(pl.multiple_of(step * PAD, PAD), PAD)

    @pl.when(step == 0)
    def _():
        xs[...] = jnp.zeros_like(xs)
        ts[...] = jnp.zeros_like(ts)

    xs[0:S, :] = image[0].astype(jnp.float32)
    ts[0:S, :] = target[0].astype(jnp.float32)
    xf = xs[...]
    mean = jnp.mean(xf, axis=1, keepdims=True)
    centered = xf - mean
    var = jnp.mean(centered * centered, axis=1, keepdims=True)
    nrm = (centered * lax.rsqrt(var + 1e-06)).astype(jnp.bfloat16)
    normed[rows, :] = nrm
    for c in range(COLS):
        cols = pl.ds(c * D, D)
        pre = dot(nrm, first[:, cols], ((1,), (0,))) * isd
        sq = pre * pre
        tval = jnp.tanh(pre * (gelu_c + (gelu_c * 0.044715) * sq))
        gate = 0.5 + 0.5 * tval
        hid = pre * gate
        hidden[rows, cols] = hid.astype(jnp.bfloat16)
        deriv[:, cols] = gate + hid * (1.0 - gate) * (
            2.0 * gelu_c + (6.0 * gelu_c * 0.044715) * sq
        )
    prod = dot(hidden[rows, :], second[...], ((1,), (0,))) * isf
    dlt = ((xs[...] + prod - ts[...]) * (1.0 / S)).astype(jnp.bfloat16)
    delta[rows, :] = dlt
    for c in range(COLS):
        cols = pl.ds(c * D, D)
        dhid = dot(dlt, second[cols, :], ((1,), (1,))) * isf
        back[rows, cols] = (dhid * deriv[:, cols]).astype(jnp.bfloat16)

    @pl.when(step == images - 1)
    def _():
        for c in range(COLS):
            cols = pl.ds(c * D, D)
            grad = dot(normed[...], back[:, cols], ((0,), (0,))) * (-factor * isd)
            score = (grad - first[:, cols].astype(jnp.float32)).astype(jnp.bfloat16)
            for r in range(D // EDGE):
                out[r * COLS + c, 0:EDGE, :] = score[r * EDGE : (r + 1) * EDGE, :]
            grad = dot(hidden[:, cols], delta[...], ((0,), (0,))) * (-factor * isf)
            score = (grad - second[cols, :].astype(jnp.float32)).astype(jnp.bfloat16)
            for r in range(D // EDGE):
                out[c * (D // EDGE) + r, EDGE : 2 * EDGE, :] = score[
                    r * EDGE : (r + 1) * EDGE, :
                ]


def particle_scores(first, second, images, targets, picks, extra):
    count = picks.shape[0]
    rows = count * PAD
    bf = jnp.bfloat16
    return pl.pallas_call(
        functools.partial(score_kernel, DATA / count),
        out_shape=jax.ShapeDtypeStruct((BLOCKS, ROWS + extra, D), bf),
        grid_spec=pltpu.PrefetchScalarGridSpec(
            num_scalar_prefetch=1,
            grid=(count,),
            in_specs=[
                pl.BlockSpec((1, S, D), lambda b, picks: (picks[b], 0, 0)),
                pl.BlockSpec((1, S, D), lambda b, picks: (picks[b], 0, 0)),
                pl.BlockSpec((D, FF), lambda b, picks: (0, 0)),
                pl.BlockSpec((FF, D), lambda b, picks: (0, 0)),
            ],
            out_specs=pl.BlockSpec((BLOCKS, ROWS, D), lambda b, picks: (0, 0, 0)),
            scratch_shapes=[
                pltpu.VMEM((PAD, D), jnp.float32),
                pltpu.VMEM((PAD, D), jnp.float32),
                pltpu.VMEM((rows, D), bf),
                pltpu.VMEM((rows, FF), bf),
                pltpu.VMEM((PAD, FF), jnp.float32),
                pltpu.VMEM((rows, D), bf),
                pltpu.VMEM((rows, FF), bf),
            ],
        ),
        compiler_params=pltpu.CompilerParams(vmem_limit_bytes=48 * 1024 * 1024),
        cost_estimate=pl.CostEstimate(
            flops=10 * count * PAD * D * FF,
            bytes_accessed=4 * (2 * D * FF + count * S * D),
            transcendentals=count * PAD * FF,
        ),
        name="score",
    )(picks, images, targets, first, second)


def gram_kernel(params, scores, out, total, parts, sem):
    members, rows, _ = params.shape
    wide = members * TILE
    total[...] = jnp.zeros_like(total)
    for r in range(rows // TILE):
        part = params[:, r * TILE : (r + 1) * TILE, :].reshape(wide, D)
        total[...] += dot(part, part, ((1,), (1,)))
    at = lax.broadcasted_iota(jnp.int32, (wide, wide), 0) % TILE
    to = lax.broadcasted_iota(jnp.int32, (wide, wide), 1) % TILE
    kept = jnp.where(at == to, total[...], 0.0)
    summed = jnp.sum(kept.reshape(members, TILE, wide), axis=1)
    turned = summed.T
    small = jnp.sum(turned.reshape(members, TILE, members), axis=1)
    packed = jnp.concatenate([small[8 * q : 8 * q + 8] for q in range(members // 8)], axis=1)
    high = packed.astype(jnp.bfloat16).astype(jnp.float32)
    middle = (packed - high).astype(jnp.bfloat16).astype(jnp.float32)
    low = packed - high - middle
    three = jnp.concatenate([high, middle, low], axis=1).astype(jnp.bfloat16)
    parts[...] = jnp.broadcast_to(three[None], parts.shape)
    copy = pltpu.make_async_copy(parts, out.at[:, pl.ds(rows, EXTRA), :], sem)
    copy.start()
    copy.wait()


def add_products(params, scores):
    members, rows, _ = params.shape
    wide = members * TILE
    return pl.pallas_call(
        gram_kernel,
        out_shape=jax.ShapeDtypeStruct(scores.shape, scores.dtype),
        in_specs=[pl.BlockSpec(memory_space=pltpu.VMEM), pl.BlockSpec(memory_space=pl.ANY)],
        out_specs=pl.BlockSpec(memory_space=pl.ANY),
        input_output_aliases={1: 0},
        scratch_shapes=[
            pltpu.VMEM((wide, wide), jnp.float32),
            pltpu.VMEM((members, EXTRA, D), jnp.bfloat16),
            pltpu.SemaphoreType.DMA,
        ],
        compiler_params=pltpu.CompilerParams(vmem_limit_bytes=32 * 1024 * 1024),
        cost_estimate=pl.CostEstimate(
            flops=2 * wide * wide * rows // TILE * D,
            bytes_accessed=2 * members * rows * D,
            transcendentals=0,
        ),
        name="gram",
    )(params, scores)


def kernel_of(scale, parts):
    members = parts.shape[0]
    lanes = members * members // 8
    three = jnp.sum(parts[...].astype(jnp.float32), axis=0)
    packed = three[:, :lanes] + three[:, lanes : 2 * lanes] + three[:, 2 * lanes : 3 * lanes]
    gram = jnp.concatenate(
        [packed[:, members * q : members * (q + 1)] for q in range(members // 8)], axis=0
    )
    row = lax.broadcasted_iota(jnp.int32, gram.shape, 0)
    col = lax.broadcasted_iota(jnp.int32, gram.shape, 1)
    own = jnp.where(row == col, gram, 0.0)
    dist = jnp.sum(own, axis=1, keepdims=True) + jnp.sum(own, axis=0, keepdims=True) - 2.0 * gram
    return jnp.exp(-dist / scale[0]).astype(jnp.bfloat16)


def spreading(kernel):
    members = kernel.shape[0]
    wide = members * TILE
    at = lax.broadcasted_iota(jnp.int32, (wide, members), 0) // TILE
    which = lax.broadcasted_iota(jnp.int32, (wide, members), 1)
    pick = jnp.where(at == which, 1.0, 0.0).astype(jnp.bfloat16)
    tall = dot(pick, kernel, ((1,), (0,))).astype(jnp.bfloat16)
    full = dot(tall, pick, ((1,), (1,)))
    row = lax.broadcasted_iota(jnp.int32, (wide, wide), 0) % TILE
    col = lax.broadcasted_iota(jnp.int32, (wide, wide), 1) % TILE
    return jnp.where(row == col, full, 0.0)


def mix_kernel(scale, parts, scores, params, out, mixing, ksum):
    members = params.shape[0]
    wide = members * TILE

    @pl.when(pl.program_id(0) == 0)
    def _():
        full = spreading(kernel_of(scale, parts))
        ksum[...] = jnp.sum(full, axis=1, keepdims=True)
        mixing[...] = full.astype(jnp.bfloat16)

    got = scores[...].reshape(wide, D)
    pulled = dot(mixing[...], got, ((1,), (0,))) * (1.0 / members)
    out[:, 0] = pulled.astype(jnp.bfloat16).reshape(members, TILE, D)
    own = params[...].reshape(wide, D)
    mixed = dot(mixing[...], own, ((1,), (0,)))
    pushed = (ksum[...] * own.astype(jnp.float32) - mixed) * (1.0 / members)
    out[:, 1] = pushed.astype(jnp.bfloat16).reshape(members, TILE, D)


def weighted(scale, scores, params):
    members, rows, _ = params.shape
    wide = members * TILE
    return pl.pallas_call(
        mix_kernel,
        out_shape=jax.ShapeDtypeStruct((members, 2, rows, D), jnp.bfloat16),
        grid=(rows // TILE,),
        in_specs=[
            pl.BlockSpec(memory_space=pltpu.SMEM),
            pl.BlockSpec((members, EXTRA, D), lambda r: (0, rows // EXTRA, 0)),
            pl.BlockSpec((members, TILE, D), lambda r: (0, r, 0)),
            pl.BlockSpec((members, TILE, D), lambda r: (0, r, 0)),
        ],
        out_specs=pl.BlockSpec((members, 2, TILE, D), lambda r: (0, 0, r, 0)),
        scratch_shapes=[
            pltpu.VMEM((wide, wide), jnp.bfloat16),
            pltpu.VMEM((wide, 1), jnp.float32),
        ],
        compiler_params=pltpu.CompilerParams(vmem_limit_bytes=32 * 1024 * 1024),
        cost_estimate=pl.CostEstimate(
            flops=4 * wide * wide * rows // TILE * D,
            bytes_accessed=8 * members * rows * D,
            transcendentals=0,
        ),
        name="mix",
    )(scale, scores, scores, params)


def plain_products(params):
    flat = params.reshape(params.shape[0], -1)
    return dot(flat, flat, ((1,), (1,)))


def plain_weighted(gram, scale, params, scores):
    members = params.shape[0]
    norms = jnp.diagonal(gram)
    dist = norms[:, None] + norms[None, :] - 2.0 * gram
    kernel = jnp.exp(-dist / scale[0]).astype(jnp.bfloat16)
    flat = params.reshape(members, -1)
    ksum = jnp.sum(kernel.astype(jnp.float32), axis=1, keepdims=True)
    attract = dot(kernel, scores.reshape(members, -1), ((1,), (0,))) / members
    mixed = dot(kernel, flat, ((1,), (0,)))
    spread = (flat.astype(jnp.float32) * ksum - mixed) / members
    return tuple(x.astype(jnp.bfloat16).reshape(params.shape) for x in (attract, spread))


def run(copies):
    for copy in copies:
        copy.start()
    for copy in copies:
        copy.wait()


def pack_kernel(first, second, out, sems):
    copies = [pltpu.make_async_copy(second, out.at[:, :, pl.ds(EDGE, EDGE), :], sems.at[COLS])]
    for c in range(COLS):
        here = first.at[:, :, pl.ds(c * D, D)]
        copies.append(pltpu.make_async_copy(here, out.at[:, c, pl.ds(0, EDGE), :], sems.at[c]))
    run(copies)


def to_blocks(first, second):
    any_space = pl.BlockSpec(memory_space=pl.ANY)
    deep = BLOCKS // COLS
    packed = pl.pallas_call(
        pack_kernel,
        out_shape=jax.ShapeDtypeStruct((deep, COLS, ROWS, D), jnp.bfloat16),
        in_specs=[any_space, any_space],
        out_specs=any_space,
        scratch_shapes=[pltpu.SemaphoreType.DMA((COLS + 1,))],
        cost_estimate=pl.CostEstimate(flops=0, bytes_accessed=8 * D * FF, transcendentals=0),
        name="pack",
    )(first.reshape(deep, EDGE, FF), second.reshape(deep, COLS, EDGE, D))
    return packed.reshape(BLOCKS, ROWS, D)


def unpack_kernel(blocks, first_a, second_a, first_s, second_s, sems):
    copies = []
    for which, (first, second) in enumerate(((first_a, second_a), (first_s, second_s))):
        at = which * ROWS
        here = blocks.at[:, :, pl.ds(at + EDGE, EDGE), :]
        copies.append(pltpu.make_async_copy(here, second, sems.at[which, COLS]))
        for c in range(COLS):
            here = blocks.at[:, c, pl.ds(at, EDGE), :]
            there = first.at[:, :, pl.ds(c * D, D)]
            copies.append(pltpu.make_async_copy(here, there, sems.at[which, c]))
    run(copies)


def from_blocks(blocks):
    any_space = pl.BlockSpec(memory_space=pl.ANY)
    deep = BLOCKS // COLS
    shapes = (
        jax.ShapeDtypeStruct((deep, EDGE, FF), jnp.bfloat16),
        jax.ShapeDtypeStruct((deep, COLS, EDGE, D), jnp.bfloat16),
    )
    outs = pl.pallas_call(
        unpack_kernel,
        out_shape=shapes + shapes,
        in_specs=[any_space],
        out_specs=(any_space,) * 4,
        scratch_shapes=[pltpu.SemaphoreType.DMA((2, COLS + 1))],
        cost_estimate=pl.CostEstimate(flops=0, bytes_accessed=16 * D * FF, transcendentals=0),
        name="unpack",
    )(blocks.reshape(deep, COLS, 2 * ROWS, D))
    return tuple(x.reshape(s) for x, s in zip(outs, ((1, D, FF), (1, FF, D)) * 2))


def exchange(blocks):
    return lax.all_to_all(blocks, AXES, split_axis=0, concat_axis=0, tiled=True)


def on_device(
    particles_first, particles_second, pool_images, pool_targets, batch_index, kernel_scale
):
    members = lax.axis_size("wide") * lax.axis_size("narrow")
    cut = (members, BLOCKS * ROWS // members, D)
    tiled = members == BLOCKS
    params = exchange(to_blocks(particles_first, particles_second).reshape(cut))
    scores = particle_scores(
        particles_first[0],
        particles_second[0],
        pool_images,
        pool_targets,
        batch_index[0],
        EXTRA if tiled else 0,
    )
    if tiled:
        scores = exchange(add_products(params, scores))
        mixed = exchange(weighted(kernel_scale, scores, params).reshape(members, 2 * ROWS, D))
    else:
        scores = exchange(scores.reshape(cut))
        gram = lax.psum(plain_products(params), AXES)
        parts = plain_weighted(gram, kernel_scale, params, scores)
        mixed = [exchange(x).reshape(BLOCKS, ROWS, D) for x in parts]
        mixed = jnp.concatenate(mixed, axis=1)
    return from_blocks(mixed)


def solution(mesh):
    split = P(AXES, None, None)
    return jax.shard_map(
        on_device,
        mesh=mesh,
        in_specs=(split, split, P(), P(), P(AXES, None), P()),
        out_specs=(split, split, split, split),
        check_vma=False,
    )
```

```python
import functools
import math

import jax
import jax.numpy as jnp
from jax import lax
from jax.experimental import pallas as pl
from jax.experimental.pallas import tpu as pltpu
from jax.sharding import PartitionSpec as P

D = 384
FF = 1536
S = 197
DATA = 10000
AXES = ("wide", "narrow")
PAD = 208
EDGE = 48
BLOCKS = D * FF // (EDGE * D)
COLS = FF // D
TILE = 16
ROWS = 2 * EDGE
EXTRA = 8

gelu_c = math.sqrt(2.0 / math.pi)
isd = 1.0 / math.sqrt(D)
isf = 1.0 / math.sqrt(FF)


def dot(a, b, dims):
    return lax.dot_general(a, b, (dims, ((), ())), preferred_element_type=jnp.float32)


def score_kernel(
    factor, picks, image, target, first, second, out, xs, ts, normed, hidden, deriv, delta, back
):
    step = pl.program_id(0)
    images = pl.num_programs(0)
    rows = pl.ds(pl.multiple_of(step * PAD, PAD), PAD)

    @pl.when(step == 0)
    def _():
        xs[...] = jnp.zeros_like(xs)
        ts[...] = jnp.zeros_like(ts)

    xs[0:S, :] = image[0].astype(jnp.float32)
    ts[0:S, :] = target[0].astype(jnp.float32)
    xf = xs[...]
    mean = jnp.mean(xf, axis=1, keepdims=True)
    centered = xf - mean
    var = jnp.mean(centered * centered, axis=1, keepdims=True)
    nrm = (centered * lax.rsqrt(var + 1e-06)).astype(jnp.bfloat16)
    normed[rows, :] = nrm
    for c in range(COLS):
        cols = pl.ds(c * D, D)
        pre = dot(nrm, first[:, cols], ((1,), (0,))) * isd
        sq = pre * pre
        tval = jnp.tanh(pre * (gelu_c + (gelu_c * 0.044715) * sq))
        gate = 0.5 + 0.5 * tval
        hid = pre * gate
        hidden[rows, cols] = hid.astype(jnp.bfloat16)
        deriv[:, cols] = gate + hid * (1.0 - gate) * (
            2.0 * gelu_c + (6.0 * gelu_c * 0.044715) * sq
        )
    prod = dot(hidden[rows, :], second[...], ((1,), (0,))) * isf
    dlt = ((xs[...] + prod - ts[...]) * (1.0 / S)).astype(jnp.bfloat16)
    delta[rows, :] = dlt
    for c in range(COLS):
        cols = pl.ds(c * D, D)
        dhid = dot(dlt, second[cols, :], ((1,), (1,))) * isf
        back[rows, cols] = (dhid * deriv[:, cols]).astype(jnp.bfloat16)

    @pl.when(step == images - 1)
    def _():
        for c in range(COLS):
            cols = pl.ds(c * D, D)
            grad = dot(normed[...], back[:, cols], ((0,), (0,))) * (-factor * isd)
            score = (grad - first[:, cols].astype(jnp.float32)).astype(jnp.bfloat16)
            for r in range(D // EDGE):
                out[r * COLS + c, 0:EDGE, :] = score[r * EDGE : (r + 1) * EDGE, :]
            grad = dot(hidden[:, cols], delta[...], ((0,), (0,))) * (-factor * isf)
            score = (grad - second[cols, :].astype(jnp.float32)).astype(jnp.bfloat16)
            for r in range(D // EDGE):
                out[c * (D // EDGE) + r, EDGE : 2 * EDGE, :] = score[
                    r * EDGE : (r + 1) * EDGE, :
                ]


def particle_scores(first, second, images, targets, picks, extra):
    count = picks.shape[0]
    rows = count * PAD
    bf = jnp.bfloat16
    return pl.pallas_call(
        functools.partial(score_kernel, DATA / count),
        out_shape=jax.ShapeDtypeStruct((BLOCKS, ROWS + extra, D), bf),
        grid_spec=pltpu.PrefetchScalarGridSpec(
            num_scalar_prefetch=1,
            grid=(count,),
            in_specs=[
                pl.BlockSpec((1, S, D), lambda b, picks: (picks[b], 0, 0)),
                pl.BlockSpec((1, S, D), lambda b, picks: (picks[b], 0, 0)),
                pl.BlockSpec((D, FF), lambda b, picks: (0, 0)),
                pl.BlockSpec((FF, D), lambda b, picks: (0, 0)),
            ],
            out_specs=pl.BlockSpec((BLOCKS, ROWS, D), lambda b, picks: (0, 0, 0)),
            scratch_shapes=[
                pltpu.VMEM((PAD, D), jnp.float32),
                pltpu.VMEM((PAD, D), jnp.float32),
                pltpu.VMEM((rows, D), bf),
                pltpu.VMEM((rows, FF), bf),
                pltpu.VMEM((PAD, FF), jnp.float32),
                pltpu.VMEM((rows, D), bf),
                pltpu.VMEM((rows, FF), bf),
            ],
        ),
        compiler_params=pltpu.CompilerParams(vmem_limit_bytes=48 * 1024 * 1024),
        cost_estimate=pl.CostEstimate(
            flops=10 * count * PAD * D * FF,
            bytes_accessed=4 * (2 * D * FF + count * S * D),
            transcendentals=count * PAD * FF,
        ),
        name="score",
    )(picks, images, targets, first, second)


def gram_kernel(params, scores, out, total, parts, sem):
    members, rows, _ = params.shape
    wide = members * TILE
    total[...] = jnp.zeros_like(total)
    for r in range(rows // TILE):
        part = params[:, r * TILE : (r + 1) * TILE, :].reshape(wide, D)
        total[...] += dot(part, part, ((1,), (1,)))
    at = lax.broadcasted_iota(jnp.int32, (wide, wide), 0) % TILE
    to = lax.broadcasted_iota(jnp.int32, (wide, wide), 1) % TILE
    kept = jnp.where(at == to, total[...], 0.0)
    summed = jnp.sum(kept.reshape(members, TILE, wide), axis=1)
    turned = summed.T
    small = jnp.sum(turned.reshape(members, TILE, members), axis=1)
    packed = jnp.concatenate([small[8 * q : 8 * q + 8] for q in range(members // 8)], axis=1)
    high = packed.astype(jnp.bfloat16).astype(jnp.float32)
    middle = (packed - high).astype(jnp.bfloat16).astype(jnp.float32)
    low = packed - high - middle
    three = jnp.concatenate([high, middle, low], axis=1).astype(jnp.bfloat16)
    parts[...] = jnp.broadcast_to(three[None], parts.shape)
    copy = pltpu.make_async_copy(parts, out.at[:, pl.ds(rows, EXTRA), :], sem)
    copy.start()
    copy.wait()


def add_products(params, scores):
    members, rows, _ = params.shape
    wide = members * TILE
    return pl.pallas_call(
        gram_kernel,
        out_shape=jax.ShapeDtypeStruct(scores.shape, scores.dtype),
        in_specs=[pl.BlockSpec(memory_space=pltpu.VMEM), pl.BlockSpec(memory_space=pltpu.HBM)],
        out_specs=pl.BlockSpec(memory_space=pltpu.HBM),
        input_output_aliases={1: 0},
        scratch_shapes=[
            pltpu.VMEM((wide, wide), jnp.float32),
            pltpu.VMEM((members, EXTRA, D), jnp.bfloat16),
            pltpu.SemaphoreType.DMA,
        ],
        compiler_params=pltpu.CompilerParams(vmem_limit_bytes=59 * 1024 * 1024),
        cost_estimate=pl.CostEstimate(
            flops=2 * wide * wide * rows // TILE * D,
            bytes_accessed=2 * members * rows * D,
            transcendentals=0,
        ),
        name="gram",
    )(params, scores)


def kernel_of(scale, parts):
    members = parts.shape[0]
    lanes = members * members // 8
    three = jnp.sum(parts[...].astype(jnp.float32), axis=0)
    packed = three[:, :lanes] + three[:, lanes : 2 * lanes] + three[:, 2 * lanes : 3 * lanes]
    gram = jnp.concatenate(
        [packed[:, members * q : members * (q + 1)] for q in range(members // 8)], axis=0
    )
    row = lax.broadcasted_iota(jnp.int32, gram.shape, 0)
    col = lax.broadcasted_iota(jnp.int32, gram.shape, 1)
    own = jnp.where(row == col, gram, 0.0)
    dist = jnp.sum(own, axis=1, keepdims=True) + jnp.sum(own, axis=0, keepdims=True) - 2.0 * gram
    return jnp.exp(-dist / scale[0]).astype(jnp.bfloat16)


def spreading(kernel):
    members = kernel.shape[0]
    wide = members * TILE
    at = lax.broadcasted_iota(jnp.int32, (wide, members), 0) // TILE
    which = lax.broadcasted_iota(jnp.int32, (wide, members), 1)
    pick = jnp.where(at == which, 1.0, 0.0).astype(jnp.bfloat16)
    tall = dot(pick, kernel, ((1,), (0,))).astype(jnp.bfloat16)
    full = dot(tall, pick, ((1,), (1,)))
    row = lax.broadcasted_iota(jnp.int32, (wide, wide), 0) % TILE
    col = lax.broadcasted_iota(jnp.int32, (wide, wide), 1) % TILE
    return jnp.where(row == col, full, 0.0)


def mix_kernel(scale, parts, scores, params, out, mixing, ksum):
    members = params.shape[0]
    wide = members * TILE

    @pl.when(pl.program_id(0) == 0)
    def _():
        full = spreading(kernel_of(scale, parts))
        ksum[...] = jnp.sum(full, axis=1, keepdims=True)
        mixing[...] = full.astype(jnp.bfloat16)

    got = scores[...].reshape(wide, D)
    pulled = dot(mixing[...], got, ((1,), (0,))) * (1.0 / members)
    out[:, 0] = pulled.astype(jnp.bfloat16).reshape(members, TILE, D)
    own = params[...].reshape(wide, D)
    mixed = dot(mixing[...], own, ((1,), (0,)))
    pushed = (ksum[...] * own.astype(jnp.float32) - mixed) * (1.0 / members)
    out[:, 1] = pushed.astype(jnp.bfloat16).reshape(members, TILE, D)


def weighted(scale, scores, params):
    members, rows, _ = params.shape
    wide = members * TILE
    return pl.pallas_call(
        mix_kernel,
        out_shape=jax.ShapeDtypeStruct((members, 2, rows, D), jnp.bfloat16),
        grid=(rows // TILE,),
        in_specs=[
            pl.BlockSpec(memory_space=pltpu.SMEM),
            pl.BlockSpec((members, EXTRA, D), lambda r: (0, rows // EXTRA, 0)),
            pl.BlockSpec((members, TILE, D), lambda r: (0, r, 0)),
            pl.BlockSpec((members, TILE, D), lambda r: (0, r, 0)),
        ],
        out_specs=pl.BlockSpec((members, 2, TILE, D), lambda r: (0, 0, r, 0)),
        scratch_shapes=[
            pltpu.VMEM((wide, wide), jnp.bfloat16),
            pltpu.VMEM((wide, 1), jnp.float32),
        ],
        compiler_params=pltpu.CompilerParams(vmem_limit_bytes=59 * 1024 * 1024),
        cost_estimate=pl.CostEstimate(
            flops=4 * wide * wide * rows // TILE * D,
            bytes_accessed=8 * members * rows * D,
            transcendentals=0,
        ),
        name="mix",
    )(scale, scores, scores, params)


def plain_products(params):
    flat = params.reshape(params.shape[0], -1)
    return dot(flat, flat, ((1,), (1,)))


def plain_weighted(gram, scale, params, scores):
    members = params.shape[0]
    norms = jnp.diagonal(gram)
    dist = norms[:, None] + norms[None, :] - 2.0 * gram
    kernel = jnp.exp(-dist / scale[0]).astype(jnp.bfloat16)
    flat = params.reshape(members, -1)
    ksum = jnp.sum(kernel.astype(jnp.float32), axis=1, keepdims=True)
    attract = dot(kernel, scores.reshape(members, -1), ((1,), (0,))) / members
    mixed = dot(kernel, flat, ((1,), (0,)))
    spread = (flat.astype(jnp.float32) * ksum - mixed) / members
    return tuple(x.astype(jnp.bfloat16).reshape(params.shape) for x in (attract, spread))


def run(copies):
    for copy in copies:
        copy.start()
    for copy in copies:
        copy.wait()


def pack_kernel(first, second, out, sems):
    copies = [pltpu.make_async_copy(second, out.at[:, :, pl.ds(EDGE, EDGE), :], sems.at[COLS])]
    for c in range(COLS):
        here = first.at[:, :, pl.ds(c * D, D)]
        copies.append(pltpu.make_async_copy(here, out.at[:, c, pl.ds(0, EDGE), :], sems.at[c]))
    run(copies)


def to_blocks(first, second):
    deep = BLOCKS // COLS
    packed = pl.pallas_call(
        pack_kernel,
        out_shape=jax.ShapeDtypeStruct((deep, COLS, ROWS, D), jnp.bfloat16),
        in_specs=[pl.BlockSpec(memory_space=pltpu.HBM)] * 2,
        out_specs=pl.BlockSpec(memory_space=pltpu.VMEM),
        scratch_shapes=[pltpu.SemaphoreType.DMA((COLS + 1,))],
        cost_estimate=pl.CostEstimate(flops=0, bytes_accessed=8 * D * FF, transcendentals=0),
        name="pack",
    )(first.reshape(deep, EDGE, FF), second.reshape(deep, COLS, EDGE, D))
    return packed.reshape(BLOCKS, ROWS, D)


def unpack_kernel(blocks, first_a, second_a, first_s, second_s, sems):
    copies = []
    for which, (first, second) in enumerate(((first_a, second_a), (first_s, second_s))):
        at = which * ROWS
        here = blocks.at[:, :, pl.ds(at + EDGE, EDGE), :]
        copies.append(pltpu.make_async_copy(here, second, sems.at[which, COLS]))
        for c in range(COLS):
            here = blocks.at[:, c, pl.ds(at, EDGE), :]
            there = first.at[:, :, pl.ds(c * D, D)]
            copies.append(pltpu.make_async_copy(here, there, sems.at[which, c]))
    run(copies)


def from_blocks(blocks):
    deep = BLOCKS // COLS
    shapes = (
        jax.ShapeDtypeStruct((deep, EDGE, FF), jnp.bfloat16),
        jax.ShapeDtypeStruct((deep, COLS, EDGE, D), jnp.bfloat16),
    )
    outs = pl.pallas_call(
        unpack_kernel,
        out_shape=shapes + shapes,
        in_specs=[pl.BlockSpec(memory_space=pltpu.VMEM)],
        out_specs=(pl.BlockSpec(memory_space=pltpu.HBM),) * 4,
        scratch_shapes=[pltpu.SemaphoreType.DMA((2, COLS + 1))],
        cost_estimate=pl.CostEstimate(flops=0, bytes_accessed=16 * D * FF, transcendentals=0),
        name="unpack",
    )(blocks.reshape(deep, COLS, 2 * ROWS, D))
    return tuple(x.reshape(s) for x, s in zip(outs, ((1, D, FF), (1, FF, D)) * 2))


def exchange(blocks):
    return lax.all_to_all(blocks, AXES, split_axis=0, concat_axis=0, tiled=True)


def on_device(
    particles_first, particles_second, pool_images, pool_targets, batch_index, kernel_scale
):
    members = lax.axis_size("wide") * lax.axis_size("narrow")
    cut = (members, BLOCKS * ROWS // members, D)
    tiled = members == BLOCKS
    params = exchange(to_blocks(particles_first, particles_second).reshape(cut))
    scores = particle_scores(
        particles_first[0],
        particles_second[0],
        pool_images,
        pool_targets,
        batch_index[0],
        EXTRA if tiled else 0,
    )
    if tiled:
        scores = exchange(add_products(params, scores))
        mixed = exchange(weighted(kernel_scale, scores, params).reshape(members, 2 * ROWS, D))
    else:
        scores = exchange(scores.reshape(cut))
        gram = lax.psum(plain_products(params), AXES)
        parts = plain_weighted(gram, kernel_scale, params, scores)
        mixed = [exchange(x).reshape(BLOCKS, ROWS, D) for x in parts]
        mixed = jnp.concatenate(mixed, axis=1)
    return from_blocks(mixed)


def solution(mesh):
    split = P(AXES, None, None)
    return jax.shard_map(
        on_device,
        mesh=mesh,
        in_specs=(split, split, P(), P(), P(AXES, None), P()),
        out_specs=(split, split, split, split),
        check_vma=False,
    )
```

```python
import functools
import math

import jax
import jax.numpy as jnp
from jax import lax
from jax.experimental import pallas as pl
from jax.experimental.pallas import tpu as pltpu
from jax.sharding import Mesh
from jax.sharding import PartitionSpec as P

D = 384
FF = 1536
S = 197
DATA = 10000
AXES = ("far", "near", "rest")
ORDER = ("rest", "near", "far")
PAD = 208
EDGE = 48
BLOCKS = D * FF // (EDGE * D)
COLS = FF // D
TILE = 16
ROWS = 2 * EDGE
EXTRA = 8

gelu_c = math.sqrt(2.0 / math.pi)
isd = 1.0 / math.sqrt(D)
isf = 1.0 / math.sqrt(FF)


def dot(a, b, dims):
    return lax.dot_general(a, b, (dims, ((), ())), preferred_element_type=jnp.float32)


def score_kernel(
    factor, picks, image, target, first, second, out, xs, ts, normed, hidden, deriv, delta, back
):
    step = pl.program_id(0)
    images = pl.num_programs(0)
    rows = pl.ds(pl.multiple_of(step * PAD, PAD), PAD)

    @pl.when(step == 0)
    def _():
        xs[...] = jnp.zeros_like(xs)
        ts[...] = jnp.zeros_like(ts)

    xs[0:S, :] = image[0].astype(jnp.float32)
    ts[0:S, :] = target[0].astype(jnp.float32)
    xf = xs[...]
    mean = jnp.mean(xf, axis=1, keepdims=True)
    centered = xf - mean
    var = jnp.mean(centered * centered, axis=1, keepdims=True)
    nrm = (centered * lax.rsqrt(var + 1e-06)).astype(jnp.bfloat16)
    normed[rows, :] = nrm
    for c in range(COLS):
        cols = pl.ds(c * D, D)
        pre = dot(nrm, first[:, cols], ((1,), (0,))) * isd
        sq = pre * pre
        tval = jnp.tanh(pre * (gelu_c + (gelu_c * 0.044715) * sq))
        gate = 0.5 + 0.5 * tval
        hid = pre * gate
        hidden[rows, cols] = hid.astype(jnp.bfloat16)
        deriv[:, cols] = gate + hid * (1.0 - gate) * (
            2.0 * gelu_c + (6.0 * gelu_c * 0.044715) * sq
        )
    prod = dot(hidden[rows, :], second[...], ((1,), (0,))) * isf
    dlt = ((xs[...] + prod - ts[...]) * (1.0 / S)).astype(jnp.bfloat16)
    delta[rows, :] = dlt
    for c in range(COLS):
        cols = pl.ds(c * D, D)
        dhid = dot(dlt, second[cols, :], ((1,), (1,))) * isf
        back[rows, cols] = (dhid * deriv[:, cols]).astype(jnp.bfloat16)

    @pl.when(step == images - 1)
    def _():
        for c in range(COLS):
            cols = pl.ds(c * D, D)
            grad = dot(normed[...], back[:, cols], ((0,), (0,))) * (-factor * isd)
            score = (grad - first[:, cols].astype(jnp.float32)).astype(jnp.bfloat16)
            for r in range(D // EDGE):
                out[r * COLS + c, 0:EDGE, :] = score[r * EDGE : (r + 1) * EDGE, :]
            grad = dot(hidden[:, cols], delta[...], ((0,), (0,))) * (-factor * isf)
            score = (grad - second[cols, :].astype(jnp.float32)).astype(jnp.bfloat16)
            for r in range(D // EDGE):
                out[c * (D // EDGE) + r, EDGE : 2 * EDGE, :] = score[
                    r * EDGE : (r + 1) * EDGE, :
                ]


def particle_scores(first, second, images, targets, picks, extra):
    count = picks.shape[0]
    rows = count * PAD
    bf = jnp.bfloat16
    return pl.pallas_call(
        functools.partial(score_kernel, DATA / count),
        out_shape=jax.ShapeDtypeStruct((BLOCKS, ROWS + extra, D), bf),
        grid_spec=pltpu.PrefetchScalarGridSpec(
            num_scalar_prefetch=1,
            grid=(count,),
            in_specs=[
                pl.BlockSpec((1, S, D), lambda b, picks: (picks[b], 0, 0)),
                pl.BlockSpec((1, S, D), lambda b, picks: (picks[b], 0, 0)),
                pl.BlockSpec((D, FF), lambda b, picks: (0, 0)),
                pl.BlockSpec((FF, D), lambda b, picks: (0, 0)),
            ],
            out_specs=pl.BlockSpec((BLOCKS, ROWS, D), lambda b, picks: (0, 0, 0)),
            scratch_shapes=[
                pltpu.VMEM((PAD, D), jnp.float32),
                pltpu.VMEM((PAD, D), jnp.float32),
                pltpu.VMEM((rows, D), bf),
                pltpu.VMEM((rows, FF), bf),
                pltpu.VMEM((PAD, FF), jnp.float32),
                pltpu.VMEM((rows, D), bf),
                pltpu.VMEM((rows, FF), bf),
            ],
        ),
        compiler_params=pltpu.CompilerParams(vmem_limit_bytes=32 * 1024 * 1024),
        cost_estimate=pl.CostEstimate(
            flops=10 * count * PAD * D * FF,
            bytes_accessed=4 * (2 * D * FF + count * S * D),
            transcendentals=count * PAD * FF,
        ),
        name="score",
    )(picks, images, targets, first, second)


def gram_kernel(params, scores, out, total, parts, sem):
    members, rows, _ = params.shape
    wide = members * TILE
    total[...] = jnp.zeros_like(total)
    for r in range(rows // TILE):
        part = params[:, r * TILE : (r + 1) * TILE, :].reshape(wide, D)
        total[...] += dot(part, part, ((1,), (1,)))
    at = lax.broadcasted_iota(jnp.int32, (wide, wide), 0) % TILE
    to = lax.broadcasted_iota(jnp.int32, (wide, wide), 1) % TILE
    kept = jnp.where(at == to, total[...], 0.0)
    summed = jnp.sum(kept.reshape(members, TILE, wide), axis=1)
    turned = summed.T
    small = jnp.sum(turned.reshape(members, TILE, members), axis=1)
    packed = jnp.concatenate([small[8 * q : 8 * q + 8] for q in range(members // 8)], axis=1)
    high = packed.astype(jnp.bfloat16).astype(jnp.float32)
    middle = (packed - high).astype(jnp.bfloat16).astype(jnp.float32)
    low = packed - high - middle
    three = jnp.concatenate([high, middle, low], axis=1).astype(jnp.bfloat16)
    parts[...] = jnp.broadcast_to(three[None], parts.shape)
    copy = pltpu.make_async_copy(parts, out.at[:, pl.ds(rows, EXTRA), :], sem)
    copy.start()
    copy.wait()


def add_products(params, scores):
    members, rows, _ = params.shape
    wide = members * TILE
    return pl.pallas_call(
        gram_kernel,
        out_shape=jax.ShapeDtypeStruct(scores.shape, scores.dtype),
        in_specs=[pl.BlockSpec(memory_space=pltpu.VMEM), pl.BlockSpec(memory_space=pltpu.HBM)],
        out_specs=pl.BlockSpec(memory_space=pltpu.HBM),
        input_output_aliases={1: 0},
        scratch_shapes=[
            pltpu.VMEM((wide, wide), jnp.float32),
            pltpu.VMEM((members, EXTRA, D), jnp.bfloat16),
            pltpu.SemaphoreType.DMA,
        ],
        compiler_params=pltpu.CompilerParams(vmem_limit_bytes=16 * 1024 * 1024),
        cost_estimate=pl.CostEstimate(
            flops=2 * wide * wide * rows // TILE * D,
            bytes_accessed=2 * members * rows * D,
            transcendentals=0,
        ),
        name="gram",
    )(params, scores)


def kernel_of(scale, parts):
    members = parts.shape[0]
    lanes = members * members // 8
    three = jnp.sum(parts.astype(jnp.float32), axis=0)
    packed = three[:, :lanes] + three[:, lanes : 2 * lanes] + three[:, 2 * lanes : 3 * lanes]
    gram = jnp.concatenate(
        [packed[:, members * q : members * (q + 1)] for q in range(members // 8)], axis=0
    )
    row = lax.broadcasted_iota(jnp.int32, gram.shape, 0)
    col = lax.broadcasted_iota(jnp.int32, gram.shape, 1)
    own = jnp.where(row == col, gram, 0.0)
    dist = jnp.sum(own, axis=1, keepdims=True) + jnp.sum(own, axis=0, keepdims=True) - 2.0 * gram
    return jnp.exp(-dist / scale[0]).astype(jnp.bfloat16)


def spreading(kernel):
    members = kernel.shape[0]
    wide = members * TILE
    at = lax.broadcasted_iota(jnp.int32, (wide, members), 0) // TILE
    which = lax.broadcasted_iota(jnp.int32, (wide, members), 1)
    pick = jnp.where(at == which, 1.0, 0.0).astype(jnp.bfloat16)
    tall = dot(pick, kernel, ((1,), (0,))).astype(jnp.bfloat16)
    full = dot(tall, pick, ((1,), (1,)))
    row = lax.broadcasted_iota(jnp.int32, (wide, wide), 0) % TILE
    col = lax.broadcasted_iota(jnp.int32, (wide, wide), 1) % TILE
    return jnp.where(row == col, full, 0.0)


def mix_kernel(scale, scores, params, out):
    members, rows, _ = params.shape
    wide = members * TILE
    full = spreading(kernel_of(scale, scores[:, rows : rows + EXTRA, :]))
    ksum = jnp.sum(full, axis=1, keepdims=True)
    mixer = full.astype(jnp.bfloat16)
    for r in range(0, rows, TILE):
        got = scores[:, r : r + TILE, :].reshape(wide, D)
        pulled = dot(mixer, got, ((1,), (0,))) * (1.0 / members)
        out[:, r : r + TILE, :] = pulled.astype(jnp.bfloat16).reshape(members, TILE, D)
        own = params[:, r : r + TILE, :].reshape(wide, D)
        mixed = dot(mixer, own, ((1,), (0,)))
        pushed = (ksum * own.astype(jnp.float32) - mixed) * (1.0 / members)
        out[:, rows + r : rows + r + TILE, :] = pushed.astype(jnp.bfloat16).reshape(
            members, TILE, D
        )


def weighted(scale, scores, params):
    members, rows, _ = params.shape
    wide = members * TILE
    vmem = pl.BlockSpec(memory_space=pltpu.VMEM)
    return pl.pallas_call(
        mix_kernel,
        out_shape=jax.ShapeDtypeStruct((members, 2 * rows, D), jnp.bfloat16),
        in_specs=[pl.BlockSpec(memory_space=pltpu.SMEM), vmem, vmem],
        compiler_params=pltpu.CompilerParams(vmem_limit_bytes=24 * 1024 * 1024),
        cost_estimate=pl.CostEstimate(
            flops=4 * wide * wide * rows // TILE * D,
            bytes_accessed=8 * members * rows * D,
            transcendentals=0,
        ),
        name="mix",
    )(scale, scores, params)


def plain_products(params):
    flat = params.reshape(params.shape[0], -1)
    return dot(flat, flat, ((1,), (1,)))


def plain_weighted(gram, scale, params, scores):
    members = params.shape[0]
    norms = jnp.diagonal(gram)
    dist = norms[:, None] + norms[None, :] - 2.0 * gram
    kernel = jnp.exp(-dist / scale[0]).astype(jnp.bfloat16)
    flat = params.reshape(members, -1)
    ksum = jnp.sum(kernel.astype(jnp.float32), axis=1, keepdims=True)
    attract = dot(kernel, scores.reshape(members, -1), ((1,), (0,))) / members
    mixed = dot(kernel, flat, ((1,), (0,)))
    spread = (flat.astype(jnp.float32) * ksum - mixed) / members
    return tuple(x.astype(jnp.bfloat16).reshape(params.shape) for x in (attract, spread))


def run(copies):
    for copy in copies:
        copy.start()
    for copy in copies:
        copy.wait()


def pack_kernel(first, second, out, sems):
    copies = [pltpu.make_async_copy(second, out.at[:, :, pl.ds(EDGE, EDGE), :], sems.at[COLS])]
    for c in range(COLS):
        here = first.at[:, :, pl.ds(c * D, D)]
        copies.append(pltpu.make_async_copy(here, out.at[:, c, pl.ds(0, EDGE), :], sems.at[c]))
    run(copies)


def to_blocks(first, second):
    deep = BLOCKS // COLS
    packed = pl.pallas_call(
        pack_kernel,
        out_shape=jax.ShapeDtypeStruct((deep, COLS, ROWS, D), jnp.bfloat16),
        in_specs=[pl.BlockSpec(memory_space=pltpu.HBM)] * 2,
        out_specs=pl.BlockSpec(memory_space=pltpu.VMEM),
        scratch_shapes=[pltpu.SemaphoreType.DMA((COLS + 1,))],
        cost_estimate=pl.CostEstimate(flops=0, bytes_accessed=8 * D * FF, transcendentals=0),
        name="pack",
    )(first.reshape(deep, EDGE, FF), second.reshape(deep, COLS, EDGE, D))
    return packed.reshape(BLOCKS, ROWS, D)


def unpack_kernel(blocks, first_a, second_a, first_s, second_s):
    for b in range(BLOCKS):
        r, c = b // COLS * EDGE, b % COLS * D
        first_a[0, r : r + EDGE, c : c + D] = blocks[b, 0:EDGE, :]
        second_a[0, b * EDGE : (b + 1) * EDGE, :] = blocks[b, EDGE : 2 * EDGE, :]
        first_s[0, r : r + EDGE, c : c + D] = blocks[b, 2 * EDGE : 3 * EDGE, :]
        second_s[0, b * EDGE : (b + 1) * EDGE, :] = blocks[b, 3 * EDGE : 4 * EDGE, :]


def from_blocks(blocks):
    shapes = (
        jax.ShapeDtypeStruct((1, D, FF), jnp.bfloat16),
        jax.ShapeDtypeStruct((1, FF, D), jnp.bfloat16),
    )
    return pl.pallas_call(
        unpack_kernel,
        out_shape=shapes + shapes,
        compiler_params=pltpu.CompilerParams(vmem_limit_bytes=24 * 1024 * 1024),
        cost_estimate=pl.CostEstimate(flops=0, bytes_accessed=16 * D * FF, transcendentals=0),
        name="unpack",
    )(blocks)


def exchange(blocks):
    return lax.all_to_all(blocks, ORDER, split_axis=0, concat_axis=0, tiled=True)


def on_device(
    particles_first, particles_second, pool_images, pool_targets, batch_index, kernel_scale
):
    members = math.prod(lax.axis_size(name) for name in AXES)
    cut = (members, BLOCKS * ROWS // members, D)
    tiled = members == BLOCKS
    params = exchange(to_blocks(particles_first, particles_second).reshape(cut))
    scores = particle_scores(
        particles_first[0],
        particles_second[0],
        pool_images,
        pool_targets,
        batch_index[0],
        EXTRA if tiled else 0,
    )
    if tiled:
        scores = exchange(add_products(params, scores))
        mixed = exchange(weighted(kernel_scale, scores, params))
    else:
        scores = exchange(scores.reshape(cut))
        gram = lax.psum(plain_products(params), AXES)
        parts = plain_weighted(gram, kernel_scale, params, scores)
        mixed = [exchange(x).reshape(BLOCKS, ROWS, D) for x in parts]
        mixed = jnp.concatenate(mixed, axis=1)
    return from_blocks(mixed)


def solution(mesh):
    split = P(AXES, None, None)
    return jax.shard_map(
        on_device,
        mesh=Mesh(mesh.devices.reshape(2, 2, -1), AXES),
        in_specs=(split, split, P(), P(), P(AXES, None), P()),
        out_specs=(split, split, split, split),
        check_vma=False,
    )
```

```python
import functools
import math

import jax
import jax.numpy as jnp
from jax import lax
from jax.experimental import pallas as pl
from jax.experimental.pallas import tpu as pltpu
from jax.sharding import PartitionSpec as P

D = 384
FF = 1536
S = 197
DATA = 10000
AXES = ("wide", "narrow")
PAD = 208
EDGE = 48
BLOCKS = D * FF // (EDGE * D)
COLS = FF // D
TILE = 16
LANES = 128
SIDE = 2 * EDGE
GROUPS = range(D // LANES)
ROWS = SIDE * len(GROUPS)
EXTRA = 8

gelu_c = math.sqrt(2.0 / math.pi)
isd = 1.0 / math.sqrt(D)
isf = 1.0 / math.sqrt(FF)


def dot(a, b, dims):
    return lax.dot_general(a, b, (dims, ((), ())), preferred_element_type=jnp.float32)


def put(out, block, row, value):
    for g in GROUPS:
        at = g * SIDE + row
        out[block, at : at + EDGE, :] = value[:, g * LANES : (g + 1) * LANES]


def tile(ref, r):
    members = ref.shape[0]
    parts = [ref[:, g * SIDE + r : g * SIDE + r + TILE, :] for g in GROUPS]
    return jnp.concatenate([p.reshape(members * TILE, LANES) for p in parts], axis=1)


def score_kernel(
    factor, picks, image, target, first, second, out, xs, ts, normed, hidden, deriv, delta, back
):
    step = pl.program_id(0)
    images = pl.num_programs(0)
    rows = pl.ds(pl.multiple_of(step * PAD, PAD), PAD)

    @pl.when(step == 0)
    def _():
        xs[...] = jnp.zeros_like(xs)
        ts[...] = jnp.zeros_like(ts)

    xs[0:S, :] = image[0].astype(jnp.float32)
    ts[0:S, :] = target[0].astype(jnp.float32)
    xf = xs[...]
    mean = jnp.mean(xf, axis=1, keepdims=True)
    centered = xf - mean
    var = jnp.mean(centered * centered, axis=1, keepdims=True)
    nrm = (centered * lax.rsqrt(var + 1e-06)).astype(jnp.bfloat16)
    normed[rows, :] = nrm
    for c in range(COLS):
        cols = pl.ds(c * D, D)
        pre = dot(nrm, first[:, cols], ((1,), (0,))) * isd
        sq = pre * pre
        tval = jnp.tanh(pre * (gelu_c + (gelu_c * 0.044715) * sq))
        gate = 0.5 + 0.5 * tval
        hid = pre * gate
        hidden[rows, cols] = hid.astype(jnp.bfloat16)
        deriv[:, cols] = gate + hid * (1.0 - gate) * (
            2.0 * gelu_c + (6.0 * gelu_c * 0.044715) * sq
        )
    prod = dot(hidden[rows, :], second[...], ((1,), (0,))) * isf
    dlt = ((xs[...] + prod - ts[...]) * (1.0 / S)).astype(jnp.bfloat16)
    delta[rows, :] = dlt
    for c in range(COLS):
        cols = pl.ds(c * D, D)
        dhid = dot(dlt, second[cols, :], ((1,), (1,))) * isf
        back[rows, cols] = (dhid * deriv[:, cols]).astype(jnp.bfloat16)

    @pl.when(step == images - 1)
    def _():
        for c in range(COLS):
            cols = pl.ds(c * D, D)
            grad = dot(normed[...], back[:, cols], ((0,), (0,))) * (-factor * isd)
            score = (grad - first[:, cols].astype(jnp.float32)).astype(jnp.bfloat16)
            for r in range(D // EDGE):
                put(out, r * COLS + c, 0, score[r * EDGE : (r + 1) * EDGE, :])
            grad = dot(hidden[:, cols], delta[...], ((0,), (0,))) * (-factor * isf)
            score = (grad - second[cols, :].astype(jnp.float32)).astype(jnp.bfloat16)
            for r in range(D // EDGE):
                put(out, c * (D // EDGE) + r, EDGE, score[r * EDGE : (r + 1) * EDGE, :])


def particle_scores(first, second, images, targets, picks, extra):
    count = picks.shape[0]
    rows = count * PAD
    bf = jnp.bfloat16
    return pl.pallas_call(
        functools.partial(score_kernel, DATA / count),
        out_shape=pltpu.HBM((BLOCKS, ROWS + extra, LANES), bf),
        grid_spec=pltpu.PrefetchScalarGridSpec(
            num_scalar_prefetch=1,
            grid=(count,),
            in_specs=[
                pl.BlockSpec((1, S, D), lambda b, picks: (picks[b], 0, 0)),
                pl.BlockSpec((1, S, D), lambda b, picks: (picks[b], 0, 0)),
                pl.BlockSpec((D, FF), lambda b, picks: (0, 0)),
                pl.BlockSpec((FF, D), lambda b, picks: (0, 0)),
            ],
            out_specs=pl.BlockSpec((BLOCKS, ROWS, LANES), lambda b, picks: (0, 0, 0)),
            scratch_shapes=[
                pltpu.VMEM((PAD, D), jnp.float32),
                pltpu.VMEM((PAD, D), jnp.float32),
                pltpu.VMEM((rows, D), bf),
                pltpu.VMEM((rows, FF), bf),
                pltpu.VMEM((PAD, FF), jnp.float32),
                pltpu.VMEM((rows, D), bf),
                pltpu.VMEM((rows, FF), bf),
            ],
        ),
        compiler_params=pltpu.CompilerParams(vmem_limit_bytes=32 * 1024 * 1024),
        cost_estimate=pl.CostEstimate(
            flops=10 * count * PAD * D * FF,
            bytes_accessed=4 * (2 * D * FF + count * S * D),
            transcendentals=count * PAD * FF,
        ),
        name="score",
    )(picks, images, targets, first, second)


def gram_kernel(params, scores, out, total, parts, sem):
    members, rows, _ = params.shape
    wide = members * TILE
    half = members // 2
    total[...] = jnp.zeros_like(total)
    for r in range(0, SIDE, TILE):
        part = tile(params, r)
        total[...] += dot(part, part, ((1,), (1,)))
    at = lax.broadcasted_iota(jnp.int32, (wide, wide), 0) % TILE
    to = lax.broadcasted_iota(jnp.int32, (wide, wide), 1) % TILE
    kept = jnp.where(at == to, total[...], 0.0)
    summed = jnp.sum(kept.reshape(members, TILE, wide), axis=1)
    turned = summed.T
    gram = jnp.sum(turned.reshape(members, TILE, members), axis=1)
    row = lax.broadcasted_iota(jnp.int32, gram.shape, 0)
    col = lax.broadcasted_iota(jnp.int32, gram.shape, 1)
    own = jnp.where(row == col, gram, 0.0)
    dist = jnp.sum(own, axis=1, keepdims=True) + jnp.sum(own, axis=0, keepdims=True) - 2.0 * gram
    low = jnp.concatenate([dist[half:, half:], dist[half:, :half]], axis=1)
    once = jnp.where(col[:half] > row[:half], dist[:half], low)
    high = once.astype(jnp.bfloat16).astype(jnp.float32)
    rest = once - high
    both = [x[q : q + EXTRA] for x in (high, rest) for q in range(0, half, EXTRA)]
    packed = jnp.concatenate(both, axis=1).astype(jnp.bfloat16)
    parts[...] = jnp.broadcast_to(packed[None], parts.shape)
    copy = pltpu.make_async_copy(parts, out.at[:, pl.ds(rows, EXTRA), :], sem)
    copy.start()
    copy.wait()


def add_distances(params, scores):
    members, rows, _ = params.shape
    wide = members * TILE
    return pl.pallas_call(
        gram_kernel,
        out_shape=pltpu.HBM(scores.shape, scores.dtype),
        in_specs=[pl.BlockSpec(memory_space=pltpu.VMEM), pl.BlockSpec(memory_space=pl.ANY)],
        out_specs=pl.BlockSpec(memory_space=pl.ANY),
        input_output_aliases={1: 0},
        scratch_shapes=[
            pltpu.VMEM((wide, wide), jnp.float32),
            pltpu.VMEM((members, EXTRA, LANES), jnp.bfloat16),
            pltpu.SemaphoreType.DMA,
        ],
        compiler_params=pltpu.CompilerParams(vmem_limit_bytes=16 * 1024 * 1024),
        cost_estimate=pl.CostEstimate(
            flops=2 * wide * wide * SIDE // TILE * D,
            bytes_accessed=2 * members * rows * LANES,
            transcendentals=0,
        ),
        name="gram",
    )(params, scores)


def kernel_of(scale, parts):
    members = parts.shape[0]
    half = members // 2
    packed = jnp.sum(parts.astype(jnp.float32), axis=0)
    both = [packed[:, q : q + members] for q in range(0, LANES, members)]
    once = jnp.concatenate(both[:2], axis=0) + jnp.concatenate(both[2:], axis=0)
    row = lax.broadcasted_iota(jnp.int32, once.shape, 0)
    col = lax.broadcasted_iota(jnp.int32, once.shape, 1)
    upper = jnp.where(col > row, once, 0.0)
    lower = jnp.where(col < row, once, 0.0)
    lower = jnp.concatenate([lower[:, half:], lower[:, :half]], axis=1)
    dist = jnp.concatenate([upper, lower], axis=0)
    return jnp.exp(-(dist + dist.T) / scale[0]).astype(jnp.bfloat16)


def spreading(kernel):
    members = kernel.shape[0]
    wide = members * TILE
    at = lax.broadcasted_iota(jnp.int32, (wide, members), 0) // TILE
    which = lax.broadcasted_iota(jnp.int32, (wide, members), 1)
    pick = jnp.where(at == which, 1.0, 0.0).astype(jnp.bfloat16)
    tall = dot(pick, kernel, ((1,), (0,))).astype(jnp.bfloat16)
    full = dot(tall, pick, ((1,), (1,)))
    row = lax.broadcasted_iota(jnp.int32, (wide, wide), 0) % TILE
    col = lax.broadcasted_iota(jnp.int32, (wide, wide), 1) % TILE
    return jnp.where(row == col, full, 0.0)


def mix_kernel(scale, scores, params, out):
    members, rows, _ = params.shape
    wide = members * TILE
    full = spreading(kernel_of(scale, scores[:, rows : rows + EXTRA, :]))
    ksum = jnp.sum(full, axis=1, keepdims=True)
    mixer = full.astype(jnp.bfloat16)
    for r in range(0, SIDE, TILE):
        own = tile(params, r)
        both = dot(mixer, jnp.concatenate([tile(scores, r), own], axis=1), ((1,), (0,)))
        pushed = ksum * own.astype(jnp.float32) - both[:, D:]
        both = jnp.concatenate([both[:, :D], pushed], axis=1) * (1.0 / members)
        both = both.astype(jnp.bfloat16)
        for g in range(2 * len(GROUPS)):
            at = g * SIDE + r
            out[:, at : at + TILE, :] = both[:, g * LANES : (g + 1) * LANES].reshape(
                members, TILE, LANES
            )


def weighted(scale, scores, params):
    members, rows, _ = params.shape
    wide = members * TILE
    vmem = pl.BlockSpec(memory_space=pltpu.VMEM)
    return pl.pallas_call(
        mix_kernel,
        out_shape=jax.ShapeDtypeStruct((members, 2 * rows, LANES), jnp.bfloat16),
        in_specs=[pl.BlockSpec(memory_space=pltpu.SMEM), vmem, vmem],
        compiler_params=pltpu.CompilerParams(vmem_limit_bytes=24 * 1024 * 1024),
        cost_estimate=pl.CostEstimate(
            flops=4 * wide * wide * SIDE // TILE * D,
            bytes_accessed=8 * members * rows * LANES,
            transcendentals=0,
        ),
        name="mix",
    )(scale, scores, params)


def plain_products(params):
    flat = params.reshape(params.shape[0], -1)
    return dot(flat, flat, ((1,), (1,)))


def plain_weighted(gram, scale, params, scores):
    members = params.shape[0]
    norms = jnp.diagonal(gram)
    dist = norms[:, None] + norms[None, :] - 2.0 * gram
    kernel = jnp.exp(-dist / scale[0]).astype(jnp.bfloat16)
    flat = params.reshape(members, -1)
    ksum = jnp.sum(kernel.astype(jnp.float32), axis=1, keepdims=True)
    attract = dot(kernel, scores.reshape(members, -1), ((1,), (0,))) / members
    mixed = dot(kernel, flat, ((1,), (0,)))
    spread = (flat.astype(jnp.float32) * ksum - mixed) / members
    return tuple(x.astype(jnp.bfloat16).reshape(params.shape) for x in (attract, spread))


STEPS = D // EDGE
TALL = FF // STEPS


def pack_kernel(first, second, out, wide, tall, packed, loads, stores):
    def load(d):
        return (
            pltpu.make_async_copy(
                first.at[0, pl.ds(d * EDGE, EDGE), :], wide.at[d], loads.at[0, d]
            ),
            pltpu.make_async_copy(
                second.at[0, pl.ds(d * TALL, TALL), :], tall.at[d], loads.at[1, d]
            ),
        )

    def store(d):
        here = pl.ds(d * COLS, COLS)
        return pltpu.make_async_copy(packed.at[here], out.at[here], stores.at[d])

    for d in range(STEPS):
        for copy in load(d):
            copy.start()
    for d in range(STEPS):
        for copy in load(d):
            copy.wait()
        for c in range(COLS):
            put(packed, d * COLS + c, 0, wide[d, :, c * D : (c + 1) * D])
            put(packed, d * COLS + c, EDGE, tall[d, c * EDGE : (c + 1) * EDGE, :])
        store(d).start()
    for d in range(STEPS):
        store(d).wait()


def to_blocks(first, second):
    bf = jnp.bfloat16
    return pl.pallas_call(
        pack_kernel,
        out_shape=pltpu.HBM((BLOCKS, ROWS, LANES), bf),
        in_specs=[pl.BlockSpec(memory_space=pl.ANY)] * 2,
        out_specs=pl.BlockSpec(memory_space=pl.ANY),
        scratch_shapes=[
            pltpu.VMEM((STEPS, EDGE, FF), bf),
            pltpu.VMEM((STEPS, TALL, D), bf),
            pltpu.VMEM((BLOCKS, ROWS, LANES), bf),
            pltpu.SemaphoreType.DMA((2, STEPS)),
            pltpu.SemaphoreType.DMA((STEPS,)),
        ],
        compiler_params=pltpu.CompilerParams(vmem_limit_bytes=56 * 1024 * 1024),
        cost_estimate=pl.CostEstimate(flops=0, bytes_accessed=8 * D * FF, transcendentals=0),
        name="pack",
    )(first, second)


def unpack_kernel(blocks, first_a, second_a, first_s, second_s, wide, tall, stores):
    def store(which, d):
        first, second = ((first_a, second_a), (first_s, second_s))[which]
        return (
            pltpu.make_async_copy(
                wide.at[which, d], first.at[0, pl.ds(d * EDGE, EDGE), :], stores.at[which, 0, d]
            ),
            pltpu.make_async_copy(
                tall.at[which, d], second.at[0, pl.ds(d * TALL, TALL), :], stores.at[which, 1, d]
            ),
        )

    for which in range(2):
        for d in range(STEPS):
            for c in range(COLS):
                for g in GROUPS:
                    at = which * ROWS + g * SIDE
                    lanes = slice(c * D + g * LANES, c * D + (g + 1) * LANES)
                    wide[which, d, :, lanes] = blocks[d * COLS + c, at : at + EDGE, :]
                    tall[which, d, c * EDGE : (c + 1) * EDGE, g * LANES : (g + 1) * LANES] = blocks[
                        d * COLS + c, at + EDGE : at + SIDE, :
                    ]
            for copy in store(which, d):
                copy.start()
    for which in range(2):
        for d in range(STEPS):
            for copy in store(which, d):
                copy.wait()


def from_blocks(blocks):
    bf = jnp.bfloat16
    return pl.pallas_call(
        unpack_kernel,
        out_shape=(pltpu.HBM((1, D, FF), bf), pltpu.HBM((1, FF, D), bf)) * 2,
        in_specs=[pl.BlockSpec(memory_space=pltpu.VMEM)],
        out_specs=(pl.BlockSpec(memory_space=pl.ANY),) * 4,
        scratch_shapes=[
            pltpu.VMEM((2, STEPS, EDGE, FF), bf),
            pltpu.VMEM((2, STEPS, TALL, D), bf),
            pltpu.SemaphoreType.DMA((2, 2, STEPS)),
        ],
        compiler_params=pltpu.CompilerParams(vmem_limit_bytes=24 * 1024 * 1024),
        cost_estimate=pl.CostEstimate(flops=0, bytes_accessed=16 * D * FF, transcendentals=0),
        name="unpack",
    )(blocks)


def exchange(blocks):
    return lax.all_to_all(blocks, AXES, split_axis=0, concat_axis=0, tiled=True)


def on_device(
    particles_first, particles_second, pool_images, pool_targets, batch_index, kernel_scale
):
    members = math.prod(lax.axis_size(name) for name in AXES)
    cut = (members, BLOCKS * ROWS // members, LANES)
    tiled = members == BLOCKS
    params = exchange(to_blocks(particles_first, particles_second).reshape(cut))
    scores = particle_scores(
        particles_first[0],
        particles_second[0],
        pool_images,
        pool_targets,
        batch_index[0],
        EXTRA if tiled else 0,
    )
    if tiled:
        scores = exchange(add_distances(params, scores))
        mixed = exchange(weighted(kernel_scale, scores, params))
    else:
        scores = exchange(scores.reshape(cut))
        gram = lax.psum(plain_products(params), AXES)
        parts = plain_weighted(gram, kernel_scale, params, scores)
        mixed = [exchange(x).reshape(BLOCKS, ROWS, LANES) for x in parts]
        mixed = jnp.concatenate(mixed, axis=1)
    return from_blocks(mixed)


def solution(mesh):
    split = P(AXES, None, None)
    return jax.shard_map(
        on_device,
        mesh=mesh,
        in_specs=(split, split, P(), P(), P(AXES, None), P()),
        out_specs=(split, split, split, split),
        check_vma=False,
    )
```

```python
import functools
import math

import jax
import jax.numpy as jnp
from jax import lax
from jax.experimental import pallas as pl
from jax.experimental.pallas import tpu as pltpu
from jax.sharding import PartitionSpec as P

D = 384
FF = 1536
S = 197
DATA = 10000
AXES = ("wide", "narrow")
PAD = 208
EDGE = 48
BLOCKS = D * FF // (EDGE * D)
COLS = FF // D
TILE = 16
LANES = 128
SIDE = 2 * EDGE
GROUPS = range(D // LANES)
ROWS = SIDE * len(GROUPS)

gelu_c = math.sqrt(2.0 / math.pi)
isd = 1.0 / math.sqrt(D)
isf = 1.0 / math.sqrt(FF)


def dot(a, b, dims):
    return lax.dot_general(a, b, (dims, ((), ())), preferred_element_type=jnp.float32)


def put(out, block, row, value):
    for g in GROUPS:
        at = g * SIDE + row
        out[block, at : at + EDGE, :] = value[:, g * LANES : (g + 1) * LANES]


def tile(ref, r):
    members = ref.shape[0]
    parts = [ref[:, g * SIDE + r : g * SIDE + r + TILE, :] for g in GROUPS]
    return jnp.concatenate([p.reshape(members * TILE, LANES) for p in parts], axis=1)


def score_kernel(
    factor, picks, image, target, first, second, out, xs, ts, normed, hidden, deriv, delta, back
):
    step = pl.program_id(0)
    images = pl.num_programs(0)
    rows = pl.ds(pl.multiple_of(step * PAD, PAD), PAD)

    @pl.when(step == 0)
    def _():
        xs[...] = jnp.zeros_like(xs)
        ts[...] = jnp.zeros_like(ts)

    xs[0:S, :] = image[0].astype(jnp.float32)
    ts[0:S, :] = target[0].astype(jnp.float32)
    xf = xs[...]
    mean = jnp.mean(xf, axis=1, keepdims=True)
    centered = xf - mean
    var = jnp.mean(centered * centered, axis=1, keepdims=True)
    nrm = (centered * lax.rsqrt(var + 1e-06)).astype(jnp.bfloat16)
    normed[rows, :] = nrm
    for c in range(COLS):
        cols = pl.ds(c * D, D)
        pre = dot(nrm, first[:, cols], ((1,), (0,))) * isd
        sq = pre * pre
        tval = jnp.tanh(pre * (gelu_c + (gelu_c * 0.044715) * sq))
        gate = 0.5 + 0.5 * tval
        hid = pre * gate
        hidden[rows, cols] = hid.astype(jnp.bfloat16)
        deriv[:, cols] = gate + hid * (1.0 - gate) * (
            2.0 * gelu_c + (6.0 * gelu_c * 0.044715) * sq
        )
    prod = dot(hidden[rows, :], second[...], ((1,), (0,))) * isf
    dlt = ((xs[...] + prod - ts[...]) * (1.0 / S)).astype(jnp.bfloat16)
    delta[rows, :] = dlt
    for c in range(COLS):
        cols = pl.ds(c * D, D)
        dhid = dot(dlt, second[cols, :], ((1,), (1,))) * isf
        back[rows, cols] = (dhid * deriv[:, cols]).astype(jnp.bfloat16)

    @pl.when(step == images - 1)
    def _():
        for c in range(COLS):
            cols = pl.ds(c * D, D)
            grad = dot(normed[...], back[:, cols], ((0,), (0,))) * (-factor * isd)
            score = (grad - first[:, cols].astype(jnp.float32)).astype(jnp.bfloat16)
            for r in range(D // EDGE):
                put(out, r * COLS + c, 0, score[r * EDGE : (r + 1) * EDGE, :])
            grad = dot(hidden[:, cols], delta[...], ((0,), (0,))) * (-factor * isf)
            score = (grad - second[cols, :].astype(jnp.float32)).astype(jnp.bfloat16)
            for r in range(D // EDGE):
                put(out, c * (D // EDGE) + r, EDGE, score[r * EDGE : (r + 1) * EDGE, :])


def particle_scores(first, second, images, targets, picks):
    count = picks.shape[0]
    rows = count * PAD
    bf = jnp.bfloat16
    return pl.pallas_call(
        functools.partial(score_kernel, DATA / count),
        out_shape=pltpu.HBM((BLOCKS, ROWS, LANES), bf),
        grid_spec=pltpu.PrefetchScalarGridSpec(
            num_scalar_prefetch=1,
            grid=(count,),
            in_specs=[
                pl.BlockSpec((1, S, D), lambda b, picks: (picks[b], 0, 0)),
                pl.BlockSpec((1, S, D), lambda b, picks: (picks[b], 0, 0)),
                pl.BlockSpec((D, FF), lambda b, picks: (0, 0)),
                pl.BlockSpec((FF, D), lambda b, picks: (0, 0)),
            ],
            out_specs=pl.BlockSpec((BLOCKS, ROWS, LANES), lambda b, picks: (0, 0, 0)),
            scratch_shapes=[
                pltpu.VMEM((PAD, D), jnp.float32),
                pltpu.VMEM((PAD, D), jnp.float32),
                pltpu.VMEM((rows, D), bf),
                pltpu.VMEM((rows, FF), bf),
                pltpu.VMEM((PAD, FF), jnp.float32),
                pltpu.VMEM((rows, D), bf),
                pltpu.VMEM((rows, FF), bf),
            ],
        ),
        compiler_params=pltpu.CompilerParams(vmem_limit_bytes=32 * 1024 * 1024),
        cost_estimate=pl.CostEstimate(
            flops=10 * count * PAD * D * FF,
            bytes_accessed=4 * (2 * D * FF + count * S * D),
            transcendentals=count * PAD * FF,
        ),
        name="score",
    )(picks, images, targets, first, second)


def gram_kernel(params, out, total):
    members, rows, _ = params.shape
    wide = members * TILE
    total[...] = jnp.zeros_like(total)
    for r in range(0, SIDE, TILE):
        part = tile(params, r)
        total[...] += dot(part, part, ((1,), (1,)))
    at = lax.broadcasted_iota(jnp.int32, (wide, wide), 0) % TILE
    to = lax.broadcasted_iota(jnp.int32, (wide, wide), 1) % TILE
    kept = jnp.where(at == to, total[...], 0.0)
    summed = jnp.sum(kept.reshape(members, TILE, wide), axis=1)
    turned = summed.T
    gram = jnp.sum(turned.reshape(members, TILE, members), axis=1)
    row = lax.broadcasted_iota(jnp.int32, gram.shape, 0)
    col = lax.broadcasted_iota(jnp.int32, gram.shape, 1)
    own = jnp.where(row == col, gram, 0.0)
    dist = jnp.sum(own, axis=1, keepdims=True) + jnp.sum(own, axis=0, keepdims=True) - 2.0 * gram
    out[...] = jnp.concatenate([dist[q : q + 8] for q in range(0, members, 8)], axis=1)


def distances(params):
    members, rows, _ = params.shape
    wide = members * TILE
    return pl.pallas_call(
        gram_kernel,
        out_shape=jax.ShapeDtypeStruct((8, members * members // 8), jnp.float32),
        scratch_shapes=[pltpu.VMEM((wide, wide), jnp.float32)],
        compiler_params=pltpu.CompilerParams(vmem_limit_bytes=16 * 1024 * 1024),
        cost_estimate=pl.CostEstimate(
            flops=2 * wide * wide * SIDE // TILE * D,
            bytes_accessed=2 * members * rows * LANES,
            transcendentals=0,
        ),
        name="gram",
    )(params)


def add_over(value, members, bits):
    got = [
        lax.ppermute(value, AXES, [(i, i ^ bit) for i in range(members)]) for bit in bits
    ]
    return sum(got, value)


def kernel_of(scale, packed):
    members = packed.shape[1] // 4
    dist = jnp.concatenate(
        [packed[:, members * q : members * (q + 1)] for q in range(members // 8)], axis=0
    )
    return jnp.exp(-dist / scale[0]).astype(jnp.bfloat16)


def spreading(kernel):
    members = kernel.shape[0]
    wide = members * TILE
    at = lax.broadcasted_iota(jnp.int32, (wide, members), 0) // TILE
    which = lax.broadcasted_iota(jnp.int32, (wide, members), 1)
    pick = jnp.where(at == which, 1.0, 0.0).astype(jnp.bfloat16)
    tall = dot(pick, kernel, ((1,), (0,))).astype(jnp.bfloat16)
    full = dot(tall, pick, ((1,), (1,)))
    row = lax.broadcasted_iota(jnp.int32, (wide, wide), 0) % TILE
    col = lax.broadcasted_iota(jnp.int32, (wide, wide), 1) % TILE
    return jnp.where(row == col, full, 0.0)


def spread_kernel(scale, packed, params, out, mixing):
    members, rows, _ = params.shape
    full = spreading(kernel_of(scale, packed[...]))
    ksum = jnp.sum(full, axis=1, keepdims=True)
    mixer = full.astype(jnp.bfloat16)
    mixing[...] = mixer
    for r in range(0, SIDE, TILE):
        own = tile(params, r)
        mixed = dot(mixer, own, ((1,), (0,)))
        pushed = (ksum * own.astype(jnp.float32) - mixed) * (1.0 / members)
        pushed = pushed.astype(jnp.bfloat16)
        for g in GROUPS:
            at = g * SIDE + r
            out[:, at : at + TILE, :] = pushed[:, g * LANES : (g + 1) * LANES].reshape(
                members, TILE, LANES
            )


def spread_part(scale, packed, params):
    members, rows, _ = params.shape
    wide = members * TILE
    vmem = pl.BlockSpec(memory_space=pltpu.VMEM)
    return pl.pallas_call(
        spread_kernel,
        out_shape=(
            pltpu.HBM((members, 2 * rows, LANES), jnp.bfloat16),
            jax.ShapeDtypeStruct((wide, wide), jnp.bfloat16),
        ),
        grid=(1,),
        in_specs=[pl.BlockSpec(memory_space=pltpu.SMEM), vmem, vmem],
        out_specs=(pl.BlockSpec((members, rows, LANES), lambda i: (0, 1, 0)), vmem),
        compiler_params=pltpu.CompilerParams(vmem_limit_bytes=24 * 1024 * 1024),
        cost_estimate=pl.CostEstimate(
            flops=2 * wide * wide * SIDE // TILE * D,
            bytes_accessed=4 * members * rows * LANES,
            transcendentals=0,
        ),
        name="spread",
    )(scale, packed, params)


def attract_kernel(mixing, scores, half_done, out, mixed, stores):
    members, rows, _ = scores.shape
    step = 2 * TILE

    def store(r, g):
        here = pl.ds(g * SIDE + r, step)
        return pltpu.make_async_copy(
            mixed.at[:, here, :], out.at[:, here, :], stores.at[r // step, g]
        )

    for r in range(0, SIDE, step):
        got = jnp.concatenate([tile(scores, r), tile(scores, r + TILE)], axis=1)
        pulled = dot(mixing[...], got, ((1,), (0,))) * (1.0 / members)
        pulled = pulled.astype(jnp.bfloat16)
        for g in GROUPS:
            for h in range(2):
                at = g * SIDE + r + h * TILE
                lanes = h * D + g * LANES
                mixed[:, at : at + TILE, :] = pulled[:, lanes : lanes + LANES].reshape(
                    members, TILE, LANES
                )
            store(r, g).start()
    for r in range(0, SIDE, step):
        for g in GROUPS:
            store(r, g).wait()


def attract_part(mixing, scores, half_done):
    members, rows, _ = scores.shape
    wide = members * TILE
    vmem = pl.BlockSpec(memory_space=pltpu.VMEM)
    anywhere = pl.BlockSpec(memory_space=pl.ANY)
    return pl.pallas_call(
        attract_kernel,
        out_shape=pltpu.HBM(half_done.shape, half_done.dtype),
        in_specs=[vmem, vmem, anywhere],
        out_specs=anywhere,
        input_output_aliases={2: 0},
        scratch_shapes=[
            pltpu.VMEM(scores.shape, jnp.bfloat16),
            pltpu.SemaphoreType.DMA((SIDE // (2 * TILE), len(GROUPS))),
        ],
        compiler_params=pltpu.CompilerParams(vmem_limit_bytes=24 * 1024 * 1024),
        cost_estimate=pl.CostEstimate(
            flops=2 * wide * wide * SIDE // TILE * D,
            bytes_accessed=4 * members * rows * LANES,
            transcendentals=0,
        ),
        name="attract",
    )(mixing, scores, half_done)


def plain_products(params):
    flat = params.reshape(params.shape[0], -1)
    return dot(flat, flat, ((1,), (1,)))


def plain_weighted(gram, scale, params, scores):
    members = params.shape[0]
    norms = jnp.diagonal(gram)
    dist = norms[:, None] + norms[None, :] - 2.0 * gram
    kernel = jnp.exp(-dist / scale[0]).astype(jnp.bfloat16)
    flat = params.reshape(members, -1)
    ksum = jnp.sum(kernel.astype(jnp.float32), axis=1, keepdims=True)
    attract = dot(kernel, scores.reshape(members, -1), ((1,), (0,))) / members
    mixed = dot(kernel, flat, ((1,), (0,)))
    spread = (flat.astype(jnp.float32) * ksum - mixed) / members
    return tuple(x.astype(jnp.bfloat16).reshape(params.shape) for x in (attract, spread))


STEPS = D // EDGE
TALL = FF // STEPS


def pack_kernel(first, second, out, wide, tall, packed, loads, stores):
    def load(d):
        return (
            pltpu.make_async_copy(
                first.at[0, pl.ds(d * EDGE, EDGE), :], wide.at[d], loads.at[0, d]
            ),
            pltpu.make_async_copy(
                second.at[0, pl.ds(d * TALL, TALL), :], tall.at[d], loads.at[1, d]
            ),
        )

    def store(d):
        here = pl.ds(d * COLS, COLS)
        return pltpu.make_async_copy(packed.at[here], out.at[here], stores.at[d])

    for d in range(STEPS):
        for copy in load(d):
            copy.start()
    for d in range(STEPS):
        for copy in load(d):
            copy.wait()
        for c in range(COLS):
            put(packed, d * COLS + c, 0, wide[d, :, c * D : (c + 1) * D])
            put(packed, d * COLS + c, EDGE, tall[d, c * EDGE : (c + 1) * EDGE, :])
        store(d).start()
    for d in range(STEPS):
        store(d).wait()


def to_blocks(first, second):
    bf = jnp.bfloat16
    return pl.pallas_call(
        pack_kernel,
        out_shape=pltpu.HBM((BLOCKS, ROWS, LANES), bf),
        in_specs=[pl.BlockSpec(memory_space=pl.ANY)] * 2,
        out_specs=pl.BlockSpec(memory_space=pl.ANY),
        scratch_shapes=[
            pltpu.VMEM((STEPS, EDGE, FF), bf),
            pltpu.VMEM((STEPS, TALL, D), bf),
            pltpu.VMEM((BLOCKS, ROWS, LANES), bf),
            pltpu.SemaphoreType.DMA((2, STEPS)),
            pltpu.SemaphoreType.DMA((STEPS,)),
        ],
        compiler_params=pltpu.CompilerParams(vmem_limit_bytes=56 * 1024 * 1024),
        cost_estimate=pl.CostEstimate(flops=0, bytes_accessed=8 * D * FF, transcendentals=0),
        name="pack",
    )(first, second)


def unpack_kernel(blocks, first_a, second_a, first_s, second_s, wide, tall, stores):
    def store(which, d):
        first, second = ((first_a, second_a), (first_s, second_s))[which]
        return (
            pltpu.make_async_copy(
                wide.at[which, d], first.at[0, pl.ds(d * EDGE, EDGE), :], stores.at[which, 0, d]
            ),
            pltpu.make_async_copy(
                tall.at[which, d], second.at[0, pl.ds(d * TALL, TALL), :], stores.at[which, 1, d]
            ),
        )

    for which in range(2):
        for d in range(STEPS):
            for c in range(COLS):
                for g in GROUPS:
                    at = which * ROWS + g * SIDE
                    lanes = slice(c * D + g * LANES, c * D + (g + 1) * LANES)
                    wide[which, d, :, lanes] = blocks[d * COLS + c, at : at + EDGE, :]
                    tall[which, d, c * EDGE : (c + 1) * EDGE, g * LANES : (g + 1) * LANES] = blocks[
                        d * COLS + c, at + EDGE : at + SIDE, :
                    ]
            for copy in store(which, d):
                copy.start()
    for which in range(2):
        for d in range(STEPS):
            for copy in store(which, d):
                copy.wait()


def from_blocks(blocks):
    bf = jnp.bfloat16
    return pl.pallas_call(
        unpack_kernel,
        out_shape=(pltpu.HBM((1, D, FF), bf), pltpu.HBM((1, FF, D), bf)) * 2,
        in_specs=[pl.BlockSpec(memory_space=pltpu.VMEM)],
        out_specs=(pl.BlockSpec(memory_space=pl.ANY),) * 4,
        scratch_shapes=[
            pltpu.VMEM((2, STEPS, EDGE, FF), bf),
            pltpu.VMEM((2, STEPS, TALL, D), bf),
            pltpu.SemaphoreType.DMA((2, 2, STEPS)),
        ],
        compiler_params=pltpu.CompilerParams(vmem_limit_bytes=24 * 1024 * 1024),
        cost_estimate=pl.CostEstimate(flops=0, bytes_accessed=16 * D * FF, transcendentals=0),
        name="unpack",
    )(blocks)


def exchange(blocks):
    return lax.all_to_all(blocks, AXES, split_axis=0, concat_axis=0, tiled=True)


def on_device(
    particles_first, particles_second, pool_images, pool_targets, batch_index, kernel_scale
):
    members = math.prod(lax.axis_size(name) for name in AXES)
    cut = (members, BLOCKS * ROWS // members, LANES)
    tiled = members == BLOCKS
    params = exchange(to_blocks(particles_first, particles_second).reshape(cut))
    scores = particle_scores(
        particles_first[0], particles_second[0], pool_images, pool_targets, batch_index[0]
    )
    if tiled:
        params, scores = lax.optimization_barrier((params, scores))
        packed = distances(params)
        scores = exchange(scores)
        for bits in ((1,), (2, 4, 6), (8, 16, 24)):
            packed = add_over(packed, members, bits)
        spread, mixing = spread_part(kernel_scale, packed, params)
        mixed = exchange(attract_part(mixing, scores, spread))
    else:
        scores = exchange(scores.reshape(cut))
        gram = lax.psum(plain_products(params), AXES)
        parts = plain_weighted(gram, kernel_scale, params, scores)
        mixed = [exchange(x).reshape(BLOCKS, ROWS, LANES) for x in parts]
        mixed = jnp.concatenate(mixed, axis=1)
    return from_blocks(mixed)


def solution(mesh):
    split = P(AXES, None, None)
    return jax.shard_map(
        on_device,
        mesh=mesh,
        in_specs=(split, split, P(), P(), P(AXES, None), P()),
        out_specs=(split, split, split, split),
        check_vma=False,
    )
```

```python
import functools
import math

import jax
import jax.numpy as jnp
from jax import lax
from jax.experimental import pallas as pl
from jax.experimental.pallas import tpu as pltpu
from jax.sharding import PartitionSpec as P

D = 384
FF = 1536
S = 197
DATA = 10000
AXES = ("wide", "narrow")
PAD = 208
EDGE = 48
BLOCKS = D * FF // (EDGE * D)
COLS = FF // D
TILE = 16
LANES = 128
SIDE = 2 * EDGE
GROUPS = range(D // LANES)
ROWS = SIDE * len(GROUPS)

gelu_c = math.sqrt(2.0 / math.pi)
isd = 1.0 / math.sqrt(D)
isf = 1.0 / math.sqrt(FF)


def dot(a, b, dims):
    return lax.dot_general(a, b, (dims, ((), ())), preferred_element_type=jnp.float32)


def put(out, block, row, value):
    for g in GROUPS:
        at = g * SIDE + row
        out[block, at : at + EDGE, :] = value[:, g * LANES : (g + 1) * LANES]


def tile(ref, r):
    members = ref.shape[0]
    parts = [ref[:, g * SIDE + r : g * SIDE + r + TILE, :] for g in GROUPS]
    return jnp.concatenate([p.reshape(members * TILE, LANES) for p in parts], axis=1)


def score_kernel(
    factor, picks, image, target, first, second, out, xs, ts, normed, hidden, deriv, delta, back
):
    step = pl.program_id(0)
    images = pl.num_programs(0)
    rows = pl.ds(pl.multiple_of(step * PAD, PAD), PAD)

    @pl.when(step == 0)
    def _():
        xs[...] = jnp.zeros_like(xs)
        ts[...] = jnp.zeros_like(ts)

    xs[0:S, :] = image[0].astype(jnp.float32)
    ts[0:S, :] = target[0].astype(jnp.float32)
    xf = xs[...]
    mean = jnp.mean(xf, axis=1, keepdims=True)
    centered = xf - mean
    var = jnp.mean(centered * centered, axis=1, keepdims=True)
    nrm = (centered * lax.rsqrt(var + 1e-06)).astype(jnp.bfloat16)
    normed[rows, :] = nrm
    for c in range(COLS):
        cols = pl.ds(c * D, D)
        pre = dot(nrm, first[:, cols], ((1,), (0,))) * isd
        sq = pre * pre
        tval = jnp.tanh(pre * (gelu_c + (gelu_c * 0.044715) * sq))
        gate = 0.5 + 0.5 * tval
        hid = pre * gate
        hidden[rows, cols] = hid.astype(jnp.bfloat16)
        deriv[:, cols] = gate + hid * (1.0 - gate) * (
            2.0 * gelu_c + (6.0 * gelu_c * 0.044715) * sq
        )
    prod = dot(hidden[rows, :], second[...], ((1,), (0,))) * isf
    dlt = ((xs[...] + prod - ts[...]) * (1.0 / S)).astype(jnp.bfloat16)
    delta[rows, :] = dlt
    for c in range(COLS):
        cols = pl.ds(c * D, D)
        dhid = dot(dlt, second[cols, :], ((1,), (1,))) * isf
        back[rows, cols] = (dhid * deriv[:, cols]).astype(jnp.bfloat16)

    @pl.when(step == images - 1)
    def _():
        for c in range(COLS):
            cols = pl.ds(c * D, D)
            grad = dot(normed[...], back[:, cols], ((0,), (0,))) * (-factor * isd)
            score = (grad - first[:, cols].astype(jnp.float32)).astype(jnp.bfloat16)
            for r in range(D // EDGE):
                put(out, r * COLS + c, 0, score[r * EDGE : (r + 1) * EDGE, :])
            grad = dot(hidden[:, cols], delta[...], ((0,), (0,))) * (-factor * isf)
            score = (grad - second[cols, :].astype(jnp.float32)).astype(jnp.bfloat16)
            for r in range(D // EDGE):
                put(out, c * (D // EDGE) + r, EDGE, score[r * EDGE : (r + 1) * EDGE, :])


def particle_scores(first, second, images, targets, picks):
    count = picks.shape[0]
    rows = count * PAD
    bf = jnp.bfloat16
    return pl.pallas_call(
        functools.partial(score_kernel, DATA / count),
        out_shape=pltpu.HBM((BLOCKS, ROWS, LANES), bf),
        grid_spec=pltpu.PrefetchScalarGridSpec(
            num_scalar_prefetch=1,
            grid=(count,),
            in_specs=[
                pl.BlockSpec((1, S, D), lambda b, picks: (picks[b], 0, 0)),
                pl.BlockSpec((1, S, D), lambda b, picks: (picks[b], 0, 0)),
                pl.BlockSpec((D, FF), lambda b, picks: (0, 0)),
                pl.BlockSpec((FF, D), lambda b, picks: (0, 0)),
            ],
            out_specs=pl.BlockSpec((BLOCKS, ROWS, LANES), lambda b, picks: (0, 0, 0)),
            scratch_shapes=[
                pltpu.VMEM((PAD, D), jnp.float32),
                pltpu.VMEM((PAD, D), jnp.float32),
                pltpu.VMEM((rows, D), bf),
                pltpu.VMEM((rows, FF), bf),
                pltpu.VMEM((PAD, FF), jnp.float32),
                pltpu.VMEM((rows, D), bf),
                pltpu.VMEM((rows, FF), bf),
            ],
        ),
        compiler_params=pltpu.CompilerParams(vmem_limit_bytes=32 * 1024 * 1024),
        cost_estimate=pl.CostEstimate(
            flops=10 * count * PAD * D * FF,
            bytes_accessed=4 * (2 * D * FF + count * S * D),
            transcendentals=count * PAD * FF,
        ),
        name="score",
    )(picks, images, targets, first, second)


def gram_kernel(params, out, total):
    members, rows, _ = params.shape
    wide = members * TILE
    total[...] = jnp.zeros_like(total)
    for r in range(0, SIDE, TILE):
        part = tile(params, r)
        total[...] += dot(part, part, ((1,), (1,)))
    at = lax.broadcasted_iota(jnp.int32, (wide, wide), 0) % TILE
    to = lax.broadcasted_iota(jnp.int32, (wide, wide), 1) % TILE
    kept = jnp.where(at == to, total[...], 0.0)
    summed = jnp.sum(kept.reshape(members, TILE, wide), axis=1)
    turned = summed.T
    gram = jnp.sum(turned.reshape(members, TILE, members), axis=1)
    row = lax.broadcasted_iota(jnp.int32, gram.shape, 0)
    col = lax.broadcasted_iota(jnp.int32, gram.shape, 1)
    own = jnp.where(row == col, gram, 0.0)
    dist = jnp.sum(own, axis=1, keepdims=True) + jnp.sum(own, axis=0, keepdims=True) - 2.0 * gram
    out[...] = jnp.concatenate([dist[q : q + 8] for q in range(0, members, 8)], axis=1)


def distances(params):
    members, rows, _ = params.shape
    wide = members * TILE
    return pl.pallas_call(
        gram_kernel,
        out_shape=jax.ShapeDtypeStruct((8, members * members // 8), jnp.float32),
        scratch_shapes=[pltpu.VMEM((wide, wide), jnp.float32)],
        compiler_params=pltpu.CompilerParams(vmem_limit_bytes=16 * 1024 * 1024),
        cost_estimate=pl.CostEstimate(
            flops=2 * wide * wide * SIDE // TILE * D,
            bytes_accessed=2 * members * rows * LANES,
            transcendentals=0,
        ),
        name="gram",
    )(params)


def add_over(value, members, bits):
    got = [
        lax.ppermute(value, AXES, [(i, i ^ bit) for i in range(members)]) for bit in bits
    ]
    return sum(got, value)


def kernel_of(scale, packed):
    members = packed.shape[1] // 4
    dist = jnp.concatenate(
        [packed[:, members * q : members * (q + 1)] for q in range(members // 8)], axis=0
    )
    return jnp.exp(-dist / scale[0]).astype(jnp.bfloat16)


def spreading(kernel):
    members = kernel.shape[0]
    wide = members * TILE
    at = lax.broadcasted_iota(jnp.int32, (wide, members), 0) // TILE
    which = lax.broadcasted_iota(jnp.int32, (wide, members), 1)
    pick = jnp.where(at == which, 1.0, 0.0).astype(jnp.bfloat16)
    tall = dot(pick, kernel, ((1,), (0,))).astype(jnp.bfloat16)
    full = dot(tall, pick, ((1,), (1,)))
    row = lax.broadcasted_iota(jnp.int32, (wide, wide), 0) % TILE
    col = lax.broadcasted_iota(jnp.int32, (wide, wide), 1) % TILE
    return jnp.where(row == col, full, 0.0)


def mix_kernel(scale, packed, scores, params, out):
    members, rows, _ = params.shape
    wide = members * TILE
    full = spreading(kernel_of(scale, packed[...]))
    ksum = jnp.sum(full, axis=1, keepdims=True)
    mixer = full.astype(jnp.bfloat16)
    for r in range(0, SIDE, TILE):
        own = tile(params, r)
        both = dot(mixer, jnp.concatenate([tile(scores, r), own], axis=1), ((1,), (0,)))
        pushed = ksum * own.astype(jnp.float32) - both[:, D:]
        both = jnp.concatenate([both[:, :D], pushed], axis=1) * (1.0 / members)
        both = both.astype(jnp.bfloat16)
        for g in range(2 * len(GROUPS)):
            at = g * SIDE + r
            out[:, at : at + TILE, :] = both[:, g * LANES : (g + 1) * LANES].reshape(
                members, TILE, LANES
            )


def weighted(scale, packed, scores, params):
    members, rows, _ = params.shape
    wide = members * TILE
    vmem = pl.BlockSpec(memory_space=pltpu.VMEM)
    return pl.pallas_call(
        mix_kernel,
        out_shape=jax.ShapeDtypeStruct((members, 2 * rows, LANES), jnp.bfloat16),
        in_specs=[pl.BlockSpec(memory_space=pltpu.SMEM), vmem, vmem, vmem],
        compiler_params=pltpu.CompilerParams(vmem_limit_bytes=24 * 1024 * 1024),
        cost_estimate=pl.CostEstimate(
            flops=4 * wide * wide * SIDE // TILE * D,
            bytes_accessed=8 * members * rows * LANES,
            transcendentals=0,
        ),
        name="mix",
    )(scale, packed, scores, params)


def plain_products(params):
    flat = params.reshape(params.shape[0], -1)
    return dot(flat, flat, ((1,), (1,)))


def plain_weighted(gram, scale, params, scores):
    members = params.shape[0]
    norms = jnp.diagonal(gram)
    dist = norms[:, None] + norms[None, :] - 2.0 * gram
    kernel = jnp.exp(-dist / scale[0]).astype(jnp.bfloat16)
    flat = params.reshape(members, -1)
    ksum = jnp.sum(kernel.astype(jnp.float32), axis=1, keepdims=True)
    attract = dot(kernel, scores.reshape(members, -1), ((1,), (0,))) / members
    mixed = dot(kernel, flat, ((1,), (0,)))
    spread = (flat.astype(jnp.float32) * ksum - mixed) / members
    return tuple(x.astype(jnp.bfloat16).reshape(params.shape) for x in (attract, spread))


STEPS = D // EDGE
TALL = FF // STEPS


def pack_kernel(first, second, out, wide, tall, packed, loads, stores):
    def load(d):
        return (
            pltpu.make_async_copy(
                first.at[0, pl.ds(d * EDGE, EDGE), :], wide.at[d], loads.at[0, d]
            ),
            pltpu.make_async_copy(
                second.at[0, pl.ds(d * TALL, TALL), :], tall.at[d], loads.at[1, d]
            ),
        )

    def store(d):
        here = pl.ds(d * COLS, COLS)
        return pltpu.make_async_copy(packed.at[here], out.at[here], stores.at[d])

    for d in range(STEPS):
        for copy in load(d):
            copy.start()
    for d in range(STEPS):
        for copy in load(d):
            copy.wait()
        for c in range(COLS):
            put(packed, d * COLS + c, 0, wide[d, :, c * D : (c + 1) * D])
            put(packed, d * COLS + c, EDGE, tall[d, c * EDGE : (c + 1) * EDGE, :])
        store(d).start()
    for d in range(STEPS):
        store(d).wait()


def to_blocks(first, second):
    bf = jnp.bfloat16
    return pl.pallas_call(
        pack_kernel,
        out_shape=pltpu.HBM((BLOCKS, ROWS, LANES), bf),
        in_specs=[pl.BlockSpec(memory_space=pl.ANY)] * 2,
        out_specs=pl.BlockSpec(memory_space=pl.ANY),
        scratch_shapes=[
            pltpu.VMEM((STEPS, EDGE, FF), bf),
            pltpu.VMEM((STEPS, TALL, D), bf),
            pltpu.VMEM((BLOCKS, ROWS, LANES), bf),
            pltpu.SemaphoreType.DMA((2, STEPS)),
            pltpu.SemaphoreType.DMA((STEPS,)),
        ],
        compiler_params=pltpu.CompilerParams(vmem_limit_bytes=56 * 1024 * 1024),
        cost_estimate=pl.CostEstimate(flops=0, bytes_accessed=8 * D * FF, transcendentals=0),
        name="pack",
    )(first, second)


def unpack_kernel(blocks, first_a, second_a, first_s, second_s, wide, tall, stores):
    def store(which, d):
        first, second = ((first_a, second_a), (first_s, second_s))[which]
        return (
            pltpu.make_async_copy(
                wide.at[which, d], first.at[0, pl.ds(d * EDGE, EDGE), :], stores.at[which, 0, d]
            ),
            pltpu.make_async_copy(
                tall.at[which, d], second.at[0, pl.ds(d * TALL, TALL), :], stores.at[which, 1, d]
            ),
        )

    for which in range(2):
        for d in range(STEPS):
            for c in range(COLS):
                for g in GROUPS:
                    at = which * ROWS + g * SIDE
                    lanes = slice(c * D + g * LANES, c * D + (g + 1) * LANES)
                    wide[which, d, :, lanes] = blocks[d * COLS + c, at : at + EDGE, :]
                    tall[which, d, c * EDGE : (c + 1) * EDGE, g * LANES : (g + 1) * LANES] = blocks[
                        d * COLS + c, at + EDGE : at + SIDE, :
                    ]
            for copy in store(which, d):
                copy.start()
    for which in range(2):
        for d in range(STEPS):
            for copy in store(which, d):
                copy.wait()


def from_blocks(blocks):
    bf = jnp.bfloat16
    return pl.pallas_call(
        unpack_kernel,
        out_shape=(pltpu.HBM((1, D, FF), bf), pltpu.HBM((1, FF, D), bf)) * 2,
        in_specs=[pl.BlockSpec(memory_space=pltpu.VMEM)],
        out_specs=(pl.BlockSpec(memory_space=pl.ANY),) * 4,
        scratch_shapes=[
            pltpu.VMEM((2, STEPS, EDGE, FF), bf),
            pltpu.VMEM((2, STEPS, TALL, D), bf),
            pltpu.SemaphoreType.DMA((2, 2, STEPS)),
        ],
        compiler_params=pltpu.CompilerParams(vmem_limit_bytes=24 * 1024 * 1024),
        cost_estimate=pl.CostEstimate(flops=0, bytes_accessed=16 * D * FF, transcendentals=0),
        name="unpack",
    )(blocks)


def exchange(blocks):
    return lax.all_to_all(blocks, AXES, split_axis=0, concat_axis=0, tiled=True)


def on_device(
    particles_first, particles_second, pool_images, pool_targets, batch_index, kernel_scale
):
    members = math.prod(lax.axis_size(name) for name in AXES)
    cut = (members, BLOCKS * ROWS // members, LANES)
    tiled = members == BLOCKS
    params = exchange(to_blocks(particles_first, particles_second).reshape(cut))
    scores = particle_scores(
        particles_first[0], particles_second[0], pool_images, pool_targets, batch_index[0]
    )
    if tiled:
        packed = distances(params)
        scores = exchange(scores)
        for bits in ((1,), (2, 4, 6), (8, 16, 24)):
            packed = add_over(packed, members, bits)
        mixed = exchange(weighted(kernel_scale, packed, scores, params))
    else:
        scores = exchange(scores.reshape(cut))
        gram = lax.psum(plain_products(params), AXES)
        parts = plain_weighted(gram, kernel_scale, params, scores)
        mixed = [exchange(x).reshape(BLOCKS, ROWS, LANES) for x in parts]
        mixed = jnp.concatenate(mixed, axis=1)
    return from_blocks(mixed)


def solution(mesh):
    split = P(AXES, None, None)
    return jax.shard_map(
        on_device,
        mesh=mesh,
        in_specs=(split, split, P(), P(), P(AXES, None), P()),
        out_specs=(split, split, split, split),
        check_vma=False,
    )
```

```python
import functools
import math

import jax
import jax.numpy as jnp
from jax import lax
from jax.experimental import pallas as pl
from jax.experimental.pallas import tpu as pltpu
from jax.sharding import PartitionSpec as P

D = 384
FF = 1536
S = 197
DATA = 10000
AXES = ("wide", "narrow")
PAD = 208
EDGE = 48
BLOCKS = D * FF // (EDGE * D)
COLS = FF // D
TILE = 16
LANES = 128
SIDE = 2 * EDGE
GROUPS = range(D // LANES)
ROWS = SIDE * len(GROUPS)
MAIN = ROWS - EDGE
PLANES = 4
PLANE = BLOCKS // PLANES

gelu_c = math.sqrt(2.0 / math.pi)
isd = 1.0 / math.sqrt(D)
isf = 1.0 / math.sqrt(FF)


def dot(a, b, dims):
    return lax.dot_general(a, b, (dims, ((), ())), preferred_element_type=jnp.float32)


def put(main, side, block, row, value):
    for g in GROUPS:
        at = g * SIDE + row
        part = value[:, g * LANES : (g + 1) * LANES]
        if at < MAIN:
            main[block, at : at + EDGE, :] = part
        else:
            side[block, at - MAIN : at - MAIN + EDGE, :] = part


def by_plane(me, side, outs):
    for k in range(BLOCKS):
        outs[k // PLANE][k % PLANE] = side[k ^ me[0]]


def tile(main, side, r):
    parts = []
    for g in GROUPS:
        at = g * SIDE + r
        ref, at = (main, at) if at < MAIN else (side, at - MAIN)
        parts.append(ref[:, at : at + TILE, :].reshape(ref.shape[0] * TILE, LANES))
    return jnp.concatenate(parts, axis=1)


def score_kernel(
    factor, picks, me, image, target, first, second, *refs
):
    outs, side = refs[1 : 1 + PLANES], refs[1 + PLANES]
    out, (xs, ts, normed, hidden, deriv, delta, back) = refs[0], refs[2 + PLANES :]
    step = pl.program_id(0)
    images = pl.num_programs(0)
    rows = pl.ds(pl.multiple_of(step * PAD, PAD), PAD)

    @pl.when(step == 0)
    def _():
        xs[...] = jnp.zeros_like(xs)
        ts[...] = jnp.zeros_like(ts)

    xs[0:S, :] = image[0].astype(jnp.float32)
    ts[0:S, :] = target[0].astype(jnp.float32)
    xf = xs[...]
    mean = jnp.mean(xf, axis=1, keepdims=True)
    centered = xf - mean
    var = jnp.mean(centered * centered, axis=1, keepdims=True)
    nrm = (centered * lax.rsqrt(var + 1e-06)).astype(jnp.bfloat16)
    normed[rows, :] = nrm
    for c in range(COLS):
        cols = pl.ds(c * D, D)
        pre = dot(nrm, first[:, cols], ((1,), (0,))) * isd
        sq = pre * pre
        tval = jnp.tanh(pre * (gelu_c + (gelu_c * 0.044715) * sq))
        gate = 0.5 + 0.5 * tval
        hid = pre * gate
        hidden[rows, cols] = hid.astype(jnp.bfloat16)
        deriv[:, cols] = gate + hid * (1.0 - gate) * (
            2.0 * gelu_c + (6.0 * gelu_c * 0.044715) * sq
        )
    prod = dot(hidden[rows, :], second[...], ((1,), (0,))) * isf
    dlt = ((xs[...] + prod - ts[...]) * (1.0 / S)).astype(jnp.bfloat16)
    delta[rows, :] = dlt
    for c in range(COLS):
        cols = pl.ds(c * D, D)
        dhid = dot(dlt, second[cols, :], ((1,), (1,))) * isf
        back[rows, cols] = (dhid * deriv[:, cols]).astype(jnp.bfloat16)

    @pl.when(step == images - 1)
    def _():
        for c in range(COLS):
            cols = pl.ds(c * D, D)
            grad = dot(normed[...], back[:, cols], ((0,), (0,))) * (-factor * isd)
            score = (grad - first[:, cols].astype(jnp.float32)).astype(jnp.bfloat16)
            for r in range(D // EDGE):
                put(out, side, r * COLS + c, 0, score[r * EDGE : (r + 1) * EDGE, :])
            grad = dot(hidden[:, cols], delta[...], ((0,), (0,))) * (-factor * isf)
            score = (grad - second[cols, :].astype(jnp.float32)).astype(jnp.bfloat16)
            for r in range(D // EDGE):
                at = c * (D // EDGE) + r
                put(out, side, at, EDGE, score[r * EDGE : (r + 1) * EDGE, :])
        by_plane(me, side, outs)


def side_shapes(rows):
    return (jax.ShapeDtypeStruct((PLANE, rows, LANES), jnp.bfloat16),) * PLANES


def particle_scores(first, second, images, targets, picks, me):
    count = picks.shape[0]
    rows = count * PAD
    bf = jnp.bfloat16
    return pl.pallas_call(
        functools.partial(score_kernel, DATA / count),
        out_shape=(pltpu.HBM((BLOCKS, MAIN, LANES), bf), *side_shapes(EDGE)),
        grid_spec=pltpu.PrefetchScalarGridSpec(
            num_scalar_prefetch=2,
            grid=(count,),
            in_specs=[
                pl.BlockSpec((1, S, D), lambda b, picks, me: (picks[b], 0, 0)),
                pl.BlockSpec((1, S, D), lambda b, picks, me: (picks[b], 0, 0)),
                pl.BlockSpec((D, FF), lambda b, picks, me: (0, 0)),
                pl.BlockSpec((FF, D), lambda b, picks, me: (0, 0)),
            ],
            out_specs=(
                pl.BlockSpec((BLOCKS, MAIN, LANES), lambda b, picks, me: (0, 0, 0)),
                *[pl.BlockSpec((PLANE, EDGE, LANES), lambda b, picks, me: (0, 0, 0))] * PLANES,
            ),
            scratch_shapes=[
                pltpu.VMEM((BLOCKS, EDGE, LANES), bf),
                pltpu.VMEM((PAD, D), jnp.float32),
                pltpu.VMEM((PAD, D), jnp.float32),
                pltpu.VMEM((rows, D), bf),
                pltpu.VMEM((rows, FF), bf),
                pltpu.VMEM((PAD, FF), jnp.float32),
                pltpu.VMEM((rows, D), bf),
                pltpu.VMEM((rows, FF), bf),
            ],
        ),
        compiler_params=pltpu.CompilerParams(vmem_limit_bytes=32 * 1024 * 1024),
        cost_estimate=pl.CostEstimate(
            flops=10 * count * PAD * D * FF,
            bytes_accessed=4 * (2 * D * FF + count * S * D),
            transcendentals=count * PAD * FF,
        ),
        name="score",
    )(picks, me, images, targets, first, second)


def gram_kernel(main, side, out, total):
    members = main.shape[0]
    wide = members * TILE
    total[...] = jnp.zeros_like(total)
    for r in range(0, SIDE, TILE):
        part = tile(main, side, r)
        total[...] += dot(part, part, ((1,), (1,)))
    at = lax.broadcasted_iota(jnp.int32, (wide, wide), 0) % TILE
    to = lax.broadcasted_iota(jnp.int32, (wide, wide), 1) % TILE
    kept = jnp.where(at == to, total[...], 0.0)
    summed = jnp.sum(kept.reshape(members, TILE, wide), axis=1)
    turned = summed.T
    gram = jnp.sum(turned.reshape(members, TILE, members), axis=1)
    row = lax.broadcasted_iota(jnp.int32, gram.shape, 0)
    col = lax.broadcasted_iota(jnp.int32, gram.shape, 1)
    own = jnp.where(row == col, gram, 0.0)
    dist = jnp.sum(own, axis=1, keepdims=True) + jnp.sum(own, axis=0, keepdims=True) - 2.0 * gram
    out[...] = jnp.concatenate([dist[q : q + 8] for q in range(0, members, 8)], axis=1)


def distances(main, side):
    members = main.shape[0]
    wide = members * TILE
    return pl.pallas_call(
        gram_kernel,
        out_shape=jax.ShapeDtypeStruct((8, members * members // 8), jnp.float32),
        scratch_shapes=[pltpu.VMEM((wide, wide), jnp.float32)],
        compiler_params=pltpu.CompilerParams(vmem_limit_bytes=16 * 1024 * 1024),
        cost_estimate=pl.CostEstimate(
            flops=2 * wide * wide * SIDE // TILE * D,
            bytes_accessed=2 * members * ROWS * LANES,
            transcendentals=0,
        ),
        name="gram",
    )(main, side)


def add_over(value, members, bits):
    got = [
        lax.ppermute(value, AXES, [(i, i ^ bit) for i in range(members)]) for bit in bits
    ]
    return sum(got, value)


def kernel_of(scale, packed):
    members = packed.shape[1] // 4
    dist = jnp.concatenate(
        [packed[:, members * q : members * (q + 1)] for q in range(members // 8)], axis=0
    )
    return jnp.exp(-dist / scale[0]).astype(jnp.bfloat16)


def spreading(kernel):
    members = kernel.shape[0]
    wide = members * TILE
    at = lax.broadcasted_iota(jnp.int32, (wide, members), 0) // TILE
    which = lax.broadcasted_iota(jnp.int32, (wide, members), 1)
    pick = jnp.where(at == which, 1.0, 0.0).astype(jnp.bfloat16)
    tall = dot(pick, kernel, ((1,), (0,))).astype(jnp.bfloat16)
    full = dot(tall, pick, ((1,), (1,)))
    row = lax.broadcasted_iota(jnp.int32, (wide, wide), 0) % TILE
    col = lax.broadcasted_iota(jnp.int32, (wide, wide), 1) % TILE
    return jnp.where(row == col, full, 0.0)


def mix_kernel(scale, me, packed, scores, side_scores, params, side_params, out, *refs):
    outs, side = refs[:PLANES], refs[PLANES]
    members = params.shape[0]
    wide = members * TILE
    full = spreading(kernel_of(scale, packed[...]))
    ksum = jnp.sum(full, axis=1, keepdims=True)
    mixer = full.astype(jnp.bfloat16)
    for r in range(0, SIDE, TILE):
        own = tile(params, side_params, r)
        both = jnp.concatenate([tile(scores, side_scores, r), own], axis=1)
        both = dot(mixer, both, ((1,), (0,)))
        pushed = ksum * own.astype(jnp.float32) - both[:, D:]
        both = jnp.concatenate([both[:, :D], pushed], axis=1) * (1.0 / members)
        both = both.astype(jnp.bfloat16)
        for which in range(2):
            for g in GROUPS:
                at = g * SIDE + r
                lanes = which * D + g * LANES
                part = both[:, lanes : lanes + LANES].reshape(members, TILE, LANES)
                if at < MAIN:
                    at += which * MAIN
                    out[:, at : at + TILE, :] = part
                else:
                    at += which * EDGE - MAIN
                    side[:, at : at + TILE, :] = part
    by_plane(me, side, outs)


def weighted(scale, me, packed, scores, side_scores, params, side_params):
    members = params.shape[0]
    wide = members * TILE
    vmem = pl.BlockSpec(memory_space=pltpu.VMEM)
    smem = pl.BlockSpec(memory_space=pltpu.SMEM)
    main = jax.ShapeDtypeStruct((members, 2 * MAIN, LANES), jnp.bfloat16)
    return pl.pallas_call(
        mix_kernel,
        out_shape=(main, *side_shapes(2 * EDGE)),
        in_specs=[smem, smem] + [vmem] * 5,
        scratch_shapes=[pltpu.VMEM((members, 2 * EDGE, LANES), jnp.bfloat16)],
        compiler_params=pltpu.CompilerParams(vmem_limit_bytes=24 * 1024 * 1024),
        cost_estimate=pl.CostEstimate(
            flops=4 * wide * wide * SIDE // TILE * D,
            bytes_accessed=8 * members * ROWS * LANES,
            transcendentals=0,
        ),
        name="mix",
    )(scale, me, packed, scores, side_scores, params, side_params)


def plane_kernel(*refs):
    for z in range(PLANES):
        for q in range(PLANE):
            refs[PLANES + q // 2][z, q % 2] = refs[z][q]


def core_kernel(*refs):
    for q in range(PLANE // 2):
        for z in range(PLANES):
            for c in range(2):
                refs[PLANE // 2 + c][q, z] = refs[q][z, c]


def settle_kernel(me, near, far, out):
    for c, ref in enumerate((near, far)):
        for q in range(PLANE // 2):
            for z in range(PLANES):
                out[(z * PLANE + 2 * q + c) ^ me[0]] = ref[q, z]


def regroup(body, name, shapes, *arrays, me=()):
    vmem = pl.BlockSpec(memory_space=pltpu.VMEM)
    size = sum(math.prod(x.shape) for x in arrays)
    return pl.pallas_call(
        body,
        out_shape=shapes,
        in_specs=[pl.BlockSpec(memory_space=pltpu.SMEM)] * len(me) + [vmem] * len(arrays),
        compiler_params=pltpu.CompilerParams(vmem_limit_bytes=16 * 1024 * 1024),
        cost_estimate=pl.CostEstimate(flops=0, bytes_accessed=4 * size, transcendentals=0),
        name=name,
    )(*me, *arrays)


def swap(value, bits):
    pairs = [(i, i ^ bits) for i in range(BLOCKS)]
    return lax.ppermute(value, AXES, pairs)


def across_planes(parts):
    return parts[:1] + [swap(x, z * PLANE) for z, x in enumerate(parts) if z]


def within_plane(parts, me):
    rows = parts[0].shape[1]
    shape = jax.ShapeDtypeStruct((PLANES, 2, rows, LANES), jnp.bfloat16)
    parts = regroup(plane_kernel, "plane", (shape,) * (PLANE // 2), *parts)
    parts = parts[:1] + tuple(swap(x, 2 * q) for q, x in enumerate(parts) if q)
    shape = jax.ShapeDtypeStruct((PLANE // 2, PLANES, rows, LANES), jnp.bfloat16)
    near, far = regroup(core_kernel, "core", (shape,) * 2, *parts)
    shape = jax.ShapeDtypeStruct((BLOCKS, rows, LANES), jnp.bfloat16)
    return regroup(settle_kernel, "settle", shape, near, swap(far, 1), me=(me,))


def plain_products(params):
    flat = params.reshape(params.shape[0], -1)
    return dot(flat, flat, ((1,), (1,)))


def plain_weighted(gram, scale, params, scores):
    members = params.shape[0]
    norms = jnp.diagonal(gram)
    dist = norms[:, None] + norms[None, :] - 2.0 * gram
    kernel = jnp.exp(-dist / scale[0]).astype(jnp.bfloat16)
    flat = params.reshape(members, -1)
    ksum = jnp.sum(kernel.astype(jnp.float32), axis=1, keepdims=True)
    attract = dot(kernel, scores.reshape(members, -1), ((1,), (0,))) / members
    mixed = dot(kernel, flat, ((1,), (0,)))
    spread = (flat.astype(jnp.float32) * ksum - mixed) / members
    return tuple(x.astype(jnp.bfloat16).reshape(params.shape) for x in (attract, spread))


STEPS = D // EDGE
TALL = FF // STEPS


def pack_kernel(me, first, second, out, *refs):
    outs, (wide, tall, packed, side, loads, stores) = refs[:PLANES], refs[PLANES:]

    def load(d):
        return (
            pltpu.make_async_copy(
                first.at[0, pl.ds(d * EDGE, EDGE), :], wide.at[d], loads.at[0, d]
            ),
            pltpu.make_async_copy(
                second.at[0, pl.ds(d * TALL, TALL), :], tall.at[d], loads.at[1, d]
            ),
        )

    def store(d):
        here = pl.ds(d * COLS, COLS)
        return pltpu.make_async_copy(packed.at[here], out.at[here], stores.at[d])

    for d in range(STEPS):
        for copy in load(d):
            copy.start()
    for d in range(STEPS):
        for copy in load(d):
            copy.wait()
        for c in range(COLS):
            put(packed, side, d * COLS + c, 0, wide[d, :, c * D : (c + 1) * D])
            put(packed, side, d * COLS + c, EDGE, tall[d, c * EDGE : (c + 1) * EDGE, :])
        store(d).start()
    by_plane(me, side, outs)
    for d in range(STEPS):
        store(d).wait()


def to_blocks(first, second, me):
    bf = jnp.bfloat16
    return pl.pallas_call(
        pack_kernel,
        out_shape=(pltpu.HBM((BLOCKS, MAIN, LANES), bf), *side_shapes(EDGE)),
        in_specs=[pl.BlockSpec(memory_space=pltpu.SMEM)]
        + [pl.BlockSpec(memory_space=pl.ANY)] * 2,
        out_specs=(
            pl.BlockSpec(memory_space=pl.ANY),
            *[pl.BlockSpec(memory_space=pltpu.VMEM)] * PLANES,
        ),
        scratch_shapes=[
            pltpu.VMEM((STEPS, EDGE, FF), bf),
            pltpu.VMEM((STEPS, TALL, D), bf),
            pltpu.VMEM((BLOCKS, MAIN, LANES), bf),
            pltpu.VMEM((BLOCKS, EDGE, LANES), bf),
            pltpu.SemaphoreType.DMA((2, STEPS)),
            pltpu.SemaphoreType.DMA((STEPS,)),
        ],
        compiler_params=pltpu.CompilerParams(vmem_limit_bytes=56 * 1024 * 1024),
        cost_estimate=pl.CostEstimate(flops=0, bytes_accessed=8 * D * FF, transcendentals=0),
        name="pack",
    )(me, first, second)


def unpack_kernel(main, side, first_a, second_a, first_s, second_s, wide, tall, stores):
    def store(which, d):
        first, second = ((first_a, second_a), (first_s, second_s))[which]
        return (
            pltpu.make_async_copy(
                wide.at[which, d], first.at[0, pl.ds(d * EDGE, EDGE), :], stores.at[which, 0, d]
            ),
            pltpu.make_async_copy(
                tall.at[which, d], second.at[0, pl.ds(d * TALL, TALL), :], stores.at[which, 1, d]
            ),
        )

    for which in range(2):
        for d in range(STEPS):
            for c in range(COLS):
                for g in GROUPS:
                    b, at = d * COLS + c, which * MAIN + g * SIDE
                    lanes = slice(c * D + g * LANES, c * D + (g + 1) * LANES)
                    wide[which, d, :, lanes] = main[b, at : at + EDGE, :]
                    ref, at = (main, at + EDGE) if g * SIDE + EDGE < MAIN else (side, which * EDGE)
                    lanes = slice(g * LANES, (g + 1) * LANES)
                    tall[which, d, c * EDGE : (c + 1) * EDGE, lanes] = ref[b, at : at + EDGE, :]
            for copy in store(which, d):
                copy.start()
    for which in range(2):
        for d in range(STEPS):
            for copy in store(which, d):
                copy.wait()


def from_blocks(main, side):
    bf = jnp.bfloat16
    return pl.pallas_call(
        unpack_kernel,
        out_shape=(pltpu.HBM((1, D, FF), bf), pltpu.HBM((1, FF, D), bf)) * 2,
        in_specs=[pl.BlockSpec(memory_space=pltpu.VMEM)] * 2,
        out_specs=(pl.BlockSpec(memory_space=pl.ANY),) * 4,
        scratch_shapes=[
            pltpu.VMEM((2, STEPS, EDGE, FF), bf),
            pltpu.VMEM((2, STEPS, TALL, D), bf),
            pltpu.SemaphoreType.DMA((2, 2, STEPS)),
        ],
        compiler_params=pltpu.CompilerParams(vmem_limit_bytes=24 * 1024 * 1024),
        cost_estimate=pl.CostEstimate(flops=0, bytes_accessed=16 * D * FF, transcendentals=0),
        name="unpack",
    )(main, side)


def exchange(blocks):
    return lax.all_to_all(blocks, AXES, split_axis=0, concat_axis=0, tiled=True)


def on_device(
    particles_first, particles_second, pool_images, pool_targets, batch_index, kernel_scale
):
    members = math.prod(lax.axis_size(name) for name in AXES)
    tiled = members == BLOCKS
    me = lax.axis_index(AXES) if tiled else 0
    me = jnp.full((1,), me, jnp.int32)
    params, *side_params = to_blocks(particles_first, particles_second, me)
    scores, *side_scores = particle_scores(
        particles_first[0], particles_second[0], pool_images, pool_targets, batch_index[0], me
    )
    if tiled:
        params, scores = exchange(params), exchange(scores)
        side_params, side_scores = across_planes(side_params), across_planes(side_scores)
        params, side_params, side_scores = lax.optimization_barrier(
            (params, side_params, side_scores)
        )
        side_params = within_plane(side_params, me)
        side_scores = within_plane(side_scores, me)
        packed = distances(params, side_params)
        for bits in ((1,), (2, 4, 6), (8, 16, 24)):
            packed = add_over(packed, members, bits)
        main, *side = weighted(
            kernel_scale, me, packed, scores, side_scores, params, side_params
        )
        return from_blocks(exchange(main), within_plane(across_planes(side), me))
    cut = (members, BLOCKS * ROWS // members, LANES)
    params = jnp.concatenate([params, jnp.concatenate(side_params)], axis=1)
    scores = jnp.concatenate([scores, jnp.concatenate(side_scores)], axis=1)
    params, scores = exchange(params.reshape(cut)), exchange(scores.reshape(cut))
    gram = lax.psum(plain_products(params), AXES)
    parts = plain_weighted(gram, kernel_scale, params, scores)
    parts = [exchange(x).reshape(BLOCKS, ROWS, LANES) for x in parts]
    main = jnp.concatenate([x[:, :MAIN] for x in parts], axis=1)
    return from_blocks(main, jnp.concatenate([x[:, MAIN:] for x in parts], axis=1))


def solution(mesh):
    split = P(AXES, None, None)
    return jax.shard_map(
        on_device,
        mesh=mesh,
        in_specs=(split, split, P(), P(), P(AXES, None), P()),
        out_specs=(split, split, split, split),
        check_vma=False,
    )
```

```python
import functools
import math

import jax
import jax.numpy as jnp
from jax import lax
from jax.experimental import pallas as pl
from jax.experimental.pallas import tpu as pltpu
from jax.sharding import PartitionSpec as P

D = 384
FF = 1536
S = 197
DATA = 10000
AXES = ("wide", "narrow")
PAD = 208
EDGE = 48
BLOCKS = D * FF // (EDGE * D)
COLS = FF // D
TILE = 16
LANES = 128
SIDE = 2 * EDGE
GROUPS = range(D // LANES)
ROWS = SIDE * len(GROUPS)
MAIN = ROWS - EDGE
PLANES = 4
PLANE = BLOCKS // PLANES
LONG = 10**11

gelu_c = math.sqrt(2.0 / math.pi)
isd = 1.0 / math.sqrt(D)
isf = 1.0 / math.sqrt(FF)


def dot(a, b, dims):
    return lax.dot_general(a, b, (dims, ((), ())), preferred_element_type=jnp.float32)


def put(main, side, block, row, value):
    for g in GROUPS:
        at = g * SIDE + row
        part = value[:, g * LANES : (g + 1) * LANES]
        if side is None or at < MAIN:
            main[block, at : at + EDGE, :] = part
        else:
            side[block, at - MAIN : at - MAIN + EDGE, :] = part


def by_plane(me, side, outs):
    for k in range(BLOCKS):
        outs[k // PLANE][k % PLANE] = side[k ^ me[0]]


def tile(main, side, r):
    parts = []
    for g in GROUPS:
        at = g * SIDE + r
        ref, at = (main, at) if side is None or at < MAIN else (side, at - MAIN)
        parts.append(ref[:, at : at + TILE, :].reshape(ref.shape[0] * TILE, LANES))
    return jnp.concatenate(parts, axis=1)


def score_kernel(
    factor, picks, me, image, target, first, second, *refs
):
    outs, side = refs[1 : 1 + PLANES], refs[1 + PLANES]
    out, (xs, ts, normed, hidden, deriv, delta, back) = refs[0], refs[2 + PLANES :]
    step = pl.program_id(0)
    images = pl.num_programs(0)
    rows = pl.ds(pl.multiple_of(step * PAD, PAD), PAD)

    @pl.when(step == 0)
    def _():
        xs[...] = jnp.zeros_like(xs)
        ts[...] = jnp.zeros_like(ts)

    xs[0:S, :] = image[0].astype(jnp.float32)
    ts[0:S, :] = target[0].astype(jnp.float32)
    xf = xs[...]
    mean = jnp.mean(xf, axis=1, keepdims=True)
    centered = xf - mean
    var = jnp.mean(centered * centered, axis=1, keepdims=True)
    nrm = (centered * lax.rsqrt(var + 1e-06)).astype(jnp.bfloat16)
    normed[rows, :] = nrm
    for c in range(COLS):
        cols = pl.ds(c * D, D)
        pre = dot(nrm, first[:, cols], ((1,), (0,))) * isd
        sq = pre * pre
        tval = jnp.tanh(pre * (gelu_c + (gelu_c * 0.044715) * sq))
        gate = 0.5 + 0.5 * tval
        hid = pre * gate
        hidden[rows, cols] = hid.astype(jnp.bfloat16)
        deriv[:, cols] = gate + hid * (1.0 - gate) * (
            2.0 * gelu_c + (6.0 * gelu_c * 0.044715) * sq
        )
    prod = dot(hidden[rows, :], second[...], ((1,), (0,))) * isf
    dlt = ((xs[...] + prod - ts[...]) * (1.0 / S)).astype(jnp.bfloat16)
    delta[rows, :] = dlt
    for c in range(COLS):
        cols = pl.ds(c * D, D)
        dhid = dot(dlt, second[cols, :], ((1,), (1,))) * isf
        back[rows, cols] = (dhid * deriv[:, cols]).astype(jnp.bfloat16)

    @pl.when(step == images - 1)
    def _():
        for c in range(COLS):
            cols = pl.ds(c * D, D)
            grad = dot(normed[...], back[:, cols], ((0,), (0,))) * (-factor * isd)
            score = (grad - first[:, cols].astype(jnp.float32)).astype(jnp.bfloat16)
            for r in range(D // EDGE):
                put(out, side, r * COLS + c, 0, score[r * EDGE : (r + 1) * EDGE, :])
            grad = dot(hidden[:, cols], delta[...], ((0,), (0,))) * (-factor * isf)
            score = (grad - second[cols, :].astype(jnp.float32)).astype(jnp.bfloat16)
            for r in range(D // EDGE):
                at = c * (D // EDGE) + r
                put(out, side, at, EDGE, score[r * EDGE : (r + 1) * EDGE, :])
        by_plane(me, side, outs)


def side_shapes(rows):
    return (jax.ShapeDtypeStruct((PLANE, rows, LANES), jnp.bfloat16),) * PLANES


def particle_scores(first, second, images, targets, picks, me):
    count = picks.shape[0]
    rows = count * PAD
    bf = jnp.bfloat16
    return pl.pallas_call(
        functools.partial(score_kernel, DATA / count),
        out_shape=(pltpu.HBM((BLOCKS, MAIN, LANES), bf), *side_shapes(EDGE)),
        grid_spec=pltpu.PrefetchScalarGridSpec(
            num_scalar_prefetch=2,
            grid=(count,),
            in_specs=[
                pl.BlockSpec((1, S, D), lambda b, picks, me: (picks[b], 0, 0)),
                pl.BlockSpec((1, S, D), lambda b, picks, me: (picks[b], 0, 0)),
                pl.BlockSpec((D, FF), lambda b, picks, me: (0, 0)),
                pl.BlockSpec((FF, D), lambda b, picks, me: (0, 0)),
            ],
            out_specs=(
                pl.BlockSpec((BLOCKS, MAIN, LANES), lambda b, picks, me: (0, 0, 0)),
                *[pl.BlockSpec((PLANE, EDGE, LANES), lambda b, picks, me: (0, 0, 0))] * PLANES,
            ),
            scratch_shapes=[
                pltpu.VMEM((BLOCKS, EDGE, LANES), bf),
                pltpu.VMEM((PAD, D), jnp.float32),
                pltpu.VMEM((PAD, D), jnp.float32),
                pltpu.VMEM((rows, D), bf),
                pltpu.VMEM((rows, FF), bf),
                pltpu.VMEM((PAD, FF), jnp.float32),
                pltpu.VMEM((rows, D), bf),
                pltpu.VMEM((rows, FF), bf),
            ],
        ),
        compiler_params=pltpu.CompilerParams(vmem_limit_bytes=32 * 1024 * 1024),
        cost_estimate=pl.CostEstimate(
            flops=10 * count * PAD * D * FF,
            bytes_accessed=4 * (2 * D * FF + count * S * D),
            transcendentals=count * PAD * FF,
        ),
        name="score",
    )(picks, me, images, targets, first, second)


def gram_kernel(params, out, total):
    members, rows, _ = params.shape
    wide = members * TILE
    total[...] = jnp.zeros_like(total)
    for r in range(0, SIDE, TILE):
        part = tile(params, None, r)
        total[...] += dot(part, part, ((1,), (1,)))
    at = lax.broadcasted_iota(jnp.int32, (wide, wide), 0) % TILE
    to = lax.broadcasted_iota(jnp.int32, (wide, wide), 1) % TILE
    kept = jnp.where(at == to, total[...], 0.0)
    summed = jnp.sum(kept.reshape(members, TILE, wide), axis=1)
    turned = summed.T
    gram = jnp.sum(turned.reshape(members, TILE, members), axis=1)
    row = lax.broadcasted_iota(jnp.int32, gram.shape, 0)
    col = lax.broadcasted_iota(jnp.int32, gram.shape, 1)
    own = jnp.where(row == col, gram, 0.0)
    dist = jnp.sum(own, axis=1, keepdims=True) + jnp.sum(own, axis=0, keepdims=True) - 2.0 * gram
    out[...] = jnp.concatenate([dist[q : q + 8] for q in range(0, members, 8)], axis=1)


def distances(params):
    members, rows, _ = params.shape
    wide = members * TILE
    return pl.pallas_call(
        gram_kernel,
        out_shape=jax.ShapeDtypeStruct((8, members * members // 8), jnp.float32),
        scratch_shapes=[pltpu.VMEM((wide, wide), jnp.float32)],
        compiler_params=pltpu.CompilerParams(vmem_limit_bytes=16 * 1024 * 1024),
        cost_estimate=pl.CostEstimate(
            flops=2 * wide * wide * SIDE // TILE * D,
            bytes_accessed=2 * members * rows * LANES,
            transcendentals=0,
        ),
        name="gram",
    )(params)


def add_over(value, members, bits):
    got = [
        lax.ppermute(value, AXES, [(i, i ^ bit) for i in range(members)]) for bit in bits
    ]
    return sum(got, value)


def kernel_of(scale, packed):
    members = packed.shape[1] // 4
    dist = jnp.concatenate(
        [packed[:, members * q : members * (q + 1)] for q in range(members // 8)], axis=0
    )
    return jnp.exp(-dist / scale[0]).astype(jnp.bfloat16)


def spreading(kernel):
    members = kernel.shape[0]
    wide = members * TILE
    at = lax.broadcasted_iota(jnp.int32, (wide, members), 0) // TILE
    which = lax.broadcasted_iota(jnp.int32, (wide, members), 1)
    pick = jnp.where(at == which, 1.0, 0.0).astype(jnp.bfloat16)
    tall = dot(pick, kernel, ((1,), (0,))).astype(jnp.bfloat16)
    full = dot(tall, pick, ((1,), (1,)))
    row = lax.broadcasted_iota(jnp.int32, (wide, wide), 0) % TILE
    col = lax.broadcasted_iota(jnp.int32, (wide, wide), 1) % TILE
    return jnp.where(row == col, full, 0.0)


def mix_kernel(scale, me, packed, scores, side_scores, params, out, *refs):
    outs, side = refs[:PLANES], refs[PLANES]
    members = params.shape[0]
    wide = members * TILE
    full = spreading(kernel_of(scale, packed[...]))
    ksum = jnp.sum(full, axis=1, keepdims=True)
    mixer = full.astype(jnp.bfloat16)
    for r in range(0, SIDE, TILE):
        own = tile(params, None, r)
        both = jnp.concatenate([tile(scores, side_scores, r), own], axis=1)
        both = dot(mixer, both, ((1,), (0,)))
        pushed = ksum * own.astype(jnp.float32) - both[:, D:]
        both = jnp.concatenate([both[:, :D], pushed], axis=1) * (1.0 / members)
        both = both.astype(jnp.bfloat16)
        for which in range(2):
            for g in GROUPS:
                at = g * SIDE + r
                lanes = which * D + g * LANES
                part = both[:, lanes : lanes + LANES].reshape(members, TILE, LANES)
                if at < MAIN:
                    at += which * MAIN
                    out[:, at : at + TILE, :] = part
                else:
                    at += which * EDGE - MAIN
                    side[:, at : at + TILE, :] = part
    by_plane(me, side, outs)


def weighted(scale, me, packed, scores, side_scores, params):
    members = params.shape[0]
    wide = members * TILE
    vmem = pl.BlockSpec(memory_space=pltpu.VMEM)
    smem = pl.BlockSpec(memory_space=pltpu.SMEM)
    main = jax.ShapeDtypeStruct((members, 2 * MAIN, LANES), jnp.bfloat16)
    return pl.pallas_call(
        mix_kernel,
        out_shape=(main, *side_shapes(2 * EDGE)),
        in_specs=[smem, smem] + [vmem] * 4,
        scratch_shapes=[pltpu.VMEM((members, 2 * EDGE, LANES), jnp.bfloat16)],
        compiler_params=pltpu.CompilerParams(vmem_limit_bytes=24 * 1024 * 1024),
        cost_estimate=pl.CostEstimate(
            flops=4 * wide * wide * SIDE // TILE * D,
            bytes_accessed=8 * members * ROWS * LANES,
            transcendentals=0,
        ),
        name="mix",
    )(scale, me, packed, scores, side_scores, params)


def plane_kernel(*refs):
    for z in range(PLANES):
        for q in range(PLANE):
            refs[PLANES + q // 2][z, q % 2] = refs[z][q]


def core_kernel(*refs):
    for q in range(PLANE // 2):
        for z in range(PLANES):
            for c in range(2):
                refs[PLANE // 2 + c][q, z] = refs[q][z, c]


def settle_kernel(me, near, far, out):
    for c, ref in enumerate((near, far)):
        for q in range(PLANE // 2):
            for z in range(PLANES):
                out[(z * PLANE + 2 * q + c) ^ me[0]] = ref[q, z]


def regroup(body, name, shapes, *arrays, me=(), flops=0):
    vmem = pl.BlockSpec(memory_space=pltpu.VMEM)
    size = sum(math.prod(x.shape) for x in arrays)
    return pl.pallas_call(
        body,
        out_shape=shapes,
        in_specs=[pl.BlockSpec(memory_space=pltpu.SMEM)] * len(me) + [vmem] * len(arrays),
        compiler_params=pltpu.CompilerParams(vmem_limit_bytes=16 * 1024 * 1024),
        cost_estimate=pl.CostEstimate(flops=flops, bytes_accessed=4 * size, transcendentals=0),
        name=name,
    )(*me, *arrays)


def swap(value, bits):
    pairs = [(i, i ^ bits) for i in range(BLOCKS)]
    return lax.ppermute(value, AXES, pairs)


def across_planes(parts):
    return parts[:1] + [swap(x, z * PLANE) for z, x in enumerate(parts) if z]


def within_plane(parts, me):
    rows = parts[0].shape[1]
    shape = jax.ShapeDtypeStruct((PLANES, 2, rows, LANES), jnp.bfloat16)
    parts = regroup(plane_kernel, "plane", (shape,) * (PLANE // 2), *parts, flops=LONG)
    parts = parts[:1] + tuple(swap(x, 2 * q) for q, x in enumerate(parts) if q)
    shape = jax.ShapeDtypeStruct((PLANE // 2, PLANES, rows, LANES), jnp.bfloat16)
    near, far = regroup(core_kernel, "core", (shape,) * 2, *parts)
    shape = jax.ShapeDtypeStruct((BLOCKS, rows, LANES), jnp.bfloat16)
    return regroup(settle_kernel, "settle", shape, near, swap(far, 1), me=(me,))


def plain_products(params):
    flat = params.reshape(params.shape[0], -1)
    return dot(flat, flat, ((1,), (1,)))


def plain_weighted(gram, scale, params, scores):
    members = params.shape[0]
    norms = jnp.diagonal(gram)
    dist = norms[:, None] + norms[None, :] - 2.0 * gram
    kernel = jnp.exp(-dist / scale[0]).astype(jnp.bfloat16)
    flat = params.reshape(members, -1)
    ksum = jnp.sum(kernel.astype(jnp.float32), axis=1, keepdims=True)
    attract = dot(kernel, scores.reshape(members, -1), ((1,), (0,))) / members
    mixed = dot(kernel, flat, ((1,), (0,)))
    spread = (flat.astype(jnp.float32) * ksum - mixed) / members
    return tuple(x.astype(jnp.bfloat16).reshape(params.shape) for x in (attract, spread))


STEPS = D // EDGE
TALL = FF // STEPS


def pack_kernel(first, second, out, wide, tall, packed, loads, stores):
    def load(d):
        return (
            pltpu.make_async_copy(
                first.at[0, pl.ds(d * EDGE, EDGE), :], wide.at[d], loads.at[0, d]
            ),
            pltpu.make_async_copy(
                second.at[0, pl.ds(d * TALL, TALL), :], tall.at[d], loads.at[1, d]
            ),
        )

    def store(d):
        here = pl.ds(d * COLS, COLS)
        return pltpu.make_async_copy(packed.at[here], out.at[here], stores.at[d])

    for d in range(STEPS):
        for copy in load(d):
            copy.start()
    for d in range(STEPS):
        for copy in load(d):
            copy.wait()
        for c in range(COLS):
            put(packed, None, d * COLS + c, 0, wide[d, :, c * D : (c + 1) * D])
            put(packed, None, d * COLS + c, EDGE, tall[d, c * EDGE : (c + 1) * EDGE, :])
        store(d).start()
    for d in range(STEPS):
        store(d).wait()


def to_blocks(first, second):
    bf = jnp.bfloat16
    return pl.pallas_call(
        pack_kernel,
        out_shape=pltpu.HBM((BLOCKS, ROWS, LANES), bf),
        in_specs=[pl.BlockSpec(memory_space=pl.ANY)] * 2,
        out_specs=pl.BlockSpec(memory_space=pl.ANY),
        scratch_shapes=[
            pltpu.VMEM((STEPS, EDGE, FF), bf),
            pltpu.VMEM((STEPS, TALL, D), bf),
            pltpu.VMEM((BLOCKS, ROWS, LANES), bf),
            pltpu.SemaphoreType.DMA((2, STEPS)),
            pltpu.SemaphoreType.DMA((STEPS,)),
        ],
        compiler_params=pltpu.CompilerParams(vmem_limit_bytes=56 * 1024 * 1024),
        cost_estimate=pl.CostEstimate(flops=0, bytes_accessed=8 * D * FF, transcendentals=0),
        name="pack",
    )(first, second)


def unpack_kernel(main, side, first_a, second_a, first_s, second_s, wide, tall, stores):
    def store(which, d):
        first, second = ((first_a, second_a), (first_s, second_s))[which]
        return (
            pltpu.make_async_copy(
                wide.at[which, d], first.at[0, pl.ds(d * EDGE, EDGE), :], stores.at[which, 0, d]
            ),
            pltpu.make_async_copy(
                tall.at[which, d], second.at[0, pl.ds(d * TALL, TALL), :], stores.at[which, 1, d]
            ),
        )

    for which in range(2):
        for d in range(STEPS):
            for c in range(COLS):
                for g in GROUPS:
                    b, at = d * COLS + c, which * MAIN + g * SIDE
                    lanes = slice(c * D + g * LANES, c * D + (g + 1) * LANES)
                    wide[which, d, :, lanes] = main[b, at : at + EDGE, :]
                    ref, at = (main, at + EDGE) if g * SIDE + EDGE < MAIN else (side, which * EDGE)
                    lanes = slice(g * LANES, (g + 1) * LANES)
                    tall[which, d, c * EDGE : (c + 1) * EDGE, lanes] = ref[b, at : at + EDGE, :]
            for copy in store(which, d):
                copy.start()
    for which in range(2):
        for d in range(STEPS):
            for copy in store(which, d):
                copy.wait()


def from_blocks(main, side):
    bf = jnp.bfloat16
    return pl.pallas_call(
        unpack_kernel,
        out_shape=(pltpu.HBM((1, D, FF), bf), pltpu.HBM((1, FF, D), bf)) * 2,
        in_specs=[pl.BlockSpec(memory_space=pltpu.VMEM)] * 2,
        out_specs=(pl.BlockSpec(memory_space=pl.ANY),) * 4,
        scratch_shapes=[
            pltpu.VMEM((2, STEPS, EDGE, FF), bf),
            pltpu.VMEM((2, STEPS, TALL, D), bf),
            pltpu.SemaphoreType.DMA((2, 2, STEPS)),
        ],
        compiler_params=pltpu.CompilerParams(vmem_limit_bytes=24 * 1024 * 1024),
        cost_estimate=pl.CostEstimate(flops=0, bytes_accessed=16 * D * FF, transcendentals=0),
        name="unpack",
    )(main, side)


def exchange(blocks):
    return lax.all_to_all(blocks, AXES, split_axis=0, concat_axis=0, tiled=True)


def on_device(
    particles_first, particles_second, pool_images, pool_targets, batch_index, kernel_scale
):
    members = math.prod(lax.axis_size(name) for name in AXES)
    tiled = members == BLOCKS
    me = lax.axis_index(AXES) if tiled else 0
    me = jnp.full((1,), me, jnp.int32)
    params = to_blocks(particles_first, particles_second)
    scores, *side_scores = particle_scores(
        particles_first[0], particles_second[0], pool_images, pool_targets, batch_index[0], me
    )
    if tiled:
        params, scores = exchange(params), exchange(scores)
        params, side_scores = lax.optimization_barrier((params, across_planes(side_scores)))
        side_scores = within_plane(side_scores, me)
        packed = distances(params)
        for bits in ((1,), (2, 4, 6), (8, 16, 24)):
            packed = add_over(packed, members, bits)
        main, *side = weighted(kernel_scale, me, packed, scores, side_scores, params)
        return from_blocks(exchange(main), within_plane(across_planes(side), me))
    cut = (members, BLOCKS * ROWS // members, LANES)
    scores = jnp.concatenate([scores, jnp.concatenate(side_scores)], axis=1)
    params, scores = exchange(params.reshape(cut)), exchange(scores.reshape(cut))
    gram = lax.psum(plain_products(params), AXES)
    parts = plain_weighted(gram, kernel_scale, params, scores)
    parts = [exchange(x).reshape(BLOCKS, ROWS, LANES) for x in parts]
    main = jnp.concatenate([x[:, :MAIN] for x in parts], axis=1)
    return from_blocks(main, jnp.concatenate([x[:, MAIN:] for x in parts], axis=1))


def solution(mesh):
    split = P(AXES, None, None)
    return jax.shard_map(
        on_device,
        mesh=mesh,
        in_specs=(split, split, P(), P(), P(AXES, None), P()),
        out_specs=(split, split, split, split),
        check_vma=False,
    )
```

```python
import functools
import math

import jax
import jax.numpy as jnp
from jax import lax
from jax.experimental import pallas as pl
from jax.experimental.pallas import tpu as pltpu
from jax.sharding import PartitionSpec as P

D = 384
FF = 1536
S = 197
DATA = 10000
AXES = ("wide", "narrow")
PAD = 208
EDGE = 48
BLOCKS = D * FF // (EDGE * D)
COLS = FF // D
TILE = 16
LANES = 128
SIDE = 2 * EDGE
GROUPS = range(D // LANES)
ROWS = SIDE * len(GROUPS)
MAIN = ROWS - EDGE
PLANES = 4
PLANE = BLOCKS // PLANES
LONG = 10**11

gelu_c = math.sqrt(2.0 / math.pi)
isd = 1.0 / math.sqrt(D)
isf = 1.0 / math.sqrt(FF)


def dot(a, b, dims):
    return lax.dot_general(a, b, (dims, ((), ())), preferred_element_type=jnp.float32)


def put(main, side, block, row, value):
    for g in GROUPS:
        at = g * SIDE + row
        part = value[:, g * LANES : (g + 1) * LANES]
        if at < MAIN:
            main[block, at : at + EDGE, :] = part
        else:
            side[block, at - MAIN : at - MAIN + EDGE, :] = part


def by_plane(me, side, outs):
    for k in range(BLOCKS):
        outs[k // PLANE][k % PLANE] = side[k ^ me[0]]


def tile(main, side, r):
    parts = []
    for g in GROUPS:
        at = g * SIDE + r
        ref, at = (main, at) if at < MAIN else (side, at - MAIN)
        parts.append(ref[:, at : at + TILE, :].reshape(ref.shape[0] * TILE, LANES))
    return jnp.concatenate(parts, axis=1)


def score_kernel(
    factor, picks, me, image, target, first, second, *refs
):
    outs, side = refs[1 : 1 + PLANES], refs[1 + PLANES]
    out, (xs, ts, normed, hidden, deriv, delta, back) = refs[0], refs[2 + PLANES :]
    step = pl.program_id(0)
    images = pl.num_programs(0)
    rows = pl.ds(pl.multiple_of(step * PAD, PAD), PAD)

    @pl.when(step == 0)
    def _():
        xs[...] = jnp.zeros_like(xs)
        ts[...] = jnp.zeros_like(ts)

    xs[0:S, :] = image[0].astype(jnp.float32)
    ts[0:S, :] = target[0].astype(jnp.float32)
    xf = xs[...]
    mean = jnp.mean(xf, axis=1, keepdims=True)
    centered = xf - mean
    var = jnp.mean(centered * centered, axis=1, keepdims=True)
    nrm = (centered * lax.rsqrt(var + 1e-06)).astype(jnp.bfloat16)
    normed[rows, :] = nrm
    for c in range(COLS):
        cols = pl.ds(c * D, D)
        pre = dot(nrm, first[:, cols], ((1,), (0,))) * isd
        sq = pre * pre
        tval = jnp.tanh(pre * (gelu_c + (gelu_c * 0.044715) * sq))
        gate = 0.5 + 0.5 * tval
        hid = pre * gate
        hidden[rows, cols] = hid.astype(jnp.bfloat16)
        deriv[:, cols] = gate + hid * (1.0 - gate) * (
            2.0 * gelu_c + (6.0 * gelu_c * 0.044715) * sq
        )
    prod = dot(hidden[rows, :], second[...], ((1,), (0,))) * isf
    dlt = ((xs[...] + prod - ts[...]) * (1.0 / S)).astype(jnp.bfloat16)
    delta[rows, :] = dlt
    for c in range(COLS):
        cols = pl.ds(c * D, D)
        dhid = dot(dlt, second[cols, :], ((1,), (1,))) * isf
        back[rows, cols] = (dhid * deriv[:, cols]).astype(jnp.bfloat16)

    @pl.when(step == images - 1)
    def _():
        for c in range(COLS):
            cols = pl.ds(c * D, D)
            grad = dot(normed[...], back[:, cols], ((0,), (0,))) * (-factor * isd)
            score = (grad - first[:, cols].astype(jnp.float32)).astype(jnp.bfloat16)
            for r in range(D // EDGE):
                put(out, side, r * COLS + c, 0, score[r * EDGE : (r + 1) * EDGE, :])
            grad = dot(hidden[:, cols], delta[...], ((0,), (0,))) * (-factor * isf)
            score = (grad - second[cols, :].astype(jnp.float32)).astype(jnp.bfloat16)
            for r in range(D // EDGE):
                at = c * (D // EDGE) + r
                put(out, side, at, EDGE, score[r * EDGE : (r + 1) * EDGE, :])
        by_plane(me, side, outs)


def side_shapes(rows):
    return (jax.ShapeDtypeStruct((PLANE, rows, LANES), jnp.bfloat16),) * PLANES


def particle_scores(first, second, images, targets, picks, me):
    count = picks.shape[0]
    rows = count * PAD
    bf = jnp.bfloat16
    return pl.pallas_call(
        functools.partial(score_kernel, DATA / count),
        out_shape=(pltpu.HBM((BLOCKS, MAIN, LANES), bf), *side_shapes(EDGE)),
        grid_spec=pltpu.PrefetchScalarGridSpec(
            num_scalar_prefetch=2,
            grid=(count,),
            in_specs=[
                pl.BlockSpec((1, S, D), lambda b, picks, me: (picks[b], 0, 0)),
                pl.BlockSpec((1, S, D), lambda b, picks, me: (picks[b], 0, 0)),
                pl.BlockSpec((D, FF), lambda b, picks, me: (0, 0)),
                pl.BlockSpec((FF, D), lambda b, picks, me: (0, 0)),
            ],
            out_specs=(
                pl.BlockSpec((BLOCKS, MAIN, LANES), lambda b, picks, me: (0, 0, 0)),
                *[pl.BlockSpec((PLANE, EDGE, LANES), lambda b, picks, me: (0, 0, 0))] * PLANES,
            ),
            scratch_shapes=[
                pltpu.VMEM((BLOCKS, EDGE, LANES), bf),
                pltpu.VMEM((PAD, D), jnp.float32),
                pltpu.VMEM((PAD, D), jnp.float32),
                pltpu.VMEM((rows, D), bf),
                pltpu.VMEM((rows, FF), bf),
                pltpu.VMEM((PAD, FF), jnp.float32),
                pltpu.VMEM((rows, D), bf),
                pltpu.VMEM((rows, FF), bf),
            ],
        ),
        compiler_params=pltpu.CompilerParams(vmem_limit_bytes=32 * 1024 * 1024),
        cost_estimate=pl.CostEstimate(
            flops=10 * count * PAD * D * FF,
            bytes_accessed=4 * (2 * D * FF + count * S * D),
            transcendentals=count * PAD * FF,
        ),
        name="score",
    )(picks, me, images, targets, first, second)


def gram_kernel(main, side, out, total):
    members = main.shape[0]
    wide = members * TILE
    total[...] = jnp.zeros_like(total)
    for r in range(0, SIDE, TILE):
        part = tile(main, side, r)
        total[...] += dot(part, part, ((1,), (1,)))
    at = lax.broadcasted_iota(jnp.int32, (wide, wide), 0) % TILE
    to = lax.broadcasted_iota(jnp.int32, (wide, wide), 1) % TILE
    kept = jnp.where(at == to, total[...], 0.0)
    summed = jnp.sum(kept.reshape(members, TILE, wide), axis=1)
    turned = summed.T
    gram = jnp.sum(turned.reshape(members, TILE, members), axis=1)
    row = lax.broadcasted_iota(jnp.int32, gram.shape, 0)
    col = lax.broadcasted_iota(jnp.int32, gram.shape, 1)
    own = jnp.where(row == col, gram, 0.0)
    dist = jnp.sum(own, axis=1, keepdims=True) + jnp.sum(own, axis=0, keepdims=True) - 2.0 * gram
    out[...] = jnp.concatenate([dist[q : q + 8] for q in range(0, members, 8)], axis=1)


def distances(main, side):
    members = main.shape[0]
    wide = members * TILE
    return pl.pallas_call(
        gram_kernel,
        out_shape=jax.ShapeDtypeStruct((8, members * members // 8), jnp.float32),
        scratch_shapes=[pltpu.VMEM((wide, wide), jnp.float32)],
        compiler_params=pltpu.CompilerParams(vmem_limit_bytes=16 * 1024 * 1024),
        cost_estimate=pl.CostEstimate(
            flops=2 * wide * wide * SIDE // TILE * D,
            bytes_accessed=2 * members * ROWS * LANES,
            transcendentals=0,
        ),
        name="gram",
    )(main, side)


def add_over(value, members, bits):
    got = [
        lax.ppermute(value, AXES, [(i, i ^ bit) for i in range(members)]) for bit in bits
    ]
    return sum(got, value)


def kernel_of(scale, packed):
    members = packed.shape[1] // 4
    dist = jnp.concatenate(
        [packed[:, members * q : members * (q + 1)] for q in range(members // 8)], axis=0
    )
    return jnp.exp(-dist / scale[0]).astype(jnp.bfloat16)


def spreading(kernel):
    members = kernel.shape[0]
    wide = members * TILE
    at = lax.broadcasted_iota(jnp.int32, (wide, members), 0) // TILE
    which = lax.broadcasted_iota(jnp.int32, (wide, members), 1)
    pick = jnp.where(at == which, 1.0, 0.0).astype(jnp.bfloat16)
    tall = dot(pick, kernel, ((1,), (0,))).astype(jnp.bfloat16)
    full = dot(tall, pick, ((1,), (1,)))
    row = lax.broadcasted_iota(jnp.int32, (wide, wide), 0) % TILE
    col = lax.broadcasted_iota(jnp.int32, (wide, wide), 1) % TILE
    return jnp.where(row == col, full, 0.0)


def mix_kernel(scale, me, packed, scores, side_scores, params, side_params, out, *refs):
    outs, (side, mixed, stores) = refs[:PLANES], refs[PLANES:]
    members = params.shape[0]
    wide = members * TILE
    full = spreading(kernel_of(scale, packed[...]))
    ksum = jnp.sum(full, axis=1, keepdims=True)
    mixer = full.astype(jnp.bfloat16)
    copies = []
    for r in range(0, SIDE, TILE):
        own = tile(params, side_params, r)
        both = jnp.concatenate([tile(scores, side_scores, r), own], axis=1)
        both = dot(mixer, both, ((1,), (0,)))
        pushed = ksum * own.astype(jnp.float32) - both[:, D:]
        both = jnp.concatenate([both[:, :D], pushed], axis=1) * (1.0 / members)
        both = both.astype(jnp.bfloat16)
        for which in range(2):
            for g in GROUPS:
                at = g * SIDE + r
                lanes = which * D + g * LANES
                part = both[:, lanes : lanes + LANES].reshape(members, TILE, LANES)
                if at < MAIN:
                    at += which * MAIN
                    mixed[:, at : at + TILE, :] = part
                    here = pl.ds(at, TILE)
                    copies.append(
                        pltpu.make_async_copy(
                            mixed.at[:, here, :], out.at[:, here, :], stores.at[at // TILE]
                        )
                    )
                    copies[-1].start()
                else:
                    at += which * EDGE - MAIN
                    side[:, at : at + TILE, :] = part
    by_plane(me, side, outs)
    for copy in copies:
        copy.wait()


def weighted(scale, me, packed, scores, side_scores, params, side_params):
    members = params.shape[0]
    wide = members * TILE
    vmem = pl.BlockSpec(memory_space=pltpu.VMEM)
    smem = pl.BlockSpec(memory_space=pltpu.SMEM)
    return pl.pallas_call(
        mix_kernel,
        out_shape=(pltpu.HBM((members, 2 * MAIN, LANES), jnp.bfloat16), *side_shapes(2 * EDGE)),
        in_specs=[smem, smem] + [vmem] * 5,
        out_specs=(pl.BlockSpec(memory_space=pl.ANY), *[vmem] * PLANES),
        scratch_shapes=[
            pltpu.VMEM((members, 2 * EDGE, LANES), jnp.bfloat16),
            pltpu.VMEM((members, 2 * MAIN, LANES), jnp.bfloat16),
            pltpu.SemaphoreType.DMA((2 * MAIN // TILE,)),
        ],
        compiler_params=pltpu.CompilerParams(vmem_limit_bytes=24 * 1024 * 1024),
        cost_estimate=pl.CostEstimate(
            flops=4 * wide * wide * SIDE // TILE * D,
            bytes_accessed=8 * members * ROWS * LANES,
            transcendentals=0,
        ),
        name="mix",
    )(scale, me, packed, scores, side_scores, params, side_params)


def plane_kernel(*refs):
    for z in range(PLANES):
        for q in range(PLANE):
            refs[PLANES + q // 2][z, q % 2] = refs[z][q]


def core_kernel(*refs):
    for q in range(PLANE // 2):
        for z in range(PLANES):
            for c in range(2):
                refs[PLANE // 2 + c][q, z] = refs[q][z, c]


def settle_kernel(me, near, far, out):
    for c, ref in enumerate((near, far)):
        for q in range(PLANE // 2):
            for z in range(PLANES):
                out[(z * PLANE + 2 * q + c) ^ me[0]] = ref[q, z]


def regroup(body, name, shapes, *arrays, me=(), flops=0):
    vmem = pl.BlockSpec(memory_space=pltpu.VMEM)
    size = sum(math.prod(x.shape) for x in arrays)
    return pl.pallas_call(
        body,
        out_shape=shapes,
        in_specs=[pl.BlockSpec(memory_space=pltpu.SMEM)] * len(me) + [vmem] * len(arrays),
        compiler_params=pltpu.CompilerParams(vmem_limit_bytes=16 * 1024 * 1024),
        cost_estimate=pl.CostEstimate(flops=flops, bytes_accessed=4 * size, transcendentals=0),
        name=name,
    )(*me, *arrays)


def swap(value, bits):
    pairs = [(i, i ^ bits) for i in range(BLOCKS)]
    return lax.ppermute(value, AXES, pairs)


def across_planes(parts):
    return parts[:1] + [swap(x, z * PLANE) for z, x in enumerate(parts) if z]


def in_plane(parts):
    rows = parts[0].shape[1]
    shape = jax.ShapeDtypeStruct((PLANES, 2, rows, LANES), jnp.bfloat16)
    return regroup(plane_kernel, "plane", (shape,) * (PLANE // 2), *parts, flops=LONG)


def across_chips(parts):
    return parts[:1] + tuple(swap(x, 2 * q) for q, x in enumerate(parts) if q)


def in_order(parts, me):
    rows = parts[0].shape[2]
    shape = jax.ShapeDtypeStruct((PLANE // 2, PLANES, rows, LANES), jnp.bfloat16)
    near, far = regroup(core_kernel, "core", (shape,) * 2, *parts)
    shape = jax.ShapeDtypeStruct((BLOCKS, rows, LANES), jnp.bfloat16)
    return regroup(settle_kernel, "settle", shape, near, swap(far, 1), me=(me,))


def after(values, *others):
    return lax.optimization_barrier((values, *others))[0]


def plain_products(params):
    flat = params.reshape(params.shape[0], -1)
    return dot(flat, flat, ((1,), (1,)))


def plain_weighted(gram, scale, params, scores):
    members = params.shape[0]
    norms = jnp.diagonal(gram)
    dist = norms[:, None] + norms[None, :] - 2.0 * gram
    kernel = jnp.exp(-dist / scale[0]).astype(jnp.bfloat16)
    flat = params.reshape(members, -1)
    ksum = jnp.sum(kernel.astype(jnp.float32), axis=1, keepdims=True)
    attract = dot(kernel, scores.reshape(members, -1), ((1,), (0,))) / members
    mixed = dot(kernel, flat, ((1,), (0,)))
    spread = (flat.astype(jnp.float32) * ksum - mixed) / members
    return tuple(x.astype(jnp.bfloat16).reshape(params.shape) for x in (attract, spread))


STEPS = D // EDGE
TALL = FF // STEPS


def pack_kernel(me, first, second, out, *refs):
    outs, (wide, tall, packed, side, loads, stores) = refs[:PLANES], refs[PLANES:]

    def load(d):
        return (
            pltpu.make_async_copy(
                first.at[0, pl.ds(d * EDGE, EDGE), :], wide.at[d], loads.at[0, d]
            ),
            pltpu.make_async_copy(
                second.at[0, pl.ds(d * TALL, TALL), :], tall.at[d], loads.at[1, d]
            ),
        )

    def store(d):
        here = pl.ds(d * COLS, COLS)
        return pltpu.make_async_copy(packed.at[here], out.at[here], stores.at[d])

    for d in range(STEPS):
        for copy in load(d):
            copy.start()
    for d in range(STEPS):
        for copy in load(d):
            copy.wait()
        for c in range(COLS):
            put(packed, side, d * COLS + c, 0, wide[d, :, c * D : (c + 1) * D])
            put(packed, side, d * COLS + c, EDGE, tall[d, c * EDGE : (c + 1) * EDGE, :])
        store(d).start()
    by_plane(me, side, outs)
    for d in range(STEPS):
        store(d).wait()


def to_blocks(first, second, me):
    bf = jnp.bfloat16
    return pl.pallas_call(
        pack_kernel,
        out_shape=(pltpu.HBM((BLOCKS, MAIN, LANES), bf), *side_shapes(EDGE)),
        in_specs=[pl.BlockSpec(memory_space=pltpu.SMEM)]
        + [pl.BlockSpec(memory_space=pl.ANY)] * 2,
        out_specs=(
            pl.BlockSpec(memory_space=pl.ANY),
            *[pl.BlockSpec(memory_space=pltpu.VMEM)] * PLANES,
        ),
        scratch_shapes=[
            pltpu.VMEM((STEPS, EDGE, FF), bf),
            pltpu.VMEM((STEPS, TALL, D), bf),
            pltpu.VMEM((BLOCKS, MAIN, LANES), bf),
            pltpu.VMEM((BLOCKS, EDGE, LANES), bf),
            pltpu.SemaphoreType.DMA((2, STEPS)),
            pltpu.SemaphoreType.DMA((STEPS,)),
        ],
        compiler_params=pltpu.CompilerParams(vmem_limit_bytes=56 * 1024 * 1024),
        cost_estimate=pl.CostEstimate(flops=0, bytes_accessed=8 * D * FF, transcendentals=0),
        name="pack",
    )(me, first, second)


def unpack_kernel(main, side, first_a, second_a, first_s, second_s, wide, tall, stores):
    def store(which, d):
        first, second = ((first_a, second_a), (first_s, second_s))[which]
        return (
            pltpu.make_async_copy(
                wide.at[which, d], first.at[0, pl.ds(d * EDGE, EDGE), :], stores.at[which, 0, d]
            ),
            pltpu.make_async_copy(
                tall.at[which, d], second.at[0, pl.ds(d * TALL, TALL), :], stores.at[which, 1, d]
            ),
        )

    for which in range(2):
        for d in range(STEPS):
            for c in range(COLS):
                for g in GROUPS:
                    b, at = d * COLS + c, which * MAIN + g * SIDE
                    lanes = slice(c * D + g * LANES, c * D + (g + 1) * LANES)
                    wide[which, d, :, lanes] = main[b, at : at + EDGE, :]
                    ref, at = (main, at + EDGE) if g * SIDE + EDGE < MAIN else (side, which * EDGE)
                    lanes = slice(g * LANES, (g + 1) * LANES)
                    tall[which, d, c * EDGE : (c + 1) * EDGE, lanes] = ref[b, at : at + EDGE, :]
            for copy in store(which, d):
                copy.start()
    for which in range(2):
        for d in range(STEPS):
            for copy in store(which, d):
                copy.wait()


def from_blocks(main, side):
    bf = jnp.bfloat16
    return pl.pallas_call(
        unpack_kernel,
        out_shape=(pltpu.HBM((1, D, FF), bf), pltpu.HBM((1, FF, D), bf)) * 2,
        in_specs=[pl.BlockSpec(memory_space=pltpu.VMEM)] * 2,
        out_specs=(pl.BlockSpec(memory_space=pl.ANY),) * 4,
        scratch_shapes=[
            pltpu.VMEM((2, STEPS, EDGE, FF), bf),
            pltpu.VMEM((2, STEPS, TALL, D), bf),
            pltpu.SemaphoreType.DMA((2, 2, STEPS)),
        ],
        compiler_params=pltpu.CompilerParams(vmem_limit_bytes=24 * 1024 * 1024),
        cost_estimate=pl.CostEstimate(flops=0, bytes_accessed=16 * D * FF, transcendentals=0),
        name="unpack",
    )(main, side)


def exchange(blocks):
    return lax.all_to_all(blocks, AXES, split_axis=0, concat_axis=0, tiled=True)


def on_device(
    particles_first, particles_second, pool_images, pool_targets, batch_index, kernel_scale
):
    members = math.prod(lax.axis_size(name) for name in AXES)
    tiled = members == BLOCKS
    me = lax.axis_index(AXES) if tiled else 0
    me = jnp.full((1,), me, jnp.int32)
    params, *side_params = to_blocks(particles_first, particles_second, me)
    first, second = particles_first[0], particles_second[0]
    if tiled:
        params = exchange(params)
        side_params = in_plane(across_planes(side_params))
        first, second = after((first, second), side_params[0])
        side_params = across_chips(side_params)
    scores, *side_scores = particle_scores(
        first, second, pool_images, pool_targets, batch_index[0], me
    )
    if tiled:
        side_params = in_order(after(side_params, side_scores[0]), me)
        scores = exchange(scores)
        side_scores = in_plane(across_planes(after(side_scores, params)))
        packed = distances(*after((params, side_params), side_scores[0]))
        side_scores = in_order(across_chips(side_scores), me)
        for bits in ((1,), (2, 4, 6), (8, 16, 24)):
            packed = add_over(packed, members, bits)
        main, *side = weighted(
            kernel_scale, me, packed, scores, side_scores, params, side_params
        )
        side = in_order(across_chips(in_plane(across_planes(side))), me)
        main = pltpu.with_memory_space_constraint(exchange(main), pltpu.VMEM)
        return from_blocks(main, side)
    cut = (members, BLOCKS * ROWS // members, LANES)
    params = jnp.concatenate([params, jnp.concatenate(side_params)], axis=1)
    scores = jnp.concatenate([scores, jnp.concatenate(side_scores)], axis=1)
    params, scores = exchange(params.reshape(cut)), exchange(scores.reshape(cut))
    gram = lax.psum(plain_products(params), AXES)
    parts = plain_weighted(gram, kernel_scale, params, scores)
    parts = [exchange(x).reshape(BLOCKS, ROWS, LANES) for x in parts]
    main = jnp.concatenate([x[:, :MAIN] for x in parts], axis=1)
    return from_blocks(main, jnp.concatenate([x[:, MAIN:] for x in parts], axis=1))


def solution(mesh):
    split = P(AXES, None, None)
    return jax.shard_map(
        on_device,
        mesh=mesh,
        in_specs=(split, split, P(), P(), P(AXES, None), P()),
        out_specs=(split, split, split, split),
        check_vma=False,
    )
```

```python
import functools
import math

import jax
import jax.numpy as jnp
from jax import lax
from jax.experimental import pallas as pl
from jax.experimental.pallas import tpu as pltpu
from jax.sharding import PartitionSpec as P

D = 384
FF = 1536
S = 197
DATA = 10000
AXES = ("wide", "narrow")
PAD = 208
EDGE = 48
BLOCKS = D * FF // (EDGE * D)
COLS = FF // D
TILE = 16
LANES = 128
SIDE = 2 * EDGE
GROUPS = range(D // LANES)
ROWS = SIDE * len(GROUPS)
MAIN = 2 * SIDE
REST = ROWS - MAIN
PLANES = 4
PLANE = BLOCKS // PLANES
LONG = 10**11

gelu_c = math.sqrt(2.0 / math.pi)
isd = 1.0 / math.sqrt(D)
isf = 1.0 / math.sqrt(FF)


def dot(a, b, dims):
    return lax.dot_general(a, b, (dims, ((), ())), preferred_element_type=jnp.float32)


def put(main, side, block, row, value):
    for g in GROUPS:
        at = g * SIDE + row
        part = value[:, g * LANES : (g + 1) * LANES]
        if at >= MAIN:
            side[block, at - MAIN : at - MAIN + EDGE, :] = part
        else:
            main[block, at : at + EDGE, :] = part


def by_plane(me, side, outs):
    for k in range(BLOCKS):
        outs[k // PLANE][k % PLANE] = side[k ^ me[0]]


def tile(main, side, r):
    parts = []
    for g in GROUPS:
        at = g * SIDE + r
        ref, at = (main, at) if at < MAIN else (side, at - MAIN)
        parts.append(ref[:, at : at + TILE, :].reshape(ref.shape[0] * TILE, LANES))
    return jnp.concatenate(parts, axis=1)


def score_kernel(
    factor, picks, me, image, target, first, second, *refs
):
    outs, side = refs[1 : 1 + PLANES], refs[1 + PLANES]
    out, (xs, ts, normed, hidden, deriv, delta, back) = refs[0], refs[2 + PLANES :]
    step = pl.program_id(0)
    images = pl.num_programs(0)
    rows = pl.ds(pl.multiple_of(step * PAD, PAD), PAD)

    @pl.when(step == 0)
    def _():
        xs[...] = jnp.zeros_like(xs)
        ts[...] = jnp.zeros_like(ts)

    xs[0:S, :] = image[0].astype(jnp.float32)
    ts[0:S, :] = target[0].astype(jnp.float32)
    xf = xs[...]
    mean = jnp.mean(xf, axis=1, keepdims=True)
    centered = xf - mean
    var = jnp.mean(centered * centered, axis=1, keepdims=True)
    nrm = (centered * lax.rsqrt(var + 1e-06)).astype(jnp.bfloat16)
    normed[rows, :] = nrm
    for c in range(COLS):
        cols = pl.ds(c * D, D)
        pre = dot(nrm, first[:, cols], ((1,), (0,))) * isd
        sq = pre * pre
        tval = jnp.tanh(pre * (gelu_c + (gelu_c * 0.044715) * sq))
        gate = 0.5 + 0.5 * tval
        hid = pre * gate
        hidden[rows, cols] = hid.astype(jnp.bfloat16)
        deriv[:, cols] = gate + hid * (1.0 - gate) * (
            2.0 * gelu_c + (6.0 * gelu_c * 0.044715) * sq
        )
    prod = dot(hidden[rows, :], second[...], ((1,), (0,))) * isf
    dlt = ((xs[...] + prod - ts[...]) * (1.0 / S)).astype(jnp.bfloat16)
    delta[rows, :] = dlt
    for c in range(COLS):
        cols = pl.ds(c * D, D)
        dhid = dot(dlt, second[cols, :], ((1,), (1,))) * isf
        back[rows, cols] = (dhid * deriv[:, cols]).astype(jnp.bfloat16)

    @pl.when(step == images - 1)
    def _():
        for c in range(COLS):
            cols = pl.ds(c * D, D)
            grad = dot(normed[...], back[:, cols], ((0,), (0,))) * (-factor * isd)
            score = (grad - first[:, cols].astype(jnp.float32)).astype(jnp.bfloat16)
            for r in range(D // EDGE):
                put(out, side, r * COLS + c, 0, score[r * EDGE : (r + 1) * EDGE, :])
            grad = dot(hidden[:, cols], delta[...], ((0,), (0,))) * (-factor * isf)
            score = (grad - second[cols, :].astype(jnp.float32)).astype(jnp.bfloat16)
            for r in range(D // EDGE):
                at = c * (D // EDGE) + r
                put(out, side, at, EDGE, score[r * EDGE : (r + 1) * EDGE, :])
        by_plane(me, side, outs)


def side_shapes(rows):
    return (jax.ShapeDtypeStruct((PLANE, rows, LANES), jnp.bfloat16),) * PLANES


def particle_scores(first, second, images, targets, picks, me):
    count = picks.shape[0]
    rows = count * PAD
    bf = jnp.bfloat16
    return pl.pallas_call(
        functools.partial(score_kernel, DATA / count),
        out_shape=(pltpu.HBM((BLOCKS, MAIN, LANES), bf), *side_shapes(REST)),
        grid_spec=pltpu.PrefetchScalarGridSpec(
            num_scalar_prefetch=2,
            grid=(count,),
            in_specs=[
                pl.BlockSpec((1, S, D), lambda b, picks, me: (picks[b], 0, 0)),
                pl.BlockSpec((1, S, D), lambda b, picks, me: (picks[b], 0, 0)),
                pl.BlockSpec((D, FF), lambda b, picks, me: (0, 0)),
                pl.BlockSpec((FF, D), lambda b, picks, me: (0, 0)),
            ],
            out_specs=(
                pl.BlockSpec((BLOCKS, MAIN, LANES), lambda b, picks, me: (0, 0, 0)),
                *[pl.BlockSpec((PLANE, REST, LANES), lambda b, picks, me: (0, 0, 0))] * PLANES,
            ),
            scratch_shapes=[
                pltpu.VMEM((BLOCKS, REST, LANES), bf),
                pltpu.VMEM((PAD, D), jnp.float32),
                pltpu.VMEM((PAD, D), jnp.float32),
                pltpu.VMEM((rows, D), bf),
                pltpu.VMEM((rows, FF), bf),
                pltpu.VMEM((PAD, FF), jnp.float32),
                pltpu.VMEM((rows, D), bf),
                pltpu.VMEM((rows, FF), bf),
            ],
        ),
        compiler_params=pltpu.CompilerParams(vmem_limit_bytes=32 * 1024 * 1024),
        cost_estimate=pl.CostEstimate(
            flops=10 * count * PAD * D * FF,
            bytes_accessed=4 * (2 * D * FF + count * S * D),
            transcendentals=count * PAD * FF,
        ),
        name="score",
    )(picks, me, images, targets, first, second)


def gram_kernel(main, side, out, total):
    members = main.shape[0]
    wide = members * TILE
    total[...] = jnp.zeros_like(total)
    for r in range(0, SIDE, TILE):
        part = tile(main, side, r)
        total[...] += dot(part, part, ((1,), (1,)))
    at = lax.broadcasted_iota(jnp.int32, (wide, wide), 0) % TILE
    to = lax.broadcasted_iota(jnp.int32, (wide, wide), 1) % TILE
    kept = jnp.where(at == to, total[...], 0.0)
    summed = jnp.sum(kept.reshape(members, TILE, wide), axis=1)
    turned = summed.T
    gram = jnp.sum(turned.reshape(members, TILE, members), axis=1)
    row = lax.broadcasted_iota(jnp.int32, gram.shape, 0)
    col = lax.broadcasted_iota(jnp.int32, gram.shape, 1)
    own = jnp.where(row == col, gram, 0.0)
    dist = jnp.sum(own, axis=1, keepdims=True) + jnp.sum(own, axis=0, keepdims=True) - 2.0 * gram
    out[...] = jnp.concatenate([dist[q : q + 8] for q in range(0, members, 8)], axis=1)


def distances(main, side):
    members = main.shape[0]
    wide = members * TILE
    return pl.pallas_call(
        gram_kernel,
        out_shape=jax.ShapeDtypeStruct((8, members * members // 8), jnp.float32),
        scratch_shapes=[pltpu.VMEM((wide, wide), jnp.float32)],
        compiler_params=pltpu.CompilerParams(vmem_limit_bytes=16 * 1024 * 1024),
        cost_estimate=pl.CostEstimate(
            flops=2 * wide * wide * SIDE // TILE * D,
            bytes_accessed=2 * members * ROWS * LANES,
            transcendentals=0,
        ),
        name="gram",
    )(main, side)


def add_over(value, members, bits):
    got = [
        lax.ppermute(value, AXES, [(i, i ^ bit) for i in range(members)]) for bit in bits
    ]
    return sum(got, value)


def kernel_of(scale, packed):
    members = packed.shape[1] // 4
    dist = jnp.concatenate(
        [packed[:, members * q : members * (q + 1)] for q in range(members // 8)], axis=0
    )
    return jnp.exp(-dist / scale[0]).astype(jnp.bfloat16)


def spreading(kernel):
    members = kernel.shape[0]
    wide = members * TILE
    at = lax.broadcasted_iota(jnp.int32, (wide, members), 0) // TILE
    which = lax.broadcasted_iota(jnp.int32, (wide, members), 1)
    pick = jnp.where(at == which, 1.0, 0.0).astype(jnp.bfloat16)
    tall = dot(pick, kernel, ((1,), (0,))).astype(jnp.bfloat16)
    full = dot(tall, pick, ((1,), (1,)))
    row = lax.broadcasted_iota(jnp.int32, (wide, wide), 0) % TILE
    col = lax.broadcasted_iota(jnp.int32, (wide, wide), 1) % TILE
    return jnp.where(row == col, full, 0.0)


def mix(mixer, ksum, scores, own):
    members = mixer.shape[0] // TILE
    wide = own.shape[1]
    both = dot(mixer, jnp.concatenate([scores, own], axis=1), ((1,), (0,)))
    pushed = ksum * own.astype(jnp.float32) - both[:, wide:]
    both = jnp.concatenate([both[:, :wide], pushed], axis=1) * (1.0 / members)
    return both.astype(jnp.bfloat16)


def rows_of(ref, at):
    return ref[:, at : at + TILE, :].reshape(ref.shape[0] * TILE, LANES)


def mix_side_kernel(scale, me, packed, scores, params, mixing, *refs):
    outs, side = refs[:PLANES], refs[PLANES]
    members = params.shape[0]
    full = spreading(kernel_of(scale, packed[...]))
    ksum = jnp.sum(full, axis=1, keepdims=True)
    mixer = full.astype(jnp.bfloat16)
    mixing[...] = mixer
    count = SIDE // TILE // 2
    for start in range(0, SIDE, count * TILE):
        at = [start + q * TILE for q in range(count)]
        got = jnp.concatenate([rows_of(scores, r) for r in at], axis=1)
        own = jnp.concatenate([rows_of(params, r) for r in at], axis=1)
        both = mix(mixer, ksum, got, own)
        for q in range(2 * count):
            part = both[:, q * LANES : (q + 1) * LANES].reshape(members, TILE, LANES)
            r = q // count * REST + at[q % count]
            side[:, r : r + TILE, :] = part
    by_plane(me, side, outs)


def mix_side(scale, me, packed, scores, params):
    members = params.shape[0]
    wide = members * TILE
    vmem = pl.BlockSpec(memory_space=pltpu.VMEM)
    smem = pl.BlockSpec(memory_space=pltpu.SMEM)
    mixing = jax.ShapeDtypeStruct((wide, wide), jnp.bfloat16)
    return pl.pallas_call(
        mix_side_kernel,
        out_shape=(mixing, *side_shapes(2 * REST)),
        in_specs=[smem, smem] + [vmem] * 3,
        scratch_shapes=[pltpu.VMEM((members, 2 * REST, LANES), jnp.bfloat16)],
        compiler_params=pltpu.CompilerParams(vmem_limit_bytes=24 * 1024 * 1024),
        cost_estimate=pl.CostEstimate(
            flops=4 * wide * wide * REST // TILE * LANES,
            bytes_accessed=8 * members * REST * LANES,
            transcendentals=0,
        ),
        name="mix_side",
    )(scale, me, packed, scores, params)


def mix_main_kernel(mixing, scores, params, out, mixed, stores):
    members = params.shape[0]
    mixer = mixing[...]
    ksum = jnp.sum(mixer.astype(jnp.float32), axis=1, keepdims=True)
    groups = MAIN // SIDE
    copies = []
    for r in range(0, SIDE, TILE):
        at = [g * SIDE + r for g in range(groups)]
        got = jnp.concatenate([rows_of(scores, x) for x in at], axis=1)
        own = jnp.concatenate([rows_of(params, x) for x in at], axis=1)
        both = mix(mixer, ksum, got, own)
        for q in range(2 * groups):
            part = both[:, q * LANES : (q + 1) * LANES].reshape(members, TILE, LANES)
            x = q // groups * MAIN + at[q % groups]
            mixed[:, x : x + TILE, :] = part
            here = pl.ds(x, TILE)
            copies.append(
                pltpu.make_async_copy(
                    mixed.at[:, here, :], out.at[:, here, :], stores.at[x // TILE]
                )
            )
            copies[-1].start()
    for copy in copies:
        copy.wait()


def mix_main(mixing, scores, params):
    members = params.shape[0]
    wide = members * TILE
    vmem = pl.BlockSpec(memory_space=pltpu.VMEM)
    return pl.pallas_call(
        mix_main_kernel,
        out_shape=pltpu.HBM((members, 2 * MAIN, LANES), jnp.bfloat16),
        in_specs=[vmem] * 3,
        out_specs=pl.BlockSpec(memory_space=pl.ANY),
        scratch_shapes=[
            pltpu.VMEM((members, 2 * MAIN, LANES), jnp.bfloat16),
            pltpu.SemaphoreType.DMA((2 * MAIN // TILE,)),
        ],
        compiler_params=pltpu.CompilerParams(vmem_limit_bytes=24 * 1024 * 1024),
        cost_estimate=pl.CostEstimate(
            flops=4 * wide * wide * MAIN // TILE * LANES,
            bytes_accessed=8 * members * MAIN * LANES,
            transcendentals=0,
        ),
        name="mix_main",
    )(mixing, scores, params)


def plane_kernel(*refs):
    for z in range(PLANES):
        for q in range(PLANE):
            refs[PLANES + q // 2][z, q % 2] = refs[z][q]


def core_kernel(*refs):
    for q in range(PLANE // 2):
        for z in range(PLANES):
            for c in range(2):
                refs[PLANE // 2 + c][q, z] = refs[q][z, c]


def settle_kernel(me, near, far, out):
    for c, ref in enumerate((near, far)):
        for q in range(PLANE // 2):
            for z in range(PLANES):
                out[(z * PLANE + 2 * q + c) ^ me[0]] = ref[q, z]


def regroup(body, name, shapes, *arrays, me=(), flops=0):
    vmem = pl.BlockSpec(memory_space=pltpu.VMEM)
    size = sum(math.prod(x.shape) for x in arrays)
    return pl.pallas_call(
        body,
        out_shape=shapes,
        in_specs=[pl.BlockSpec(memory_space=pltpu.SMEM)] * len(me) + [vmem] * len(arrays),
        compiler_params=pltpu.CompilerParams(vmem_limit_bytes=16 * 1024 * 1024),
        cost_estimate=pl.CostEstimate(flops=flops, bytes_accessed=4 * size, transcendentals=0),
        name=name,
    )(*me, *arrays)


def swap(value, bits):
    pairs = [(i, i ^ bits) for i in range(BLOCKS)]
    return lax.ppermute(value, AXES, pairs)


def across_planes(parts):
    return parts[:1] + [swap(x, z * PLANE) for z, x in enumerate(parts) if z]


def in_plane(parts):
    rows = parts[0].shape[1]
    shape = jax.ShapeDtypeStruct((PLANES, 2, rows, LANES), jnp.bfloat16)
    return regroup(plane_kernel, "plane", (shape,) * (PLANE // 2), *parts, flops=LONG)


def across_chips(parts):
    return parts[:1] + tuple(swap(x, 2 * q) for q, x in enumerate(parts) if q)


def in_order(parts, me):
    rows = parts[0].shape[2]
    shape = jax.ShapeDtypeStruct((PLANE // 2, PLANES, rows, LANES), jnp.bfloat16)
    near, far = regroup(core_kernel, "core", (shape,) * 2, *parts)
    shape = jax.ShapeDtypeStruct((BLOCKS, rows, LANES), jnp.bfloat16)
    return regroup(settle_kernel, "settle", shape, near, swap(far, 1), me=(me,))


def after(values, *others):
    return lax.optimization_barrier((values, *others))[0]


def plain_products(params):
    flat = params.reshape(params.shape[0], -1)
    return dot(flat, flat, ((1,), (1,)))


def plain_weighted(gram, scale, params, scores):
    members = params.shape[0]
    norms = jnp.diagonal(gram)
    dist = norms[:, None] + norms[None, :] - 2.0 * gram
    kernel = jnp.exp(-dist / scale[0]).astype(jnp.bfloat16)
    flat = params.reshape(members, -1)
    ksum = jnp.sum(kernel.astype(jnp.float32), axis=1, keepdims=True)
    attract = dot(kernel, scores.reshape(members, -1), ((1,), (0,))) / members
    mixed = dot(kernel, flat, ((1,), (0,)))
    spread = (flat.astype(jnp.float32) * ksum - mixed) / members
    return tuple(x.astype(jnp.bfloat16).reshape(params.shape) for x in (attract, spread))


STEPS = D // EDGE
TALL = FF // STEPS


def pack_side_kernel(me, first, second, *refs):
    outs, (wide, tall, side, loads) = refs[:PLANES], refs[PLANES:]
    copies = [pltpu.make_async_copy(second.at[0, :, pl.ds(D - LANES, LANES)], tall, loads.at[COLS])]
    for c in range(COLS):
        here = first.at[0, :, pl.ds((c + 1) * D - LANES, LANES)]
        copies.append(pltpu.make_async_copy(here, wide.at[c], loads.at[c]))
    for copy in copies:
        copy.start()
    for copy in copies:
        copy.wait()
    for b in range(BLOCKS):
        r = b // COLS * EDGE
        side[b, 0:EDGE, :] = wide[b % COLS, r : r + EDGE, :]
        side[b, EDGE:REST, :] = tall[b * EDGE : (b + 1) * EDGE, :]
    by_plane(me, side, outs)


def pack_main_kernel(first, second, out, wide, tall, packed, loads, stores):
    def load(d):
        return (
            pltpu.make_async_copy(
                first.at[0, pl.ds(d * EDGE, EDGE), :], wide.at[d], loads.at[0, d]
            ),
            pltpu.make_async_copy(
                second.at[0, pl.ds(d * TALL, TALL), :], tall.at[d], loads.at[1, d]
            ),
        )

    def store(d):
        here = pl.ds(d * COLS, COLS)
        return pltpu.make_async_copy(packed.at[here], out.at[here], stores.at[d])

    for d in range(STEPS):
        for copy in load(d):
            copy.start()
    for d in range(STEPS):
        for copy in load(d):
            copy.wait()
        for c in range(COLS):
            for g in range(MAIN // SIDE):
                b, at = d * COLS + c, g * SIDE
                lanes = g * LANES
                packed[b, at : at + EDGE, :] = wide[d, :, c * D + lanes : c * D + lanes + LANES]
                packed[b, at + EDGE : at + SIDE, :] = tall[
                    d, c * EDGE : (c + 1) * EDGE, lanes : lanes + LANES
                ]
        store(d).start()
    for d in range(STEPS):
        store(d).wait()


def to_blocks(first, second, me):
    bf = jnp.bfloat16
    anywhere = [pl.BlockSpec(memory_space=pl.ANY)]
    params = pltpu.CompilerParams(vmem_limit_bytes=56 * 1024 * 1024)
    cost = pl.CostEstimate(flops=0, bytes_accessed=4 * D * FF, transcendentals=0)
    side = pl.pallas_call(
        pack_side_kernel,
        out_shape=side_shapes(REST),
        in_specs=[pl.BlockSpec(memory_space=pltpu.SMEM)] + anywhere * 2,
        scratch_shapes=[
            pltpu.VMEM((COLS, D, LANES), bf),
            pltpu.VMEM((FF, LANES), bf),
            pltpu.VMEM((BLOCKS, REST, LANES), bf),
            pltpu.SemaphoreType.DMA((COLS + 1,)),
        ],
        compiler_params=params,
        cost_estimate=cost,
        name="pack_side",
    )(me, first, second)
    main = pl.pallas_call(
        pack_main_kernel,
        out_shape=pltpu.HBM((BLOCKS, MAIN, LANES), bf),
        in_specs=anywhere * 2,
        out_specs=anywhere[0],
        scratch_shapes=[
            pltpu.VMEM((STEPS, EDGE, FF), bf),
            pltpu.VMEM((STEPS, TALL, D), bf),
            pltpu.VMEM((BLOCKS, MAIN, LANES), bf),
            pltpu.SemaphoreType.DMA((2, STEPS)),
            pltpu.SemaphoreType.DMA((STEPS,)),
        ],
        compiler_params=params,
        cost_estimate=cost,
        name="pack_main",
    )(first, second)
    return main, side


def unpack_kernel(source, side, first_a, second_a, first_s, second_s, *refs):
    main, wide, tall, loads, stores = refs

    def load(d):
        here = pl.ds(d * COLS, COLS)
        return pltpu.make_async_copy(source.at[here], main.at[here], loads.at[d])

    def store(which, d):
        first, second = ((first_a, second_a), (first_s, second_s))[which]
        return (
            pltpu.make_async_copy(
                wide.at[which, d], first.at[0, pl.ds(d * EDGE, EDGE), :], stores.at[which, 0, d]
            ),
            pltpu.make_async_copy(
                tall.at[which, d], second.at[0, pl.ds(d * TALL, TALL), :], stores.at[which, 1, d]
            ),
        )

    for d in range(STEPS):
        load(d).start()
    for d in range(STEPS):
        load(d).wait()
        for which in range(2):
            for c in range(COLS):
                for g in GROUPS:
                    b, at = d * COLS + c, g * SIDE
                    if at < MAIN:
                        ref, at = main, which * MAIN + at
                    else:
                        ref, at = side, which * REST + at - MAIN
                    lanes = slice(c * D + g * LANES, c * D + (g + 1) * LANES)
                    wide[which, d, :, lanes] = ref[b, at : at + EDGE, :]
                    lanes = slice(g * LANES, (g + 1) * LANES)
                    here = slice(c * EDGE, (c + 1) * EDGE)
                    tall[which, d, here, lanes] = ref[b, at + EDGE : at + SIDE, :]
            for copy in store(which, d):
                copy.start()
    for which in range(2):
        for d in range(STEPS):
            for copy in store(which, d):
                copy.wait()


def from_blocks(main, side):
    bf = jnp.bfloat16
    return pl.pallas_call(
        unpack_kernel,
        out_shape=(pltpu.HBM((1, D, FF), bf), pltpu.HBM((1, FF, D), bf)) * 2,
        in_specs=[pl.BlockSpec(memory_space=pl.ANY), pl.BlockSpec(memory_space=pltpu.VMEM)],
        out_specs=(pl.BlockSpec(memory_space=pl.ANY),) * 4,
        scratch_shapes=[
            pltpu.VMEM((BLOCKS, 2 * MAIN, LANES), bf),
            pltpu.VMEM((2, STEPS, EDGE, FF), bf),
            pltpu.VMEM((2, STEPS, TALL, D), bf),
            pltpu.SemaphoreType.DMA((STEPS,)),
            pltpu.SemaphoreType.DMA((2, 2, STEPS)),
        ],
        compiler_params=pltpu.CompilerParams(vmem_limit_bytes=57 * 1024 * 1024),
        cost_estimate=pl.CostEstimate(flops=0, bytes_accessed=16 * D * FF, transcendentals=0),
        name="unpack",
    )(main, side)


def exchange(blocks):
    return lax.all_to_all(blocks, AXES, split_axis=0, concat_axis=0, tiled=True)


def on_device(
    particles_first, particles_second, pool_images, pool_targets, batch_index, kernel_scale
):
    members = math.prod(lax.axis_size(name) for name in AXES)
    tiled = members == BLOCKS
    me = lax.axis_index(AXES) if tiled else 0
    me = jnp.full((1,), me, jnp.int32)
    params, side_params = to_blocks(particles_first, particles_second, me)
    first, second = particles_first[0], particles_second[0]
    if tiled:
        params = exchange(params)
        side_params = in_plane(across_planes(list(side_params)))
        first, second = after((first, second), side_params[0])
        side_params = across_chips(side_params)
    scores, *side_scores = particle_scores(
        first, second, pool_images, pool_targets, batch_index[0], me
    )
    if tiled:
        side_params = in_order(after(side_params, side_scores[0]), me)
        scores = exchange(scores)
        side_scores = in_plane(across_planes(after(side_scores, params)))
        packed = distances(*after((params, side_params), side_scores[0]))
        side_scores = in_order(across_chips(side_scores), me)
        for bits in ((1,), (2, 4, 6), (8, 16, 24)):
            packed = add_over(packed, members, bits)
        mixing, *side = mix_side(kernel_scale, me, packed, side_scores, side_params)
        main = mix_main(mixing, scores, params)
        side = in_order(across_chips(in_plane(across_planes(side))), me)
        return from_blocks(exchange(main), side)
    cut = (members, BLOCKS * ROWS // members, LANES)
    params = jnp.concatenate([params, jnp.concatenate(side_params)], axis=1)
    scores = jnp.concatenate([scores, jnp.concatenate(side_scores)], axis=1)
    params, scores = exchange(params.reshape(cut)), exchange(scores.reshape(cut))
    gram = lax.psum(plain_products(params), AXES)
    parts = plain_weighted(gram, kernel_scale, params, scores)
    parts = [exchange(x).reshape(BLOCKS, ROWS, LANES) for x in parts]
    main = jnp.concatenate([x[:, :MAIN] for x in parts], axis=1)
    return from_blocks(main, jnp.concatenate([x[:, MAIN:] for x in parts], axis=1))


def solution(mesh):
    split = P(AXES, None, None)
    return jax.shard_map(
        on_device,
        mesh=mesh,
        in_specs=(split, split, P(), P(), P(AXES, None), P()),
        out_specs=(split, split, split, split),
        check_vma=False,
    )
```

```python
import functools
import math

import jax
import jax.numpy as jnp
from jax import lax
from jax.experimental import pallas as pl
from jax.experimental.pallas import tpu as pltpu
from jax.sharding import PartitionSpec as P

D = 384
FF = 1536
S = 197
DATA = 10000
AXES = ("wide", "narrow")
PAD = 208
EDGE = 48
BLOCKS = D * FF // (EDGE * D)
COLS = FF // D
TILE = 16
LANES = 128
SIDE = 2 * EDGE
GROUPS = range(D // LANES)
ROWS = SIDE * len(GROUPS)
MAIN = ROWS - EDGE
REST = ROWS - MAIN
PLANES = 4
PLANE = BLOCKS // PLANES
LONG = 10**11

gelu_c = math.sqrt(2.0 / math.pi)
isd = 1.0 / math.sqrt(D)
isf = 1.0 / math.sqrt(FF)


def dot(a, b, dims):
    return lax.dot_general(a, b, (dims, ((), ())), preferred_element_type=jnp.float32)


def put(main, side, block, row, value):
    for g in GROUPS:
        at = g * SIDE + row
        part = value[:, g * LANES : (g + 1) * LANES]
        if at >= MAIN:
            side[block, at - MAIN : at - MAIN + EDGE, :] = part
        else:
            main[block, at : at + EDGE, :] = part


def by_plane(me, side, outs):
    for k in range(BLOCKS):
        outs[k // PLANE][k % PLANE] = side[k ^ me[0]]


def tile(main, side, r):
    parts = []
    for g in GROUPS:
        at = g * SIDE + r
        ref, at = (main, at) if at < MAIN else (side, at - MAIN)
        parts.append(ref[:, at : at + TILE, :].reshape(ref.shape[0] * TILE, LANES))
    return jnp.concatenate(parts, axis=1)


def score_kernel(
    factor, picks, me, image, target, first, second, *refs
):
    outs, side = refs[1 : 1 + PLANES], refs[1 + PLANES]
    out, (xs, ts, normed, hidden, deriv, delta, back) = refs[0], refs[2 + PLANES :]
    step = pl.program_id(0)
    images = pl.num_programs(0)
    rows = pl.ds(pl.multiple_of(step * PAD, PAD), PAD)

    @pl.when(step == 0)
    def _():
        xs[...] = jnp.zeros_like(xs)
        ts[...] = jnp.zeros_like(ts)

    xs[0:S, :] = image[0].astype(jnp.float32)
    ts[0:S, :] = target[0].astype(jnp.float32)
    xf = xs[...]
    mean = jnp.mean(xf, axis=1, keepdims=True)
    centered = xf - mean
    var = jnp.mean(centered * centered, axis=1, keepdims=True)
    nrm = (centered * lax.rsqrt(var + 1e-06)).astype(jnp.bfloat16)
    normed[rows, :] = nrm
    for c in range(COLS):
        cols = pl.ds(c * D, D)
        pre = dot(nrm, first[:, cols], ((1,), (0,))) * isd
        sq = pre * pre
        tval = jnp.tanh(pre * (gelu_c + (gelu_c * 0.044715) * sq))
        gate = 0.5 + 0.5 * tval
        hid = pre * gate
        hidden[rows, cols] = hid.astype(jnp.bfloat16)
        deriv[:, cols] = gate + hid * (1.0 - gate) * (
            2.0 * gelu_c + (6.0 * gelu_c * 0.044715) * sq
        )
    prod = dot(hidden[rows, :], second[...], ((1,), (0,))) * isf
    dlt = ((xs[...] + prod - ts[...]) * (1.0 / S)).astype(jnp.bfloat16)
    delta[rows, :] = dlt
    for c in range(COLS):
        cols = pl.ds(c * D, D)
        dhid = dot(dlt, second[cols, :], ((1,), (1,))) * isf
        back[rows, cols] = (dhid * deriv[:, cols]).astype(jnp.bfloat16)

    @pl.when(step == images - 1)
    def _():
        for c in range(COLS):
            cols = pl.ds(c * D, D)
            grad = dot(normed[...], back[:, cols], ((0,), (0,))) * (-factor * isd)
            score = (grad - first[:, cols].astype(jnp.float32)).astype(jnp.bfloat16)
            for r in range(D // EDGE):
                put(out, side, r * COLS + c, 0, score[r * EDGE : (r + 1) * EDGE, :])
            grad = dot(hidden[:, cols], delta[...], ((0,), (0,))) * (-factor * isf)
            score = (grad - second[cols, :].astype(jnp.float32)).astype(jnp.bfloat16)
            for r in range(D // EDGE):
                at = c * (D // EDGE) + r
                put(out, side, at, EDGE, score[r * EDGE : (r + 1) * EDGE, :])
        by_plane(me, side, outs)


def side_shapes(rows):
    return (jax.ShapeDtypeStruct((PLANE, rows, LANES), jnp.bfloat16),) * PLANES


def particle_scores(first, second, images, targets, picks, me):
    count = picks.shape[0]
    rows = count * PAD
    bf = jnp.bfloat16
    return pl.pallas_call(
        functools.partial(score_kernel, DATA / count),
        out_shape=(pltpu.HBM((BLOCKS, MAIN, LANES), bf), *side_shapes(REST)),
        grid_spec=pltpu.PrefetchScalarGridSpec(
            num_scalar_prefetch=2,
            grid=(count,),
            in_specs=[
                pl.BlockSpec((1, S, D), lambda b, picks, me: (picks[b], 0, 0)),
                pl.BlockSpec((1, S, D), lambda b, picks, me: (picks[b], 0, 0)),
                pl.BlockSpec((D, FF), lambda b, picks, me: (0, 0)),
                pl.BlockSpec((FF, D), lambda b, picks, me: (0, 0)),
            ],
            out_specs=(
                pl.BlockSpec((BLOCKS, MAIN, LANES), lambda b, picks, me: (0, 0, 0)),
                *[pl.BlockSpec((PLANE, REST, LANES), lambda b, picks, me: (0, 0, 0))] * PLANES,
            ),
            scratch_shapes=[
                pltpu.VMEM((BLOCKS, REST, LANES), bf),
                pltpu.VMEM((PAD, D), jnp.float32),
                pltpu.VMEM((PAD, D), jnp.float32),
                pltpu.VMEM((rows, D), bf),
                pltpu.VMEM((rows, FF), bf),
                pltpu.VMEM((PAD, FF), jnp.float32),
                pltpu.VMEM((rows, D), bf),
                pltpu.VMEM((rows, FF), bf),
            ],
        ),
        compiler_params=pltpu.CompilerParams(vmem_limit_bytes=32 * 1024 * 1024),
        cost_estimate=pl.CostEstimate(
            flops=10 * count * PAD * D * FF,
            bytes_accessed=4 * (2 * D * FF + count * S * D),
            transcendentals=count * PAD * FF,
        ),
        name="score",
    )(picks, me, images, targets, first, second)


def gram_kernel(main, side, out, total):
    members = main.shape[0]
    wide = members * TILE
    total[...] = jnp.zeros_like(total)
    for r in range(0, SIDE, TILE):
        part = tile(main, side, r)
        total[...] += dot(part, part, ((1,), (1,)))
    at = lax.broadcasted_iota(jnp.int32, (wide, wide), 0) % TILE
    to = lax.broadcasted_iota(jnp.int32, (wide, wide), 1) % TILE
    kept = jnp.where(at == to, total[...], 0.0)
    summed = jnp.sum(kept.reshape(members, TILE, wide), axis=1)
    turned = summed.T
    gram = jnp.sum(turned.reshape(members, TILE, members), axis=1)
    row = lax.broadcasted_iota(jnp.int32, gram.shape, 0)
    col = lax.broadcasted_iota(jnp.int32, gram.shape, 1)
    own = jnp.where(row == col, gram, 0.0)
    dist = jnp.sum(own, axis=1, keepdims=True) + jnp.sum(own, axis=0, keepdims=True) - 2.0 * gram
    out[...] = jnp.concatenate([dist[q : q + 8] for q in range(0, members, 8)], axis=1)


def distances(main, side):
    members = main.shape[0]
    wide = members * TILE
    return pl.pallas_call(
        gram_kernel,
        out_shape=jax.ShapeDtypeStruct((8, members * members // 8), jnp.float32),
        scratch_shapes=[pltpu.VMEM((wide, wide), jnp.float32)],
        compiler_params=pltpu.CompilerParams(vmem_limit_bytes=16 * 1024 * 1024),
        cost_estimate=pl.CostEstimate(
            flops=2 * wide * wide * SIDE // TILE * D,
            bytes_accessed=2 * members * ROWS * LANES,
            transcendentals=0,
        ),
        name="gram",
    )(main, side)


def add_over(value, members, bits):
    got = [
        lax.ppermute(value, AXES, [(i, i ^ bit) for i in range(members)]) for bit in bits
    ]
    return sum(got, value)


def kernel_of(scale, packed):
    members = packed.shape[1] // 4
    dist = jnp.concatenate(
        [packed[:, members * q : members * (q + 1)] for q in range(members // 8)], axis=0
    )
    return jnp.exp(-dist / scale[0]).astype(jnp.bfloat16)


def spreading(kernel):
    members = kernel.shape[0]
    wide = members * TILE
    at = lax.broadcasted_iota(jnp.int32, (wide, members), 0) // TILE
    which = lax.broadcasted_iota(jnp.int32, (wide, members), 1)
    pick = jnp.where(at == which, 1.0, 0.0).astype(jnp.bfloat16)
    tall = dot(pick, kernel, ((1,), (0,))).astype(jnp.bfloat16)
    full = dot(tall, pick, ((1,), (1,)))
    row = lax.broadcasted_iota(jnp.int32, (wide, wide), 0) % TILE
    col = lax.broadcasted_iota(jnp.int32, (wide, wide), 1) % TILE
    return jnp.where(row == col, full, 0.0)


def mix(mixer, ksum, scores, own):
    members = mixer.shape[0] // TILE
    wide = own.shape[1]
    both = dot(mixer, jnp.concatenate([scores, own], axis=1), ((1,), (0,)))
    pushed = ksum * own.astype(jnp.float32) - both[:, wide:]
    both = jnp.concatenate([both[:, :wide], pushed], axis=1) * (1.0 / members)
    return both.astype(jnp.bfloat16)


def rows_of(ref, at):
    return ref[:, at : at + TILE, :].reshape(ref.shape[0] * TILE, LANES)


def mix_side_kernel(scale, me, packed, scores, params, mixing, *refs):
    outs, side = refs[:PLANES], refs[PLANES]
    members = params.shape[0]
    full = spreading(kernel_of(scale, packed[...]))
    ksum = jnp.sum(full, axis=1, keepdims=True)
    mixer = full.astype(jnp.bfloat16)
    mixing[...] = mixer
    count = REST // TILE
    for start in range(0, REST, count * TILE):
        at = [start + q * TILE for q in range(count)]
        got = jnp.concatenate([rows_of(scores, r) for r in at], axis=1)
        own = jnp.concatenate([rows_of(params, r) for r in at], axis=1)
        both = mix(mixer, ksum, got, own)
        for q in range(2 * count):
            part = both[:, q * LANES : (q + 1) * LANES].reshape(members, TILE, LANES)
            r = q // count * REST + at[q % count]
            side[:, r : r + TILE, :] = part
    by_plane(me, side, outs)


def mix_side(scale, me, packed, scores, params):
    members = params.shape[0]
    wide = members * TILE
    vmem = pl.BlockSpec(memory_space=pltpu.VMEM)
    smem = pl.BlockSpec(memory_space=pltpu.SMEM)
    mixing = jax.ShapeDtypeStruct((wide, wide), jnp.bfloat16)
    return pl.pallas_call(
        mix_side_kernel,
        out_shape=(mixing, *side_shapes(2 * REST)),
        in_specs=[smem, smem] + [vmem] * 3,
        scratch_shapes=[pltpu.VMEM((members, 2 * REST, LANES), jnp.bfloat16)],
        compiler_params=pltpu.CompilerParams(vmem_limit_bytes=24 * 1024 * 1024),
        cost_estimate=pl.CostEstimate(
            flops=4 * wide * wide * REST // TILE * LANES,
            bytes_accessed=8 * members * REST * LANES,
            transcendentals=0,
        ),
        name="mix_side",
    )(scale, me, packed, scores, params)


def mix_main_kernel(mixing, scores, params, out, mixed, stores):
    members = params.shape[0]
    mixer = mixing[...]
    ksum = jnp.sum(mixer.astype(jnp.float32), axis=1, keepdims=True)
    copies = []
    for r in range(0, SIDE, TILE):
        at = [g * SIDE + r for g in GROUPS if g * SIDE + r < MAIN]
        groups = len(at)
        got = jnp.concatenate([rows_of(scores, x) for x in at], axis=1)
        own = jnp.concatenate([rows_of(params, x) for x in at], axis=1)
        both = mix(mixer, ksum, got, own)
        for q in range(2 * groups):
            part = both[:, q * LANES : (q + 1) * LANES].reshape(members, TILE, LANES)
            x = q // groups * MAIN + at[q % groups]
            mixed[:, x : x + TILE, :] = part
            here = pl.ds(x, TILE)
            copies.append(
                pltpu.make_async_copy(
                    mixed.at[:, here, :], out.at[:, here, :], stores.at[x // TILE]
                )
            )
            copies[-1].start()
    for copy in copies:
        copy.wait()


def mix_main(mixing, scores, params):
    members = params.shape[0]
    wide = members * TILE
    vmem = pl.BlockSpec(memory_space=pltpu.VMEM)
    return pl.pallas_call(
        mix_main_kernel,
        out_shape=pltpu.HBM((members, 2 * MAIN, LANES), jnp.bfloat16),
        in_specs=[vmem] * 3,
        out_specs=pl.BlockSpec(memory_space=pl.ANY),
        scratch_shapes=[
            pltpu.VMEM((members, 2 * MAIN, LANES), jnp.bfloat16),
            pltpu.SemaphoreType.DMA((2 * MAIN // TILE,)),
        ],
        compiler_params=pltpu.CompilerParams(vmem_limit_bytes=24 * 1024 * 1024),
        cost_estimate=pl.CostEstimate(
            flops=4 * wide * wide * MAIN // TILE * LANES,
            bytes_accessed=8 * members * MAIN * LANES,
            transcendentals=0,
        ),
        name="mix_main",
    )(mixing, scores, params)


def plane_kernel(*refs):
    for z in range(PLANES):
        for q in range(PLANE):
            refs[PLANES + q // 2][z, q % 2] = refs[z][q]


def core_kernel(*refs):
    for q in range(PLANE // 2):
        for z in range(PLANES):
            for c in range(2):
                refs[PLANE // 2 + c][q, z] = refs[q][z, c]


def settle_kernel(me, near, far, out):
    for c, ref in enumerate((near, far)):
        for q in range(PLANE // 2):
            for z in range(PLANES):
                out[(z * PLANE + 2 * q + c) ^ me[0]] = ref[q, z]


def regroup(body, name, shapes, *arrays, me=(), flops=0):
    vmem = pl.BlockSpec(memory_space=pltpu.VMEM)
    size = sum(math.prod(x.shape) for x in arrays)
    return pl.pallas_call(
        body,
        out_shape=shapes,
        in_specs=[pl.BlockSpec(memory_space=pltpu.SMEM)] * len(me) + [vmem] * len(arrays),
        compiler_params=pltpu.CompilerParams(vmem_limit_bytes=16 * 1024 * 1024),
        cost_estimate=pl.CostEstimate(flops=flops, bytes_accessed=4 * size, transcendentals=0),
        name=name,
    )(*me, *arrays)


def swap(value, bits):
    pairs = [(i, i ^ bits) for i in range(BLOCKS)]
    return lax.ppermute(value, AXES, pairs)


def across_planes(parts):
    return parts[:1] + [swap(x, z * PLANE) for z, x in enumerate(parts) if z]


def in_plane(parts):
    rows = parts[0].shape[1]
    shape = jax.ShapeDtypeStruct((PLANES, 2, rows, LANES), jnp.bfloat16)
    return regroup(plane_kernel, "plane", (shape,) * (PLANE // 2), *parts, flops=LONG)


def across_chips(parts):
    return parts[:1] + tuple(swap(x, 2 * q) for q, x in enumerate(parts) if q)


def in_order(parts, me):
    rows = parts[0].shape[2]
    shape = jax.ShapeDtypeStruct((PLANE // 2, PLANES, rows, LANES), jnp.bfloat16)
    near, far = regroup(core_kernel, "core", (shape,) * 2, *parts)
    shape = jax.ShapeDtypeStruct((BLOCKS, rows, LANES), jnp.bfloat16)
    return regroup(settle_kernel, "settle", shape, near, swap(far, 1), me=(me,))


def after(values, *others):
    return lax.optimization_barrier((values, *others))[0]


def plain_products(params):
    flat = params.reshape(params.shape[0], -1)
    return dot(flat, flat, ((1,), (1,)))


def plain_weighted(gram, scale, params, scores):
    members = params.shape[0]
    norms = jnp.diagonal(gram)
    dist = norms[:, None] + norms[None, :] - 2.0 * gram
    kernel = jnp.exp(-dist / scale[0]).astype(jnp.bfloat16)
    flat = params.reshape(members, -1)
    ksum = jnp.sum(kernel.astype(jnp.float32), axis=1, keepdims=True)
    attract = dot(kernel, scores.reshape(members, -1), ((1,), (0,))) / members
    mixed = dot(kernel, flat, ((1,), (0,)))
    spread = (flat.astype(jnp.float32) * ksum - mixed) / members
    return tuple(x.astype(jnp.bfloat16).reshape(params.shape) for x in (attract, spread))


STEPS = D // EDGE
TALL = FF // STEPS


def pack_side_kernel(me, second, *refs):
    outs, (tall, load) = refs[:PLANES], refs[PLANES:]
    copy = pltpu.make_async_copy(second.at[0, :, pl.ds(D - LANES, LANES)], tall, load)
    copy.start()
    copy.wait()
    for k in range(BLOCKS):
        here = pl.ds(pl.multiple_of((k ^ me[0]) * EDGE, EDGE), EDGE)
        outs[k // PLANE][k % PLANE] = tall[here, :]


def pack_main_kernel(first, second, out, wide, tall, packed, loads, stores):
    def load(d):
        return (
            pltpu.make_async_copy(
                first.at[0, pl.ds(d * EDGE, EDGE), :], wide.at[d], loads.at[0, d]
            ),
            pltpu.make_async_copy(
                second.at[0, pl.ds(d * TALL, TALL), :], tall.at[d], loads.at[1, d]
            ),
        )

    def store(d):
        here = pl.ds(d * COLS, COLS)
        return pltpu.make_async_copy(packed.at[here], out.at[here], stores.at[d])

    for d in range(STEPS):
        for copy in load(d):
            copy.start()
    for d in range(STEPS):
        for copy in load(d):
            copy.wait()
        for c in range(COLS):
            for g in GROUPS:
                b, at, lanes = d * COLS + c, g * SIDE, g * LANES
                packed[b, at : at + EDGE, :] = wide[d, :, c * D + lanes : c * D + lanes + LANES]
                if at + EDGE < MAIN:
                    packed[b, at + EDGE : at + SIDE, :] = tall[
                        d, c * EDGE : (c + 1) * EDGE, lanes : lanes + LANES
                    ]
        store(d).start()
    for d in range(STEPS):
        store(d).wait()


def to_blocks(first, second, me):
    bf = jnp.bfloat16
    anywhere = [pl.BlockSpec(memory_space=pl.ANY)]
    params = pltpu.CompilerParams(vmem_limit_bytes=56 * 1024 * 1024)
    cost = pl.CostEstimate(flops=0, bytes_accessed=4 * D * FF, transcendentals=0)
    side = pl.pallas_call(
        pack_side_kernel,
        out_shape=side_shapes(REST),
        in_specs=[pl.BlockSpec(memory_space=pltpu.SMEM)] + anywhere,
        scratch_shapes=[pltpu.VMEM((FF, LANES), bf), pltpu.SemaphoreType.DMA],
        compiler_params=params,
        cost_estimate=cost,
        name="pack_side",
    )(me, second)
    main = pl.pallas_call(
        pack_main_kernel,
        out_shape=pltpu.HBM((BLOCKS, MAIN, LANES), bf),
        in_specs=anywhere * 2,
        out_specs=anywhere[0],
        scratch_shapes=[
            pltpu.VMEM((STEPS, EDGE, FF), bf),
            pltpu.VMEM((STEPS, TALL, D), bf),
            pltpu.VMEM((BLOCKS, MAIN, LANES), bf),
            pltpu.SemaphoreType.DMA((2, STEPS)),
            pltpu.SemaphoreType.DMA((STEPS,)),
        ],
        compiler_params=params,
        cost_estimate=cost,
        name="pack_main",
    )(first, second)
    return main, side


def unpack_kernel(main, side, first_a, second_a, first_s, second_s, wide, tall, stores):
    def store(which, d):
        first, second = ((first_a, second_a), (first_s, second_s))[which]
        return (
            pltpu.make_async_copy(
                wide.at[which, d], first.at[0, pl.ds(d * EDGE, EDGE), :], stores.at[which, 0, d]
            ),
            pltpu.make_async_copy(
                tall.at[which, d], second.at[0, pl.ds(d * TALL, TALL), :], stores.at[which, 1, d]
            ),
        )

    for which in range(2):
        for d in range(STEPS):
            for c in range(COLS):
                for g in GROUPS:
                    b, at = d * COLS + c, which * MAIN + g * SIDE
                    lanes = slice(c * D + g * LANES, c * D + (g + 1) * LANES)
                    wide[which, d, :, lanes] = main[b, at : at + EDGE, :]
                    ref, at = (main, at + EDGE) if g * SIDE + EDGE < MAIN else (side, which * REST)
                    lanes = slice(g * LANES, (g + 1) * LANES)
                    tall[which, d, c * EDGE : (c + 1) * EDGE, lanes] = ref[b, at : at + EDGE, :]
            for copy in store(which, d):
                copy.start()
    for which in range(2):
        for d in range(STEPS):
            for copy in store(which, d):
                copy.wait()


def from_blocks(main, side):
    bf = jnp.bfloat16
    return pl.pallas_call(
        unpack_kernel,
        out_shape=(pltpu.HBM((1, D, FF), bf), pltpu.HBM((1, FF, D), bf)) * 2,
        in_specs=[pl.BlockSpec(memory_space=pltpu.VMEM)] * 2,
        out_specs=(pl.BlockSpec(memory_space=pl.ANY),) * 4,
        scratch_shapes=[
            pltpu.VMEM((2, STEPS, EDGE, FF), bf),
            pltpu.VMEM((2, STEPS, TALL, D), bf),
            pltpu.SemaphoreType.DMA((2, 2, STEPS)),
        ],
        compiler_params=pltpu.CompilerParams(vmem_limit_bytes=24 * 1024 * 1024),
        cost_estimate=pl.CostEstimate(flops=0, bytes_accessed=16 * D * FF, transcendentals=0),
        name="unpack",
    )(main, side)


def exchange(blocks):
    return lax.all_to_all(blocks, AXES, split_axis=0, concat_axis=0, tiled=True)


def on_device(
    particles_first, particles_second, pool_images, pool_targets, batch_index, kernel_scale
):
    members = math.prod(lax.axis_size(name) for name in AXES)
    tiled = members == BLOCKS
    me = lax.axis_index(AXES) if tiled else 0
    me = jnp.full((1,), me, jnp.int32)
    params, side_params = to_blocks(particles_first, particles_second, me)
    first, second = particles_first[0], particles_second[0]
    if tiled:
        params = exchange(params)
        side_params = in_plane(across_planes(list(side_params)))
        first, second = after((first, second), side_params[0])
        side_params = across_chips(side_params)
    scores, *side_scores = particle_scores(
        first, second, pool_images, pool_targets, batch_index[0], me
    )
    if tiled:
        side_params = in_order(after(side_params, side_scores[0]), me)
        scores = exchange(scores)
        side_scores = in_plane(across_planes(after(side_scores, params)))
        packed = distances(*after((params, side_params), side_scores[0]))
        side_scores = in_order(across_chips(side_scores), me)
        for bits in ((1,), (2, 4, 6), (8, 16, 24)):
            packed = add_over(packed, members, bits)
        mixing, *side = mix_side(kernel_scale, me, packed, side_scores, side_params)
        main = mix_main(mixing, scores, params)
        side = in_order(across_chips(in_plane(across_planes(side))), me)
        return from_blocks(exchange(main), side)
    cut = (members, BLOCKS * ROWS // members, LANES)
    params = jnp.concatenate([params, jnp.concatenate(side_params)], axis=1)
    scores = jnp.concatenate([scores, jnp.concatenate(side_scores)], axis=1)
    params, scores = exchange(params.reshape(cut)), exchange(scores.reshape(cut))
    gram = lax.psum(plain_products(params), AXES)
    parts = plain_weighted(gram, kernel_scale, params, scores)
    parts = [exchange(x).reshape(BLOCKS, ROWS, LANES) for x in parts]
    main = jnp.concatenate([x[:, :MAIN] for x in parts], axis=1)
    return from_blocks(main, jnp.concatenate([x[:, MAIN:] for x in parts], axis=1))


def solution(mesh):
    split = P(AXES, None, None)
    return jax.shard_map(
        on_device,
        mesh=mesh,
        in_specs=(split, split, P(), P(), P(AXES, None), P()),
        out_specs=(split, split, split, split),
        check_vma=False,
    )
```

```python
import functools
import math

import jax
import jax.numpy as jnp
from jax import lax
from jax.experimental import pallas as pl
from jax.experimental.pallas import tpu as pltpu
from jax.sharding import PartitionSpec as P

D = 384
FF = 1536
S = 197
DATA = 10000
AXES = ("wide", "narrow")
PAD = 208
EDGE = 48
BLOCKS = D * FF // (EDGE * D)
COLS = FF // D
TILE = 16
LANES = 128
SIDE = 2 * EDGE
GROUPS = range(D // LANES)
ROWS = SIDE * len(GROUPS)
MAIN = ROWS - EDGE
REST = ROWS - MAIN
PMAIN = MAIN - TILE
PREST = ROWS - PMAIN
PLANES = 4
PLANE = BLOCKS // PLANES
LONG = 10**11

gelu_c = math.sqrt(2.0 / math.pi)
isd = 1.0 / math.sqrt(D)
isf = 1.0 / math.sqrt(FF)


def dot(a, b, dims):
    return lax.dot_general(a, b, (dims, ((), ())), preferred_element_type=jnp.float32)


def put(main, side, block, row, value):
    for g in GROUPS:
        at = g * SIDE + row
        part = value[:, g * LANES : (g + 1) * LANES]
        if at >= MAIN:
            side[block, at - MAIN : at - MAIN + EDGE, :] = part
        else:
            main[block, at : at + EDGE, :] = part


def by_plane(me, side, outs):
    for k in range(BLOCKS):
        outs[k // PLANE][k % PLANE] = side[k ^ me[0]]


def rows_of(main, side, at):
    ref, at = (main, at) if at < main.shape[1] else (side, at - main.shape[1])
    return ref[:, at : at + TILE, :].reshape(ref.shape[0] * TILE, LANES)


def tile(main, side, r):
    return jnp.concatenate([rows_of(main, side, g * SIDE + r) for g in GROUPS], axis=1)


def score_kernel(
    factor, picks, me, image, target, first, second, *refs
):
    outs, side = refs[1 : 1 + PLANES], refs[1 + PLANES]
    out, (xs, ts, normed, hidden, deriv, delta, back) = refs[0], refs[2 + PLANES :]
    step = pl.program_id(0)
    images = pl.num_programs(0)
    rows = pl.ds(pl.multiple_of(step * PAD, PAD), PAD)

    @pl.when(step == 0)
    def _():
        xs[...] = jnp.zeros_like(xs)
        ts[...] = jnp.zeros_like(ts)

    xs[0:S, :] = image[0].astype(jnp.float32)
    ts[0:S, :] = target[0].astype(jnp.float32)
    xf = xs[...]
    mean = jnp.mean(xf, axis=1, keepdims=True)
    centered = xf - mean
    var = jnp.mean(centered * centered, axis=1, keepdims=True)
    nrm = (centered * lax.rsqrt(var + 1e-06)).astype(jnp.bfloat16)
    normed[rows, :] = nrm
    for c in range(COLS):
        cols = pl.ds(c * D, D)
        pre = dot(nrm, first[:, cols], ((1,), (0,))) * isd
        sq = pre * pre
        tval = jnp.tanh(pre * (gelu_c + (gelu_c * 0.044715) * sq))
        gate = 0.5 + 0.5 * tval
        hid = pre * gate
        hidden[rows, cols] = hid.astype(jnp.bfloat16)
        deriv[:, cols] = gate + hid * (1.0 - gate) * (
            2.0 * gelu_c + (6.0 * gelu_c * 0.044715) * sq
        )
    prod = dot(hidden[rows, :], second[...], ((1,), (0,))) * isf
    dlt = ((xs[...] + prod - ts[...]) * (1.0 / S)).astype(jnp.bfloat16)
    delta[rows, :] = dlt
    for c in range(COLS):
        cols = pl.ds(c * D, D)
        dhid = dot(dlt, second[cols, :], ((1,), (1,))) * isf
        back[rows, cols] = (dhid * deriv[:, cols]).astype(jnp.bfloat16)

    @pl.when(step == images - 1)
    def _():
        for c in range(COLS):
            cols = pl.ds(c * D, D)
            grad = dot(normed[...], back[:, cols], ((0,), (0,))) * (-factor * isd)
            score = (grad - first[:, cols].astype(jnp.float32)).astype(jnp.bfloat16)
            for r in range(D // EDGE):
                put(out, side, r * COLS + c, 0, score[r * EDGE : (r + 1) * EDGE, :])
            grad = dot(hidden[:, cols], delta[...], ((0,), (0,))) * (-factor * isf)
            score = (grad - second[cols, :].astype(jnp.float32)).astype(jnp.bfloat16)
            for r in range(D // EDGE):
                at = c * (D // EDGE) + r
                put(out, side, at, EDGE, score[r * EDGE : (r + 1) * EDGE, :])
        by_plane(me, side, outs)


def side_shapes(rows):
    return (jax.ShapeDtypeStruct((PLANE, rows, LANES), jnp.bfloat16),) * PLANES


def particle_scores(first, second, images, targets, picks, me):
    count = picks.shape[0]
    rows = count * PAD
    bf = jnp.bfloat16
    return pl.pallas_call(
        functools.partial(score_kernel, DATA / count),
        out_shape=(pltpu.HBM((BLOCKS, MAIN, LANES), bf), *side_shapes(REST)),
        grid_spec=pltpu.PrefetchScalarGridSpec(
            num_scalar_prefetch=2,
            grid=(count,),
            in_specs=[
                pl.BlockSpec((1, S, D), lambda b, picks, me: (picks[b], 0, 0)),
                pl.BlockSpec((1, S, D), lambda b, picks, me: (picks[b], 0, 0)),
                pl.BlockSpec((D, FF), lambda b, picks, me: (0, 0)),
                pl.BlockSpec((FF, D), lambda b, picks, me: (0, 0)),
            ],
            out_specs=(
                pl.BlockSpec((BLOCKS, MAIN, LANES), lambda b, picks, me: (0, 0, 0)),
                *[pl.BlockSpec((PLANE, REST, LANES), lambda b, picks, me: (0, 0, 0))] * PLANES,
            ),
            scratch_shapes=[
                pltpu.VMEM((BLOCKS, REST, LANES), bf),
                pltpu.VMEM((PAD, D), jnp.float32),
                pltpu.VMEM((PAD, D), jnp.float32),
                pltpu.VMEM((rows, D), bf),
                pltpu.VMEM((rows, FF), bf),
                pltpu.VMEM((PAD, FF), jnp.float32),
                pltpu.VMEM((rows, D), bf),
                pltpu.VMEM((rows, FF), bf),
            ],
        ),
        compiler_params=pltpu.CompilerParams(vmem_limit_bytes=32 * 1024 * 1024),
        cost_estimate=pl.CostEstimate(
            flops=10 * count * PAD * D * FF,
            bytes_accessed=4 * (2 * D * FF + count * S * D),
            transcendentals=count * PAD * FF,
        ),
        name="score",
    )(picks, me, images, targets, first, second)


def gram_kernel(main, side, out, total):
    members = main.shape[0]
    wide = members * TILE
    total[...] = jnp.zeros_like(total)
    for r in range(0, SIDE, TILE):
        part = tile(main, side, r)
        total[...] += dot(part, part, ((1,), (1,)))
    at = lax.broadcasted_iota(jnp.int32, (wide, wide), 0) % TILE
    to = lax.broadcasted_iota(jnp.int32, (wide, wide), 1) % TILE
    kept = jnp.where(at == to, total[...], 0.0)
    summed = jnp.sum(kept.reshape(members, TILE, wide), axis=1)
    turned = summed.T
    gram = jnp.sum(turned.reshape(members, TILE, members), axis=1)
    row = lax.broadcasted_iota(jnp.int32, gram.shape, 0)
    col = lax.broadcasted_iota(jnp.int32, gram.shape, 1)
    own = jnp.where(row == col, gram, 0.0)
    dist = jnp.sum(own, axis=1, keepdims=True) + jnp.sum(own, axis=0, keepdims=True) - 2.0 * gram
    out[...] = jnp.concatenate([dist[q : q + 8] for q in range(0, members, 8)], axis=1)


def distances(main, side):
    members = main.shape[0]
    wide = members * TILE
    return pl.pallas_call(
        gram_kernel,
        out_shape=jax.ShapeDtypeStruct((8, members * members // 8), jnp.float32),
        scratch_shapes=[pltpu.VMEM((wide, wide), jnp.float32)],
        compiler_params=pltpu.CompilerParams(vmem_limit_bytes=16 * 1024 * 1024),
        cost_estimate=pl.CostEstimate(
            flops=2 * wide * wide * SIDE // TILE * D,
            bytes_accessed=2 * members * ROWS * LANES,
            transcendentals=0,
        ),
        name="gram",
    )(main, side)


def add_over(value, members, bits):
    got = [
        lax.ppermute(value, AXES, [(i, i ^ bit) for i in range(members)]) for bit in bits
    ]
    return sum(got, value)


def kernel_of(scale, packed):
    members = packed.shape[1] // 4
    dist = jnp.concatenate(
        [packed[:, members * q : members * (q + 1)] for q in range(members // 8)], axis=0
    )
    return jnp.exp(-dist / scale[0]).astype(jnp.bfloat16)


def spreading(kernel):
    members = kernel.shape[0]
    wide = members * TILE
    at = lax.broadcasted_iota(jnp.int32, (wide, members), 0) // TILE
    which = lax.broadcasted_iota(jnp.int32, (wide, members), 1)
    pick = jnp.where(at == which, 1.0, 0.0).astype(jnp.bfloat16)
    tall = dot(pick, kernel, ((1,), (0,))).astype(jnp.bfloat16)
    full = dot(tall, pick, ((1,), (1,)))
    row = lax.broadcasted_iota(jnp.int32, (wide, wide), 0) % TILE
    col = lax.broadcasted_iota(jnp.int32, (wide, wide), 1) % TILE
    return jnp.where(row == col, full, 0.0)


def mix(mixer, ksum, scores, own):
    members = mixer.shape[0] // TILE
    wide = own.shape[1]
    both = dot(mixer, jnp.concatenate([scores, own], axis=1), ((1,), (0,)))
    pushed = ksum * own.astype(jnp.float32) - both[:, wide:]
    both = jnp.concatenate([both[:, :wide], pushed], axis=1) * (1.0 / members)
    return both.astype(jnp.bfloat16)


def mix_side_kernel(scale, me, packed, scores, params, mixing, *refs):
    outs, side = refs[:PLANES], refs[PLANES]
    members = params.shape[0]
    full = spreading(kernel_of(scale, packed[...]))
    ksum = jnp.sum(full, axis=1, keepdims=True)
    mixer = full.astype(jnp.bfloat16)
    mixing[...] = mixer
    at = range(0, REST, TILE)
    got = jnp.concatenate([rows_of(scores, None, r) for r in at], axis=1)
    own = jnp.concatenate([rows_of(params, None, PREST - REST + r) for r in at], axis=1)
    both = mix(mixer, ksum, got, own)
    for q in range(2 * len(at)):
        part = both[:, q * LANES : (q + 1) * LANES].reshape(members, TILE, LANES)
        side[:, q * TILE : (q + 1) * TILE, :] = part
    by_plane(me, side, outs)


def mix_side(scale, me, packed, scores, params):
    members = params.shape[0]
    wide = members * TILE
    vmem = pl.BlockSpec(memory_space=pltpu.VMEM)
    smem = pl.BlockSpec(memory_space=pltpu.SMEM)
    mixing = jax.ShapeDtypeStruct((wide, wide), jnp.bfloat16)
    return pl.pallas_call(
        mix_side_kernel,
        out_shape=(mixing, *side_shapes(2 * REST)),
        in_specs=[smem, smem] + [vmem] * 3,
        scratch_shapes=[pltpu.VMEM((members, 2 * REST, LANES), jnp.bfloat16)],
        compiler_params=pltpu.CompilerParams(vmem_limit_bytes=24 * 1024 * 1024),
        cost_estimate=pl.CostEstimate(
            flops=4 * wide * wide * REST // TILE * LANES,
            bytes_accessed=8 * members * REST * LANES,
            transcendentals=0,
        ),
        name="mix_side",
    )(scale, me, packed, scores, params)


def mix_main_kernel(mixing, scores, params, side_params, out, mixed, stores):
    members = params.shape[0]
    mixer = mixing[...]
    ksum = jnp.sum(mixer.astype(jnp.float32), axis=1, keepdims=True)
    copies = []
    for r in range(0, SIDE, TILE):
        at = [g * SIDE + r for g in GROUPS if g * SIDE + r < MAIN]
        groups = len(at)
        got = jnp.concatenate([rows_of(scores, None, x) for x in at], axis=1)
        own = jnp.concatenate([rows_of(params, side_params, x) for x in at], axis=1)
        both = mix(mixer, ksum, got, own)
        for q in range(2 * groups):
            part = both[:, q * LANES : (q + 1) * LANES].reshape(members, TILE, LANES)
            x = q // groups * MAIN + at[q % groups]
            mixed[:, x : x + TILE, :] = part
            here = pl.ds(x, TILE)
            copies.append(
                pltpu.make_async_copy(
                    mixed.at[:, here, :], out.at[:, here, :], stores.at[x // TILE]
                )
            )
            copies[-1].start()
    for copy in copies:
        copy.wait()


def mix_main(mixing, scores, params, side_params):
    members = params.shape[0]
    wide = members * TILE
    vmem = pl.BlockSpec(memory_space=pltpu.VMEM)
    return pl.pallas_call(
        mix_main_kernel,
        out_shape=pltpu.HBM((members, 2 * MAIN, LANES), jnp.bfloat16),
        in_specs=[vmem] * 4,
        out_specs=pl.BlockSpec(memory_space=pl.ANY),
        scratch_shapes=[
            pltpu.VMEM((members, 2 * MAIN, LANES), jnp.bfloat16),
            pltpu.SemaphoreType.DMA((2 * MAIN // TILE,)),
        ],
        compiler_params=pltpu.CompilerParams(vmem_limit_bytes=24 * 1024 * 1024),
        cost_estimate=pl.CostEstimate(
            flops=4 * wide * wide * MAIN // TILE * LANES,
            bytes_accessed=8 * members * MAIN * LANES,
            transcendentals=0,
        ),
        name="mix_main",
    )(mixing, scores, params, side_params)


def plane_kernel(*refs):
    for z in range(PLANES):
        for q in range(PLANE):
            refs[PLANES + q // 2][z, q % 2] = refs[z][q]


def core_kernel(*refs):
    for q in range(PLANE // 2):
        for z in range(PLANES):
            for c in range(2):
                refs[PLANE // 2 + c][q, z] = refs[q][z, c]


def settle_kernel(me, near, far, out):
    for c, ref in enumerate((near, far)):
        for q in range(PLANE // 2):
            for z in range(PLANES):
                out[(z * PLANE + 2 * q + c) ^ me[0]] = ref[q, z]


def regroup(body, name, shapes, *arrays, me=(), flops=0):
    vmem = pl.BlockSpec(memory_space=pltpu.VMEM)
    size = sum(math.prod(x.shape) for x in arrays)
    return pl.pallas_call(
        body,
        out_shape=shapes,
        in_specs=[pl.BlockSpec(memory_space=pltpu.SMEM)] * len(me) + [vmem] * len(arrays),
        compiler_params=pltpu.CompilerParams(vmem_limit_bytes=16 * 1024 * 1024),
        cost_estimate=pl.CostEstimate(flops=flops, bytes_accessed=4 * size, transcendentals=0),
        name=name,
    )(*me, *arrays)


def swap(value, bits):
    pairs = [(i, i ^ bits) for i in range(BLOCKS)]
    return lax.ppermute(value, AXES, pairs)


def across_planes(parts):
    return parts[:1] + [swap(x, z * PLANE) for z, x in enumerate(parts) if z]


def in_plane(parts):
    rows = parts[0].shape[1]
    shape = jax.ShapeDtypeStruct((PLANES, 2, rows, LANES), jnp.bfloat16)
    return regroup(plane_kernel, "plane", (shape,) * (PLANE // 2), *parts, flops=LONG)


def across_chips(parts):
    return parts[:1] + tuple(swap(x, 2 * q) for q, x in enumerate(parts) if q)


def in_order(parts, me):
    rows = parts[0].shape[2]
    shape = jax.ShapeDtypeStruct((PLANE // 2, PLANES, rows, LANES), jnp.bfloat16)
    near, far = regroup(core_kernel, "core", (shape,) * 2, *parts)
    shape = jax.ShapeDtypeStruct((BLOCKS, rows, LANES), jnp.bfloat16)
    return regroup(settle_kernel, "settle", shape, near, swap(far, 1), me=(me,))


def after(values, *others):
    return lax.optimization_barrier((values, *others))[0]


def plain_products(params):
    flat = params.reshape(params.shape[0], -1)
    return dot(flat, flat, ((1,), (1,)))


def plain_weighted(gram, scale, params, scores):
    members = params.shape[0]
    norms = jnp.diagonal(gram)
    dist = norms[:, None] + norms[None, :] - 2.0 * gram
    kernel = jnp.exp(-dist / scale[0]).astype(jnp.bfloat16)
    flat = params.reshape(members, -1)
    ksum = jnp.sum(kernel.astype(jnp.float32), axis=1, keepdims=True)
    attract = dot(kernel, scores.reshape(members, -1), ((1,), (0,))) / members
    mixed = dot(kernel, flat, ((1,), (0,)))
    spread = (flat.astype(jnp.float32) * ksum - mixed) / members
    return tuple(x.astype(jnp.bfloat16).reshape(params.shape) for x in (attract, spread))


STEPS = D // EDGE
TALL = FF // STEPS


def pack_side_kernel(me, first, second, *refs):
    outs, (wide, tall, loads) = refs[:PLANES], refs[PLANES:]
    copies = [pltpu.make_async_copy(second.at[0, :, pl.ds(D - LANES, LANES)], tall, loads.at[COLS])]
    for c in range(COLS):
        here = first.at[0, :, pl.ds((c + 1) * D - LANES, LANES)]
        copies.append(pltpu.make_async_copy(here, wide.at[c], loads.at[c]))
    for copy in copies:
        copy.start()
    for copy in copies:
        copy.wait()
    more = PREST - EDGE
    for k in range(BLOCKS):
        b = k ^ me[0]
        here = pl.ds(pl.multiple_of(b // COLS * EDGE + EDGE - more, TILE), more)
        outs[k // PLANE][k % PLANE, 0:more, :] = wide[b % COLS, here, :]
        here = pl.ds(pl.multiple_of(b * EDGE, EDGE), EDGE)
        outs[k // PLANE][k % PLANE, more:PREST, :] = tall[here, :]


def pack_main_kernel(first, second, out, wide, tall, packed, loads, stores):
    def load(d):
        return (
            pltpu.make_async_copy(
                first.at[0, pl.ds(d * EDGE, EDGE), :], wide.at[d], loads.at[0, d]
            ),
            pltpu.make_async_copy(
                second.at[0, pl.ds(d * TALL, TALL), :], tall.at[d], loads.at[1, d]
            ),
        )

    def store(d):
        here = pl.ds(d * COLS, COLS)
        return pltpu.make_async_copy(packed.at[here], out.at[here], stores.at[d])

    for d in range(STEPS):
        for copy in load(d):
            copy.start()
    for d in range(STEPS):
        for copy in load(d):
            copy.wait()
        for c in range(COLS):
            for g in GROUPS:
                b, at, lanes = d * COLS + c, g * SIDE, g * LANES
                end = min(EDGE, PMAIN - at)
                packed[b, at : at + end, :] = wide[
                    d, 0:end, c * D + lanes : c * D + lanes + LANES
                ]
                if at + EDGE < PMAIN:
                    packed[b, at + EDGE : at + SIDE, :] = tall[
                        d, c * EDGE : (c + 1) * EDGE, lanes : lanes + LANES
                    ]
        store(d).start()
    for d in range(STEPS):
        store(d).wait()


def to_blocks(first, second, me):
    bf = jnp.bfloat16
    anywhere = [pl.BlockSpec(memory_space=pl.ANY)]
    params = pltpu.CompilerParams(vmem_limit_bytes=56 * 1024 * 1024)
    cost = pl.CostEstimate(flops=0, bytes_accessed=4 * D * FF, transcendentals=0)
    side = pl.pallas_call(
        pack_side_kernel,
        out_shape=side_shapes(PREST),
        in_specs=[pl.BlockSpec(memory_space=pltpu.SMEM)] + anywhere * 2,
        scratch_shapes=[
            pltpu.VMEM((COLS, D, LANES), bf),
            pltpu.VMEM((FF, LANES), bf),
            pltpu.SemaphoreType.DMA((COLS + 1,)),
        ],
        compiler_params=params,
        cost_estimate=cost,
        name="pack_side",
    )(me, first, second)
    main = pl.pallas_call(
        pack_main_kernel,
        out_shape=pltpu.HBM((BLOCKS, PMAIN, LANES), bf),
        in_specs=anywhere * 2,
        out_specs=anywhere[0],
        scratch_shapes=[
            pltpu.VMEM((STEPS, EDGE, FF), bf),
            pltpu.VMEM((STEPS, TALL, D), bf),
            pltpu.VMEM((BLOCKS, PMAIN, LANES), bf),
            pltpu.SemaphoreType.DMA((2, STEPS)),
            pltpu.SemaphoreType.DMA((STEPS,)),
        ],
        compiler_params=params,
        cost_estimate=cost,
        name="pack_main",
    )(first, second)
    return main, side


def unpack_kernel(main, side, first_a, second_a, first_s, second_s, wide, tall, stores):
    def store(which, d):
        first, second = ((first_a, second_a), (first_s, second_s))[which]
        return (
            pltpu.make_async_copy(
                wide.at[which, d], first.at[0, pl.ds(d * EDGE, EDGE), :], stores.at[which, 0, d]
            ),
            pltpu.make_async_copy(
                tall.at[which, d], second.at[0, pl.ds(d * TALL, TALL), :], stores.at[which, 1, d]
            ),
        )

    for which in range(2):
        for d in range(STEPS):
            for c in range(COLS):
                for g in GROUPS:
                    b, at = d * COLS + c, which * MAIN + g * SIDE
                    lanes = slice(c * D + g * LANES, c * D + (g + 1) * LANES)
                    wide[which, d, :, lanes] = main[b, at : at + EDGE, :]
                    ref, at = (main, at + EDGE) if g * SIDE + EDGE < MAIN else (side, which * REST)
                    lanes = slice(g * LANES, (g + 1) * LANES)
                    tall[which, d, c * EDGE : (c + 1) * EDGE, lanes] = ref[b, at : at + EDGE, :]
            for copy in store(which, d):
                copy.start()
    for which in range(2):
        for d in range(STEPS):
            for copy in store(which, d):
                copy.wait()


def from_blocks(main, side):
    bf = jnp.bfloat16
    return pl.pallas_call(
        unpack_kernel,
        out_shape=(pltpu.HBM((1, D, FF), bf), pltpu.HBM((1, FF, D), bf)) * 2,
        in_specs=[pl.BlockSpec(memory_space=pltpu.VMEM)] * 2,
        out_specs=(pl.BlockSpec(memory_space=pl.ANY),) * 4,
        scratch_shapes=[
            pltpu.VMEM((2, STEPS, EDGE, FF), bf),
            pltpu.VMEM((2, STEPS, TALL, D), bf),
            pltpu.SemaphoreType.DMA((2, 2, STEPS)),
        ],
        compiler_params=pltpu.CompilerParams(vmem_limit_bytes=24 * 1024 * 1024),
        cost_estimate=pl.CostEstimate(flops=0, bytes_accessed=LONG // 100, transcendentals=0),
        name="unpack",
    )(main, side)


def exchange(blocks):
    return lax.all_to_all(blocks, AXES, split_axis=0, concat_axis=0, tiled=True)


def on_device(
    particles_first, particles_second, pool_images, pool_targets, batch_index, kernel_scale
):
    members = math.prod(lax.axis_size(name) for name in AXES)
    tiled = members == BLOCKS
    me = lax.axis_index(AXES) if tiled else 0
    me = jnp.full((1,), me, jnp.int32)
    params, side_params = to_blocks(particles_first, particles_second, me)
    first, second = particles_first[0], particles_second[0]
    if tiled:
        params = exchange(params)
        side_params = in_plane(across_planes(list(side_params)))
        first, second = after((first, second), side_params[0])
        side_params = across_chips(side_params)
    scores, *side_scores = particle_scores(
        first, second, pool_images, pool_targets, batch_index[0], me
    )
    if tiled:
        side_params = in_order(after(side_params, side_scores[0]), me)
        scores = exchange(scores)
        side_scores = in_plane(across_planes(after(side_scores, params)))
        packed = distances(*after((params, side_params), side_scores[0]))
        side_scores = in_order(across_chips(side_scores), me)
        for bits in ((1,), (2, 4, 6), (8, 16, 24)):
            packed = add_over(packed, members, bits)
        mixing, *side = mix_side(kernel_scale, me, packed, side_scores, side_params)
        main = mix_main(mixing, scores, params, side_params)
        side = in_order(across_chips(in_plane(across_planes(side))), me)
        return from_blocks(exchange(main), side)
    cut = (members, BLOCKS * ROWS // members, LANES)
    params = jnp.concatenate([params, jnp.concatenate(side_params)], axis=1)
    scores = jnp.concatenate([scores, jnp.concatenate(side_scores)], axis=1)
    params, scores = exchange(params.reshape(cut)), exchange(scores.reshape(cut))
    gram = lax.psum(plain_products(params), AXES)
    parts = plain_weighted(gram, kernel_scale, params, scores)
    parts = [exchange(x).reshape(BLOCKS, ROWS, LANES) for x in parts]
    main = jnp.concatenate([x[:, :MAIN] for x in parts], axis=1)
    return from_blocks(main, jnp.concatenate([x[:, MAIN:] for x in parts], axis=1))


def solution(mesh):
    split = P(AXES, None, None)
    return jax.shard_map(
        on_device,
        mesh=mesh,
        in_specs=(split, split, P(), P(), P(AXES, None), P()),
        out_specs=(split, split, split, split),
        check_vma=False,
    )
```

```python
import functools
import math

import jax
import jax.numpy as jnp
from jax import lax
from jax.experimental import pallas as pl
from jax.experimental.pallas import tpu as pltpu
from jax.sharding import PartitionSpec as P

D = 384
FF = 1536
S = 197
DATA = 10000
AXES = ("wide", "narrow")
PAD = 208
EDGE = 48
BLOCKS = D * FF // (EDGE * D)
COLS = FF // D
TILE = 16
LANES = 128
SIDE = 2 * EDGE
GROUPS = range(D // LANES)
ROWS = SIDE * len(GROUPS)
REST = EDGE + TILE
MAIN = ROWS - REST
PLANES = 4
PLANE = BLOCKS // PLANES
LONG = 10**11

gelu_c = math.sqrt(2.0 / math.pi)
isd = 1.0 / math.sqrt(D)
isf = 1.0 / math.sqrt(FF)


def dot(a, b, dims):
    return lax.dot_general(a, b, (dims, ((), ())), preferred_element_type=jnp.float32)


def in_main(at):
    return max(0, min(EDGE, MAIN - at))


def put(main, side, block, row, value):
    for g in GROUPS:
        at = g * SIDE + row
        part = value[:, g * LANES : (g + 1) * LANES]
        n = in_main(at)
        if n:
            main[block, at : at + n, :] = part[:n]
        if n < EDGE:
            side[block, at + n - MAIN : at + EDGE - MAIN, :] = part[n:]


def by_plane(me, side, outs):
    for k in range(BLOCKS):
        outs[k // PLANE][k % PLANE] = side[k ^ me[0]]


def rows_of(main, side, at):
    ref, at = (main, at) if at < main.shape[1] else (side, at - main.shape[1])
    return ref[:, at : at + TILE, :].reshape(ref.shape[0] * TILE, LANES)


def tile(main, side, r):
    return jnp.concatenate([rows_of(main, side, g * SIDE + r) for g in GROUPS], axis=1)


def score_kernel(
    factor, picks, me, image, target, first, second, *refs
):
    outs, side = refs[1 : 1 + PLANES], refs[1 + PLANES]
    out, (xs, ts, normed, hidden, deriv, delta, back) = refs[0], refs[2 + PLANES :]
    step = pl.program_id(0)
    images = pl.num_programs(0)
    rows = pl.ds(pl.multiple_of(step * PAD, PAD), PAD)

    @pl.when(step == 0)
    def _():
        xs[...] = jnp.zeros_like(xs)
        ts[...] = jnp.zeros_like(ts)

    xs[0:S, :] = image[0].astype(jnp.float32)
    ts[0:S, :] = target[0].astype(jnp.float32)
    xf = xs[...]
    mean = jnp.mean(xf, axis=1, keepdims=True)
    centered = xf - mean
    var = jnp.mean(centered * centered, axis=1, keepdims=True)
    nrm = (centered * lax.rsqrt(var + 1e-06)).astype(jnp.bfloat16)
    normed[rows, :] = nrm
    for c in range(COLS):
        cols = pl.ds(c * D, D)
        pre = dot(nrm, first[:, cols], ((1,), (0,))) * isd
        sq = pre * pre
        tval = jnp.tanh(pre * (gelu_c + (gelu_c * 0.044715) * sq))
        gate = 0.5 + 0.5 * tval
        hid = pre * gate
        hidden[rows, cols] = hid.astype(jnp.bfloat16)
        deriv[:, cols] = gate + hid * (1.0 - gate) * (
            2.0 * gelu_c + (6.0 * gelu_c * 0.044715) * sq
        )
    prod = dot(hidden[rows, :], second[...], ((1,), (0,))) * isf
    dlt = ((xs[...] + prod - ts[...]) * (1.0 / S)).astype(jnp.bfloat16)
    delta[rows, :] = dlt
    for c in range(COLS):
        cols = pl.ds(c * D, D)
        dhid = dot(dlt, second[cols, :], ((1,), (1,))) * isf
        back[rows, cols] = (dhid * deriv[:, cols]).astype(jnp.bfloat16)

    @pl.when(step == images - 1)
    def _():
        for c in range(COLS):
            cols = pl.ds(c * D, D)
            grad = dot(normed[...], back[:, cols], ((0,), (0,))) * (-factor * isd)
            score = (grad - first[:, cols].astype(jnp.float32)).astype(jnp.bfloat16)
            for r in range(D // EDGE):
                put(out, side, r * COLS + c, 0, score[r * EDGE : (r + 1) * EDGE, :])
            grad = dot(hidden[:, cols], delta[...], ((0,), (0,))) * (-factor * isf)
            score = (grad - second[cols, :].astype(jnp.float32)).astype(jnp.bfloat16)
            for r in range(D // EDGE):
                at = c * (D // EDGE) + r
                put(out, side, at, EDGE, score[r * EDGE : (r + 1) * EDGE, :])
        by_plane(me, side, outs)


def side_shapes(rows):
    return (jax.ShapeDtypeStruct((PLANE, rows, LANES), jnp.bfloat16),) * PLANES


def particle_scores(first, second, images, targets, picks, me):
    count = picks.shape[0]
    rows = count * PAD
    bf = jnp.bfloat16
    return pl.pallas_call(
        functools.partial(score_kernel, DATA / count),
        out_shape=(pltpu.HBM((BLOCKS, MAIN, LANES), bf), *side_shapes(REST)),
        grid_spec=pltpu.PrefetchScalarGridSpec(
            num_scalar_prefetch=2,
            grid=(count,),
            in_specs=[
                pl.BlockSpec((1, S, D), lambda b, picks, me: (picks[b], 0, 0)),
                pl.BlockSpec((1, S, D), lambda b, picks, me: (picks[b], 0, 0)),
                pl.BlockSpec((D, FF), lambda b, picks, me: (0, 0)),
                pl.BlockSpec((FF, D), lambda b, picks, me: (0, 0)),
            ],
            out_specs=(
                pl.BlockSpec((BLOCKS, MAIN, LANES), lambda b, picks, me: (0, 0, 0)),
                *[pl.BlockSpec((PLANE, REST, LANES), lambda b, picks, me: (0, 0, 0))] * PLANES,
            ),
            scratch_shapes=[
                pltpu.VMEM((BLOCKS, REST, LANES), bf),
                pltpu.VMEM((PAD, D), jnp.float32),
                pltpu.VMEM((PAD, D), jnp.float32),
                pltpu.VMEM((rows, D), bf),
                pltpu.VMEM((rows, FF), bf),
                pltpu.VMEM((PAD, FF), jnp.float32),
                pltpu.VMEM((rows, D), bf),
                pltpu.VMEM((rows, FF), bf),
            ],
        ),
        compiler_params=pltpu.CompilerParams(vmem_limit_bytes=32 * 1024 * 1024),
        cost_estimate=pl.CostEstimate(
            flops=10 * count * PAD * D * FF,
            bytes_accessed=4 * (2 * D * FF + count * S * D),
            transcendentals=count * PAD * FF,
        ),
        name="score",
    )(picks, me, images, targets, first, second)


def gram_kernel(main, side, out, total):
    members = main.shape[0]
    wide = members * TILE
    total[...] = jnp.zeros_like(total)
    for r in range(0, SIDE, TILE):
        part = tile(main, side, r)
        total[...] += dot(part, part, ((1,), (1,)))
    at = lax.broadcasted_iota(jnp.int32, (wide, wide), 0) % TILE
    to = lax.broadcasted_iota(jnp.int32, (wide, wide), 1) % TILE
    kept = jnp.where(at == to, total[...], 0.0)
    summed = jnp.sum(kept.reshape(members, TILE, wide), axis=1)
    turned = summed.T
    gram = jnp.sum(turned.reshape(members, TILE, members), axis=1)
    row = lax.broadcasted_iota(jnp.int32, gram.shape, 0)
    col = lax.broadcasted_iota(jnp.int32, gram.shape, 1)
    own = jnp.where(row == col, gram, 0.0)
    dist = jnp.sum(own, axis=1, keepdims=True) + jnp.sum(own, axis=0, keepdims=True) - 2.0 * gram
    out[...] = jnp.concatenate([dist[q : q + 8] for q in range(0, members, 8)], axis=1)


def distances(main, side):
    members = main.shape[0]
    wide = members * TILE
    return pl.pallas_call(
        gram_kernel,
        out_shape=jax.ShapeDtypeStruct((8, members * members // 8), jnp.float32),
        scratch_shapes=[pltpu.VMEM((wide, wide), jnp.float32)],
        compiler_params=pltpu.CompilerParams(vmem_limit_bytes=16 * 1024 * 1024),
        cost_estimate=pl.CostEstimate(
            flops=2 * wide * wide * SIDE // TILE * D,
            bytes_accessed=2 * members * ROWS * LANES,
            transcendentals=0,
        ),
        name="gram",
    )(main, side)


def add_over(value, members, bits):
    got = [
        lax.ppermute(value, AXES, [(i, i ^ bit) for i in range(members)]) for bit in bits
    ]
    return sum(got, value)


def kernel_of(scale, packed):
    members = packed.shape[1] // 4
    dist = jnp.concatenate(
        [packed[:, members * q : members * (q + 1)] for q in range(members // 8)], axis=0
    )
    return jnp.exp(-dist / scale[0]).astype(jnp.bfloat16)


def spreading(kernel):
    members = kernel.shape[0]
    wide = members * TILE
    at = lax.broadcasted_iota(jnp.int32, (wide, members), 0) // TILE
    which = lax.broadcasted_iota(jnp.int32, (wide, members), 1)
    pick = jnp.where(at == which, 1.0, 0.0).astype(jnp.bfloat16)
    tall = dot(pick, kernel, ((1,), (0,))).astype(jnp.bfloat16)
    full = dot(tall, pick, ((1,), (1,)))
    row = lax.broadcasted_iota(jnp.int32, (wide, wide), 0) % TILE
    col = lax.broadcasted_iota(jnp.int32, (wide, wide), 1) % TILE
    return jnp.where(row == col, full, 0.0)


def mix(mixer, ksum, scores, own):
    members = mixer.shape[0] // TILE
    wide = own.shape[1]
    both = dot(mixer, jnp.concatenate([scores, own], axis=1), ((1,), (0,)))
    pushed = ksum * own.astype(jnp.float32) - both[:, wide:]
    both = jnp.concatenate([both[:, :wide], pushed], axis=1) * (1.0 / members)
    return both.astype(jnp.bfloat16)


def mix_side_kernel(scale, me, packed, scores, params, mixing, *refs):
    outs, side = refs[:PLANES], refs[PLANES]
    members = params.shape[0]
    full = spreading(kernel_of(scale, packed[...]))
    ksum = jnp.sum(full, axis=1, keepdims=True)
    mixer = full.astype(jnp.bfloat16)
    mixing[...] = mixer
    at = range(0, REST, TILE)
    got = jnp.concatenate([rows_of(scores, None, r) for r in at], axis=1)
    own = jnp.concatenate([rows_of(params, None, r) for r in at], axis=1)
    both = mix(mixer, ksum, got, own)
    for q in range(2 * len(at)):
        part = both[:, q * LANES : (q + 1) * LANES].reshape(members, TILE, LANES)
        side[:, q * TILE : (q + 1) * TILE, :] = part
    by_plane(me, side, outs)


def mix_side(scale, me, packed, scores, params):
    members = params.shape[0]
    wide = members * TILE
    vmem = pl.BlockSpec(memory_space=pltpu.VMEM)
    smem = pl.BlockSpec(memory_space=pltpu.SMEM)
    mixing = jax.ShapeDtypeStruct((wide, wide), jnp.bfloat16)
    return pl.pallas_call(
        mix_side_kernel,
        out_shape=(mixing, *side_shapes(2 * REST)),
        in_specs=[smem, smem] + [vmem] * 3,
        scratch_shapes=[pltpu.VMEM((members, 2 * REST, LANES), jnp.bfloat16)],
        compiler_params=pltpu.CompilerParams(vmem_limit_bytes=24 * 1024 * 1024),
        cost_estimate=pl.CostEstimate(
            flops=4 * wide * wide * REST // TILE * LANES,
            bytes_accessed=8 * members * REST * LANES,
            transcendentals=0,
        ),
        name="mix_side",
    )(scale, me, packed, scores, params)


def mix_main_kernel(mixing, scores, params, side_params, out, mixed, stores):
    members = params.shape[0]
    mixer = mixing[...]
    ksum = jnp.sum(mixer.astype(jnp.float32), axis=1, keepdims=True)
    copies = []
    for r in range(0, SIDE, TILE):
        at = [g * SIDE + r for g in GROUPS if g * SIDE + r < MAIN]
        groups = len(at)
        got = jnp.concatenate([rows_of(scores, None, x) for x in at], axis=1)
        own = jnp.concatenate([rows_of(params, side_params, x) for x in at], axis=1)
        both = mix(mixer, ksum, got, own)
        for q in range(2 * groups):
            part = both[:, q * LANES : (q + 1) * LANES].reshape(members, TILE, LANES)
            x = q // groups * MAIN + at[q % groups]
            mixed[:, x : x + TILE, :] = part
            here = pl.ds(x, TILE)
            copies.append(
                pltpu.make_async_copy(
                    mixed.at[:, here, :], out.at[:, here, :], stores.at[x // TILE]
                )
            )
            copies[-1].start()
    for copy in copies:
        copy.wait()


def mix_main(mixing, scores, params, side_params):
    members = params.shape[0]
    wide = members * TILE
    vmem = pl.BlockSpec(memory_space=pltpu.VMEM)
    return pl.pallas_call(
        mix_main_kernel,
        out_shape=pltpu.HBM((members, 2 * MAIN, LANES), jnp.bfloat16),
        in_specs=[vmem] * 4,
        out_specs=pl.BlockSpec(memory_space=pl.ANY),
        scratch_shapes=[
            pltpu.VMEM((members, 2 * MAIN, LANES), jnp.bfloat16),
            pltpu.SemaphoreType.DMA((2 * MAIN // TILE,)),
        ],
        compiler_params=pltpu.CompilerParams(vmem_limit_bytes=24 * 1024 * 1024),
        cost_estimate=pl.CostEstimate(
            flops=4 * wide * wide * MAIN // TILE * LANES,
            bytes_accessed=8 * members * MAIN * LANES,
            transcendentals=0,
        ),
        name="mix_main",
    )(mixing, scores, params, side_params)


def plane_kernel(*refs):
    for z in range(PLANES):
        for q in range(PLANE):
            refs[PLANES + q // 2][z, q % 2] = refs[z][q]


def core_kernel(*refs):
    for q in range(PLANE // 2):
        for z in range(PLANES):
            for c in range(2):
                refs[PLANE // 2 + c][q, z] = refs[q][z, c]


def settle_kernel(me, near, far, out):
    for c, ref in enumerate((near, far)):
        for q in range(PLANE // 2):
            for z in range(PLANES):
                out[(z * PLANE + 2 * q + c) ^ me[0]] = ref[q, z]


def regroup(body, name, shapes, *arrays, me=(), flops=0):
    vmem = pl.BlockSpec(memory_space=pltpu.VMEM)
    size = sum(math.prod(x.shape) for x in arrays)
    return pl.pallas_call(
        body,
        out_shape=shapes,
        in_specs=[pl.BlockSpec(memory_space=pltpu.SMEM)] * len(me) + [vmem] * len(arrays),
        compiler_params=pltpu.CompilerParams(vmem_limit_bytes=16 * 1024 * 1024),
        cost_estimate=pl.CostEstimate(flops=flops, bytes_accessed=4 * size, transcendentals=0),
        name=name,
    )(*me, *arrays)


def swap(value, bits):
    pairs = [(i, i ^ bits) for i in range(BLOCKS)]
    return lax.ppermute(value, AXES, pairs)


def across_planes(parts):
    return parts[:1] + [swap(x, z * PLANE) for z, x in enumerate(parts) if z]


def in_plane(parts):
    rows = parts[0].shape[1]
    shape = jax.ShapeDtypeStruct((PLANES, 2, rows, LANES), jnp.bfloat16)
    return regroup(plane_kernel, "plane", (shape,) * (PLANE // 2), *parts, flops=LONG)


def across_chips(parts):
    return parts[:1] + tuple(swap(x, 2 * q) for q, x in enumerate(parts) if q)


def in_order(parts, me):
    rows = parts[0].shape[2]
    shape = jax.ShapeDtypeStruct((PLANE // 2, PLANES, rows, LANES), jnp.bfloat16)
    near, far = regroup(core_kernel, "core", (shape,) * 2, *parts)
    shape = jax.ShapeDtypeStruct((BLOCKS, rows, LANES), jnp.bfloat16)
    return regroup(settle_kernel, "settle", shape, near, swap(far, 1), me=(me,))


def after(values, *others):
    return lax.optimization_barrier((values, *others))[0]


def plain_products(params):
    flat = params.reshape(params.shape[0], -1)
    return dot(flat, flat, ((1,), (1,)))


def plain_weighted(gram, scale, params, scores):
    members = params.shape[0]
    norms = jnp.diagonal(gram)
    dist = norms[:, None] + norms[None, :] - 2.0 * gram
    kernel = jnp.exp(-dist / scale[0]).astype(jnp.bfloat16)
    flat = params.reshape(members, -1)
    ksum = jnp.sum(kernel.astype(jnp.float32), axis=1, keepdims=True)
    attract = dot(kernel, scores.reshape(members, -1), ((1,), (0,))) / members
    mixed = dot(kernel, flat, ((1,), (0,)))
    spread = (flat.astype(jnp.float32) * ksum - mixed) / members
    return tuple(x.astype(jnp.bfloat16).reshape(params.shape) for x in (attract, spread))


STEPS = D // EDGE
TALL = FF // STEPS


def pack_side_kernel(me, first, second, *refs):
    outs, (wide, tall, loads) = refs[:PLANES], refs[PLANES:]
    copies = [pltpu.make_async_copy(second.at[0, :, pl.ds(D - LANES, LANES)], tall, loads.at[COLS])]
    for c in range(COLS):
        here = first.at[0, :, pl.ds((c + 1) * D - LANES, LANES)]
        copies.append(pltpu.make_async_copy(here, wide.at[c], loads.at[c]))
    for copy in copies:
        copy.start()
    for copy in copies:
        copy.wait()
    more = REST - EDGE
    for k in range(BLOCKS):
        b = k ^ me[0]
        here = pl.ds(pl.multiple_of(b // COLS * EDGE + EDGE - more, TILE), more)
        outs[k // PLANE][k % PLANE, 0:more, :] = wide[b % COLS, here, :]
        here = pl.ds(pl.multiple_of(b * EDGE, EDGE), EDGE)
        outs[k // PLANE][k % PLANE, more:REST, :] = tall[here, :]


def pack_main_kernel(first, second, out, wide, tall, packed, loads, stores):
    def load(d):
        return (
            pltpu.make_async_copy(
                first.at[0, pl.ds(d * EDGE, EDGE), :], wide.at[d], loads.at[0, d]
            ),
            pltpu.make_async_copy(
                second.at[0, pl.ds(d * TALL, TALL), :], tall.at[d], loads.at[1, d]
            ),
        )

    def store(d):
        here = pl.ds(d * COLS, COLS)
        return pltpu.make_async_copy(packed.at[here], out.at[here], stores.at[d])

    for d in range(STEPS):
        for copy in load(d):
            copy.start()
    for d in range(STEPS):
        for copy in load(d):
            copy.wait()
        for c in range(COLS):
            for g in GROUPS:
                b, at, lanes = d * COLS + c, g * SIDE, g * LANES
                end = in_main(at)
                packed[b, at : at + end, :] = wide[
                    d, 0:end, c * D + lanes : c * D + lanes + LANES
                ]
                if at + EDGE < MAIN:
                    packed[b, at + EDGE : at + SIDE, :] = tall[
                        d, c * EDGE : (c + 1) * EDGE, lanes : lanes + LANES
                    ]
        store(d).start()
    for d in range(STEPS):
        store(d).wait()


def to_blocks(first, second, me):
    bf = jnp.bfloat16
    anywhere = [pl.BlockSpec(memory_space=pl.ANY)]
    params = pltpu.CompilerParams(vmem_limit_bytes=56 * 1024 * 1024)
    cost = pl.CostEstimate(flops=0, bytes_accessed=4 * D * FF, transcendentals=0)
    side = pl.pallas_call(
        pack_side_kernel,
        out_shape=side_shapes(REST),
        in_specs=[pl.BlockSpec(memory_space=pltpu.SMEM)] + anywhere * 2,
        scratch_shapes=[
            pltpu.VMEM((COLS, D, LANES), bf),
            pltpu.VMEM((FF, LANES), bf),
            pltpu.SemaphoreType.DMA((COLS + 1,)),
        ],
        compiler_params=params,
        cost_estimate=cost,
        name="pack_side",
    )(me, first, second)
    main = pl.pallas_call(
        pack_main_kernel,
        out_shape=pltpu.HBM((BLOCKS, MAIN, LANES), bf),
        in_specs=anywhere * 2,
        out_specs=anywhere[0],
        scratch_shapes=[
            pltpu.VMEM((STEPS, EDGE, FF), bf),
            pltpu.VMEM((STEPS, TALL, D), bf),
            pltpu.VMEM((BLOCKS, MAIN, LANES), bf),
            pltpu.SemaphoreType.DMA((2, STEPS)),
            pltpu.SemaphoreType.DMA((STEPS,)),
        ],
        compiler_params=params,
        cost_estimate=cost,
        name="pack_main",
    )(first, second)
    return main, side


def pieces(main, side, which, at):
    n = in_main(at)
    found = [(0, n, main, which * MAIN + at), (n, EDGE - n, side, which * REST + at + n - MAIN)]
    return [piece for piece in found if piece[1]]


def unpack_kernel(main, side, first_a, second_a, first_s, second_s, wide, tall, stores):
    def store(which, d):
        first, second = ((first_a, second_a), (first_s, second_s))[which]
        return (
            pltpu.make_async_copy(
                wide.at[which, d], first.at[0, pl.ds(d * EDGE, EDGE), :], stores.at[which, 0, d]
            ),
            pltpu.make_async_copy(
                tall.at[which, d], second.at[0, pl.ds(d * TALL, TALL), :], stores.at[which, 1, d]
            ),
        )

    for which in range(2):
        for d in range(STEPS):
            for c in range(COLS):
                for g in GROUPS:
                    b = d * COLS + c
                    lanes = slice(c * D + g * LANES, c * D + (g + 1) * LANES)
                    for row, n, ref, at in pieces(main, side, which, g * SIDE):
                        wide[which, d, row : row + n, lanes] = ref[b, at : at + n, :]
                    lanes = slice(g * LANES, (g + 1) * LANES)
                    for row, n, ref, at in pieces(main, side, which, g * SIDE + EDGE):
                        here = slice(c * EDGE + row, c * EDGE + row + n)
                        tall[which, d, here, lanes] = ref[b, at : at + n, :]
            for copy in store(which, d):
                copy.start()
    for which in range(2):
        for d in range(STEPS):
            for copy in store(which, d):
                copy.wait()


def from_blocks(main, side):
    bf = jnp.bfloat16
    return pl.pallas_call(
        unpack_kernel,
        out_shape=(pltpu.HBM((1, D, FF), bf), pltpu.HBM((1, FF, D), bf)) * 2,
        in_specs=[pl.BlockSpec(memory_space=pltpu.VMEM)] * 2,
        out_specs=(pl.BlockSpec(memory_space=pl.ANY),) * 4,
        scratch_shapes=[
            pltpu.VMEM((2, STEPS, EDGE, FF), bf),
            pltpu.VMEM((2, STEPS, TALL, D), bf),
            pltpu.SemaphoreType.DMA((2, 2, STEPS)),
        ],
        compiler_params=pltpu.CompilerParams(vmem_limit_bytes=24 * 1024 * 1024),
        cost_estimate=pl.CostEstimate(flops=0, bytes_accessed=16 * D * FF, transcendentals=0),
        name="unpack",
    )(main, side)


def exchange(blocks):
    return lax.all_to_all(blocks, AXES, split_axis=0, concat_axis=0, tiled=True)


def on_device(
    particles_first, particles_second, pool_images, pool_targets, batch_index, kernel_scale
):
    members = math.prod(lax.axis_size(name) for name in AXES)
    tiled = members == BLOCKS
    me = lax.axis_index(AXES) if tiled else 0
    me = jnp.full((1,), me, jnp.int32)
    params, side_params = to_blocks(particles_first, particles_second, me)
    first, second = particles_first[0], particles_second[0]
    if tiled:
        params = exchange(params)
        side_params = in_plane(across_planes(list(side_params)))
        first, second = after((first, second), side_params[0])
        side_params = across_chips(side_params)
    scores, *side_scores = particle_scores(
        first, second, pool_images, pool_targets, batch_index[0], me
    )
    if tiled:
        side_params = in_order(after(side_params, side_scores[0]), me)
        scores = exchange(scores)
        side_scores = in_plane(across_planes(after(side_scores, params)))
        packed = distances(*after((params, side_params), side_scores[0]))
        side_scores = in_order(across_chips(side_scores), me)
        for bits in ((1,), (2, 4, 6), (8, 16, 24)):
            packed = add_over(packed, members, bits)
        mixing, *side = mix_side(kernel_scale, me, packed, side_scores, side_params)
        main = mix_main(mixing, scores, params, side_params)
        side = in_order(across_chips(in_plane(across_planes(side))), me)
        return from_blocks(exchange(main), side)
    cut = (members, BLOCKS * ROWS // members, LANES)
    params = jnp.concatenate([params, jnp.concatenate(side_params)], axis=1)
    scores = jnp.concatenate([scores, jnp.concatenate(side_scores)], axis=1)
    params, scores = exchange(params.reshape(cut)), exchange(scores.reshape(cut))
    gram = lax.psum(plain_products(params), AXES)
    parts = plain_weighted(gram, kernel_scale, params, scores)
    parts = [exchange(x).reshape(BLOCKS, ROWS, LANES) for x in parts]
    main = jnp.concatenate([x[:, :MAIN] for x in parts], axis=1)
    return from_blocks(main, jnp.concatenate([x[:, MAIN:] for x in parts], axis=1))


def solution(mesh):
    split = P(AXES, None, None)
    return jax.shard_map(
        on_device,
        mesh=mesh,
        in_specs=(split, split, P(), P(), P(AXES, None), P()),
        out_specs=(split, split, split, split),
        check_vma=False,
    )
```

```python
import functools
import math

import jax
import jax.numpy as jnp
from jax import lax
from jax.experimental import pallas as pl
from jax.experimental.pallas import tpu as pltpu
from jax.sharding import PartitionSpec as P

D = 384
FF = 1536
S = 197
DATA = 10000
AXES = ("wide", "narrow")
PAD = 208
EDGE = 48
BLOCKS = D * FF // (EDGE * D)
COLS = FF // D
TILE = 16
LANES = 128
SIDE = 2 * EDGE
GROUPS = range(D // LANES)
ROWS = SIDE * len(GROUPS)
REST = EDGE + TILE
MAIN = ROWS - REST
PLANES = 4
PLANE = BLOCKS // PLANES
LONG = 10**11

gelu_c = math.sqrt(2.0 / math.pi)
isd = 1.0 / math.sqrt(D)
isf = 1.0 / math.sqrt(FF)


def dot(a, b, dims):
    return lax.dot_general(a, b, (dims, ((), ())), preferred_element_type=jnp.float32)


def in_main(at):
    return max(0, min(EDGE, MAIN - at))


def put(main, side, block, row, value):
    for g in GROUPS:
        at = g * SIDE + row
        part = value[:, g * LANES : (g + 1) * LANES]
        n = in_main(at)
        if n:
            main[block, at : at + n, :] = part[:n]
        if n < EDGE:
            side[block, at + n - MAIN : at + EDGE - MAIN, :] = part[n:]


def by_plane(me, side, outs):
    for k in range(BLOCKS):
        outs[k // PLANE][k % PLANE] = side[k ^ me[0]]


def rows_of(main, side, at):
    ref, at = (main, at) if at < main.shape[1] else (side, at - main.shape[1])
    return ref[:, at : at + TILE, :].reshape(ref.shape[0] * TILE, LANES)


def tile(main, side, r):
    return jnp.concatenate([rows_of(main, side, g * SIDE + r) for g in GROUPS], axis=1)


def score_kernel(
    factor, picks, me, image, target, first, second, *refs
):
    outs, side = refs[1 : 1 + PLANES], refs[1 + PLANES]
    out, (xs, ts, normed, hidden, deriv, delta, back) = refs[0], refs[2 + PLANES :]
    step = pl.program_id(0)
    images = pl.num_programs(0)
    rows = pl.ds(pl.multiple_of(step * PAD, PAD), PAD)

    @pl.when(step == 0)
    def _():
        xs[...] = jnp.zeros_like(xs)
        ts[...] = jnp.zeros_like(ts)

    xs[0:S, :] = image[0].astype(jnp.float32)
    ts[0:S, :] = target[0].astype(jnp.float32)
    xf = xs[...]
    mean = jnp.mean(xf, axis=1, keepdims=True)
    centered = xf - mean
    var = jnp.mean(centered * centered, axis=1, keepdims=True)
    nrm = (centered * lax.rsqrt(var + 1e-06)).astype(jnp.bfloat16)
    normed[rows, :] = nrm
    for c in range(COLS):
        cols = pl.ds(c * D, D)
        pre = dot(nrm, first[:, cols], ((1,), (0,))) * isd
        sq = pre * pre
        tval = jnp.tanh(pre * (gelu_c + (gelu_c * 0.044715) * sq))
        gate = 0.5 + 0.5 * tval
        hid = pre * gate
        hidden[rows, cols] = hid.astype(jnp.bfloat16)
        deriv[:, cols] = gate + hid * (1.0 - gate) * (
            2.0 * gelu_c + (6.0 * gelu_c * 0.044715) * sq
        )
    prod = dot(hidden[rows, :], second[...], ((1,), (0,))) * isf
    dlt = ((xs[...] + prod - ts[...]) * (1.0 / S)).astype(jnp.bfloat16)
    delta[rows, :] = dlt
    for c in range(COLS):
        cols = pl.ds(c * D, D)
        dhid = dot(dlt, second[cols, :], ((1,), (1,))) * isf
        back[rows, cols] = (dhid * deriv[:, cols]).astype(jnp.bfloat16)

    @pl.when(step == images - 1)
    def _():
        for c in range(COLS):
            cols = pl.ds(c * D, D)
            grad = dot(normed[...], back[:, cols], ((0,), (0,))) * (-factor * isd)
            score = (grad - first[:, cols].astype(jnp.float32)).astype(jnp.bfloat16)
            for r in range(D // EDGE):
                put(out, side, r * COLS + c, 0, score[r * EDGE : (r + 1) * EDGE, :])
            grad = dot(hidden[:, cols], delta[...], ((0,), (0,))) * (-factor * isf)
            score = (grad - second[cols, :].astype(jnp.float32)).astype(jnp.bfloat16)
            for r in range(D // EDGE):
                at = c * (D // EDGE) + r
                put(out, side, at, EDGE, score[r * EDGE : (r + 1) * EDGE, :])
        by_plane(me, side, outs)


def side_shapes(rows):
    return (jax.ShapeDtypeStruct((PLANE, rows, LANES), jnp.bfloat16),) * PLANES


def particle_scores(first, second, images, targets, picks, me):
    count = picks.shape[0]
    rows = count * PAD
    bf = jnp.bfloat16
    return pl.pallas_call(
        functools.partial(score_kernel, DATA / count),
        out_shape=(pltpu.HBM((BLOCKS, MAIN, LANES), bf), *side_shapes(REST)),
        grid_spec=pltpu.PrefetchScalarGridSpec(
            num_scalar_prefetch=2,
            grid=(count,),
            in_specs=[
                pl.BlockSpec((1, S, D), lambda b, picks, me: (picks[b], 0, 0)),
                pl.BlockSpec((1, S, D), lambda b, picks, me: (picks[b], 0, 0)),
                pl.BlockSpec((D, FF), lambda b, picks, me: (0, 0)),
                pl.BlockSpec((FF, D), lambda b, picks, me: (0, 0)),
            ],
            out_specs=(
                pl.BlockSpec((BLOCKS, MAIN, LANES), lambda b, picks, me: (0, 0, 0)),
                *[pl.BlockSpec((PLANE, REST, LANES), lambda b, picks, me: (0, 0, 0))] * PLANES,
            ),
            scratch_shapes=[
                pltpu.VMEM((BLOCKS, REST, LANES), bf),
                pltpu.VMEM((PAD, D), jnp.float32),
                pltpu.VMEM((PAD, D), jnp.float32),
                pltpu.VMEM((rows, D), bf),
                pltpu.VMEM((rows, FF), bf),
                pltpu.VMEM((PAD, FF), jnp.float32),
                pltpu.VMEM((rows, D), bf),
                pltpu.VMEM((rows, FF), bf),
            ],
        ),
        compiler_params=pltpu.CompilerParams(vmem_limit_bytes=32 * 1024 * 1024),
        cost_estimate=pl.CostEstimate(
            flops=10 * count * PAD * D * FF,
            bytes_accessed=4 * (2 * D * FF + count * S * D),
            transcendentals=count * PAD * FF,
        ),
        name="score",
    )(picks, me, images, targets, first, second)


def gram_kernel(main, side, out, total):
    members = main.shape[0]
    wide = members * TILE
    total[...] = jnp.zeros_like(total)
    for r in range(0, SIDE, TILE):
        part = tile(main, side, r)
        total[...] += dot(part, part, ((1,), (1,)))
    at = lax.broadcasted_iota(jnp.int32, (wide, wide), 0) % TILE
    to = lax.broadcasted_iota(jnp.int32, (wide, wide), 1) % TILE
    kept = jnp.where(at == to, total[...], 0.0)
    summed = jnp.sum(kept.reshape(members, TILE, wide), axis=1)
    turned = summed.T
    gram = jnp.sum(turned.reshape(members, TILE, members), axis=1)
    row = lax.broadcasted_iota(jnp.int32, gram.shape, 0)
    col = lax.broadcasted_iota(jnp.int32, gram.shape, 1)
    own = jnp.where(row == col, gram, 0.0)
    dist = jnp.sum(own, axis=1, keepdims=True) + jnp.sum(own, axis=0, keepdims=True) - 2.0 * gram
    out[...] = jnp.concatenate([dist[q : q + 8] for q in range(0, members, 8)], axis=1)


def distances(main, side):
    members = main.shape[0]
    wide = members * TILE
    return pl.pallas_call(
        gram_kernel,
        out_shape=jax.ShapeDtypeStruct((8, members * members // 8), jnp.float32),
        scratch_shapes=[pltpu.VMEM((wide, wide), jnp.float32)],
        compiler_params=pltpu.CompilerParams(vmem_limit_bytes=16 * 1024 * 1024),
        cost_estimate=pl.CostEstimate(
            flops=2 * wide * wide * SIDE // TILE * D,
            bytes_accessed=2 * members * ROWS * LANES,
            transcendentals=0,
        ),
        name="gram",
    )(main, side)


def add_over(value, members, bits):
    got = [
        lax.ppermute(value, AXES, [(i, i ^ bit) for i in range(members)]) for bit in bits
    ]
    return sum(got, value)


def kernel_of(scale, packed):
    members = packed.shape[1] // 4
    dist = jnp.concatenate(
        [packed[:, members * q : members * (q + 1)] for q in range(members // 8)], axis=0
    )
    return jnp.exp(-dist / scale[0]).astype(jnp.bfloat16)


def spreading(kernel):
    members = kernel.shape[0]
    wide = members * TILE
    at = lax.broadcasted_iota(jnp.int32, (wide, members), 0) // TILE
    which = lax.broadcasted_iota(jnp.int32, (wide, members), 1)
    pick = jnp.where(at == which, 1.0, 0.0).astype(jnp.bfloat16)
    tall = dot(pick, kernel, ((1,), (0,))).astype(jnp.bfloat16)
    full = dot(tall, pick, ((1,), (1,)))
    row = lax.broadcasted_iota(jnp.int32, (wide, wide), 0) % TILE
    col = lax.broadcasted_iota(jnp.int32, (wide, wide), 1) % TILE
    return jnp.where(row == col, full, 0.0)


def mix(mixer, ksum, scores, own):
    members = mixer.shape[0] // TILE
    wide = own.shape[1]
    both = dot(mixer, jnp.concatenate([scores, own], axis=1), ((1,), (0,)))
    pushed = ksum * own.astype(jnp.float32) - both[:, wide:]
    both = jnp.concatenate([both[:, :wide], pushed], axis=1) * (1.0 / members)
    return both.astype(jnp.bfloat16)


def mix_side_kernel(scale, me, packed, scores, params, mixing, *refs):
    outs, side = refs[:PLANES], refs[PLANES]
    members = params.shape[0]
    full = spreading(kernel_of(scale, packed[...]))
    ksum = jnp.sum(full, axis=1, keepdims=True)
    mixer = full.astype(jnp.bfloat16)
    mixing[...] = mixer
    at = range(0, REST, TILE)
    got = jnp.concatenate([rows_of(scores, None, r) for r in at], axis=1)
    own = jnp.concatenate([rows_of(params, None, r) for r in at], axis=1)
    both = mix(mixer, ksum, got, own)
    for q in range(2 * len(at)):
        part = both[:, q * LANES : (q + 1) * LANES].reshape(members, TILE, LANES)
        side[:, q * TILE : (q + 1) * TILE, :] = part
    by_plane(me, side, outs)


def mix_side(scale, me, packed, scores, params):
    members = params.shape[0]
    wide = members * TILE
    vmem = pl.BlockSpec(memory_space=pltpu.VMEM)
    smem = pl.BlockSpec(memory_space=pltpu.SMEM)
    mixing = jax.ShapeDtypeStruct((wide, wide), jnp.bfloat16)
    return pl.pallas_call(
        mix_side_kernel,
        out_shape=(mixing, *side_shapes(2 * REST)),
        in_specs=[smem, smem] + [vmem] * 3,
        scratch_shapes=[pltpu.VMEM((members, 2 * REST, LANES), jnp.bfloat16)],
        compiler_params=pltpu.CompilerParams(vmem_limit_bytes=24 * 1024 * 1024),
        cost_estimate=pl.CostEstimate(
            flops=4 * wide * wide * REST // TILE * LANES,
            bytes_accessed=8 * members * REST * LANES,
            transcendentals=0,
        ),
        name="mix_side",
    )(scale, me, packed, scores, params)


def mix_main_kernel(mixing, scores, params, side_params, out, mixed, stores):
    members = params.shape[0]
    mixer = mixing[...]
    ksum = jnp.sum(mixer.astype(jnp.float32), axis=1, keepdims=True)
    copies = []
    for r in range(0, SIDE, TILE):
        at = [g * SIDE + r for g in GROUPS if g * SIDE + r < MAIN]
        groups = len(at)
        got = jnp.concatenate([rows_of(scores, None, x) for x in at], axis=1)
        own = jnp.concatenate([rows_of(params, side_params, x) for x in at], axis=1)
        both = mix(mixer, ksum, got, own)
        for q in range(2 * groups):
            part = both[:, q * LANES : (q + 1) * LANES].reshape(members, TILE, LANES)
            x = q // groups * MAIN + at[q % groups]
            mixed[:, x : x + TILE, :] = part
            here = pl.ds(x, TILE)
            copies.append(
                pltpu.make_async_copy(
                    mixed.at[:, here, :], out.at[:, here, :], stores.at[x // TILE]
                )
            )
            copies[-1].start()
    for copy in copies:
        copy.wait()


def mix_main(mixing, scores, params, side_params):
    members = params.shape[0]
    wide = members * TILE
    vmem = pl.BlockSpec(memory_space=pltpu.VMEM)
    return pl.pallas_call(
        mix_main_kernel,
        out_shape=pltpu.HBM((members, 2 * MAIN, LANES), jnp.bfloat16),
        in_specs=[vmem] * 4,
        out_specs=pl.BlockSpec(memory_space=pl.ANY),
        scratch_shapes=[
            pltpu.VMEM((members, 2 * MAIN, LANES), jnp.bfloat16),
            pltpu.SemaphoreType.DMA((2 * MAIN // TILE,)),
        ],
        compiler_params=pltpu.CompilerParams(vmem_limit_bytes=24 * 1024 * 1024),
        cost_estimate=pl.CostEstimate(
            flops=4 * wide * wide * MAIN // TILE * LANES,
            bytes_accessed=8 * members * MAIN * LANES,
            transcendentals=0,
        ),
        name="mix_main",
    )(mixing, scores, params, side_params)


def plane_kernel(*refs):
    for z in range(PLANES):
        for q in range(PLANE):
            refs[PLANES + q // 2][z, q % 2] = refs[z][q]


def core_kernel(*refs):
    for q in range(PLANE // 2):
        for z in range(PLANES):
            for c in range(2):
                refs[PLANE // 2 + c][q, z] = refs[q][z, c]


def settle_kernel(me, near, far, out):
    for c, ref in enumerate((near, far)):
        for q in range(PLANE // 2):
            for z in range(PLANES):
                out[(z * PLANE + 2 * q + c) ^ me[0]] = ref[q, z]


def regroup(body, name, shapes, *arrays, me=(), flops=0):
    vmem = pl.BlockSpec(memory_space=pltpu.VMEM)
    size = sum(math.prod(x.shape) for x in arrays)
    return pl.pallas_call(
        body,
        out_shape=shapes,
        in_specs=[pl.BlockSpec(memory_space=pltpu.SMEM)] * len(me) + [vmem] * len(arrays),
        compiler_params=pltpu.CompilerParams(vmem_limit_bytes=16 * 1024 * 1024),
        cost_estimate=pl.CostEstimate(flops=flops, bytes_accessed=4 * size, transcendentals=0),
        name=name,
    )(*me, *arrays)


def swap(value, bits):
    pairs = [(i, i ^ bits) for i in range(BLOCKS)]
    return lax.ppermute(value, AXES, pairs)


def across_planes(parts):
    return parts[:1] + [swap(x, z * PLANE) for z, x in enumerate(parts) if z]


def in_plane(parts):
    rows = parts[0].shape[1]
    shape = jax.ShapeDtypeStruct((PLANES, 2, rows, LANES), jnp.bfloat16)
    return regroup(plane_kernel, "plane", (shape,) * (PLANE // 2), *parts, flops=LONG)


def across_chips(parts):
    return parts[:1] + tuple(swap(x, 2 * q) for q, x in enumerate(parts) if q)


def in_order(parts, me):
    rows = parts[0].shape[2]
    shape = jax.ShapeDtypeStruct((PLANE // 2, PLANES, rows, LANES), jnp.bfloat16)
    near, far = regroup(core_kernel, "core", (shape,) * 2, *parts)
    shape = jax.ShapeDtypeStruct((BLOCKS, rows, LANES), jnp.bfloat16)
    return regroup(settle_kernel, "settle", shape, near, swap(far, 1), me=(me,))


def after(values, *others):
    return lax.optimization_barrier((values, *others))[0]


def plain_products(params):
    flat = params.reshape(params.shape[0], -1)
    return dot(flat, flat, ((1,), (1,)))


def plain_weighted(gram, scale, params, scores):
    members = params.shape[0]
    norms = jnp.diagonal(gram)
    dist = norms[:, None] + norms[None, :] - 2.0 * gram
    kernel = jnp.exp(-dist / scale[0]).astype(jnp.bfloat16)
    flat = params.reshape(members, -1)
    ksum = jnp.sum(kernel.astype(jnp.float32), axis=1, keepdims=True)
    attract = dot(kernel, scores.reshape(members, -1), ((1,), (0,))) / members
    mixed = dot(kernel, flat, ((1,), (0,)))
    spread = (flat.astype(jnp.float32) * ksum - mixed) / members
    return tuple(x.astype(jnp.bfloat16).reshape(params.shape) for x in (attract, spread))


STEPS = D // EDGE
TALL = FF // STEPS


def pack_side_kernel(me, first, second, *refs):
    outs, (wide, tall, loads) = refs[:PLANES], refs[PLANES:]
    copies = [pltpu.make_async_copy(second.at[0, :, pl.ds(D - LANES, LANES)], tall, loads.at[COLS])]
    for c in range(COLS):
        here = first.at[0, :, pl.ds((c + 1) * D - LANES, LANES)]
        copies.append(pltpu.make_async_copy(here, wide.at[c], loads.at[c]))
    for copy in copies:
        copy.start()
    for copy in copies:
        copy.wait()
    more = REST - EDGE
    for k in range(BLOCKS):
        b = k ^ me[0]
        here = pl.ds(pl.multiple_of(b // COLS * EDGE + EDGE - more, TILE), more)
        outs[k // PLANE][k % PLANE, 0:more, :] = wide[b % COLS, here, :]
        here = pl.ds(pl.multiple_of(b * EDGE, EDGE), EDGE)
        outs[k // PLANE][k % PLANE, more:REST, :] = tall[here, :]


def pack_main_kernel(first, second, out, wide, tall, packed, loads, stores):
    def load(d):
        return (
            pltpu.make_async_copy(
                first.at[0, pl.ds(d * EDGE, EDGE), :], wide.at[d], loads.at[0, d]
            ),
            pltpu.make_async_copy(
                second.at[0, pl.ds(d * TALL, TALL), :], tall.at[d], loads.at[1, d]
            ),
        )

    def store(d):
        here = pl.ds(d * COLS, COLS)
        return pltpu.make_async_copy(packed.at[here], out.at[here], stores.at[d])

    for d in range(STEPS):
        for copy in load(d):
            copy.start()
    for d in range(STEPS):
        for copy in load(d):
            copy.wait()
        for c in range(COLS):
            for g in GROUPS:
                b, at, lanes = d * COLS + c, g * SIDE, g * LANES
                end = in_main(at)
                packed[b, at : at + end, :] = wide[
                    d, 0:end, c * D + lanes : c * D + lanes + LANES
                ]
                if at + EDGE < MAIN:
                    packed[b, at + EDGE : at + SIDE, :] = tall[
                        d, c * EDGE : (c + 1) * EDGE, lanes : lanes + LANES
                    ]
        store(d).start()
    for d in range(STEPS):
        store(d).wait()


def to_blocks(first, second, me):
    bf = jnp.bfloat16
    anywhere = [pl.BlockSpec(memory_space=pl.ANY)]
    params = pltpu.CompilerParams(vmem_limit_bytes=56 * 1024 * 1024)
    cost = pl.CostEstimate(flops=0, bytes_accessed=4 * D * FF, transcendentals=0)
    side = pl.pallas_call(
        pack_side_kernel,
        out_shape=side_shapes(REST),
        in_specs=[pl.BlockSpec(memory_space=pltpu.SMEM)] + anywhere * 2,
        scratch_shapes=[
            pltpu.VMEM((COLS, D, LANES), bf),
            pltpu.VMEM((FF, LANES), bf),
            pltpu.SemaphoreType.DMA((COLS + 1,)),
        ],
        compiler_params=params,
        cost_estimate=cost,
        name="pack_side",
    )(me, first, second)
    main = pl.pallas_call(
        pack_main_kernel,
        out_shape=pltpu.HBM((BLOCKS, MAIN, LANES), bf),
        in_specs=anywhere * 2,
        out_specs=anywhere[0],
        scratch_shapes=[
            pltpu.VMEM((STEPS, EDGE, FF), bf),
            pltpu.VMEM((STEPS, TALL, D), bf),
            pltpu.VMEM((BLOCKS, MAIN, LANES), bf),
            pltpu.SemaphoreType.DMA((2, STEPS)),
            pltpu.SemaphoreType.DMA((STEPS,)),
        ],
        compiler_params=params,
        cost_estimate=cost,
        name="pack_main",
    )(first, second)
    return main, side


def pieces(main, side, which, at):
    n = in_main(at)
    found = [(0, n, main, which * MAIN + at), (n, EDGE - n, side, which * REST + at + n - MAIN)]
    return [piece for piece in found if piece[1]]


def unpack_kernel(main, side, first_a, second_a, first_s, second_s, wide, tall, stores):
    def store(which, d):
        first, second = ((first_a, second_a), (first_s, second_s))[which]
        return (
            pltpu.make_async_copy(
                wide.at[which, d], first.at[0, pl.ds(d * EDGE, EDGE), :], stores.at[which, 0, d]
            ),
            pltpu.make_async_copy(
                tall.at[which, d], second.at[0, pl.ds(d * TALL, TALL), :], stores.at[which, 1, d]
            ),
        )

    for which in range(2):
        for d in range(STEPS):
            for c in range(COLS):
                for g in GROUPS:
                    b = d * COLS + c
                    lanes = slice(c * D + g * LANES, c * D + (g + 1) * LANES)
                    for row, n, ref, at in pieces(main, side, which, g * SIDE):
                        wide[which, d, row : row + n, lanes] = ref[b, at : at + n, :]
                    lanes = slice(g * LANES, (g + 1) * LANES)
                    for row, n, ref, at in pieces(main, side, which, g * SIDE + EDGE):
                        here = slice(c * EDGE + row, c * EDGE + row + n)
                        tall[which, d, here, lanes] = ref[b, at : at + n, :]
            for copy in store(which, d):
                copy.start()
    for which in range(2):
        for d in range(STEPS):
            for copy in store(which, d):
                copy.wait()


def from_blocks(main, side):
    bf = jnp.bfloat16
    return pl.pallas_call(
        unpack_kernel,
        out_shape=(pltpu.HBM((1, D, FF), bf), pltpu.HBM((1, FF, D), bf)) * 2,
        in_specs=[pl.BlockSpec(memory_space=pltpu.VMEM)] * 2,
        out_specs=(pl.BlockSpec(memory_space=pl.ANY),) * 4,
        scratch_shapes=[
            pltpu.VMEM((2, STEPS, EDGE, FF), bf),
            pltpu.VMEM((2, STEPS, TALL, D), bf),
            pltpu.SemaphoreType.DMA((2, 2, STEPS)),
        ],
        compiler_params=pltpu.CompilerParams(vmem_limit_bytes=24 * 1024 * 1024),
        cost_estimate=pl.CostEstimate(flops=0, bytes_accessed=16 * D * FF, transcendentals=0),
        name="unpack",
    )(main, side)


def exchange(blocks):
    return lax.all_to_all(blocks, AXES, split_axis=0, concat_axis=0, tiled=True)


def on_device(
    particles_first, particles_second, pool_images, pool_targets, batch_index, kernel_scale
):
    members = math.prod(lax.axis_size(name) for name in AXES)
    tiled = members == BLOCKS
    me = lax.axis_index(AXES) if tiled else 0
    me = jnp.full((1,), me, jnp.int32)
    params, side_params = to_blocks(particles_first, particles_second, me)
    first, second = particles_first[0], particles_second[0]
    if tiled:
        params = exchange(params)
        side_params = in_plane(across_planes(list(side_params)))
        first, second = after((first, second), side_params[0])
        side_params = across_chips(side_params)
    scores, *side_scores = particle_scores(
        first, second, pool_images, pool_targets, batch_index[0], me
    )
    if tiled:
        side_params = in_order(after(side_params, side_scores[0]), me)
        side_scores = across_planes(after(side_scores, params))
        packed = distances(params, side_params)
        got = [swap(packed, z * PLANE) for z in range(1, PLANES)]
        scores = exchange(after(scores, packed))
        side_scores = in_plane(side_scores)
        packed = sum(after(got, side_scores[0]), packed)
        side_scores = in_order(across_chips(side_scores), me)
        for bits in ((2, 4, 6), (1,)):
            packed = add_over(packed, members, bits)
        mixing, *side = mix_side(kernel_scale, me, packed, side_scores, side_params)
        main = mix_main(mixing, scores, params, side_params)
        side = in_order(across_chips(in_plane(across_planes(side))), me)
        return from_blocks(exchange(main), side)
    cut = (members, BLOCKS * ROWS // members, LANES)
    params = jnp.concatenate([params, jnp.concatenate(side_params)], axis=1)
    scores = jnp.concatenate([scores, jnp.concatenate(side_scores)], axis=1)
    params, scores = exchange(params.reshape(cut)), exchange(scores.reshape(cut))
    gram = lax.psum(plain_products(params), AXES)
    parts = plain_weighted(gram, kernel_scale, params, scores)
    parts = [exchange(x).reshape(BLOCKS, ROWS, LANES) for x in parts]
    main = jnp.concatenate([x[:, :MAIN] for x in parts], axis=1)
    return from_blocks(main, jnp.concatenate([x[:, MAIN:] for x in parts], axis=1))


def solution(mesh):
    split = P(AXES, None, None)
    return jax.shard_map(
        on_device,
        mesh=mesh,
        in_specs=(split, split, P(), P(), P(AXES, None), P()),
        out_specs=(split, split, split, split),
        check_vma=False,
    )
```

```python
import functools
import math

import jax
import jax.numpy as jnp
from jax import lax
from jax.experimental import pallas as pl
from jax.experimental.pallas import tpu as pltpu
from jax.sharding import PartitionSpec as P

D = 384
FF = 1536
S = 197
DATA = 10000
AXES = ("wide", "narrow")
PAD = 208
EDGE = 48
BLOCKS = D * FF // (EDGE * D)
COLS = FF // D
TILE = 16
LANES = 128
SIDE = 2 * EDGE
GROUPS = range(D // LANES)
ROWS = SIDE * len(GROUPS)
REST = EDGE + TILE
MAIN = ROWS - REST
PLANES = 4
PLANE = BLOCKS // PLANES
LONG = 10**11

gelu_c = math.sqrt(2.0 / math.pi)
isd = 1.0 / math.sqrt(D)
isf = 1.0 / math.sqrt(FF)


def dot(a, b, dims):
    return lax.dot_general(a, b, (dims, ((), ())), preferred_element_type=jnp.float32)


def in_main(at):
    return max(0, min(EDGE, MAIN - at))


def put(main, side, block, row, value):
    for g in GROUPS:
        at = g * SIDE + row
        part = value[:, g * LANES : (g + 1) * LANES]
        n = in_main(at)
        if n:
            main[block, at : at + n, :] = part[:n]
        if n < EDGE:
            side[block, at + n - MAIN : at + EDGE - MAIN, :] = part[n:]


def by_plane(me, side, outs):
    for k in range(BLOCKS):
        outs[k // PLANE][k % PLANE] = side[k ^ me[0]]


def rows_of(main, side, at):
    ref, at = (main, at) if at < main.shape[1] else (side, at - main.shape[1])
    return ref[:, at : at + TILE, :].reshape(ref.shape[0] * TILE, LANES)


def tile(main, side, r):
    return jnp.concatenate([rows_of(main, side, g * SIDE + r) for g in GROUPS], axis=1)


def score_kernel(
    factor, picks, me, image, target, first, second, *refs
):
    outs, side = refs[1 : 1 + PLANES], refs[1 + PLANES]
    out, (xs, ts, normed, hidden, deriv, delta, back) = refs[0], refs[2 + PLANES :]
    step = pl.program_id(0)
    images = pl.num_programs(0)
    rows = pl.ds(pl.multiple_of(step * PAD, PAD), PAD)

    @pl.when(step == 0)
    def _():
        xs[...] = jnp.zeros_like(xs)
        ts[...] = jnp.zeros_like(ts)

    xs[0:S, :] = image[0].astype(jnp.float32)
    ts[0:S, :] = target[0].astype(jnp.float32)
    xf = xs[...]
    mean = jnp.mean(xf, axis=1, keepdims=True)
    centered = xf - mean
    var = jnp.mean(centered * centered, axis=1, keepdims=True)
    nrm = (centered * lax.rsqrt(var + 1e-06)).astype(jnp.bfloat16)
    normed[rows, :] = nrm
    for c in range(COLS):
        cols = pl.ds(c * D, D)
        pre = dot(nrm, first[:, cols], ((1,), (0,))) * isd
        sq = pre * pre
        tval = jnp.tanh(pre * (gelu_c + (gelu_c * 0.044715) * sq))
        gate = 0.5 + 0.5 * tval
        hid = pre * gate
        hidden[rows, cols] = hid.astype(jnp.bfloat16)
        deriv[:, cols] = gate + hid * (1.0 - gate) * (
            2.0 * gelu_c + (6.0 * gelu_c * 0.044715) * sq
        )
    prod = dot(hidden[rows, :], second[...], ((1,), (0,))) * isf
    dlt = ((xs[...] + prod - ts[...]) * (1.0 / S)).astype(jnp.bfloat16)
    delta[rows, :] = dlt
    for c in range(COLS):
        cols = pl.ds(c * D, D)
        dhid = dot(dlt, second[cols, :], ((1,), (1,))) * isf
        back[rows, cols] = (dhid * deriv[:, cols]).astype(jnp.bfloat16)

    @pl.when(step == images - 1)
    def _():
        for c in range(COLS):
            cols = pl.ds(c * D, D)
            grad = dot(normed[...], back[:, cols], ((0,), (0,))) * (-factor * isd)
            score = (grad - first[:, cols].astype(jnp.float32)).astype(jnp.bfloat16)
            for r in range(D // EDGE):
                put(out, side, r * COLS + c, 0, score[r * EDGE : (r + 1) * EDGE, :])
            grad = dot(hidden[:, cols], delta[...], ((0,), (0,))) * (-factor * isf)
            score = (grad - second[cols, :].astype(jnp.float32)).astype(jnp.bfloat16)
            for r in range(D // EDGE):
                at = c * (D // EDGE) + r
                put(out, side, at, EDGE, score[r * EDGE : (r + 1) * EDGE, :])
        by_plane(me, side, outs)


def side_shapes(rows):
    return (jax.ShapeDtypeStruct((PLANE, rows, LANES), jnp.bfloat16),) * PLANES


def particle_scores(first, second, images, targets, picks, me):
    count = picks.shape[0]
    rows = count * PAD
    bf = jnp.bfloat16
    return pl.pallas_call(
        functools.partial(score_kernel, DATA / count),
        out_shape=(pltpu.HBM((BLOCKS, MAIN, LANES), bf), *side_shapes(REST)),
        grid_spec=pltpu.PrefetchScalarGridSpec(
            num_scalar_prefetch=2,
            grid=(count,),
            in_specs=[
                pl.BlockSpec((1, S, D), lambda b, picks, me: (picks[b], 0, 0)),
                pl.BlockSpec((1, S, D), lambda b, picks, me: (picks[b], 0, 0)),
                pl.BlockSpec((D, FF), lambda b, picks, me: (0, 0)),
                pl.BlockSpec((FF, D), lambda b, picks, me: (0, 0)),
            ],
            out_specs=(
                pl.BlockSpec((BLOCKS, MAIN, LANES), lambda b, picks, me: (0, 0, 0)),
                *[pl.BlockSpec((PLANE, REST, LANES), lambda b, picks, me: (0, 0, 0))] * PLANES,
            ),
            scratch_shapes=[
                pltpu.VMEM((BLOCKS, REST, LANES), bf),
                pltpu.VMEM((PAD, D), jnp.float32),
                pltpu.VMEM((PAD, D), jnp.float32),
                pltpu.VMEM((rows, D), bf),
                pltpu.VMEM((rows, FF), bf),
                pltpu.VMEM((PAD, FF), jnp.float32),
                pltpu.VMEM((rows, D), bf),
                pltpu.VMEM((rows, FF), bf),
            ],
        ),
        compiler_params=pltpu.CompilerParams(vmem_limit_bytes=32 * 1024 * 1024),
        cost_estimate=pl.CostEstimate(
            flops=10 * count * PAD * D * FF,
            bytes_accessed=4 * (2 * D * FF + count * S * D),
            transcendentals=count * PAD * FF,
        ),
        name="score",
    )(picks, me, images, targets, first, second)


def gram_kernel(main, side, out, total):
    members = main.shape[0]
    wide = members * TILE
    total[...] = jnp.zeros_like(total)
    for r in range(0, SIDE, TILE):
        part = tile(main, side, r)
        total[...] += dot(part, part, ((1,), (1,)))
    at = lax.broadcasted_iota(jnp.int32, (wide, wide), 0) % TILE
    to = lax.broadcasted_iota(jnp.int32, (wide, wide), 1) % TILE
    kept = jnp.where(at == to, total[...], 0.0)
    summed = jnp.sum(kept.reshape(members, TILE, wide), axis=1)
    turned = summed.T
    gram = jnp.sum(turned.reshape(members, TILE, members), axis=1)
    row = lax.broadcasted_iota(jnp.int32, gram.shape, 0)
    col = lax.broadcasted_iota(jnp.int32, gram.shape, 1)
    own = jnp.where(row == col, gram, 0.0)
    dist = jnp.sum(own, axis=1, keepdims=True) + jnp.sum(own, axis=0, keepdims=True) - 2.0 * gram
    out[...] = jnp.concatenate([dist[q : q + 8] for q in range(0, members, 8)], axis=1)


def distances(main, side):
    members = main.shape[0]
    wide = members * TILE
    return pl.pallas_call(
        gram_kernel,
        out_shape=jax.ShapeDtypeStruct((8, members * members // 8), jnp.float32),
        scratch_shapes=[pltpu.VMEM((wide, wide), jnp.float32)],
        compiler_params=pltpu.CompilerParams(vmem_limit_bytes=16 * 1024 * 1024),
        cost_estimate=pl.CostEstimate(
            flops=2 * wide * wide * SIDE // TILE * D,
            bytes_accessed=2 * members * ROWS * LANES,
            transcendentals=0,
        ),
        name="gram",
    )(main, side)


def add_over(value, members, bits):
    got = [
        lax.ppermute(value, AXES, [(i, i ^ bit) for i in range(members)]) for bit in bits
    ]
    return sum(got, value)


def kernel_of(scale, packed):
    members = packed.shape[1] // 4
    dist = jnp.concatenate(
        [packed[:, members * q : members * (q + 1)] for q in range(members // 8)], axis=0
    )
    return jnp.exp(-dist / scale[0]).astype(jnp.bfloat16)


def spreading(kernel):
    members = kernel.shape[0]
    wide = members * TILE
    at = lax.broadcasted_iota(jnp.int32, (wide, members), 0) // TILE
    which = lax.broadcasted_iota(jnp.int32, (wide, members), 1)
    pick = jnp.where(at == which, 1.0, 0.0).astype(jnp.bfloat16)
    tall = dot(pick, kernel, ((1,), (0,))).astype(jnp.bfloat16)
    full = dot(tall, pick, ((1,), (1,)))
    row = lax.broadcasted_iota(jnp.int32, (wide, wide), 0) % TILE
    col = lax.broadcasted_iota(jnp.int32, (wide, wide), 1) % TILE
    return jnp.where(row == col, full, 0.0)


def mix(mixer, ksum, scores, own):
    members = mixer.shape[0] // TILE
    wide = own.shape[1]
    both = dot(mixer, jnp.concatenate([scores, own], axis=1), ((1,), (0,)))
    pushed = ksum * own.astype(jnp.float32) - both[:, wide:]
    both = jnp.concatenate([both[:, :wide], pushed], axis=1) * (1.0 / members)
    return both.astype(jnp.bfloat16)


def mix_side_kernel(scale, me, packed, scores, params, mixing, *refs):
    outs, side = refs[:PLANES], refs[PLANES]
    members = params.shape[0]
    full = spreading(kernel_of(scale, packed[...]))
    ksum = jnp.sum(full, axis=1, keepdims=True)
    mixer = full.astype(jnp.bfloat16)
    mixing[...] = mixer
    at = range(0, REST, TILE)
    got = jnp.concatenate([rows_of(scores, None, r) for r in at], axis=1)
    own = jnp.concatenate([rows_of(params, None, r) for r in at], axis=1)
    both = mix(mixer, ksum, got, own)
    for q in range(2 * len(at)):
        part = both[:, q * LANES : (q + 1) * LANES].reshape(members, TILE, LANES)
        side[:, q * TILE : (q + 1) * TILE, :] = part
    by_plane(me, side, outs)


def mix_side(scale, me, packed, scores, params):
    members = params.shape[0]
    wide = members * TILE
    vmem = pl.BlockSpec(memory_space=pltpu.VMEM)
    smem = pl.BlockSpec(memory_space=pltpu.SMEM)
    mixing = jax.ShapeDtypeStruct((wide, wide), jnp.bfloat16)
    return pl.pallas_call(
        mix_side_kernel,
        out_shape=(mixing, *side_shapes(2 * REST)),
        in_specs=[smem, smem] + [vmem] * 3,
        scratch_shapes=[pltpu.VMEM((members, 2 * REST, LANES), jnp.bfloat16)],
        compiler_params=pltpu.CompilerParams(vmem_limit_bytes=24 * 1024 * 1024),
        cost_estimate=pl.CostEstimate(
            flops=4 * wide * wide * REST // TILE * LANES,
            bytes_accessed=8 * members * REST * LANES,
            transcendentals=0,
        ),
        name="mix_side",
    )(scale, me, packed, scores, params)


def mix_main_kernel(mixing, scores, params, side_params, out, mixed, stores):
    members = params.shape[0]
    mixer = mixing[...]
    ksum = jnp.sum(mixer.astype(jnp.float32), axis=1, keepdims=True)
    copies = []
    for r in range(0, SIDE, TILE):
        at = [g * SIDE + r for g in GROUPS if g * SIDE + r < MAIN]
        groups = len(at)
        got = jnp.concatenate([rows_of(scores, None, x) for x in at], axis=1)
        own = jnp.concatenate([rows_of(params, side_params, x) for x in at], axis=1)
        both = mix(mixer, ksum, got, own)
        for q in range(2 * groups):
            part = both[:, q * LANES : (q + 1) * LANES].reshape(members, TILE, LANES)
            x = q // groups * MAIN + at[q % groups]
            mixed[:, x : x + TILE, :] = part
            here = pl.ds(x, TILE)
            copies.append(
                pltpu.make_async_copy(
                    mixed.at[:, here, :], out.at[:, here, :], stores.at[x // TILE]
                )
            )
            copies[-1].start()
    for copy in copies:
        copy.wait()


def mix_main(mixing, scores, params, side_params):
    members = params.shape[0]
    wide = members * TILE
    vmem = pl.BlockSpec(memory_space=pltpu.VMEM)
    return pl.pallas_call(
        mix_main_kernel,
        out_shape=pltpu.HBM((members, 2 * MAIN, LANES), jnp.bfloat16),
        in_specs=[vmem] * 4,
        out_specs=pl.BlockSpec(memory_space=pl.ANY),
        scratch_shapes=[
            pltpu.VMEM((members, 2 * MAIN, LANES), jnp.bfloat16),
            pltpu.SemaphoreType.DMA((2 * MAIN // TILE,)),
        ],
        compiler_params=pltpu.CompilerParams(vmem_limit_bytes=24 * 1024 * 1024),
        cost_estimate=pl.CostEstimate(
            flops=4 * wide * wide * MAIN // TILE * LANES,
            bytes_accessed=8 * members * MAIN * LANES,
            transcendentals=0,
        ),
        name="mix_main",
    )(mixing, scores, params, side_params)


def plane_kernel(*refs):
    for z in range(PLANES):
        for q in range(PLANE):
            refs[PLANES + q // 2][z, q % 2] = refs[z][q]


def core_kernel(*refs):
    for q in range(PLANE // 2):
        for z in range(PLANES):
            for c in range(2):
                refs[PLANE // 2 + c][q, z] = refs[q][z, c]


def settle_kernel(me, near, far, out):
    for c, ref in enumerate((near, far)):
        for q in range(PLANE // 2):
            for z in range(PLANES):
                out[(z * PLANE + 2 * q + c) ^ me[0]] = ref[q, z]


def regroup(body, name, shapes, *arrays, me=(), flops=0):
    vmem = pl.BlockSpec(memory_space=pltpu.VMEM)
    size = sum(math.prod(x.shape) for x in arrays)
    return pl.pallas_call(
        body,
        out_shape=shapes,
        in_specs=[pl.BlockSpec(memory_space=pltpu.SMEM)] * len(me) + [vmem] * len(arrays),
        compiler_params=pltpu.CompilerParams(vmem_limit_bytes=16 * 1024 * 1024),
        cost_estimate=pl.CostEstimate(flops=flops, bytes_accessed=4 * size, transcendentals=0),
        name=name,
    )(*me, *arrays)


def swap(value, bits):
    pairs = [(i, i ^ bits) for i in range(BLOCKS)]
    return lax.ppermute(value, AXES, pairs)


def across_planes(parts):
    return parts[:1] + [swap(x, z * PLANE) for z, x in enumerate(parts) if z]


def in_plane(parts):
    rows = parts[0].shape[1]
    shape = jax.ShapeDtypeStruct((PLANES, 2, rows, LANES), jnp.bfloat16)
    return regroup(plane_kernel, "plane", (shape,) * (PLANE // 2), *parts, flops=LONG)


def across_chips(parts):
    return parts[:1] + tuple(swap(x, 2 * q) for q, x in enumerate(parts) if q)


def in_order(parts, me):
    rows = parts[0].shape[2]
    shape = jax.ShapeDtypeStruct((PLANE // 2, PLANES, rows, LANES), jnp.bfloat16)
    near, far = regroup(core_kernel, "core", (shape,) * 2, *parts)
    shape = jax.ShapeDtypeStruct((BLOCKS, rows, LANES), jnp.bfloat16)
    return regroup(settle_kernel, "settle", shape, near, swap(far, 1), me=(me,))


def after(values, *others):
    return lax.optimization_barrier((values, *others))[0]


def plain_products(params):
    flat = params.reshape(params.shape[0], -1)
    return dot(flat, flat, ((1,), (1,)))


def plain_weighted(gram, scale, params, scores):
    members = params.shape[0]
    norms = jnp.diagonal(gram)
    dist = norms[:, None] + norms[None, :] - 2.0 * gram
    kernel = jnp.exp(-dist / scale[0]).astype(jnp.bfloat16)
    flat = params.reshape(members, -1)
    ksum = jnp.sum(kernel.astype(jnp.float32), axis=1, keepdims=True)
    attract = dot(kernel, scores.reshape(members, -1), ((1,), (0,))) / members
    mixed = dot(kernel, flat, ((1,), (0,)))
    spread = (flat.astype(jnp.float32) * ksum - mixed) / members
    return tuple(x.astype(jnp.bfloat16).reshape(params.shape) for x in (attract, spread))


STEPS = D // EDGE
TALL = FF // STEPS


def pack_side_kernel(me, first, second, *refs):
    outs, (wide, tall, loads) = refs[:PLANES], refs[PLANES:]
    copies = [pltpu.make_async_copy(second.at[0, :, pl.ds(D - LANES, LANES)], tall, loads.at[COLS])]
    for c in range(COLS):
        here = first.at[0, :, pl.ds((c + 1) * D - LANES, LANES)]
        copies.append(pltpu.make_async_copy(here, wide.at[c], loads.at[c]))
    for copy in copies:
        copy.start()
    for copy in copies:
        copy.wait()
    more = REST - EDGE
    for k in range(BLOCKS):
        b = k ^ me[0]
        here = pl.ds(pl.multiple_of(b // COLS * EDGE + EDGE - more, TILE), more)
        outs[k // PLANE][k % PLANE, 0:more, :] = wide[b % COLS, here, :]
        here = pl.ds(pl.multiple_of(b * EDGE, EDGE), EDGE)
        outs[k // PLANE][k % PLANE, more:REST, :] = tall[here, :]


def pack_main_kernel(first, second, out, wide, tall, packed, loads, stores):
    def load(d):
        return (
            pltpu.make_async_copy(
                first.at[0, pl.ds(d * EDGE, EDGE), :], wide.at[d], loads.at[0, d]
            ),
            pltpu.make_async_copy(
                second.at[0, pl.ds(d * TALL, TALL), :], tall.at[d], loads.at[1, d]
            ),
        )

    def store(d):
        here = pl.ds(d * COLS, COLS)
        return pltpu.make_async_copy(packed.at[here], out.at[here], stores.at[d])

    for d in range(STEPS):
        for copy in load(d):
            copy.start()
    for d in range(STEPS):
        for copy in load(d):
            copy.wait()
        for c in range(COLS):
            for g in GROUPS:
                b, at, lanes = d * COLS + c, g * SIDE, g * LANES
                end = in_main(at)
                packed[b, at : at + end, :] = wide[
                    d, 0:end, c * D + lanes : c * D + lanes + LANES
                ]
                if at + EDGE < MAIN:
                    packed[b, at + EDGE : at + SIDE, :] = tall[
                        d, c * EDGE : (c + 1) * EDGE, lanes : lanes + LANES
                    ]
        store(d).start()
    for d in range(STEPS):
        store(d).wait()


def to_blocks(first, second, me):
    bf = jnp.bfloat16
    anywhere = [pl.BlockSpec(memory_space=pl.ANY)]
    params = pltpu.CompilerParams(vmem_limit_bytes=56 * 1024 * 1024)
    cost = pl.CostEstimate(flops=0, bytes_accessed=4 * D * FF, transcendentals=0)
    side = pl.pallas_call(
        pack_side_kernel,
        out_shape=side_shapes(REST),
        in_specs=[pl.BlockSpec(memory_space=pltpu.SMEM)] + anywhere * 2,
        scratch_shapes=[
            pltpu.VMEM((COLS, D, LANES), bf),
            pltpu.VMEM((FF, LANES), bf),
            pltpu.SemaphoreType.DMA((COLS + 1,)),
        ],
        compiler_params=params,
        cost_estimate=cost,
        name="pack_side",
    )(me, first, second)
    main = pl.pallas_call(
        pack_main_kernel,
        out_shape=pltpu.HBM((BLOCKS, MAIN, LANES), bf),
        in_specs=anywhere * 2,
        out_specs=anywhere[0],
        scratch_shapes=[
            pltpu.VMEM((STEPS, EDGE, FF), bf),
            pltpu.VMEM((STEPS, TALL, D), bf),
            pltpu.VMEM((BLOCKS, MAIN, LANES), bf),
            pltpu.SemaphoreType.DMA((2, STEPS)),
            pltpu.SemaphoreType.DMA((STEPS,)),
        ],
        compiler_params=params,
        cost_estimate=cost,
        name="pack_main",
    )(first, second)
    return main, side


def pieces(main, side, which, at):
    n = in_main(at)
    found = [(0, n, main, which * MAIN + at), (n, EDGE - n, side, which * REST + at + n - MAIN)]
    return [piece for piece in found if piece[1]]


def unpack_kernel(main, side, first_a, second_a, first_s, second_s, wide, tall, stores):
    def store(which, d):
        first, second = ((first_a, second_a), (first_s, second_s))[which]
        return (
            pltpu.make_async_copy(
                wide.at[which, d], first.at[0, pl.ds(d * EDGE, EDGE), :], stores.at[which, 0, d]
            ),
            pltpu.make_async_copy(
                tall.at[which, d], second.at[0, pl.ds(d * TALL, TALL), :], stores.at[which, 1, d]
            ),
        )

    for which in range(2):
        for d in range(STEPS):
            for c in range(COLS):
                for g in GROUPS:
                    b = d * COLS + c
                    lanes = slice(c * D + g * LANES, c * D + (g + 1) * LANES)
                    for row, n, ref, at in pieces(main, side, which, g * SIDE):
                        wide[which, d, row : row + n, lanes] = ref[b, at : at + n, :]
                    lanes = slice(g * LANES, (g + 1) * LANES)
                    for row, n, ref, at in pieces(main, side, which, g * SIDE + EDGE):
                        here = slice(c * EDGE + row, c * EDGE + row + n)
                        tall[which, d, here, lanes] = ref[b, at : at + n, :]
            for copy in store(which, d):
                copy.start()
    for which in range(2):
        for d in range(STEPS):
            for copy in store(which, d):
                copy.wait()


def from_blocks(main, side):
    bf = jnp.bfloat16
    return pl.pallas_call(
        unpack_kernel,
        out_shape=(pltpu.HBM((1, D, FF), bf), pltpu.HBM((1, FF, D), bf)) * 2,
        in_specs=[pl.BlockSpec(memory_space=pltpu.VMEM)] * 2,
        out_specs=(pl.BlockSpec(memory_space=pl.ANY),) * 4,
        scratch_shapes=[
            pltpu.VMEM((2, STEPS, EDGE, FF), bf),
            pltpu.VMEM((2, STEPS, TALL, D), bf),
            pltpu.SemaphoreType.DMA((2, 2, STEPS)),
        ],
        compiler_params=pltpu.CompilerParams(vmem_limit_bytes=24 * 1024 * 1024),
        cost_estimate=pl.CostEstimate(flops=0, bytes_accessed=16 * D * FF, transcendentals=0),
        name="unpack",
    )(main, side)


def exchange(blocks):
    return lax.all_to_all(blocks, AXES, split_axis=0, concat_axis=0, tiled=True)


def on_device(
    particles_first, particles_second, pool_images, pool_targets, batch_index, kernel_scale
):
    members = math.prod(lax.axis_size(name) for name in AXES)
    tiled = members == BLOCKS
    me = lax.axis_index(AXES) if tiled else 0
    me = jnp.full((1,), me, jnp.int32)
    params, side_params = to_blocks(particles_first, particles_second, me)
    first, second = particles_first[0], particles_second[0]
    if tiled:
        params = exchange(params)
        side_params = in_plane(across_planes(list(side_params)))
        first, second = after((first, second), side_params[0])
        side_params = across_chips(side_params)
    scores, *side_scores = particle_scores(
        first, second, pool_images, pool_targets, batch_index[0], me
    )
    if tiled:
        side_params = in_order(after(side_params, side_scores[0]), me)
        side_scores = across_planes(after(side_scores, params))
        packed = distances(params, side_params)
        got = [swap(packed, z * PLANE) for z in range(1, PLANES)]
        scores = exchange(scores)
        side_scores = in_plane(after(side_scores, got))
        packed = sum(got, packed)
        side_scores = in_order(across_chips(side_scores), me)
        for bits in ((2, 4, 6), (1,)):
            packed = add_over(packed, members, bits)
        mixing, *side = mix_side(kernel_scale, me, packed, side_scores, side_params)
        main = mix_main(mixing, scores, params, side_params)
        side = in_order(across_chips(in_plane(across_planes(side))), me)
        return from_blocks(exchange(main), side)
    cut = (members, BLOCKS * ROWS // members, LANES)
    params = jnp.concatenate([params, jnp.concatenate(side_params)], axis=1)
    scores = jnp.concatenate([scores, jnp.concatenate(side_scores)], axis=1)
    params, scores = exchange(params.reshape(cut)), exchange(scores.reshape(cut))
    gram = lax.psum(plain_products(params), AXES)
    parts = plain_weighted(gram, kernel_scale, params, scores)
    parts = [exchange(x).reshape(BLOCKS, ROWS, LANES) for x in parts]
    main = jnp.concatenate([x[:, :MAIN] for x in parts], axis=1)
    return from_blocks(main, jnp.concatenate([x[:, MAIN:] for x in parts], axis=1))


def solution(mesh):
    split = P(AXES, None, None)
    return jax.shard_map(
        on_device,
        mesh=mesh,
        in_specs=(split, split, P(), P(), P(AXES, None), P()),
        out_specs=(split, split, split, split),
        check_vma=False,
    )
```

```python
import functools
import math

import jax
import jax.numpy as jnp
from jax import lax
from jax.experimental import pallas as pl
from jax.experimental.pallas import tpu as pltpu
from jax.sharding import PartitionSpec as P

D = 384
FF = 1536
S = 197
DATA = 10000
AXES = ("wide", "narrow")
PAD = 208
EDGE = 48
BLOCKS = D * FF // (EDGE * D)
COLS = FF // D
TILE = 16
LANES = 128
SIDE = 2 * EDGE
GROUPS = range(D // LANES)
ROWS = SIDE * len(GROUPS)
REST = EDGE + 2 * TILE
MAIN = ROWS - REST
PLANES = 4
PLANE = BLOCKS // PLANES
LONG = 10**11

gelu_c = math.sqrt(2.0 / math.pi)
isd = 1.0 / math.sqrt(D)
isf = 1.0 / math.sqrt(FF)


def dot(a, b, dims):
    return lax.dot_general(a, b, (dims, ((), ())), preferred_element_type=jnp.float32)


def in_main(at):
    return max(0, min(EDGE, MAIN - at))


def put(main, side, block, row, value):
    for g in GROUPS:
        at = g * SIDE + row
        part = value[:, g * LANES : (g + 1) * LANES]
        n = in_main(at)
        if n:
            main[block, at : at + n, :] = part[:n]
        if n < EDGE:
            side[block, at + n - MAIN : at + EDGE - MAIN, :] = part[n:]


def by_plane(me, side, outs):
    for k in range(BLOCKS):
        outs[k // PLANE][k % PLANE] = side[k ^ me[0]]


def rows_of(main, side, at):
    ref, at = (main, at) if at < main.shape[1] else (side, at - main.shape[1])
    return ref[:, at : at + TILE, :].reshape(ref.shape[0] * TILE, LANES)


def tile(main, side, r):
    return jnp.concatenate([rows_of(main, side, g * SIDE + r) for g in GROUPS], axis=1)


def score_kernel(
    factor, picks, me, image, target, first, second, *refs
):
    outs, side = refs[1 : 1 + PLANES], refs[1 + PLANES]
    out, (xs, ts, normed, hidden, deriv, delta, back) = refs[0], refs[2 + PLANES :]
    step = pl.program_id(0)
    images = pl.num_programs(0)
    rows = pl.ds(pl.multiple_of(step * PAD, PAD), PAD)

    @pl.when(step == 0)
    def _():
        xs[...] = jnp.zeros_like(xs)
        ts[...] = jnp.zeros_like(ts)

    xs[0:S, :] = image[0].astype(jnp.float32)
    ts[0:S, :] = target[0].astype(jnp.float32)
    xf = xs[...]
    mean = jnp.mean(xf, axis=1, keepdims=True)
    centered = xf - mean
    var = jnp.mean(centered * centered, axis=1, keepdims=True)
    nrm = (centered * lax.rsqrt(var + 1e-06)).astype(jnp.bfloat16)
    normed[rows, :] = nrm
    for c in range(COLS):
        cols = pl.ds(c * D, D)
        pre = dot(nrm, first[:, cols], ((1,), (0,))) * isd
        sq = pre * pre
        tval = jnp.tanh(pre * (gelu_c + (gelu_c * 0.044715) * sq))
        gate = 0.5 + 0.5 * tval
        hid = pre * gate
        hidden[rows, cols] = hid.astype(jnp.bfloat16)
        deriv[:, cols] = gate + hid * (1.0 - gate) * (
            2.0 * gelu_c + (6.0 * gelu_c * 0.044715) * sq
        )
    prod = dot(hidden[rows, :], second[...], ((1,), (0,))) * isf
    dlt = ((xs[...] + prod - ts[...]) * (1.0 / S)).astype(jnp.bfloat16)
    delta[rows, :] = dlt
    for c in range(COLS):
        cols = pl.ds(c * D, D)
        dhid = dot(dlt, second[cols, :], ((1,), (1,))) * isf
        back[rows, cols] = (dhid * deriv[:, cols]).astype(jnp.bfloat16)

    @pl.when(step == images - 1)
    def _():
        for c in range(COLS):
            cols = pl.ds(c * D, D)
            grad = dot(normed[...], back[:, cols], ((0,), (0,))) * (-factor * isd)
            score = (grad - first[:, cols].astype(jnp.float32)).astype(jnp.bfloat16)
            for r in range(D // EDGE):
                put(out, side, r * COLS + c, 0, score[r * EDGE : (r + 1) * EDGE, :])
            grad = dot(hidden[:, cols], delta[...], ((0,), (0,))) * (-factor * isf)
            score = (grad - second[cols, :].astype(jnp.float32)).astype(jnp.bfloat16)
            for r in range(D // EDGE):
                at = c * (D // EDGE) + r
                put(out, side, at, EDGE, score[r * EDGE : (r + 1) * EDGE, :])
        by_plane(me, side, outs)


def side_shapes(rows):
    return (jax.ShapeDtypeStruct((PLANE, rows, LANES), jnp.bfloat16),) * PLANES


def particle_scores(first, second, images, targets, picks, me):
    count = picks.shape[0]
    rows = count * PAD
    bf = jnp.bfloat16
    return pl.pallas_call(
        functools.partial(score_kernel, DATA / count),
        out_shape=(pltpu.HBM((BLOCKS, MAIN, LANES), bf), *side_shapes(REST)),
        grid_spec=pltpu.PrefetchScalarGridSpec(
            num_scalar_prefetch=2,
            grid=(count,),
            in_specs=[
                pl.BlockSpec((1, S, D), lambda b, picks, me: (picks[b], 0, 0)),
                pl.BlockSpec((1, S, D), lambda b, picks, me: (picks[b], 0, 0)),
                pl.BlockSpec((D, FF), lambda b, picks, me: (0, 0)),
                pl.BlockSpec((FF, D), lambda b, picks, me: (0, 0)),
            ],
            out_specs=(
                pl.BlockSpec((BLOCKS, MAIN, LANES), lambda b, picks, me: (0, 0, 0)),
                *[pl.BlockSpec((PLANE, REST, LANES), lambda b, picks, me: (0, 0, 0))] * PLANES,
            ),
            scratch_shapes=[
                pltpu.VMEM((BLOCKS, REST, LANES), bf),
                pltpu.VMEM((PAD, D), jnp.float32),
                pltpu.VMEM((PAD, D), jnp.float32),
                pltpu.VMEM((rows, D), bf),
                pltpu.VMEM((rows, FF), bf),
                pltpu.VMEM((PAD, FF), jnp.float32),
                pltpu.VMEM((rows, D), bf),
                pltpu.VMEM((rows, FF), bf),
            ],
        ),
        compiler_params=pltpu.CompilerParams(vmem_limit_bytes=32 * 1024 * 1024),
        cost_estimate=pl.CostEstimate(
            flops=10 * count * PAD * D * FF,
            bytes_accessed=4 * (2 * D * FF + count * S * D),
            transcendentals=count * PAD * FF,
        ),
        name="score",
    )(picks, me, images, targets, first, second)


def gram_kernel(main, side, out, total):
    members = main.shape[0]
    wide = members * TILE
    total[...] = jnp.zeros_like(total)
    for r in range(0, SIDE, TILE):
        part = tile(main, side, r)
        total[...] += dot(part, part, ((1,), (1,)))
    at = lax.broadcasted_iota(jnp.int32, (wide, wide), 0) % TILE
    to = lax.broadcasted_iota(jnp.int32, (wide, wide), 1) % TILE
    kept = jnp.where(at == to, total[...], 0.0)
    summed = jnp.sum(kept.reshape(members, TILE, wide), axis=1)
    turned = summed.T
    gram = jnp.sum(turned.reshape(members, TILE, members), axis=1)
    row = lax.broadcasted_iota(jnp.int32, gram.shape, 0)
    col = lax.broadcasted_iota(jnp.int32, gram.shape, 1)
    own = jnp.where(row == col, gram, 0.0)
    dist = jnp.sum(own, axis=1, keepdims=True) + jnp.sum(own, axis=0, keepdims=True) - 2.0 * gram
    out[...] = jnp.concatenate([dist[q : q + 8] for q in range(0, members, 8)], axis=1)


def distances(main, side):
    members = main.shape[0]
    wide = members * TILE
    return pl.pallas_call(
        gram_kernel,
        out_shape=jax.ShapeDtypeStruct((8, members * members // 8), jnp.float32),
        scratch_shapes=[pltpu.VMEM((wide, wide), jnp.float32)],
        compiler_params=pltpu.CompilerParams(vmem_limit_bytes=16 * 1024 * 1024),
        cost_estimate=pl.CostEstimate(
            flops=2 * wide * wide * SIDE // TILE * D,
            bytes_accessed=2 * members * ROWS * LANES,
            transcendentals=0,
        ),
        name="gram",
    )(main, side)


def add_over(value, members, bits):
    got = [
        lax.ppermute(value, AXES, [(i, i ^ bit) for i in range(members)]) for bit in bits
    ]
    return sum(got, value)


def kernel_of(scale, packed):
    members = packed.shape[1] // 4
    dist = jnp.concatenate(
        [packed[:, members * q : members * (q + 1)] for q in range(members // 8)], axis=0
    )
    return jnp.exp(-dist / scale[0]).astype(jnp.bfloat16)


def spreading(kernel):
    members = kernel.shape[0]
    wide = members * TILE
    at = lax.broadcasted_iota(jnp.int32, (wide, members), 0) // TILE
    which = lax.broadcasted_iota(jnp.int32, (wide, members), 1)
    pick = jnp.where(at == which, 1.0, 0.0).astype(jnp.bfloat16)
    tall = dot(pick, kernel, ((1,), (0,))).astype(jnp.bfloat16)
    full = dot(tall, pick, ((1,), (1,)))
    row = lax.broadcasted_iota(jnp.int32, (wide, wide), 0) % TILE
    col = lax.broadcasted_iota(jnp.int32, (wide, wide), 1) % TILE
    return jnp.where(row == col, full, 0.0)


def mix(mixer, ksum, scores, own):
    members = mixer.shape[0] // TILE
    wide = own.shape[1]
    both = dot(mixer, jnp.concatenate([scores, own], axis=1), ((1,), (0,)))
    pushed = ksum * own.astype(jnp.float32) - both[:, wide:]
    both = jnp.concatenate([both[:, :wide], pushed], axis=1) * (1.0 / members)
    return both.astype(jnp.bfloat16)


def mix_side_kernel(scale, me, packed, scores, params, mixing, *refs):
    outs, side = refs[:PLANES], refs[PLANES]
    members = params.shape[0]
    full = spreading(kernel_of(scale, packed[...]))
    ksum = jnp.sum(full, axis=1, keepdims=True)
    mixer = full.astype(jnp.bfloat16)
    mixing[...] = mixer
    at = range(0, REST, TILE)
    got = jnp.concatenate([rows_of(scores, None, r) for r in at], axis=1)
    own = jnp.concatenate([rows_of(params, None, r) for r in at], axis=1)
    both = mix(mixer, ksum, got, own)
    for q in range(2 * len(at)):
        part = both[:, q * LANES : (q + 1) * LANES].reshape(members, TILE, LANES)
        side[:, q * TILE : (q + 1) * TILE, :] = part
    by_plane(me, side, outs)


def mix_side(scale, me, packed, scores, params):
    members = params.shape[0]
    wide = members * TILE
    vmem = pl.BlockSpec(memory_space=pltpu.VMEM)
    smem = pl.BlockSpec(memory_space=pltpu.SMEM)
    mixing = jax.ShapeDtypeStruct((wide, wide), jnp.bfloat16)
    return pl.pallas_call(
        mix_side_kernel,
        out_shape=(mixing, *side_shapes(2 * REST)),
        in_specs=[smem, smem] + [vmem] * 3,
        scratch_shapes=[pltpu.VMEM((members, 2 * REST, LANES), jnp.bfloat16)],
        compiler_params=pltpu.CompilerParams(vmem_limit_bytes=24 * 1024 * 1024),
        cost_estimate=pl.CostEstimate(
            flops=4 * wide * wide * REST // TILE * LANES,
            bytes_accessed=8 * members * REST * LANES,
            transcendentals=0,
        ),
        name="mix_side",
    )(scale, me, packed, scores, params)


def mix_main_kernel(mixing, scores, params, side_params, out, mixed, stores):
    members = params.shape[0]
    mixer = mixing[...]
    ksum = jnp.sum(mixer.astype(jnp.float32), axis=1, keepdims=True)
    copies = []
    for r in range(0, SIDE, TILE):
        at = [g * SIDE + r for g in GROUPS if g * SIDE + r < MAIN]
        groups = len(at)
        got = jnp.concatenate([rows_of(scores, None, x) for x in at], axis=1)
        own = jnp.concatenate([rows_of(params, side_params, x) for x in at], axis=1)
        both = mix(mixer, ksum, got, own)
        for q in range(2 * groups):
            part = both[:, q * LANES : (q + 1) * LANES].reshape(members, TILE, LANES)
            x = q // groups * MAIN + at[q % groups]
            mixed[:, x : x + TILE, :] = part
            here = pl.ds(x, TILE)
            copies.append(
                pltpu.make_async_copy(
                    mixed.at[:, here, :], out.at[:, here, :], stores.at[x // TILE]
                )
            )
            copies[-1].start()
    for copy in copies:
        copy.wait()


def mix_main(mixing, scores, params, side_params):
    members = params.shape[0]
    wide = members * TILE
    vmem = pl.BlockSpec(memory_space=pltpu.VMEM)
    return pl.pallas_call(
        mix_main_kernel,
        out_shape=pltpu.HBM((members, 2 * MAIN, LANES), jnp.bfloat16),
        in_specs=[vmem] * 4,
        out_specs=pl.BlockSpec(memory_space=pl.ANY),
        scratch_shapes=[
            pltpu.VMEM((members, 2 * MAIN, LANES), jnp.bfloat16),
            pltpu.SemaphoreType.DMA((2 * MAIN // TILE,)),
        ],
        compiler_params=pltpu.CompilerParams(vmem_limit_bytes=24 * 1024 * 1024),
        cost_estimate=pl.CostEstimate(
            flops=4 * wide * wide * MAIN // TILE * LANES,
            bytes_accessed=8 * members * MAIN * LANES,
            transcendentals=0,
        ),
        name="mix_main",
    )(mixing, scores, params, side_params)


def plane_kernel(*refs):
    for z in range(PLANES):
        for q in range(PLANE):
            refs[PLANES + q // 2][z, q % 2] = refs[z][q]


def core_kernel(*refs):
    for q in range(PLANE // 2):
        for z in range(PLANES):
            for c in range(2):
                refs[PLANE // 2 + c][q, z] = refs[q][z, c]


def settle_kernel(me, near, far, out):
    for c, ref in enumerate((near, far)):
        for q in range(PLANE // 2):
            for z in range(PLANES):
                out[(z * PLANE + 2 * q + c) ^ me[0]] = ref[q, z]


def regroup(body, name, shapes, *arrays, me=(), flops=0):
    vmem = pl.BlockSpec(memory_space=pltpu.VMEM)
    size = sum(math.prod(x.shape) for x in arrays)
    return pl.pallas_call(
        body,
        out_shape=shapes,
        in_specs=[pl.BlockSpec(memory_space=pltpu.SMEM)] * len(me) + [vmem] * len(arrays),
        compiler_params=pltpu.CompilerParams(vmem_limit_bytes=16 * 1024 * 1024),
        cost_estimate=pl.CostEstimate(flops=flops, bytes_accessed=4 * size, transcendentals=0),
        name=name,
    )(*me, *arrays)


def swap(value, bits):
    pairs = [(i, i ^ bits) for i in range(BLOCKS)]
    return lax.ppermute(value, AXES, pairs)


def across_planes(parts):
    return parts[:1] + [swap(x, z * PLANE) for z, x in enumerate(parts) if z]


def in_plane(parts):
    rows = parts[0].shape[1]
    shape = jax.ShapeDtypeStruct((PLANES, 2, rows, LANES), jnp.bfloat16)
    return regroup(plane_kernel, "plane", (shape,) * (PLANE // 2), *parts, flops=LONG)


def across_chips(parts):
    return parts[:1] + tuple(swap(x, 2 * q) for q, x in enumerate(parts) if q)


def in_order(parts, me):
    rows = parts[0].shape[2]
    shape = jax.ShapeDtypeStruct((PLANE // 2, PLANES, rows, LANES), jnp.bfloat16)
    near, far = regroup(core_kernel, "core", (shape,) * 2, *parts)
    shape = jax.ShapeDtypeStruct((BLOCKS, rows, LANES), jnp.bfloat16)
    return regroup(settle_kernel, "settle", shape, near, swap(far, 1), me=(me,))


def after(values, *others):
    return lax.optimization_barrier((values, *others))[0]


def plain_products(params):
    flat = params.reshape(params.shape[0], -1)
    return dot(flat, flat, ((1,), (1,)))


def plain_weighted(gram, scale, params, scores):
    members = params.shape[0]
    norms = jnp.diagonal(gram)
    dist = norms[:, None] + norms[None, :] - 2.0 * gram
    kernel = jnp.exp(-dist / scale[0]).astype(jnp.bfloat16)
    flat = params.reshape(members, -1)
    ksum = jnp.sum(kernel.astype(jnp.float32), axis=1, keepdims=True)
    attract = dot(kernel, scores.reshape(members, -1), ((1,), (0,))) / members
    mixed = dot(kernel, flat, ((1,), (0,)))
    spread = (flat.astype(jnp.float32) * ksum - mixed) / members
    return tuple(x.astype(jnp.bfloat16).reshape(params.shape) for x in (attract, spread))


STEPS = D // EDGE
TALL = FF // STEPS


def pack_side_kernel(me, first, second, *refs):
    outs, (wide, tall, loads) = refs[:PLANES], refs[PLANES:]
    copies = [pltpu.make_async_copy(second.at[0, :, pl.ds(D - LANES, LANES)], tall, loads.at[COLS])]
    for c in range(COLS):
        here = first.at[0, :, pl.ds((c + 1) * D - LANES, LANES)]
        copies.append(pltpu.make_async_copy(here, wide.at[c], loads.at[c]))
    for copy in copies:
        copy.start()
    for copy in copies:
        copy.wait()
    more = REST - EDGE
    for k in range(BLOCKS):
        b = k ^ me[0]
        here = pl.ds(pl.multiple_of(b // COLS * EDGE + EDGE - more, TILE), more)
        outs[k // PLANE][k % PLANE, 0:more, :] = wide[b % COLS, here, :]
        here = pl.ds(pl.multiple_of(b * EDGE, EDGE), EDGE)
        outs[k // PLANE][k % PLANE, more:REST, :] = tall[here, :]


def pack_main_kernel(first, second, out, wide, tall, packed, loads, stores):
    def load(d):
        return (
            pltpu.make_async_copy(
                first.at[0, pl.ds(d * EDGE, EDGE), :], wide.at[d], loads.at[0, d]
            ),
            pltpu.make_async_copy(
                second.at[0, pl.ds(d * TALL, TALL), :], tall.at[d], loads.at[1, d]
            ),
        )

    def store(d):
        here = pl.ds(d * COLS, COLS)
        return pltpu.make_async_copy(packed.at[here], out.at[here], stores.at[d])

    for d in range(STEPS):
        for copy in load(d):
            copy.start()
    for d in range(STEPS):
        for copy in load(d):
            copy.wait()
        for c in range(COLS):
            for g in GROUPS:
                b, at, lanes = d * COLS + c, g * SIDE, g * LANES
                end = in_main(at)
                packed[b, at : at + end, :] = wide[
                    d, 0:end, c * D + lanes : c * D + lanes + LANES
                ]
                if at + EDGE < MAIN:
                    packed[b, at + EDGE : at + SIDE, :] = tall[
                        d, c * EDGE : (c + 1) * EDGE, lanes : lanes + LANES
                    ]
        store(d).start()
    for d in range(STEPS):
        store(d).wait()


def to_blocks(first, second, me):
    bf = jnp.bfloat16
    anywhere = [pl.BlockSpec(memory_space=pl.ANY)]
    params = pltpu.CompilerParams(vmem_limit_bytes=56 * 1024 * 1024)
    cost = pl.CostEstimate(flops=0, bytes_accessed=4 * D * FF, transcendentals=0)
    side = pl.pallas_call(
        pack_side_kernel,
        out_shape=side_shapes(REST),
        in_specs=[pl.BlockSpec(memory_space=pltpu.SMEM)] + anywhere * 2,
        scratch_shapes=[
            pltpu.VMEM((COLS, D, LANES), bf),
            pltpu.VMEM((FF, LANES), bf),
            pltpu.SemaphoreType.DMA((COLS + 1,)),
        ],
        compiler_params=params,
        cost_estimate=cost,
        name="pack_side",
    )(me, first, second)
    main = pl.pallas_call(
        pack_main_kernel,
        out_shape=pltpu.HBM((BLOCKS, MAIN, LANES), bf),
        in_specs=anywhere * 2,
        out_specs=anywhere[0],
        scratch_shapes=[
            pltpu.VMEM((STEPS, EDGE, FF), bf),
            pltpu.VMEM((STEPS, TALL, D), bf),
            pltpu.VMEM((BLOCKS, MAIN, LANES), bf),
            pltpu.SemaphoreType.DMA((2, STEPS)),
            pltpu.SemaphoreType.DMA((STEPS,)),
        ],
        compiler_params=params,
        cost_estimate=cost,
        name="pack_main",
    )(first, second)
    return main, side


def pieces(main, side, which, at):
    n = in_main(at)
    found = [(0, n, main, which * MAIN + at), (n, EDGE - n, side, which * REST + at + n - MAIN)]
    return [piece for piece in found if piece[1]]


def unpack_kernel(main, side, first_a, second_a, first_s, second_s, wide, tall, stores):
    def store(which, d):
        first, second = ((first_a, second_a), (first_s, second_s))[which]
        return (
            pltpu.make_async_copy(
                wide.at[which, d], first.at[0, pl.ds(d * EDGE, EDGE), :], stores.at[which, 0, d]
            ),
            pltpu.make_async_copy(
                tall.at[which, d], second.at[0, pl.ds(d * TALL, TALL), :], stores.at[which, 1, d]
            ),
        )

    for which in range(2):
        for d in range(STEPS):
            for c in range(COLS):
                for g in GROUPS:
                    b = d * COLS + c
                    lanes = slice(c * D + g * LANES, c * D + (g + 1) * LANES)
                    for row, n, ref, at in pieces(main, side, which, g * SIDE):
                        wide[which, d, row : row + n, lanes] = ref[b, at : at + n, :]
                    lanes = slice(g * LANES, (g + 1) * LANES)
                    for row, n, ref, at in pieces(main, side, which, g * SIDE + EDGE):
                        here = slice(c * EDGE + row, c * EDGE + row + n)
                        tall[which, d, here, lanes] = ref[b, at : at + n, :]
            for copy in store(which, d):
                copy.start()
    for which in range(2):
        for d in range(STEPS):
            for copy in store(which, d):
                copy.wait()


def from_blocks(main, side):
    bf = jnp.bfloat16
    return pl.pallas_call(
        unpack_kernel,
        out_shape=(pltpu.HBM((1, D, FF), bf), pltpu.HBM((1, FF, D), bf)) * 2,
        in_specs=[pl.BlockSpec(memory_space=pltpu.VMEM)] * 2,
        out_specs=(pl.BlockSpec(memory_space=pl.ANY),) * 4,
        scratch_shapes=[
            pltpu.VMEM((2, STEPS, EDGE, FF), bf),
            pltpu.VMEM((2, STEPS, TALL, D), bf),
            pltpu.SemaphoreType.DMA((2, 2, STEPS)),
        ],
        compiler_params=pltpu.CompilerParams(vmem_limit_bytes=24 * 1024 * 1024),
        cost_estimate=pl.CostEstimate(flops=0, bytes_accessed=16 * D * FF, transcendentals=0),
        name="unpack",
    )(main, side)


def exchange(blocks):
    return lax.all_to_all(blocks, AXES, split_axis=0, concat_axis=0, tiled=True)


def on_device(
    particles_first, particles_second, pool_images, pool_targets, batch_index, kernel_scale
):
    members = math.prod(lax.axis_size(name) for name in AXES)
    tiled = members == BLOCKS
    me = lax.axis_index(AXES) if tiled else 0
    me = jnp.full((1,), me, jnp.int32)
    params, side_params = to_blocks(particles_first, particles_second, me)
    first, second = particles_first[0], particles_second[0]
    if tiled:
        params = exchange(params)
        side_params = in_plane(across_planes(list(side_params)))
        first, second = after((first, second), side_params[0])
        side_params = across_chips(side_params)
    scores, *side_scores = particle_scores(
        first, second, pool_images, pool_targets, batch_index[0], me
    )
    if tiled:
        side_params = in_order(after(side_params, side_scores[0]), me)
        side_scores = across_planes(after(side_scores, params))
        packed = distances(params, side_params)
        got = [swap(packed, z * PLANE) for z in range(1, PLANES)]
        scores = exchange(scores)
        side_scores = in_plane(after(side_scores, got))
        packed = sum(got, packed)
        side_scores = in_order(across_chips(side_scores), me)
        for bits in ((2, 4, 6), (1,)):
            packed = add_over(packed, members, bits)
        mixing, *side = mix_side(kernel_scale, me, packed, side_scores, side_params)
        main = mix_main(mixing, scores, params, side_params)
        side = in_order(across_chips(in_plane(across_planes(side))), me)
        return from_blocks(exchange(main), side)
    cut = (members, BLOCKS * ROWS // members, LANES)
    params = jnp.concatenate([params, jnp.concatenate(side_params)], axis=1)
    scores = jnp.concatenate([scores, jnp.concatenate(side_scores)], axis=1)
    params, scores = exchange(params.reshape(cut)), exchange(scores.reshape(cut))
    gram = lax.psum(plain_products(params), AXES)
    parts = plain_weighted(gram, kernel_scale, params, scores)
    parts = [exchange(x).reshape(BLOCKS, ROWS, LANES) for x in parts]
    main = jnp.concatenate([x[:, :MAIN] for x in parts], axis=1)
    return from_blocks(main, jnp.concatenate([x[:, MAIN:] for x in parts], axis=1))


def solution(mesh):
    split = P(AXES, None, None)
    return jax.shard_map(
        on_device,
        mesh=mesh,
        in_specs=(split, split, P(), P(), P(AXES, None), P()),
        out_specs=(split, split, split, split),
        check_vma=False,
    )
```
